32 devices in a mesh: seq: 4 (over y, x), exp: 8 (over z, core).
Axes of the slice: x: 2, y: 2, z: 4, core: 2. Of those that a mesh axis runs over, the one named last changes fastest.
Arguments:
- x_in: bfloat16 [1024, 8192], P('seq', 'exp'), may hold values from -6 to 6
- z_gate: bfloat16 [1024, 8192], P('seq', 'exp'), may hold values from -6 to 6
- b_in: bfloat16 [1024, 128], P('seq'), may hold values from -0.52734375 to 0.52734375
- c_out: bfloat16 [1024, 128], P('seq'), may hold values from -0.375 to 0.375
- dt_step: float32 [1024, 128], P('seq', 'exp'), may hold values from 0.12 to 516, as said below
- rate: float32 [128], P('exp'), may hold values from 0 to 0.06, as said below
- skip: float32 [128], P('exp'), may hold values from 0.5 to 1.5
- init_state: float32 [128, 64, 128], P('exp'), may hold values from -8.485281 to 8.485281
- residual: bfloat16 [1024, 8192], P(('seq', 'exp')), may hold values from -6 to 6
- norm_gain: float32 [8192], replicated, may hold values from 0.5 to 1.5
- expert_ids: int32 [1024, 2], P(('seq', 'exp')), may hold values from 0 to 7, all different within a row; in each aligned block of 32 rows (0 to 31, 32 to 63, ...) at most 9 rows name the same one
- gate_weights: float32 [1024, 2], P(('seq', 'exp')), may hold values from 0.2 to 1
- w_gate: bfloat16 [8, 8192, 2048], P('exp', None, 'seq'), may hold values from -0.0625 to 0.0625
- w_up: bfloat16 [8, 8192, 2048], P('exp', None, 'seq'), may hold values from -0.0625 to 0.0625
- w_down: bfloat16 [8, 2048, 8192], P('exp', 'seq'), may hold values from -0.125 to 0.125
Outputs:
- layer_out: bfloat16 [1024, 8192], P(('seq', 'exp'))
The draws below stay inside these ranges and needn't reach their ends.
Inputs may be any that keep to these rules, and one draw needn't show every extreme that they name: `dt_step`: positive step sizes. `rate`: positive rates. `expert_ids`: each row names two different experts; among the rows of one device (aligned blocks of 32 rows) no expert is named by more than 9 rows, and in every draw some expert is named by exactly 9 rows of some block.
All inputs are finite; a program needn't handle non-finite values.
Results may differ from the reference program's by a relative error of at most 0.0095.
Values may be sent and summed in bfloat16 or wider, within the bound.
No kernel may reach another device: no remote copies, remote signals or barrier semaphores. Data moves between devices by JAX's collectives and lax.ppermute only.
A program may use at most 128 MiB of HBM per device.

```python
import math
import jax
import jax.numpy as jnp
import numpy as np
from jax import lax

D = 8192
HEADS = 128
HEAD_DIM = 64
STATE = 128
FF = 2048
GROUP = 128
TOK_SEQ = 256
TOK_DEV = 32
TOKENS = 1024
EXPERTS = 8
CAP = 9
N_SEQ = 4


def draw_dt_step(key, part):
    first, second, third = jax.random.split(key, 3)
    shards = TOKENS // TOK_SEQ
    base = jnp.exp(jax.random.uniform(first, (TOKENS, HEADS), jnp.float32, math.log(0.5), math.log(1.5)))
    level = jnp.exp(jax.random.uniform(second, (shards, 1, HEADS), jnp.float32, -0.7, 0.7))
    base = (base.reshape(shards, TOK_SEQ, HEADS) * level).reshape(TOKENS, HEADS)
    spots = jax.random.randint(third, (3,), 0, TOKENS)
    struck = jnp.any(jnp.arange(TOKENS)[:, None] == spots[None, :], axis=1)
    return base + jnp.where(struck, 0.5 * TOKENS, 0.0).astype(jnp.float32)[:, None]


def draw_rate(key, part):
    first, second, third = jax.random.split(key, 3)
    slowest = 0.5 / TOKENS
    pick = jax.random.uniform(first, (HEADS,), jnp.float32)
    slow_rate = slowest * jnp.exp(jax.random.uniform(second, (HEADS,), jnp.float32, 0.0, math.log(1.5)))
    fast_rate = jnp.exp(jax.random.uniform(third, (HEADS,), jnp.float32, math.log(1.0 / 60.0), math.log(1.0 / 20.0)))
    share = 0.5
    return jnp.where(pick < share, slow_rate, fast_rate)


def block_scale(key, extent, pieces, smallest, high):
    factor_of, own = 1.0, jax.random.fold_in(key, 6)
    for dim, shards_of in pieces:
        draws = jnp.exp(jax.random.uniform(jax.random.fold_in(own, dim), (shards_of,), jnp.float32, smallest / len(pieces), high / len(pieces)))
        factor_of = factor_of * jnp.repeat(draws, extent[dim] // shards_of).reshape([-1 if axis == dim else 1 for axis in range(len(extent))])
    return factor_of


def deal_out(stream_key, own, number, rows, amount, top, most, lean):
    sequence = jax.random.permutation(stream_key, amount)
    packed, usual = portions_of(amount, rows * top, most, lean, True), portions_of(amount, rows * top, most, lean, False)
    places = jnp.arange(amount)

    def named(tallies, rotation):
        used = int((tallies > 0).sum())
        fixed = max(1, used // 4)
        moved = fixed + (places - fixed + rotation * (used - fixed)) % max(1, amount - fixed)
        return jnp.zeros((amount,), jnp.int32).at[sequence[jnp.where(places < fixed, places, moved)]].set(jnp.asarray(tallies, jnp.int32))

    tallies = jnp.where(number % 4 == 0, named(packed, number // 4), named(usual, number - number // 4 - 1))
    mixed = jax.random.permutation(jax.random.fold_in(own, 3), amount)
    source_of, taker = mixed[0:amount // 2 * 2:2], mixed[1:amount // 2 * 2:2]
    slack = jnp.minimum(tallies[source_of] - 1, most - tallies[taker]) // 2
    slack = jnp.where((source_of == sequence[0]) | (taker == sequence[0]) | (tallies[taker] == 0), 0, jnp.maximum(slack, 0))
    moved = jax.random.randint(jax.random.fold_in(own, 4), (amount // 2,), 0, 1 << 20) % (slack + 1)
    tallies = tallies.at[source_of].add(-moved).at[taker].add(moved)
    members = jnp.searchsorted(jnp.cumsum(tallies), jnp.arange(rows * top), side="right").astype(jnp.int32)
    listing = members.reshape(top, rows).T
    listing = listing[jax.random.permutation(jax.random.fold_in(own, 1), rows)]
    rotation = jax.random.randint(jax.random.fold_in(own, 2), (rows, 1), 0, top)
    return jnp.take_along_axis(listing, (jnp.arange(top)[None, :] + rotation) % top, axis=1)


def portions_of(number_of, total, bound, slope, full):
    loads = [(1 << 20) // math.isqrt(standing ** slope) + 1 for standing in range(1, number_of + 1)]
    largest = bound if full else min(bound, max(-(-total // number_of), total * loads[0] // sum(loads)))
    least = 1 if total - largest >= number_of - 1 else 0
    counts, surplus = [largest] + [least] * (number_of - 1), total - largest - least * (number_of - 1)
    while surplus > 0:
        candidates = [i for i in range(1, number_of) if counts[i] < largest] or [i for i in range(1, number_of) if counts[i] < bound]
        pool, remaining = sum([loads[i] for i in candidates]), surplus
        for i in candidates:
            addition = min(bound - counts[i], max(1, remaining * loads[i] // pool), surplus)
            counts[i] = counts[i] + addition
            surplus = surplus - addition
    return np.array(counts)


def normal_values(rng, extent, deviation, bound, pieces=(), held_as=jnp.bfloat16):
    result = jax.random.normal(rng, extent, jnp.float32) * deviation
    if len(pieces) > 0:
        result = block_scale(rng, extent, pieces, -0.22, 0.18) * result
    return jnp.clip(result, min=-bound, max=bound).astype(held_as)


def setup_inputs(seed: int = 0) -> dict:
    key_list = jax.random.split(jax.random.key(seed), 16)
    x_in = normal_values(key_list[0], (TOKENS, D), 1.0, 6.0, ((0, 4), (1, 8)))
    z_gate = normal_values(key_list[1], (TOKENS, D), 1.0, 6.0, ((0, 4), (1, 8)))
    b_in = normal_values(key_list[2], (TOKENS, STATE), (1.0 / STATE ** 0.5), 0.52734375, ((0, 4),))
    c_out = normal_values(key_list[3], (TOKENS, STATE), (2.0 / TOKENS ** 0.5), 0.375, ((0, 4),))
    dt_step = draw_dt_step(jax.random.fold_in(key_list[15], 71), 0)
    rate = draw_rate(jax.random.fold_in(key_list[15], 71), 0)
    skip = jnp.clip(0.5 + 1.0 * jax.random.uniform(key_list[6], (HEADS,), jnp.float32) ** block_scale(key_list[6], (HEADS,), ((0, 8),), -0.2, 0.2), 0.5, 1.5)
    init_state = normal_values(key_list[7], (HEADS, HEAD_DIM, STATE), (0.5 * (TOKENS / STATE) ** 0.5), 8.485281, ((0, 8),), jnp.float32)
    residual = normal_values(key_list[8], (TOKENS, D), 1.0, 6.0, ((0, 32),))
    norm_gain = jnp.clip(1.0 + 0.1 * jax.random.normal(key_list[9], (D,), jnp.float32), 0.5, 1.5)
    expert_ids_keys = jax.random.split(jax.random.fold_in(key_list[10], 1), TOKENS // TOK_DEV)
    expert_ids_turns = jax.random.permutation(jax.random.fold_in(key_list[10], 3), TOKENS // TOK_DEV)
    expert_ids = jax.vmap(lambda own, number: deal_out(jax.random.fold_in(key_list[10], 2), own, number, TOK_DEV, EXPERTS, 2, CAP, 2))(expert_ids_keys, expert_ids_turns).reshape((TOKENS, 2))
    gate_weights = jnp.clip(0.2 + 0.8 * jax.random.uniform(key_list[11], (TOKENS, 2), jnp.float32) ** block_scale(key_list[11], (TOKENS, 2), ((0, 32),), -0.2, 0.2), 0.2, 1.0)
    w_gate = normal_values(key_list[12], (EXPERTS, D, FF), D ** -0.5, 0.0625, ((0, 8), (2, 4)))
    w_up = normal_values(key_list[13], (EXPERTS, D, FF), D ** -0.5, 0.0625, ((0, 8), (2, 4)))
    w_down = normal_values(key_list[14], (EXPERTS, FF, D), FF ** -0.5, 0.125, ((0, 8), (1, 4)))
    return dict(x_in=x_in, z_gate=z_gate, b_in=b_in, c_out=c_out, dt_step=dt_step, rate=rate, skip=skip, init_state=init_state, residual=residual, norm_gain=norm_gain, expert_ids=expert_ids, gate_weights=gate_weights, w_gate=w_gate, w_up=w_up, w_down=w_down)


PRECISE = lax.Precision.HIGHEST

def mixer_layer(x_in, z_gate, b_in, c_out, dt_step, rate, skip, init_state):
    blocks = TOKENS // GROUP
    inputs = x_in.astype(jnp.float32).reshape(blocks, GROUP, HEADS, HEAD_DIM)
    keys_in = b_in.astype(jnp.float32).reshape(blocks, GROUP, STATE)
    queries = c_out.astype(jnp.float32).reshape(blocks, GROUP, STATE)
    log_steps = (-rate[None, :] * dt_step).reshape(blocks, GROUP, HEADS)
    causal = jnp.arange(GROUP)[:, None] >= jnp.arange(GROUP)[None, :]

    def advance(state, element):
        block_in, block_keys, block_queries, block_logs = element
        cumulative = jnp.cumsum(block_logs, axis=0)
        scores = jnp.dot(block_queries, block_keys.T, precision=PRECISE)
        spread = cumulative[:, None, :] - cumulative[None, :, :]
        weights = jnp.exp(jnp.where(causal[:, :, None], spread, -jnp.inf)) * scores[:, :, None]
        intra_out = jnp.einsum('tsh,shp->thp', weights, block_in, precision=PRECISE)
        inter_out = jnp.exp(cumulative)[:, :, None] * jnp.einsum('hpn,tn->thp', state, block_queries, precision=PRECISE)
        output = intra_out + inter_out + skip[None, :, None] * block_in
        tail_decay = jnp.exp(cumulative[-1:, :] - cumulative)
        new_state = jnp.exp(cumulative[-1])[:, None, None] * state + jnp.einsum('sh,shp,sn->hpn', tail_decay, block_in, block_keys, precision=PRECISE)
        return (new_state, output)
    _, outputs = lax.scan(advance, init_state, (inputs, keys_in, queries, log_steps))
    mixed_out = outputs.reshape(TOKENS, HEADS * HEAD_DIM)
    return (mixed_out * jax.nn.silu(z_gate.astype(jnp.float32))).astype(jnp.bfloat16)

def reference(x_in, z_gate, b_in, c_out, dt_step, rate, skip, init_state, residual, norm_gain, expert_ids, gate_weights, w_gate, w_up, w_down):
    mixer = mixer_layer(x_in, z_gate, b_in, c_out, dt_step, rate, skip, init_state)
    stream = (residual.astype(jnp.float32) + mixer.astype(jnp.float32)).astype(jnp.bfloat16)
    widened = stream.astype(jnp.float32)
    normed = (widened * lax.rsqrt(lax.optimization_barrier(jnp.mean(widened * widened, axis=-1, keepdims=True)) + 1e-06) * norm_gain[None, :]).astype(jnp.bfloat16)
    blocks = TOKENS // TOK_DEV
    chosen = expert_ids.reshape(blocks, 2 * TOK_DEV).astype(jnp.int32)
    onehot = (chosen[:, :, None] == jnp.arange(EXPERTS, dtype=jnp.int32)[None, None, :]).astype(jnp.int32)
    slot_index = lax.optimization_barrier(jnp.sum((jnp.cumsum(onehot, axis=1) - onehot) * onehot, axis=2)).astype(jnp.int32)
    block_ids = jnp.arange(blocks, dtype=jnp.int32)[:, None]
    target = (chosen * (blocks * CAP) + block_ids * CAP + slot_index).reshape(-1).astype(jnp.int32)
    pair_rows = jnp.repeat(normed, 2, axis=0)
    buffers = jnp.zeros((EXPERTS * blocks * CAP, D), jnp.bfloat16).at[target].set(pair_rows)
    buffers = buffers.reshape(EXPERTS, blocks * CAP, D)
    width_part = FF // N_SEQ

    def run_expert(operands):
        rows_in, gate_matrix, up_matrix, down_matrix = operands
        running = jnp.zeros((rows_in.shape[0], D), jnp.float32)
        for portion in range(N_SEQ):
            first_unit = portion * width_part
            last_unit = first_unit + width_part
            gate_proj = jnp.dot(rows_in, gate_matrix[:, first_unit:last_unit], preferred_element_type=jnp.float32)
            up_proj = jnp.dot(rows_in, up_matrix[:, first_unit:last_unit], preferred_element_type=jnp.float32)
            active = (jax.nn.silu(gate_proj) * up_proj).astype(jnp.bfloat16)
            partial_value = jnp.dot(active, down_matrix[first_unit:last_unit, :], preferred_element_type=jnp.float32).astype(jnp.bfloat16)
            partial_value = lax.optimization_barrier(partial_value)
            running = running + partial_value.astype(jnp.float32)
        return running.astype(jnp.bfloat16)
    outputs = lax.map(run_expert, (buffers, w_gate, w_up, w_down))
    picked = outputs.reshape(-1, D)[target].astype(jnp.float32).reshape(TOKENS, 2, D)
    mixture = lax.optimization_barrier(jnp.sum(picked * gate_weights[:, :, None], axis=1))
    return (widened + mixture).astype(jnp.bfloat16)
```

```python
import functools

import jax
import jax.numpy as jnp
from jax import lax
from jax.experimental import pallas as pl
from jax.experimental.pallas import tpu as pltpu
from jax.sharding import PartitionSpec as P

GROUP = 128
PRECISE = lax.Precision.HIGHEST
F32 = jnp.float32
BF16 = jnp.bfloat16
MIB = 1 << 20


def spec_vmem():
    return pl.BlockSpec(memory_space=pltpu.VMEM)


def spec_smem():
    return pl.BlockSpec(memory_space=pltpu.SMEM)


def whole_call(body, outs, specs, args, flops, nbytes, scratch=(), limit=40):
    return pl.pallas_call(
        body,
        out_shape=outs,
        in_specs=specs,
        out_specs=jax.tree.map(lambda _: spec_vmem(), outs),
        scratch_shapes=list(scratch),
        compiler_params=pltpu.CompilerParams(vmem_limit_bytes=limit * MIB),
        cost_estimate=pl.CostEstimate(flops=flops, bytes_accessed=nbytes, transcendentals=0),
    )(*args)


def iota(shape, dim):
    return lax.broadcasted_iota(jnp.int32, shape, dim)


def dot(a, b, precision=None):
    return jnp.dot(a, b, precision=precision, preferred_element_type=F32)


def head_spread(heads, channels):
    shape = (heads, channels)
    return (iota(shape, 1) // (channels // heads) == iota(shape, 0)).astype(F32)


def state_kernel(place, x_ref, b_ref, dt_ref, rate_ref, init_ref, payload_ref, init_t_ref):
    tokens, channels = x_ref.shape
    heads = dt_ref.shape[1]
    width = b_ref.shape[1]
    logs = -rate_ref[...] * dt_ref[...]
    tri = (iota((tokens, tokens), 0) >= iota((tokens, tokens), 1)).astype(F32)
    cum = dot(tri, logs, PRECISE)
    total = cum[tokens - 1 : tokens, :]
    spread = head_spread(heads, channels)
    tail = dot(jnp.exp(total - cum), spread, PRECISE)
    scaled = (x_ref[...].astype(F32) * tail).astype(BF16)
    keys = b_ref[...].astype(F32).T.astype(BF16)
    own = dot(keys, scaled)
    decay = dot(jnp.broadcast_to(jnp.exp(total), (8, heads)), spread, PRECISE)
    init_t = init_ref[...].T
    init_t_ref[...] = init_t
    first = (place[0] == 0).astype(F32)
    payload_ref[0:width, :] = (own + first * (decay[0:1, :] * init_t)).astype(BF16)
    high = decay.astype(BF16).astype(F32)
    rows = iota((16, channels), 0)
    high16 = jnp.broadcast_to(high[0:1, :], (16, channels))
    low16 = jnp.broadcast_to(decay[0:1, :], (16, channels)) - high16
    payload_ref[width : width + 16, :] = jnp.where(
        rows == 0, high16, jnp.where(rows == 1, low16, 0.0)
    ).astype(BF16)


def intra_kernel(x_ref, b_ref, c_ref, dt_ref, dt_t_ref, rate_ref, rate_t_ref, skip_ref, y_ref):
    tokens, channels = x_ref.shape
    heads = dt_ref.shape[1]
    width = channels // heads
    shape = (tokens, tokens)
    causal = iota(shape, 0) >= iota(shape, 1)
    tri = causal.astype(F32)
    tri_t = (iota(shape, 0) <= iota(shape, 1)).astype(F32)
    cum = dot(tri, -rate_ref[...] * dt_ref[...], PRECISE)
    cum_t = dot(-rate_t_ref[...] * dt_t_ref[...], tri_t, PRECISE)
    scores = lax.dot_general(
        c_ref[...], b_ref[...], (((1,), (1,)), ((), ())), preferred_element_type=F32
    )
    direct = dot(
        jnp.broadcast_to(skip_ref[...], (8, heads)), head_spread(heads, channels), PRECISE
    )[0:1, :]
    per = 128 // width
    lane_head = iota((tokens, 128), 1) // width
    for group in range(heads // per):
        cols = slice(group * 128, (group + 1) * 128)
        x = x_ref[:, cols]
        total = x.astype(F32) * direct[:, cols]
        for k in range(per):
            h = group * per + k
            gap = jnp.where(causal, cum[:, h : h + 1] - cum_t[h : h + 1, :], -1e30)
            weights = (jnp.exp(gap) * scores).astype(BF16)
            part = dot(weights, x)
            total = total + jnp.where(lane_head == k, part, 0.0)
        y_ref[:, cols] = total


def place_kernel(cap, experts, ids_ref, out_ref):
    tokens = ids_ref.shape[1]
    slots = out_ref.shape[0] // experts
    blocks = slots // cap
    rows = tokens // blocks
    shape = (tokens, tokens)
    before = ((iota(shape, 0) < iota(shape, 1)) & (iota(shape, 0) // rows == iota(shape, 1) // rows))
    named = iota((experts, tokens), 0)
    hit = (ids_ref[0:1, :] == named) | (ids_ref[1:2, :] == named)
    rank = dot(hit.astype(BF16), before.astype(BF16)).astype(jnp.int32)
    block = iota((experts, tokens), 1) // rows
    whole = cap - 1
    row = jnp.where(rank < whole, block * whole + rank, blocks * whole + block)
    row = jnp.where(hit, row, -1)
    for e in range(experts):
        out_ref[e * slots : (e + 1) * slots, :] = (
            iota((slots, tokens), 0) == row[e : e + 1, :]
        ).astype(F32).astype(BF16)


def join_kernel(place, own_ref, other_ref, out_ref):
    width = out_ref.shape[0]
    odd = place[0] % 2 == 1
    own, other = own_ref[0:width, :].astype(F32), other_ref[0:width, :].astype(F32)
    own_decay = own_ref[width : width + 16, :].astype(F32)
    other_decay = other_ref[width : width + 16, :].astype(F32)
    own_decay = own_decay[0:1, :] + own_decay[1:2, :]
    other_decay = other_decay[0:1, :] + other_decay[1:2, :]
    early = jnp.where(odd, other, own)
    late = jnp.where(odd, own, other)
    decay = jnp.where(odd, own_decay, other_decay)
    out_ref[...] = (decay * early + late).astype(BF16)


def stream_kernel(
    place,
    y_ref,
    c_ref,
    dt_ref,
    rate_ref,
    init_t_ref,
    pair_ref,
    early_ref,
    z_ref,
    res_ref,
    sel_ref,
    stream_ref,
    *out_refs,
):
    tokens, channels = y_ref.shape
    heads = dt_ref.shape[1]
    width = init_t_ref.shape[0]
    at = place[0]
    zero = (at == 0).astype(F32)
    odd = (at % 2 == 1).astype(F32)
    second = at >= 2
    pair = pair_ref[...].astype(F32)
    decay = pair[width : width + 1, :] + pair[width + 1 : width + 2, :]
    factor = jnp.where(second, jnp.where(at % 2 == 1, decay, 1.0), 0.0)
    entering = zero * init_t_ref[...] + odd * pair[0:width, :] + factor * early_ref[...].astype(F32)
    tri = (iota((tokens, tokens), 0) >= iota((tokens, tokens), 1)).astype(F32)
    cum = dot(tri, -rate_ref[...] * dt_ref[...], PRECISE)
    fade = dot(jnp.exp(cum), head_spread(heads, channels), PRECISE)
    mixed = y_ref[...] + fade * dot(c_ref[...], entering.astype(BF16))
    z = z_ref[...].astype(F32)
    mixer = (mixed * (z / (1.0 + jnp.exp(-z)))).astype(BF16).astype(F32)
    stream = (res_ref[...].astype(F32) + mixer).astype(BF16)
    stream_ref[...] = stream
    laid = dot(sel_ref[...], stream).astype(BF16)
    count = len(out_refs)
    part = channels // count
    slots = out_refs[0].shape[1]
    for k, out in enumerate(out_refs):
        for e in range(out.shape[0]):
            out[e] = laid[e * slots : (e + 1) * slots, k * part : (k + 1) * part]


def up_kernel(first, last, *refs):
    own, rx, ry, d0, d1, gain, wg, wu = refs[:8]
    rest = refs[8:]
    if first:
        carry = None
    else:
        carry, rest = rest[:3], rest[3:]
    if last:
        outs, scratch = rest[:1], rest[1:]
    else:
        outs, scratch = rest[:3], rest[3:]
    gate, up, square = scratch
    step = pl.program_id(0)
    steps = pl.num_programs(0)

    @pl.when(step == 0)
    def _():
        for i, acc in enumerate((gate, up, square)):
            acc[...] = jnp.zeros_like(acc) if first else carry[i][...]

    far = jnp.where(step < steps // 2, d0[0].astype(F32), d1[0].astype(F32))
    rows = jnp.concatenate([own[0].astype(F32), rx[0].astype(F32), ry[0].astype(F32), far], axis=0)
    square[...] += jnp.broadcast_to(jnp.sum(rows * rows, axis=1, keepdims=True), square.shape)
    scaled = (rows * gain[0]).astype(BF16)
    gate[...] += dot(scaled, wg[0])
    up[...] += dot(scaled, wu[0])

    @pl.when(step == steps - 1)
    def _():
        if last:
            features = gain.shape[2] * steps * last
            inverse = lax.rsqrt(square[:, 0:1] * (1.0 / features) + 1e-06)
            g = gate[...] * inverse
            outs[0][...] = (g / (1.0 + jnp.exp(-g)) * (up[...] * inverse)).astype(BF16)
        else:
            for out, acc in zip(outs, (gate, up, square)):
                out[...] = acc[...]


def up_project(chunk, chunks, pieces, gain, w_gate, w_up, carry):
    own, rx, ry, d0, d1 = pieces
    steps, slots, part = own.shape
    half = d0.shape[0]
    hidden = w_gate.shape[2]
    total = 4 * slots
    last = chunk == chunks - 1
    row = lambda index: pl.BlockSpec((1, slots, part), lambda x: (index(x), 0, 0))
    weight = pl.BlockSpec((1, part, hidden), lambda x: (x, chunk, 0))
    specs = [
        row(lambda x: x),
        row(lambda x: x),
        row(lambda x: x),
        row(lambda x: jnp.minimum(x, half - 1)),
        row(lambda x: jnp.maximum(x - half, 0)),
        pl.BlockSpec((1, 1, part), lambda x: (x, 0, chunk)),
        weight,
        weight,
    ]
    sums = [
        jax.ShapeDtypeStruct((total, hidden), F32),
        jax.ShapeDtypeStruct((total, hidden), F32),
        jax.ShapeDtypeStruct((total, 128), F32),
    ]
    fixed = lambda s: pl.BlockSpec(s.shape, lambda x: (0, 0))
    if carry is not None:
        specs += [fixed(s) for s in sums]
    outs = [jax.ShapeDtypeStruct((total, hidden), BF16)] if last else sums
    return pl.pallas_call(
        functools.partial(up_kernel, carry is None, chunks if last else 0),
        grid=(steps,),
        out_shape=outs,
        in_specs=specs,
        out_specs=[fixed(s) for s in outs],
        scratch_shapes=[pltpu.VMEM(s.shape, s.dtype) for s in sums],
        compiler_params=pltpu.CompilerParams(vmem_limit_bytes=40 * MIB),
        cost_estimate=pl.CostEstimate(
            flops=4 * total * steps * part * hidden,
            bytes_accessed=4 * steps * part * hidden,
            transcendentals=0,
        ),
    )(own, rx, ry, d0, d1, gain, w_gate, w_up, *(carry or ()))


def down_kernel(act_ref, w_ref, own_ref, x_ref, y_ref, d_ref):
    slots = own_ref.shape[1]
    part = dot(act_ref[...], w_ref[...])
    for k, out in enumerate((own_ref, x_ref, y_ref, d_ref)):
        out[0] = part[k * slots : (k + 1) * slots, :].astype(BF16)


def down_project(chunk, chunks, active, w_down):
    total, hidden = active.shape
    slots = total // 4
    wide = w_down.shape[1] // chunks
    tile = wide // 4
    out = jax.ShapeDtypeStruct((2, slots, wide // 2), BF16)
    return pl.pallas_call(
        down_kernel,
        grid=(4,),
        out_shape=[out] * 4,
        in_specs=[
            pl.BlockSpec((total, hidden), lambda i: (0, 0)),
            pl.BlockSpec((hidden, tile), lambda i: (0, chunk * 4 + i)),
        ],
        out_specs=[pl.BlockSpec((1, slots, tile), lambda i: (i // 2, 0, i % 2))] * 4,
        compiler_params=pltpu.CompilerParams(vmem_limit_bytes=40 * MIB),
        cost_estimate=pl.CostEstimate(
            flops=2 * total * hidden * wide, bytes_accessed=2 * hidden * wide, transcendentals=0
        ),
    )(active, w_down)


def gather_sum_kernel(own_ref, xa, xb, ya, yb, out_ref, spare):
    halves, slots, half = own_ref.shape
    dests = out_ref.shape[0]
    pieces = out_ref.shape[1] - 1
    tile = out_ref.shape[3]
    for h, (vx, vy) in enumerate(((xa, ya), (xb, yb))):
        total = own_ref[h].astype(F32) + vx[...].astype(F32) + vy[...].astype(F32)
        for k in range(pieces // 2):
            piece = total[:, k * tile : (k + 1) * tile]
            col = h * (pieces // 2) + k
            for d in range(dests):
                out_ref[d, col] = piece[d * 8 : (d + 1) * 8, :].astype(BF16)
                spare[d, col : col + 1, :] = piece[dests * 8 + d : dests * 8 + d + 1, :]
    for d in range(dests):
        out_ref[d, pieces] = spare[d].astype(BF16)


def mix_kernel(ids_ref, weight_ref, stream_ref, *refs):
    parts, out_ref = refs[:-1], refs[-1]
    rows = ids_ref.shape[0]
    experts = parts[0].shape[0]
    pieces = parts[0].shape[1] - 1
    tile = parts[0].shape[3]
    named = iota((rows, experts), 1)
    first, second = ids_ref[:, 0:1] == named, ids_ref[:, 1:2] == named
    weight = jnp.where(first, weight_ref[:, 0:1], jnp.where(second, weight_ref[:, 1:2], 0.0))
    hit = (first | second).astype(F32)
    before = (iota((rows, rows), 0) > iota((rows, rows), 1)).astype(F32)
    rank = dot(before, hit)
    lanes = 2 * experts * 8
    shape = (experts, lanes)
    spread = ((iota(shape, 1) // 8) % experts == iota(shape, 0)).astype(F32)
    weight = dot(weight, spread, PRECISE)
    rank = dot(rank, spread, PRECISE).astype(jnp.int32)
    lane = iota((rows, lanes), 1)
    main = (lane < experts * 8) & (rank == lane % 8)
    extra = (lane >= experts * 8) & (rank == 8)
    for c, part in enumerate(parts):
        last = [part[e, pieces].astype(F32) for e in range(experts)]
        for k in range(pieces):
            coef = jnp.where(main | (extra & (lane % 8 == k)), weight, 0.0)
            high = coef.astype(BF16)
            low = (coef - high.astype(F32)).astype(BF16)
            data = jnp.concatenate([part[e, k].astype(F32) for e in range(experts)] + last, axis=0)
            data = data.astype(BF16)
            cols = slice((c * pieces + k) * tile, (c * pieces + k + 1) * tile)
            out_ref[:, cols] = (
                stream_ref[:, cols].astype(F32) + (dot(high, data) + dot(low, data))
            ).astype(BF16)


DISPATCH_CHUNKS = 2
RETURN_CHUNKS = 2


def on_square(
    x_in,
    z_gate,
    b_in,
    c_out,
    dt_step,
    rate,
    skip,
    init_state,
    residual,
    norm_gain,
    expert_ids,
    gate_weights,
    w_gate,
    w_up,
    w_down,
):
    tokens, channels = x_in.shape
    heads = rate.shape[0]
    state = b_in.shape[1]
    owners = lax.axis_size("exp")
    rows, features = residual.shape
    experts = owners
    cap = max(2, 2 * rows // experts + 1)
    slots = owners * cap
    at = lax.axis_index("seq")
    me = lax.axis_index("exp")
    place = jnp.reshape(at, (1,)).astype(jnp.int32)

    def over_x(v):
        return lax.ppermute(v, "seq", [(i, i ^ 1) for i in range(4)])

    def over_y(v):
        return lax.ppermute(v, "seq", [(i, i ^ 2) for i in range(4)])

    rate_row = rate[None, :]
    init_flat = init_state.reshape(channels, state)
    payload, init_t = whole_call(
        state_kernel,
        [
            jax.ShapeDtypeStruct((state + 16, channels), BF16),
            jax.ShapeDtypeStruct((state, channels), F32),
        ],
        [spec_smem()] + [spec_vmem()] * 5,
        (place, x_in, b_in, dt_step, rate_row, init_flat),
        200_000_000,
        2_000_000,
    )
    pair = over_x(payload)

    ids = expert_ids.T[None]
    bit = 1
    while bit < owners:
        other = lax.ppermute(ids, "exp", [(i, i ^ bit) for i in range(owners)])
        low = (me & bit) == 0
        ids = jnp.concatenate([jnp.where(low, ids, other), jnp.where(low, other, ids)], axis=0)
        bit *= 2
    ids = jnp.swapaxes(ids, 0, 1).reshape(2, tokens)
    res_here = lax.all_to_all(residual, "exp", split_axis=1, concat_axis=0, tiled=True)

    y = whole_call(
        intra_kernel,
        jax.ShapeDtypeStruct((tokens, channels), F32),
        [spec_vmem()] * 8,
        (x_in, b_in, c_out, dt_step, dt_step.T, rate_row, rate[:, None], skip[None, :]),
        2 * tokens * tokens * channels * 2,
        4_000_000,
    )
    select = whole_call(
        functools.partial(place_kernel, cap, experts),
        jax.ShapeDtypeStruct((experts * slots, tokens), BF16),
        [spec_vmem()],
        (ids,),
        2 * tokens * tokens * experts,
        600_000,
    )
    joined = whole_call(
        join_kernel,
        jax.ShapeDtypeStruct((state, channels), BF16),
        [spec_smem(), spec_vmem(), spec_vmem()],
        (place, payload, pair),
        1_000_000,
        800_000,
    )
    early = over_y(joined)
    part = channels // DISPATCH_CHUNKS
    stream_here, *rows_out = whole_call(
        stream_kernel,
        [jax.ShapeDtypeStruct((tokens, channels), BF16)]
        + [jax.ShapeDtypeStruct((experts, slots, part), BF16)] * DISPATCH_CHUNKS,
        [spec_smem()] + [spec_vmem()] * 10,
        (place, y, c_out, dt_step, rate_row, init_t, pair, early, z_gate, res_here, select),
        400_000_000,
        4_000_000,
    )

    gain = norm_gain.reshape(owners, 1, features // owners)
    wg = w_gate.reshape(owners, features // owners, w_gate.shape[2])
    wu = w_up.reshape(owners, features // owners, w_up.shape[2])
    carry = None
    half = owners // 2
    for chunk in range(DISPATCH_CHUNKS):
        own = lax.all_to_all(rows_out[chunk], "exp", split_axis=0, concat_axis=0, tiled=True)
        rx, ry = over_x(own), over_y(own)
        d0, d1 = over_y(rx[:half]), over_x(ry[half:])
        carry = up_project(chunk, DISPATCH_CHUNKS, (own, rx, ry, d0, d1), gain, wg, wu, carry)
    active = carry[0]
    stream = lax.all_to_all(stream_here, "exp", split_axis=0, concat_axis=1, tiled=True)

    wd = w_down.reshape(w_down.shape[1], features)
    back = []
    for chunk in range(RETURN_CHUNKS):
        own, px, py, pd = down_project(chunk, RETURN_CHUNKS, active, wd)
        to_y, to_x = over_x(pd[0]), over_y(pd[1])
        xa, yb = over_x(px[0]), over_y(py[1])
        xb = over_x((px[1].astype(F32) + to_x.astype(F32)).astype(BF16))
        ya = over_y((py[0].astype(F32) + to_y.astype(F32)).astype(BF16))
        wide = features // RETURN_CHUNKS
        laid = whole_call(
            gather_sum_kernel,
            jax.ShapeDtypeStruct((owners, cap, 8, wide // 8), BF16),
            [spec_vmem()] * 5,
            (own, xa, xb, ya, yb),
            1_000_000,
            6 * slots * wide,
            scratch=[pltpu.VMEM((owners, 8, wide // 8), F32)],
        )
        back.append(lax.all_to_all(laid, "exp", split_axis=0, concat_axis=0, tiled=True))
    return whole_call(
        mix_kernel,
        jax.ShapeDtypeStruct((rows, features), BF16),
        [spec_vmem()] * (3 + RETURN_CHUNKS),
        (expert_ids, gate_weights, stream, *back),
        100_000_000,
        3_000_000,
    )


def entering_2(array, axis, combine, identity):
    devices, mine = (lax.axis_size(axis), lax.axis_index(axis))
    everything = jax.tree.map(
        lambda part, kind: lax.all_gather(part.astype(kind), axis),
        array,
        (jnp.bfloat16, jnp.bfloat16),
    )
    start = jax.tree.map(
        lambda part, zero: jnp.broadcast_to(jnp.asarray(zero, part.dtype), part.shape),
        array,
        identity,
    )

    def hop(k, before):
        reached = k < mine
        new = combine(
            before, jax.tree.map(lambda part, own: part[k].astype(own.dtype), everything, array)
        )
        return jax.tree.map(lambda a, b: jnp.where(reached, a, b), new, before)

    return lax.fori_loop(0, devices, hop, start)


def chain_combine(earlier, later):
    return (earlier[0] + later[0], jnp.exp(later[0])[:, None, None] * earlier[1] + later[1])


def on_device(
    x_in,
    z_gate,
    b_in,
    c_out,
    dt_step,
    rate,
    skip,
    init_state,
    residual,
    norm_gain,
    expert_ids,
    gate_weights,
    w_gate,
    w_up,
    w_down,
):
    token_count, channels = x_in.shape
    heads_here = rate.shape[0]
    head_width = channels // heads_here
    state_width = b_in.shape[1]
    blocks = token_count // GROUP
    inputs = x_in.astype(jnp.float32).reshape(blocks, GROUP, heads_here, head_width)
    keys_in = b_in.astype(jnp.float32).reshape(blocks, GROUP, state_width)
    queries = c_out.astype(jnp.float32).reshape(blocks, GROUP, state_width)
    log_steps = (-rate[None, :] * dt_step).reshape(blocks, GROUP, heads_here)
    cumulative = jnp.cumsum(log_steps, axis=1)
    scores = jnp.einsum("ctn,csn->cts", queries, keys_in, precision=PRECISE)
    causal = jnp.arange(GROUP)[:, None] >= jnp.arange(GROUP)[None, :]
    spread = cumulative[:, :, None, :] - cumulative[:, None, :, :]
    weights = jnp.exp(jnp.where(causal[None, :, :, None], spread, -jnp.inf)) * scores[..., None]
    intra_out = jnp.einsum("ctsh,cshp->cthp", weights, inputs, precision=PRECISE)
    tail_decay = jnp.exp(cumulative[:, -1:, :] - cumulative)
    block_state = jnp.einsum("csh,cshp,csn->chpn", tail_decay, inputs, keys_in, precision=PRECISE)
    block_log = cumulative[:, -1, :]

    def advance(carried, element):
        total_log, total_state = carried
        step_log, step_state = element
        updated = (
            total_log + step_log,
            jnp.exp(step_log)[:, None, None] * total_state + step_state,
        )
        return (updated, (total_log, total_state))

    zero_state = jnp.zeros((heads_here, head_width, state_width), jnp.float32)
    zero_log = jnp.zeros((heads_here,), jnp.float32)
    (device_log, device_state), (enter_log, enter_state) = lax.scan(
        advance, (zero_log, zero_state), (block_log, block_state)
    )
    prior_log, prior_state = entering_2(
        (device_log, device_state), "seq", chain_combine, (zero_log, zero_state)
    )
    incoming = prior_state + jnp.exp(prior_log)[:, None, None] * init_state
    entering = enter_state + jnp.exp(enter_log)[:, :, None, None] * incoming[None]
    inter_out = jnp.exp(cumulative)[..., None] * jnp.einsum(
        "chpn,ctn->cthp", entering, queries, precision=PRECISE
    )
    mixed_out = (intra_out + inter_out + skip[None, None, :, None] * inputs).reshape(
        token_count, channels
    )
    mixer = (mixed_out * jax.nn.silu(z_gate.astype(jnp.float32))).astype(jnp.bfloat16)
    token_mix = lax.all_to_all(mixer, "exp", split_axis=0, concat_axis=1, tiled=True)
    stream = (residual.astype(jnp.float32) + token_mix.astype(jnp.float32)).astype(jnp.bfloat16)
    widened = stream.astype(jnp.float32)
    normed = (
        widened
        * lax.rsqrt(jnp.mean(widened * widened, axis=-1, keepdims=True) + 1e-06)
        * norm_gain[None, :]
    ).astype(jnp.bfloat16)
    rows_here = residual.shape[0]
    owners = lax.axis_size("exp")
    local_experts = w_gate.shape[0]
    experts = owners * local_experts
    capacity = max(2, 2 * rows_here // experts + 1)
    width = residual.shape[1]
    chosen = expert_ids.reshape(-1)
    onehot = (chosen[:, None] == jnp.arange(experts)[None, :]).astype(jnp.int32)
    slot_index = jnp.sum((jnp.cumsum(onehot, axis=0) - onehot) * onehot, axis=1)
    target = chosen * capacity + slot_index
    placing = (target[None, :] == jnp.arange(experts * capacity)[:, None]).astype(jnp.bfloat16)
    pair_rows = jnp.repeat(normed, 2, axis=0)
    outgoing = jnp.dot(placing, pair_rows, preferred_element_type=jnp.float32).astype(jnp.bfloat16)
    outgoing = outgoing.reshape(owners, local_experts, 1, capacity, width)
    arrived = lax.all_to_all(outgoing, "exp", split_axis=0, concat_axis=2, tiled=True)
    segment = lax.all_gather(arrived, "seq", axis=1, tiled=True)
    flattened = segment.reshape(segment.shape[0], -1, segment.shape[-1])
    gate_proj = jnp.einsum("erd,edf->erf", flattened, w_gate, preferred_element_type=jnp.float32)
    up_proj = jnp.einsum("erd,edf->erf", flattened, w_up, preferred_element_type=jnp.float32)
    active = (jax.nn.silu(gate_proj) * up_proj).astype(jnp.bfloat16)
    partial_value = jnp.einsum("erf,efd->erd", active, w_down, preferred_element_type=jnp.float32)
    partials = partial_value.reshape(segment.shape[:-1] + (partial_value.shape[-1],))
    summed = lax.psum_scatter(partials.astype(jnp.bfloat16), "seq", scatter_dimension=1, tiled=True)
    returned = lax.all_to_all(summed, "exp", split_axis=2, concat_axis=0, tiled=True)
    results = returned.reshape(experts * capacity, width)
    picked = results[target].astype(jnp.float32).reshape(rows_here, 2, width)
    mixture = jnp.sum(picked * gate_weights[:, :, None], axis=1)
    return (widened + mixture).astype(jnp.bfloat16)


def solution(mesh):
    square = mesh.shape["seq"] == 4 and mesh.shape["exp"] == 8

    def body(*args):
        rows = args[8].shape[0]
        experts = mesh.shape["exp"] * args[12].shape[0]
        fits = args[12].shape[0] == 1 and 2 * rows // experts + 1 == 9
        return (on_square if square and fits else on_device)(*args)

    return jax.shard_map(
        body,
        mesh=mesh,
        in_specs=(
            P("seq", "exp"),
            P("seq", "exp"),
            P("seq", None),
            P("seq", None),
            P("seq", "exp"),
            P("exp"),
            P("exp"),
            P("exp", None, None),
            P(("seq", "exp"), None),
            P(),
            P(("seq", "exp"), None),
            P(("seq", "exp"), None),
            P("exp", None, "seq"),
            P("exp", None, "seq"),
            P("exp", "seq", None),
        ),
        out_specs=P(("seq", "exp"), None),
        check_vma=False,
    )
```

```python
import functools

import jax
import jax.numpy as jnp
from jax import lax
from jax.experimental import pallas as pl
from jax.experimental.pallas import tpu as pltpu
from jax.sharding import PartitionSpec as P

GROUP = 128
PRECISE = lax.Precision.HIGHEST
F32 = jnp.float32
BF16 = jnp.bfloat16
MIB = 1 << 20


def block_call(body, outs, scalars, args, flops, nbytes, limit=48):
    whole = lambda v: pl.BlockSpec(v.shape, lambda i, *_: (0,) * len(v.shape))
    return pl.pallas_call(
        body,
        out_shape=outs,
        grid_spec=pltpu.PrefetchScalarGridSpec(
            num_scalar_prefetch=scalars,
            grid=(1,),
            in_specs=[whole(v) for v in args[scalars:]],
            out_specs=[whole(v) for v in outs],
        ),
        compiler_params=pltpu.CompilerParams(vmem_limit_bytes=limit * MIB),
        cost_estimate=pl.CostEstimate(flops=flops, bytes_accessed=nbytes, transcendentals=0),
    )(*args)


def iota(shape, dim):
    return lax.broadcasted_iota(jnp.int32, shape, dim)


def dot(a, b, precision=None):
    return jnp.dot(a, b, precision=precision, preferred_element_type=F32)


def head_spread(heads, channels):
    shape = (heads, channels)
    return (iota(shape, 1) // (channels // heads) == iota(shape, 0)).astype(F32)


def running_logs(dt_t_ref, rate_ref):
    logs = -rate_ref[...] * dt_t_ref[...].T
    tokens = logs.shape[0]
    tri = (iota((tokens, tokens), 0) >= iota((tokens, tokens), 1)).astype(F32)
    return dot(tri, logs, PRECISE)


def state_kernel(place, x_ref, b_ref, dt_t_ref, rate_ref, init_ref, payload_ref, init_t_ref):
    tokens, channels = x_ref.shape
    heads = dt_t_ref.shape[0]
    width = b_ref.shape[1]
    cum = running_logs(dt_t_ref, rate_ref)
    total = cum[tokens - 1 : tokens, :]
    spread = head_spread(heads, channels)
    tail = dot(jnp.exp(total - cum), spread, PRECISE)
    scaled = (x_ref[...].astype(F32) * tail).astype(BF16)
    keys = b_ref[...].astype(F32).T.astype(BF16)
    own = dot(keys, scaled)
    decay = dot(jnp.broadcast_to(jnp.exp(total), (8, heads)), spread, PRECISE)
    init_t = init_ref[...].T
    init_t_ref[...] = init_t
    first = (place[0] == 0).astype(F32)
    payload_ref[0:width, :] = (own + first * (decay[0:1, :] * init_t)).astype(BF16)
    high = decay.astype(BF16).astype(F32)
    rows = iota((16, channels), 0)
    high16 = jnp.broadcast_to(high[0:1, :], (16, channels))
    low16 = jnp.broadcast_to(decay[0:1, :], (16, channels)) - high16
    payload_ref[width : width + 16, :] = jnp.where(
        rows == 0, high16, jnp.where(rows == 1, low16, 0.0)
    ).astype(BF16)


def intra_kernel(x_ref, z_ref, b_ref, c_ref, dt_t_ref, rate_ref, skip_ref, own_ref, fade_ref):
    tokens, channels = x_ref.shape
    heads = dt_t_ref.shape[0]
    width = channels // heads
    shape = (tokens, tokens)
    causal = iota(shape, 0) >= iota(shape, 1)
    cum = running_logs(dt_t_ref, rate_ref)
    cum_t = cum.T
    scores = lax.dot_general(
        c_ref[...], b_ref[...], (((1,), (1,)), ((), ())), preferred_element_type=F32
    )
    spread = head_spread(heads, channels)
    direct = dot(jnp.broadcast_to(skip_ref[...], (8, heads)), spread, PRECISE)[0:1, :]
    fade = dot(jnp.exp(cum), spread, PRECISE)
    per = 128 // width
    lane_head = iota((tokens, 128), 1) // width
    for group in range(heads // per):
        cols = slice(group * 128, (group + 1) * 128)
        x = x_ref[:, cols]
        total = x.astype(F32) * direct[:, cols]
        for k in range(per):
            h = group * per + k
            gap = jnp.where(causal, cum[:, h : h + 1] - cum_t[h : h + 1, :], -1e30)
            weights = (jnp.exp(gap) * scores).astype(BF16)
            part = dot(weights, x)
            total = total + jnp.where(lane_head == k, part, 0.0)
        z = z_ref[:, cols].astype(F32)
        gate = z / (1.0 + jnp.exp(-z))
        own_ref[:, cols] = total * gate
        fade_ref[:, cols] = fade[:, cols] * gate


def place_kernel(cap, experts, me, ids_ref, out_ref):
    tokens = ids_ref.shape[1]
    slots = out_ref.shape[1]
    blocks = slots // cap
    rows = tokens // blocks
    shape = (tokens, tokens)
    before = (iota(shape, 0) < iota(shape, 1)) & (iota(shape, 0) // rows == iota(shape, 1) // rows)
    named = iota((experts, tokens), 0) ^ me[0]
    hit = (ids_ref[0:1, :] == named) | (ids_ref[1:2, :] == named)
    rank = dot(hit.astype(BF16), before.astype(BF16)).astype(jnp.int32)
    block = (iota((experts, tokens), 1) // rows) ^ named
    whole = cap - 1
    row = jnp.where(rank < whole, block * whole + rank, blocks * whole + block)
    row = jnp.where(hit, row, -1)
    for e in range(experts):
        out_ref[e] = (iota((slots, tokens), 0) == row[e : e + 1, :]).astype(F32).astype(BF16)


def join_kernel(place, own_ref, other_ref, out_ref):
    width = out_ref.shape[0]
    odd = place[0] % 2 == 1
    own, other = own_ref[0:width, :].astype(F32), other_ref[0:width, :].astype(F32)
    own_decay = own_ref[width : width + 16, :].astype(F32)
    other_decay = other_ref[width : width + 16, :].astype(F32)
    own_decay = own_decay[0:1, :] + own_decay[1:2, :]
    other_decay = other_decay[0:1, :] + other_decay[1:2, :]
    early = jnp.where(odd, other, own)
    late = jnp.where(odd, own, other)
    decay = jnp.where(odd, own_decay, other_decay)
    out_ref[...] = (decay * early + late).astype(BF16)


def stream_kernel(
    place, own_ref, fade_ref, c_ref, init_t_ref, pair_ref, early_ref, res_ref, sel_ref, stream_ref, *out_refs
):
    width = init_t_ref.shape[0]
    at = place[0]
    zero = (at == 0).astype(F32)
    odd = (at % 2 == 1).astype(F32)
    pair = pair_ref[...].astype(F32)
    decay = pair[width : width + 1, :] + pair[width + 1 : width + 2, :]
    factor = jnp.where(at >= 2, jnp.where(at % 2 == 1, decay, 1.0), 0.0)
    entering = zero * init_t_ref[...] + odd * pair[0:width, :] + factor * early_ref[...].astype(F32)
    mixed = own_ref[...] + fade_ref[...] * dot(c_ref[...], entering.astype(BF16))
    mixer = mixed.astype(BF16).astype(F32)
    stream = (res_ref[...].astype(F32) + mixer).astype(BF16)
    stream_ref[...] = stream
    for m, out in enumerate(out_refs):
        out[...] = dot(sel_ref[m], stream).astype(BF16)


def up_kernel(first, last, me, *refs):
    own, rx, ry, far, gain, wg, wu = refs[:7]
    rest = refs[7:]
    if first:
        carry = None
    else:
        carry, rest = rest[:3], rest[3:]
    if last:
        outs, scratch = rest[:2], rest[2:]
    else:
        outs, scratch = rest[:3], rest[3:]
    gate, up, square = scratch
    step = pl.program_id(0)
    steps = pl.num_programs(0)

    @pl.when(step == 0)
    def _():
        for i, acc in enumerate((gate, up, square)):
            acc[...] = jnp.zeros_like(acc) if first else carry[i][...]

    rows = jnp.concatenate([r[0].astype(F32) for r in (own, rx, ry, far)], axis=0)
    square[...] += jnp.broadcast_to(jnp.sum(rows * rows, axis=1, keepdims=True), square.shape)
    scaled = (rows * gain[0]).astype(BF16)
    gate[...] += dot(scaled, wg[0])
    up[...] += dot(scaled, wu[0])

    @pl.when(step == steps - 1)
    def _():
        if last:
            features = last
            inverse = lax.rsqrt(square[:, 0:1] * (1.0 / features) + 1e-06)
            g = gate[...] * inverse
            active = g / (1.0 + jnp.exp(-g)) * (up[...] * inverse)
            slots = own.shape[1]
            main = slots // 9 * 8
            near, far_rows = [], []
            for d in range(4):
                at = d * slots
                near += [active[at : at + main // 2], active[at + main : at + slots]]
                far_rows += [active[at + main // 2 : at + slots]]
            outs[0][...] = jnp.concatenate(near, axis=0).astype(BF16)
            outs[1][...] = jnp.concatenate(far_rows, axis=0).astype(BF16)
        else:
            for out, acc in zip(outs, (gate, up, square)):
                out[...] = acc[...]


def up_project(group, last, me, pieces, gain, w_gate, w_up, carry):
    two, slots, part = pieces[0].shape
    cut = 2
    tile = part // cut
    hidden = w_gate.shape[2]
    total = 4 * slots
    source = lambda i, me: me[0] ^ (2 * group + i // cut)
    row = pl.BlockSpec((1, slots, tile), lambda i, me: (i // cut, 0, i % cut))
    weight = pl.BlockSpec((1, tile, hidden), lambda i, me: (source(i, me), i % cut, 0))
    specs = [row] * 4 + [
        pl.BlockSpec((1, 1, tile), lambda i, me: (source(i, me), 0, i % cut)),
        weight,
        weight,
    ]
    sums = [
        jax.ShapeDtypeStruct((total, hidden), F32),
        jax.ShapeDtypeStruct((total, hidden), F32),
        jax.ShapeDtypeStruct((total, 128), F32),
    ]
    fixed = lambda s: pl.BlockSpec(s.shape, lambda i, me: (0, 0))
    if carry is not None:
        specs += [fixed(s) for s in sums]
    main = slots // 9 * 8
    outs = [jax.ShapeDtypeStruct((4 * (slots - main // 2), hidden), BF16)] * 2 if last else sums
    return pl.pallas_call(
        functools.partial(up_kernel, carry is None, gain.shape[0] * part if last else 0),
        out_shape=outs,
        grid_spec=pltpu.PrefetchScalarGridSpec(
            num_scalar_prefetch=1,
            grid=(two * cut,),
            in_specs=specs,
            out_specs=[fixed(s) for s in outs],
            scratch_shapes=[pltpu.VMEM(s.shape, s.dtype) for s in sums],
        ),
        compiler_params=pltpu.CompilerParams(vmem_limit_bytes=48 * MIB),
        cost_estimate=pl.CostEstimate(
            flops=4 * total * two * part * hidden,
            bytes_accessed=4 * two * part * hidden,
            transcendentals=0,
        ),
    )(me, *pieces, gain, w_gate, w_up, *(carry or ()))


def down_kernel(first, act_ref, w_ref, *refs):
    outs, spare = refs[:-1], refs[-1]
    step = pl.program_id(0)
    part = dot(act_ref[...], w_ref[...])
    stride = part.shape[0] // 4

    def target(place, shard):
        own, sx, sy, kx, ky = outs[place // 2 * 5 : place // 2 * 5 + 5]
        odd = place % 2
        if shard == 0:
            return own.at[odd]
        if shard == 1:
            return kx if odd else sx.at[1]
        if shard == 2:
            return sy.at[1] if odd else ky
        return sy.at[0] if odd else sx.at[0]

    for shard in range(4):
        for place in range(4):
            at = shard * stride + place * 8
            target(place, shard)[step] = part[at : at + 8, :].astype(BF16)
            at = shard * stride + 32 + first + place
            spare[shard, place, pl.ds(step, 1), :] = part[at : at + 1, :]

    @pl.when(step == pl.num_programs(0) - 1)
    def _():
        for shard in range(4):
            for place in range(4):
                target(place, shard)[8] = spare[shard, place].astype(BF16)


def down_project(first, active, w_down):
    total, hidden = active.shape
    features = w_down.shape[1]
    tile = features // 8
    piece = (9, 8, tile)
    outs = []
    for _ in range(2):
        outs += [jax.ShapeDtypeStruct((2,) + piece, BF16)] * 3 + [jax.ShapeDtypeStruct(piece, BF16)] * 2
    zeros = {3: lambda i: (0, 0, 0), 4: lambda i: (0, 0, 0, 0)}
    return pl.pallas_call(
        functools.partial(down_kernel, first),
        grid=(8,),
        out_shape=outs,
        in_specs=[
            pl.BlockSpec((total, hidden), lambda i: (0, 0)),
            pl.BlockSpec((hidden, tile), lambda i: (0, i)),
        ],
        out_specs=[pl.BlockSpec(o.shape, zeros[len(o.shape)]) for o in outs],
        scratch_shapes=[pltpu.VMEM((4, 4, 8, tile), F32)],
        compiler_params=pltpu.CompilerParams(vmem_limit_bytes=48 * MIB),
        cost_estimate=pl.CostEstimate(
            flops=2 * total * hidden * features,
            bytes_accessed=2 * hidden * features,
            transcendentals=0,
        ),
    )(active, w_down)


def relay_kernel(kx, ky, rx, ry, out_x, out_y):
    out_x[...] = (kx[...].astype(F32) + ry[0].astype(F32)).astype(BF16)
    out_y[...] = (ky[...].astype(F32) + rx[0].astype(F32)).astype(BF16)


def finish_kernel(own, rx, ry, last_x, last_y, even, odd):
    even[...] = (own[0].astype(F32) + rx[1].astype(F32) + last_y[...].astype(F32)).astype(BF16)
    odd[...] = (own[1].astype(F32) + ry[1].astype(F32) + last_x[...].astype(F32)).astype(BF16)


def mix_kernel(me, ids_t_ref, weight_t_ref, stream_ref, *refs):
    parts, out_ref = refs[:-1], refs[-1]
    rows = ids_t_ref.shape[1]
    experts = len(parts)
    pieces = parts[0].shape[0] - 1
    tile = parts[0].shape[2]
    ids, weights = ids_t_ref[...].T, weight_t_ref[...].T
    named = iota((rows, experts), 1) ^ me[0]
    first, second = ids[:, 0:1] == named, ids[:, 1:2] == named
    weight = jnp.where(first, weights[:, 0:1], jnp.where(second, weights[:, 1:2], 0.0))
    hit = (first | second).astype(F32)
    before = (iota((rows, rows), 0) > iota((rows, rows), 1)).astype(F32)
    rank = dot(before, hit)
    lanes = 2 * experts * 8
    shape = (experts, lanes)
    spread = ((iota(shape, 1) // 8) % experts == iota(shape, 0)).astype(F32)
    weight = dot(weight, spread, PRECISE)
    rank = dot(rank, spread, PRECISE).astype(jnp.int32)
    lane = iota((rows, lanes), 1)
    main = (lane < experts * 8) & (rank == lane % 8)
    extra = (lane >= experts * 8) & (rank == 8)
    last = [part[pieces].astype(F32) for part in parts]
    for k in range(pieces):
        coef = jnp.where(main | (extra & (lane % 8 == k)), weight, 0.0)
        high = coef.astype(BF16)
        low = (coef - high.astype(F32)).astype(BF16)
        data = jnp.concatenate([part[k].astype(F32) for part in parts] + last, axis=0).astype(BF16)
        cols = slice(k * tile, (k + 1) * tile)
        out_ref[:, cols] = (
            stream_ref[:, cols].astype(F32) + (dot(high, data) + dot(low, data))
        ).astype(BF16)


def on_square(
    x_in,
    z_gate,
    b_in,
    c_out,
    dt_step,
    rate,
    skip,
    init_state,
    residual,
    norm_gain,
    expert_ids,
    gate_weights,
    w_gate,
    w_up,
    w_down,
):
    tokens, channels = x_in.shape
    heads = rate.shape[0]
    state = b_in.shape[1]
    owners = lax.axis_size("exp")
    rows, features = residual.shape
    experts = owners
    cap = max(2, 2 * rows // experts + 1)
    slots = owners * cap
    at = lax.axis_index("seq")
    me = lax.axis_index("exp")
    place = jnp.reshape(at, (1,)).astype(jnp.int32)
    self_id = jnp.reshape(me, (1,)).astype(jnp.int32)

    def over_x(v):
        return lax.ppermute(v, "seq", [(i, i ^ 1) for i in range(4)])

    def over_y(v):
        return lax.ppermute(v, "seq", [(i, i ^ 2) for i in range(4)])

    def along(v, mask):
        return lax.ppermute(v, "exp", [(i, i ^ mask) for i in range(owners)])

    rate_row = rate[None, :]
    dt_t = dt_step.T
    payload, init_t = block_call(
        state_kernel,
        [
            jax.ShapeDtypeStruct((state + 16, channels), BF16),
            jax.ShapeDtypeStruct((state, channels), F32),
        ],
        1,
        (place, x_in, b_in, dt_t, rate_row, init_state.reshape(channels, state)),
        200_000_000,
        2_000_000,
    )
    pair = over_x(payload)

    ids_t = expert_ids.T
    ids = ids_t[None]
    bit = 1
    while bit < owners:
        other = along(ids, bit)
        low = (me & bit) == 0
        ids = jnp.concatenate([jnp.where(low, ids, other), jnp.where(low, other, ids)], axis=0)
        bit *= 2
    ids = jnp.swapaxes(ids, 0, 1).reshape(2, tokens)
    residual_after, _ = lax.optimization_barrier((residual, payload))
    res_here = lax.all_to_all(residual_after, "exp", split_axis=1, concat_axis=0, tiled=True)

    own_part, fade = block_call(
        intra_kernel,
        [jax.ShapeDtypeStruct((tokens, channels), F32)] * 2,
        0,
        (x_in, z_gate, b_in, c_out, dt_t, rate_row, skip[None, :]),
        2 * tokens * tokens * channels * 2,
        4_000_000,
    )
    select = block_call(
        functools.partial(place_kernel, cap, experts),
        [jax.ShapeDtypeStruct((experts, slots, tokens), BF16)],
        1,
        (self_id, ids),
        2 * tokens * tokens * experts,
        600_000,
    )[0]
    joined = block_call(
        join_kernel,
        [jax.ShapeDtypeStruct((state, channels), BF16)],
        1,
        (place, payload, pair),
        1_000_000,
        800_000,
    )[0]
    early = over_y(joined)
    stream_here, *pieces = block_call(
        stream_kernel,
        [jax.ShapeDtypeStruct((tokens, channels), BF16)]
        + [jax.ShapeDtypeStruct((slots, channels), BF16)] * experts,
        1,
        (place, own_part, fade, c_out, init_t, pair, early, res_here, select),
        400_000_000,
        4_000_000,
    )

    gain = norm_gain.reshape(owners, 1, channels)
    wg = w_gate.reshape(owners, channels, w_gate.shape[2])
    wu = w_up.reshape(owners, channels, w_up.shape[2])
    groups = owners // 2
    arrived = {0: pieces[0]}
    for mask in (1, 4, 5, 2, 3, 6, 7):
        arrived[mask] = along(pieces[mask], mask)
    carry = None
    for group in range(groups):
        own = jnp.stack([arrived[2 * group], arrived[2 * group + 1]])
        rx, ry = over_x(own), over_y(own)
        far = over_y(rx) if group % 2 == 0 else over_x(ry)
        carry = up_project(group, group == groups - 1, self_id, (own, rx, ry, far), gain, wg, wu, carry)
    active_near, active_far = carry
    stream = lax.all_to_all(stream_here, "exp", split_axis=0, concat_axis=1, tiled=True)

    wd = w_down.reshape(w_down.shape[1], features)
    piece = jax.ShapeDtypeStruct((9, 8, features // 8), BF16)
    back = [None] * owners
    for half, active in ((1, active_far), (0, active_near)):
        sent = down_project(4 * half, active, wd)
        for local in (1, 0):
            group = 2 * half + local
            own, sx, sy, kx, ky = sent[5 * local : 5 * local + 5]
            rx, ry = over_x(sx), over_y(sy)
            to_x, to_y = block_call(
                relay_kernel, [piece] * 2, 0, (kx, ky, rx, ry), 1_000_000, 1_000_000
            )
            last_x, last_y = over_x(to_x), over_y(to_y)
            even, odd = block_call(
                finish_kernel, [piece] * 2, 0, (own, rx, ry, last_x, last_y), 1_000_000, 1_500_000
            )
            back[2 * group] = along(even, 2 * group) if group else even
            back[2 * group + 1] = along(odd, 2 * group + 1)
    return block_call(
        mix_kernel,
        [jax.ShapeDtypeStruct((rows, features), BF16)],
        1,
        (self_id, ids_t, gate_weights.T, stream, *back),
        100_000_000,
        3_000_000,
    )[0]


def entering_2(array, axis, combine, identity):
    devices, mine = (lax.axis_size(axis), lax.axis_index(axis))
    everything = jax.tree.map(
        lambda part, kind: lax.all_gather(part.astype(kind), axis),
        array,
        (jnp.bfloat16, jnp.bfloat16),
    )
    start = jax.tree.map(
        lambda part, zero: jnp.broadcast_to(jnp.asarray(zero, part.dtype), part.shape),
        array,
        identity,
    )

    def hop(k, before):
        reached = k < mine
        new = combine(
            before, jax.tree.map(lambda part, own: part[k].astype(own.dtype), everything, array)
        )
        return jax.tree.map(lambda a, b: jnp.where(reached, a, b), new, before)

    return lax.fori_loop(0, devices, hop, start)


def chain_combine(earlier, later):
    return (earlier[0] + later[0], jnp.exp(later[0])[:, None, None] * earlier[1] + later[1])


def on_device(
    x_in,
    z_gate,
    b_in,
    c_out,
    dt_step,
    rate,
    skip,
    init_state,
    residual,
    norm_gain,
    expert_ids,
    gate_weights,
    w_gate,
    w_up,
    w_down,
):
    token_count, channels = x_in.shape
    heads_here = rate.shape[0]
    head_width = channels // heads_here
    state_width = b_in.shape[1]
    blocks = token_count // GROUP
    inputs = x_in.astype(jnp.float32).reshape(blocks, GROUP, heads_here, head_width)
    keys_in = b_in.astype(jnp.float32).reshape(blocks, GROUP, state_width)
    queries = c_out.astype(jnp.float32).reshape(blocks, GROUP, state_width)
    log_steps = (-rate[None, :] * dt_step).reshape(blocks, GROUP, heads_here)
    cumulative = jnp.cumsum(log_steps, axis=1)
    scores = jnp.einsum("ctn,csn->cts", queries, keys_in, precision=PRECISE)
    causal = jnp.arange(GROUP)[:, None] >= jnp.arange(GROUP)[None, :]
    spread = cumulative[:, :, None, :] - cumulative[:, None, :, :]
    weights = jnp.exp(jnp.where(causal[None, :, :, None], spread, -jnp.inf)) * scores[..., None]
    intra_out = jnp.einsum("ctsh,cshp->cthp", weights, inputs, precision=PRECISE)
    tail_decay = jnp.exp(cumulative[:, -1:, :] - cumulative)
    block_state = jnp.einsum("csh,cshp,csn->chpn", tail_decay, inputs, keys_in, precision=PRECISE)
    block_log = cumulative[:, -1, :]

    def advance(carried, element):
        total_log, total_state = carried
        step_log, step_state = element
        updated = (
            total_log + step_log,
            jnp.exp(step_log)[:, None, None] * total_state + step_state,
        )
        return (updated, (total_log, total_state))

    zero_state = jnp.zeros((heads_here, head_width, state_width), jnp.float32)
    zero_log = jnp.zeros((heads_here,), jnp.float32)
    (device_log, device_state), (enter_log, enter_state) = lax.scan(
        advance, (zero_log, zero_state), (block_log, block_state)
    )
    prior_log, prior_state = entering_2(
        (device_log, device_state), "seq", chain_combine, (zero_log, zero_state)
    )
    incoming = prior_state + jnp.exp(prior_log)[:, None, None] * init_state
    entering = enter_state + jnp.exp(enter_log)[:, :, None, None] * incoming[None]
    inter_out = jnp.exp(cumulative)[..., None] * jnp.einsum(
        "chpn,ctn->cthp", entering, queries, precision=PRECISE
    )
    mixed_out = (intra_out + inter_out + skip[None, None, :, None] * inputs).reshape(
        token_count, channels
    )
    mixer = (mixed_out * jax.nn.silu(z_gate.astype(jnp.float32))).astype(jnp.bfloat16)
    token_mix = lax.all_to_all(mixer, "exp", split_axis=0, concat_axis=1, tiled=True)
    stream = (residual.astype(jnp.float32) + token_mix.astype(jnp.float32)).astype(jnp.bfloat16)
    widened = stream.astype(jnp.float32)
    normed = (
        widened
        * lax.rsqrt(jnp.mean(widened * widened, axis=-1, keepdims=True) + 1e-06)
        * norm_gain[None, :]
    ).astype(jnp.bfloat16)
    rows_here = residual.shape[0]
    owners = lax.axis_size("exp")
    local_experts = w_gate.shape[0]
    experts = owners * local_experts
    capacity = max(2, 2 * rows_here // experts + 1)
    width = residual.shape[1]
    chosen = expert_ids.reshape(-1)
    onehot = (chosen[:, None] == jnp.arange(experts)[None, :]).astype(jnp.int32)
    slot_index = jnp.sum((jnp.cumsum(onehot, axis=0) - onehot) * onehot, axis=1)
    target = chosen * capacity + slot_index
    placing = (target[None, :] == jnp.arange(experts * capacity)[:, None]).astype(jnp.bfloat16)
    pair_rows = jnp.repeat(normed, 2, axis=0)
    outgoing = jnp.dot(placing, pair_rows, preferred_element_type=jnp.float32).astype(jnp.bfloat16)
    outgoing = outgoing.reshape(owners, local_experts, 1, capacity, width)
    arrived = lax.all_to_all(outgoing, "exp", split_axis=0, concat_axis=2, tiled=True)
    segment = lax.all_gather(arrived, "seq", axis=1, tiled=True)
    flattened = segment.reshape(segment.shape[0], -1, segment.shape[-1])
    gate_proj = jnp.einsum("erd,edf->erf", flattened, w_gate, preferred_element_type=jnp.float32)
    up_proj = jnp.einsum("erd,edf->erf", flattened, w_up, preferred_element_type=jnp.float32)
    active = (jax.nn.silu(gate_proj) * up_proj).astype(jnp.bfloat16)
    partial_value = jnp.einsum("erf,efd->erd", active, w_down, preferred_element_type=jnp.float32)
    partials = partial_value.reshape(segment.shape[:-1] + (partial_value.shape[-1],))
    summed = lax.psum_scatter(partials.astype(jnp.bfloat16), "seq", scatter_dimension=1, tiled=True)
    returned = lax.all_to_all(summed, "exp", split_axis=2, concat_axis=0, tiled=True)
    results = returned.reshape(experts * capacity, width)
    picked = results[target].astype(jnp.float32).reshape(rows_here, 2, width)
    mixture = jnp.sum(picked * gate_weights[:, :, None], axis=1)
    return (widened + mixture).astype(jnp.bfloat16)


def solution(mesh):
    square = mesh.shape["seq"] == 4 and mesh.shape["exp"] == 8

    def body(*args):
        rows = args[8].shape[0]
        experts = mesh.shape["exp"] * args[12].shape[0]
        fits = args[12].shape[0] == 1 and 2 * rows // experts + 1 == 9
        return (on_square if square and fits else on_device)(*args)

    return jax.shard_map(
        body,
        mesh=mesh,
        in_specs=(
            P("seq", "exp"),
            P("seq", "exp"),
            P("seq", None),
            P("seq", None),
            P("seq", "exp"),
            P("exp"),
            P("exp"),
            P("exp", None, None),
            P(("seq", "exp"), None),
            P(),
            P(("seq", "exp"), None),
            P(("seq", "exp"), None),
            P("exp", None, "seq"),
            P("exp", None, "seq"),
            P("exp", "seq", None),
        ),
        out_specs=P(("seq", "exp"), None),
        check_vma=False,
    )
```

```python
import functools

import jax
import jax.numpy as jnp
from jax import lax
from jax.experimental import pallas as pl
from jax.experimental.pallas import tpu as pltpu
from jax.sharding import PartitionSpec as P

GROUP = 128
PRECISE = lax.Precision.HIGHEST
F32 = jnp.float32
BF16 = jnp.bfloat16
MIB = 1 << 20


def block_call(body, outs, scalars, args, flops, nbytes, held=0, after=(), limit=16):
    n_args = len(args)
    kept = args[scalars : scalars + held]

    def kernel(*refs):
        refs, sems = (refs[:-1], refs[-1]) if held else (refs, None)
        local = refs[len(refs) - held :] if held else ()
        inputs, results = refs[:n_args], refs[n_args + len(after) : len(refs) - held]
        remote = inputs[scalars : scalars + held]
        copies = [
            pltpu.make_async_copy(src, dst, sems.at[k]) for k, (src, dst) in enumerate(zip(remote, local))
        ]
        for copy in copies:
            copy.start()
        for copy in copies:
            copy.wait()
        body(*inputs[:scalars], *local, *inputs[scalars + held :], *results)

    scratch = [pltpu.VMEM(v.shape, v.dtype) for v in kept]
    if held:
        scratch.append(pltpu.SemaphoreType.DMA((held,)))
    return pl.pallas_call(
        kernel,
        out_shape=outs,
        in_specs=[pl.BlockSpec(memory_space=pltpu.SMEM)] * scalars
        + [pl.BlockSpec(memory_space=pltpu.HBM)] * held
        + [pl.BlockSpec(memory_space=pltpu.VMEM)] * (n_args - scalars - held)
        + [pl.BlockSpec(memory_space=pl.ANY)] * len(after),
        out_specs=[pl.BlockSpec(memory_space=pltpu.VMEM)] * len(outs),
        scratch_shapes=scratch,
        compiler_params=pltpu.CompilerParams(vmem_limit_bytes=limit * MIB),
        cost_estimate=pl.CostEstimate(flops=flops, bytes_accessed=nbytes, transcendentals=0),
    )(*args, *after)


def iota(shape, dim):
    return lax.broadcasted_iota(jnp.int32, shape, dim)


def dot(a, b, precision=None):
    return jnp.dot(a, b, precision=precision, preferred_element_type=F32)


def head_spread(heads, channels):
    shape = (heads, channels)
    return (iota(shape, 1) // (channels // heads) == iota(shape, 0)).astype(F32)


def running_logs(dt_t_ref, rate_ref):
    logs = -rate_ref[...] * dt_t_ref[...].T
    tokens = logs.shape[0]
    tri = (iota((tokens, tokens), 0) >= iota((tokens, tokens), 1)).astype(F32)
    return dot(tri, logs, PRECISE)


def pack_kernel(ids_t_ref, residual_ref, out_ref):
    parts, rows, wide = out_ref.shape
    part = wide - 128
    ids = ids_t_ref[...].astype(F32).T
    lane = iota((rows, 128), 1)
    named = jnp.where(lane == 0, ids[:, 0:1], jnp.where(lane == 1, ids[:, 1:2], 0.0)).astype(BF16)
    for k in range(parts):
        out_ref[k, :, 0:part] = residual_ref[:, k * part : (k + 1) * part]
        out_ref[k, :, part:wide] = named


def state_kernel(place, x_ref, b_ref, dt_t_ref, rate_ref, init_ref, payload_ref, init_t_ref):
    tokens, channels = x_ref.shape
    heads = dt_t_ref.shape[0]
    width = b_ref.shape[1]
    cum = running_logs(dt_t_ref, rate_ref)
    total = cum[tokens - 1 : tokens, :]
    spread = head_spread(heads, channels)
    tail = dot(jnp.exp(total - cum), spread, PRECISE)
    scaled = (x_ref[...].astype(F32) * tail).astype(BF16)
    keys = b_ref[...].astype(F32).T.astype(BF16)
    own = dot(keys, scaled)
    decay = dot(jnp.broadcast_to(jnp.exp(total), (8, heads)), spread, PRECISE)
    init_t = init_ref[...].T
    init_t_ref[...] = init_t
    first = (place[0] == 0).astype(F32)
    payload_ref[0:width, :] = (own + first * (decay[0:1, :] * init_t)).astype(BF16)
    high = decay.astype(BF16).astype(F32)
    rows = iota((16, channels), 0)
    high16 = jnp.broadcast_to(high[0:1, :], (16, channels))
    low16 = jnp.broadcast_to(decay[0:1, :], (16, channels)) - high16
    payload_ref[width : width + 16, :] = jnp.where(
        rows == 0, high16, jnp.where(rows == 1, low16, 0.0)
    ).astype(BF16)


def intra_kernel(x_ref, z_ref, b_ref, c_ref, dt_t_ref, rate_ref, skip_ref, own_ref, fade_ref):
    tokens, channels = x_ref.shape
    heads = dt_t_ref.shape[0]
    width = channels // heads
    shape = (tokens, tokens)
    causal = iota(shape, 0) >= iota(shape, 1)
    cum = running_logs(dt_t_ref, rate_ref)
    cum_t = cum.T
    scores = lax.dot_general(
        c_ref[...], b_ref[...], (((1,), (1,)), ((), ())), preferred_element_type=F32
    )
    spread = head_spread(heads, channels)
    direct = dot(jnp.broadcast_to(skip_ref[...], (8, heads)), spread, PRECISE)[0:1, :]
    fade = dot(jnp.exp(cum), spread, PRECISE)
    per = 128 // width
    lane_head = iota((tokens, 128), 1) // width
    for group in range(heads // per):
        cols = slice(group * 128, (group + 1) * 128)
        x = x_ref[:, cols]
        total = x.astype(F32) * direct[:, cols]
        for k in range(per):
            h = group * per + k
            gap = jnp.where(causal, cum[:, h : h + 1] - cum_t[h : h + 1, :], -1e30)
            weights = (jnp.exp(gap) * scores).astype(BF16)
            part = dot(weights, x)
            total = total + jnp.where(lane_head == k, part, 0.0)
        z = z_ref[:, cols].astype(F32)
        gate = z / (1.0 + jnp.exp(-z))
        own_ref[:, cols] = total * gate
        fade_ref[:, cols] = fade[:, cols] * gate


def place_kernel(cap, experts, me, packed_ref, out_ref):
    blocks, rows, wide = packed_ref.shape
    tokens = blocks * rows
    slots = out_ref.shape[1]
    ids = packed_ref[:, :, wide - 128 : wide].astype(F32).reshape(tokens, 128).T
    ids = ids[0:8, :].astype(jnp.int32)
    shape = (tokens, tokens)
    before = (iota(shape, 0) < iota(shape, 1)) & (iota(shape, 0) // rows == iota(shape, 1) // rows)
    named = iota((experts, tokens), 0) ^ me[0]
    hit = (ids[0:1, :] == named) | (ids[1:2, :] == named)
    rank = dot(hit.astype(BF16), before.astype(BF16)).astype(jnp.int32)
    block = (iota((experts, tokens), 1) // rows) ^ named
    whole = cap - 1
    row = jnp.where(rank < whole, block * whole + rank, blocks * whole + block)
    row = jnp.where(hit, row, -1)
    for e in range(experts):
        out_ref[e] = (iota((slots, tokens), 0) == row[e : e + 1, :]).astype(F32).astype(BF16)


def join_kernel(place, own_ref, other_ref, out_ref):
    width = out_ref.shape[0]
    odd = place[0] % 2 == 1
    own, other = own_ref[0:width, :].astype(F32), other_ref[0:width, :].astype(F32)
    own_decay = own_ref[width : width + 16, :].astype(F32)
    other_decay = other_ref[width : width + 16, :].astype(F32)
    own_decay = own_decay[0:1, :] + own_decay[1:2, :]
    other_decay = other_decay[0:1, :] + other_decay[1:2, :]
    early = jnp.where(odd, other, own)
    late = jnp.where(odd, own, other)
    decay = jnp.where(odd, own_decay, other_decay)
    out_ref[...] = (decay * early + late).astype(BF16)


def stream_kernel(
    place, c_ref, own_ref, fade_ref, init_t_ref, pair_ref, early_ref, res_ref, sel_ref, stream_ref, *out_refs
):
    width = init_t_ref.shape[0]
    at = place[0]
    zero = (at == 0).astype(F32)
    odd = (at % 2 == 1).astype(F32)
    pair = pair_ref[...].astype(F32)
    decay = pair[width : width + 1, :] + pair[width + 1 : width + 2, :]
    factor = jnp.where(at >= 2, jnp.where(at % 2 == 1, decay, 1.0), 0.0)
    entering = zero * init_t_ref[...] + odd * pair[0:width, :] + factor * early_ref[...].astype(F32)
    mixed = own_ref[...] + fade_ref[...] * dot(c_ref[...], entering.astype(BF16))
    mixer = mixed.astype(BF16).astype(F32)
    tokens, channels = mixer.shape
    residual = res_ref[:, :, 0:channels].astype(F32).reshape(tokens, channels)
    stream = (residual + mixer).astype(BF16)
    stream_ref[...] = stream
    for m, out in enumerate(out_refs):
        out[...] = dot(sel_ref[m], stream).astype(BF16)


def up_kernel(first, features, me, *refs):
    own, rx, ry, far, gain, wg, wu = refs[:7]
    carry = () if first else refs[7:10]
    rest = refs[7 if first else 10 :]
    sums = rest[2:] if features else rest
    gate, up, square = sums
    step = pl.program_id(0)
    steps = pl.num_programs(0)

    if first or features:

        @pl.when(step == 0)
        def _():
            for i, acc in enumerate(sums):
                acc[...] = jnp.zeros_like(acc) if first else carry[i][...]

    rows = jnp.concatenate([r[0].astype(F32) for r in (own, rx, ry, far)], axis=0)
    square[...] += jnp.broadcast_to(jnp.sum(rows * rows, axis=1, keepdims=True), square.shape)
    scaled = (rows * gain[0]).astype(BF16)
    gate[...] += dot(scaled, wg[0])
    up[...] += dot(scaled, wu[0])

    if features:

        @pl.when(step == steps - 1)
        def _():
            inverse = lax.rsqrt(square[:, 0:1] * (1.0 / features) + 1e-06)
            g = gate[...] * inverse
            active = g / (1.0 + jnp.exp(-g)) * (up[...] * inverse)
            slots, hidden = own.shape[1], active.shape[1]
            for half, out in enumerate(rest[:2]):
                for d in range(4):
                    at = d * slots + 32 * half
                    out[d * 32 : (d + 1) * 32, :] = active[at : at + 32].astype(BF16)
                    ninth = [
                        jnp.broadcast_to(active[at : at + 1], (8, hidden))
                        for at in range(d * slots + 64 + 4 * half, d * slots + 68 + 4 * half)
                    ]
                    out[128 + d * 32 : 160 + d * 32, :] = jnp.concatenate(ninth, axis=0).astype(BF16)


def up_project(group, last, me, pieces, gain, w_gate, w_up, carry):
    two, slots, part = pieces[0].shape
    cut = 2
    tile = part // cut
    hidden = w_gate.shape[2]
    total = 4 * slots
    source = lambda i, me: me[0] ^ (2 * group + i // cut)
    row = pl.BlockSpec((1, slots, tile), lambda i, me: (i // cut, 0, i % cut))
    weight = pl.BlockSpec((1, tile, hidden), lambda i, me: (source(i, me), i % cut, 0))
    in_place = pl.BlockSpec(memory_space=pltpu.VMEM)
    specs = [row] * 4 + [
        pl.BlockSpec((1, 1, tile), lambda i, me: (source(i, me), 0, i % cut)),
        weight,
        weight,
    ]
    sums = [
        jax.ShapeDtypeStruct((total, hidden), F32),
        jax.ShapeDtypeStruct((total, hidden), F32),
        jax.ShapeDtypeStruct((total, 128), F32),
    ]
    aliases = {}
    if carry is not None:
        specs += [in_place] * 3
        if not last:
            aliases = {8 + i: i for i in range(3)}
    outs = [jax.ShapeDtypeStruct((256, hidden), BF16)] * 2 if last else sums
    return pl.pallas_call(
        functools.partial(up_kernel, carry is None, gain.shape[0] * part if last else 0),
        out_shape=outs,
        grid_spec=pltpu.PrefetchScalarGridSpec(
            num_scalar_prefetch=1,
            grid=(two * cut,),
            in_specs=specs,
            out_specs=[in_place] * len(outs),
            scratch_shapes=[pltpu.VMEM(s.shape, s.dtype) for s in sums] if last else [],
        ),
        input_output_aliases=aliases,
        compiler_params=pltpu.CompilerParams(vmem_limit_bytes=40 * MIB),
        cost_estimate=pl.CostEstimate(
            flops=4 * total * two * part * hidden,
            bytes_accessed=4 * two * part * hidden,
            transcendentals=0,
        ),
    )(me, *pieces, gain, w_gate, w_up, *(carry or ()))


def down_kernel(after, act_ref, w_ref, *refs):
    outs, spare = refs[after:-1], refs[-1]
    step = pl.program_id(0)
    part = dot(act_ref[...], w_ref[...])
    main = part.shape[0] // 2

    def target(place, shard):
        own, sx, sy, kx, ky = outs[place // 2 * 5 : place // 2 * 5 + 5]
        odd = place % 2
        if shard == 0:
            return own.at[odd]
        if shard == 1:
            return kx if odd else sx.at[1]
        if shard == 2:
            return sy.at[1] if odd else ky
        return sy.at[0] if odd else sx.at[0]

    for shard in range(4):
        for place in range(4):
            at = (shard * 4 + place) * 8
            target(place, shard)[step] = part[at : at + 8, :].astype(BF16)
    ninth = part[main:, :]
    spare[...] = jnp.where(iota(ninth.shape, 0) % 8 == step, ninth, spare[...])

    @pl.when(step == pl.num_programs(0) - 1)
    def _():
        for shard in range(4):
            for place in range(4):
                at = (shard * 4 + place) * 8
                target(place, shard)[8] = spare[at : at + 8, :].astype(BF16)


def down_project(active, w_down, after=()):
    total, hidden = active.shape
    features = w_down.shape[1]
    tile = features // 8
    piece = (9, 8, tile)
    outs = []
    for _ in range(2):
        outs += [jax.ShapeDtypeStruct((2,) + piece, BF16)] * 3 + [jax.ShapeDtypeStruct(piece, BF16)] * 2
    return pl.pallas_call(
        functools.partial(down_kernel, len(after)),
        grid=(8,),
        out_shape=outs,
        in_specs=[
            pl.BlockSpec(memory_space=pltpu.VMEM),
            pl.BlockSpec((hidden, tile), lambda i: (0, i)),
        ]
        + [pl.BlockSpec(memory_space=pl.ANY)] * len(after),
        out_specs=[pl.BlockSpec(memory_space=pltpu.VMEM)] * len(outs),
        scratch_shapes=[pltpu.VMEM((total // 2, tile), F32)],
        compiler_params=pltpu.CompilerParams(vmem_limit_bytes=40 * MIB),
        cost_estimate=pl.CostEstimate(
            flops=2 * total * hidden * features,
            bytes_accessed=2 * hidden * features,
            transcendentals=0,
        ),
    )(active, w_down, *after)


def stack_kernel(a, b, out):
    out[0] = a[...]
    out[1] = b[...]


def relay_kernel(kx, ky, rx, ry, out_x, out_y):
    out_x[...] = (kx[...].astype(F32) + ry[0].astype(F32)).astype(BF16)
    out_y[...] = (ky[...].astype(F32) + rx[0].astype(F32)).astype(BF16)


def finish_kernel(own, rx, ry, last_x, last_y, even, odd):
    even[...] = (own[0].astype(F32) + rx[1].astype(F32) + last_y[...].astype(F32)).astype(BF16)
    odd[...] = (own[1].astype(F32) + ry[1].astype(F32) + last_x[...].astype(F32)).astype(BF16)


def mix_kernel(me, ids_t_ref, weight_t_ref, stream_ref, *refs):
    parts, out_ref = refs[:-1], refs[-1]
    rows = ids_t_ref.shape[1]
    experts = len(parts)
    pieces = parts[0].shape[0] - 1
    tile = parts[0].shape[2]
    ids, weights = ids_t_ref[...].T, weight_t_ref[...].T
    named = iota((rows, experts), 1) ^ me[0]
    first, second = ids[:, 0:1] == named, ids[:, 1:2] == named
    weight = jnp.where(first, weights[:, 0:1], jnp.where(second, weights[:, 1:2], 0.0))
    hit = (first | second).astype(F32)
    before = (iota((rows, rows), 0) > iota((rows, rows), 1)).astype(F32)
    rank = dot(before, hit)
    lanes = 2 * experts * 8
    shape = (experts, lanes)
    spread = ((iota(shape, 1) // 8) % experts == iota(shape, 0)).astype(F32)
    weight = dot(weight, spread, PRECISE)
    rank = dot(rank, spread, PRECISE).astype(jnp.int32)
    lane = iota((rows, lanes), 1)
    main = (lane < experts * 8) & (rank == lane % 8)
    extra = (lane >= experts * 8) & (rank == 8)
    last = [part[pieces].astype(F32) for part in parts]
    for k in range(pieces):
        coef = jnp.where(main | (extra & (lane % 8 == k)), weight, 0.0)
        high = coef.astype(BF16)
        low = (coef - high.astype(F32)).astype(BF16)
        data = jnp.concatenate([part[k].astype(F32) for part in parts] + last, axis=0).astype(BF16)
        cols = slice(k * tile, (k + 1) * tile)
        out_ref[:, cols] = (
            stream_ref[k].astype(F32) + (dot(high, data) + dot(low, data))
        ).astype(BF16)


def on_square(
    x_in,
    z_gate,
    b_in,
    c_out,
    dt_step,
    rate,
    skip,
    init_state,
    residual,
    norm_gain,
    expert_ids,
    gate_weights,
    w_gate,
    w_up,
    w_down,
):
    tokens, channels = x_in.shape
    heads = rate.shape[0]
    state = b_in.shape[1]
    owners = lax.axis_size("exp")
    rows, features = residual.shape
    experts = owners
    cap = max(2, 2 * rows // experts + 1)
    slots = owners * cap
    at = lax.axis_index("seq")
    me = lax.axis_index("exp")
    place = jnp.reshape(at, (1,)).astype(jnp.int32)
    self_id = jnp.reshape(me, (1,)).astype(jnp.int32)

    def over_x(v):
        return lax.ppermute(v, "seq", [(i, i ^ 1) for i in range(4)])

    def over_y(v):
        return lax.ppermute(v, "seq", [(i, i ^ 2) for i in range(4)])

    def along(v, mask):
        return lax.ppermute(v, "exp", [(i, i ^ mask) for i in range(owners)])

    rate_row = rate[None, :]
    dt_t = dt_step.T
    ids_t = expert_ids.T
    packed = block_call(
        pack_kernel,
        [jax.ShapeDtypeStruct((owners, rows, channels + 128), BF16)],
        0,
        (ids_t, residual),
        0,
        1_000_000,
        held=2,
    )[0]
    packed = lax.all_to_all(packed, "exp", split_axis=0, concat_axis=0, tiled=True)
    payload, init_t = block_call(
        state_kernel,
        [
            jax.ShapeDtypeStruct((state + 16, channels), BF16),
            jax.ShapeDtypeStruct((state, channels), F32),
        ],
        1,
        (place, x_in, b_in, dt_t, rate_row, init_state.reshape(channels, state)),
        200_000_000,
        2_000_000,
        held=5,
    )
    pair = over_x(payload)
    own_part, fade = block_call(
        intra_kernel,
        [jax.ShapeDtypeStruct((tokens, channels), F32)] * 2,
        0,
        (x_in, z_gate, b_in, c_out, dt_t, rate_row, skip[None, :]),
        2 * tokens * tokens * channels * 2,
        4_000_000,
        held=7,
        after=(payload,),
    )
    joined = block_call(
        join_kernel,
        [jax.ShapeDtypeStruct((state, channels), BF16)],
        1,
        (place, payload, pair),
        1_000_000,
        800_000,
        after=(own_part,),
    )[0]
    early = over_y(joined)
    select = block_call(
        functools.partial(place_kernel, cap, experts),
        [jax.ShapeDtypeStruct((experts, slots, tokens), BF16)],
        1,
        (self_id, packed),
        2 * tokens * tokens * experts,
        600_000,
        after=(joined,),
    )[0]
    stream_here, *pieces = block_call(
        stream_kernel,
        [jax.ShapeDtypeStruct((tokens, channels), BF16)]
        + [jax.ShapeDtypeStruct((slots, channels), BF16)] * experts,
        1,
        (place, c_out, own_part, fade, init_t, pair, early, packed, select),
        400_000_000,
        4_000_000,
        held=1,
    )

    gain = norm_gain.reshape(owners, 1, channels)
    wg = w_gate.reshape(owners, channels, w_gate.shape[2])
    wu = w_up.reshape(owners, channels, w_up.shape[2])
    groups = owners // 2
    arrived = {0: pieces[0]}
    for mask in (1, 4, 5, 2, 3, 6, 7):
        arrived[mask] = along(pieces[mask], mask)
    carry = None
    seen = {}
    for group in range(groups):
        after = {2: ("rx0", "ry1"), 3: ("sum0",)}.get(group, ())
        own = block_call(
            stack_kernel,
            [jax.ShapeDtypeStruct((2, slots, channels), BF16)],
            0,
            (arrived[2 * group], arrived[2 * group + 1]),
            0,
            600_000,
            after=[seen[k] for k in after],
        )[0]
        rx, ry = over_x(own), over_y(own)
        far = over_y(rx) if group % 2 == 0 else over_x(ry)
        carry = up_project(group, group == groups - 1, self_id, (own, rx, ry, far), gain, wg, wu, carry)
        seen.update({f"rx{group}": rx, f"ry{group}": ry, f"sum{group}": carry[0]})
    active_near, active_far = carry

    wd = w_down.reshape(w_down.shape[1], features)
    piece = jax.ShapeDtypeStruct((9, 8, features // 8), BF16)
    back = [None] * owners
    sums = {}

    def relay(group, sent, after=()):
        own, sx, sy, kx, ky = sent
        rx, ry = over_x(sx), over_y(sy)
        to_x, to_y = block_call(
            relay_kernel, [piece] * 2, 0, (kx, ky, rx, ry), 1_000_000, 1_000_000, after=after
        )
        return own, rx, ry, over_x(to_x), over_y(to_y), to_x

    def finish(group, own, rx, ry, last_x, last_y, _):
        even, odd = block_call(
            finish_kernel, [piece] * 2, 0, (own, rx, ry, last_x, last_y), 1_000_000, 1_500_000
        )
        back[2 * group] = along(even, 2 * group) if group else even
        back[2 * group + 1] = along(odd, 2 * group + 1)
        return even

    sent = down_project(active_far, wd)
    third, second = relay(3, sent[5:]), relay(2, sent[:5])
    sent = down_project(active_near, wd, after=(third[-1], second[-1]))
    done = (finish(3, *third), finish(2, *second))
    first, zeroth = relay(1, sent[5:], done), relay(0, sent[:5], done)
    finish(1, *first)
    finish(0, *zeroth)
    stream = lax.all_to_all(
        stream_here.reshape(owners, rows, channels), "exp", split_axis=0, concat_axis=0, tiled=True
    )
    return block_call(
        mix_kernel,
        [jax.ShapeDtypeStruct((rows, features), BF16)],
        1,
        (self_id, ids_t, gate_weights.T, stream, *back),
        100_000_000,
        3_000_000,
    )[0]


def entering_2(array, axis, combine, identity):
    devices, mine = (lax.axis_size(axis), lax.axis_index(axis))
    everything = jax.tree.map(
        lambda part, kind: lax.all_gather(part.astype(kind), axis),
        array,
        (jnp.bfloat16, jnp.bfloat16),
    )
    start = jax.tree.map(
        lambda part, zero: jnp.broadcast_to(jnp.asarray(zero, part.dtype), part.shape),
        array,
        identity,
    )

    def hop(k, before):
        reached = k < mine
        new = combine(
            before, jax.tree.map(lambda part, own: part[k].astype(own.dtype), everything, array)
        )
        return jax.tree.map(lambda a, b: jnp.where(reached, a, b), new, before)

    return lax.fori_loop(0, devices, hop, start)


def chain_combine(earlier, later):
    return (earlier[0] + later[0], jnp.exp(later[0])[:, None, None] * earlier[1] + later[1])


def on_device(
    x_in,
    z_gate,
    b_in,
    c_out,
    dt_step,
    rate,
    skip,
    init_state,
    residual,
    norm_gain,
    expert_ids,
    gate_weights,
    w_gate,
    w_up,
    w_down,
):
    token_count, channels = x_in.shape
    heads_here = rate.shape[0]
    head_width = channels // heads_here
    state_width = b_in.shape[1]
    blocks = token_count // GROUP
    inputs = x_in.astype(jnp.float32).reshape(blocks, GROUP, heads_here, head_width)
    keys_in = b_in.astype(jnp.float32).reshape(blocks, GROUP, state_width)
    queries = c_out.astype(jnp.float32).reshape(blocks, GROUP, state_width)
    log_steps = (-rate[None, :] * dt_step).reshape(blocks, GROUP, heads_here)
    cumulative = jnp.cumsum(log_steps, axis=1)
    scores = jnp.einsum("ctn,csn->cts", queries, keys_in, precision=PRECISE)
    causal = jnp.arange(GROUP)[:, None] >= jnp.arange(GROUP)[None, :]
    spread = cumulative[:, :, None, :] - cumulative[:, None, :, :]
    weights = jnp.exp(jnp.where(causal[None, :, :, None], spread, -jnp.inf)) * scores[..., None]
    intra_out = jnp.einsum("ctsh,cshp->cthp", weights, inputs, precision=PRECISE)
    tail_decay = jnp.exp(cumulative[:, -1:, :] - cumulative)
    block_state = jnp.einsum("csh,cshp,csn->chpn", tail_decay, inputs, keys_in, precision=PRECISE)
    block_log = cumulative[:, -1, :]

    def advance(carried, element):
        total_log, total_state = carried
        step_log, step_state = element
        updated = (
            total_log + step_log,
            jnp.exp(step_log)[:, None, None] * total_state + step_state,
        )
        return (updated, (total_log, total_state))

    zero_state = jnp.zeros((heads_here, head_width, state_width), jnp.float32)
    zero_log = jnp.zeros((heads_here,), jnp.float32)
    (device_log, device_state), (enter_log, enter_state) = lax.scan(
        advance, (zero_log, zero_state), (block_log, block_state)
    )
    prior_log, prior_state = entering_2(
        (device_log, device_state), "seq", chain_combine, (zero_log, zero_state)
    )
    incoming = prior_state + jnp.exp(prior_log)[:, None, None] * init_state
    entering = enter_state + jnp.exp(enter_log)[:, :, None, None] * incoming[None]
    inter_out = jnp.exp(cumulative)[..., None] * jnp.einsum(
        "chpn,ctn->cthp", entering, queries, precision=PRECISE
    )
    mixed_out = (intra_out + inter_out + skip[None, None, :, None] * inputs).reshape(
        token_count, channels
    )
    mixer = (mixed_out * jax.nn.silu(z_gate.astype(jnp.float32))).astype(jnp.bfloat16)
    token_mix = lax.all_to_all(mixer, "exp", split_axis=0, concat_axis=1, tiled=True)
    stream = (residual.astype(jnp.float32) + token_mix.astype(jnp.float32)).astype(jnp.bfloat16)
    widened = stream.astype(jnp.float32)
    normed = (
        widened
        * lax.rsqrt(jnp.mean(widened * widened, axis=-1, keepdims=True) + 1e-06)
        * norm_gain[None, :]
    ).astype(jnp.bfloat16)
    rows_here = residual.shape[0]
    owners = lax.axis_size("exp")
    local_experts = w_gate.shape[0]
    experts = owners * local_experts
    capacity = max(2, 2 * rows_here // experts + 1)
    width = residual.shape[1]
    chosen = expert_ids.reshape(-1)
    onehot = (chosen[:, None] == jnp.arange(experts)[None, :]).astype(jnp.int32)
    slot_index = jnp.sum((jnp.cumsum(onehot, axis=0) - onehot) * onehot, axis=1)
    target = chosen * capacity + slot_index
    placing = (target[None, :] == jnp.arange(experts * capacity)[:, None]).astype(jnp.bfloat16)
    pair_rows = jnp.repeat(normed, 2, axis=0)
    outgoing = jnp.dot(placing, pair_rows, preferred_element_type=jnp.float32).astype(jnp.bfloat16)
    outgoing = outgoing.reshape(owners, local_experts, 1, capacity, width)
    arrived = lax.all_to_all(outgoing, "exp", split_axis=0, concat_axis=2, tiled=True)
    segment = lax.all_gather(arrived, "seq", axis=1, tiled=True)
    flattened = segment.reshape(segment.shape[0], -1, segment.shape[-1])
    gate_proj = jnp.einsum("erd,edf->erf", flattened, w_gate, preferred_element_type=jnp.float32)
    up_proj = jnp.einsum("erd,edf->erf", flattened, w_up, preferred_element_type=jnp.float32)
    active = (jax.nn.silu(gate_proj) * up_proj).astype(jnp.bfloat16)
    partial_value = jnp.einsum("erf,efd->erd", active, w_down, preferred_element_type=jnp.float32)
    partials = partial_value.reshape(segment.shape[:-1] + (partial_value.shape[-1],))
    summed = lax.psum_scatter(partials.astype(jnp.bfloat16), "seq", scatter_dimension=1, tiled=True)
    returned = lax.all_to_all(summed, "exp", split_axis=2, concat_axis=0, tiled=True)
    results = returned.reshape(experts * capacity, width)
    picked = results[target].astype(jnp.float32).reshape(rows_here, 2, width)
    mixture = jnp.sum(picked * gate_weights[:, :, None], axis=1)
    return (widened + mixture).astype(jnp.bfloat16)


def solution(mesh):
    square = mesh.shape["seq"] == 4 and mesh.shape["exp"] == 8

    def body(*args):
        rows = args[8].shape[0]
        experts = mesh.shape["exp"] * args[12].shape[0]
        fits = args[12].shape[0] == 1 and 2 * rows // experts + 1 == 9
        return (on_square if square and fits else on_device)(*args)

    return jax.shard_map(
        body,
        mesh=mesh,
        in_specs=(
            P("seq", "exp"),
            P("seq", "exp"),
            P("seq", None),
            P("seq", None),
            P("seq", "exp"),
            P("exp"),
            P("exp"),
            P("exp", None, None),
            P(("seq", "exp"), None),
            P(),
            P(("seq", "exp"), None),
            P(("seq", "exp"), None),
            P("exp", None, "seq"),
            P("exp", None, "seq"),
            P("exp", "seq", None),
        ),
        out_specs=P(("seq", "exp"), None),
        check_vma=False,
    )
```

```python
import functools

import jax
import jax.numpy as jnp
from jax import lax
from jax.experimental import pallas as pl
from jax.experimental.pallas import tpu as pltpu
from jax.sharding import PartitionSpec as P

GROUP = 128
PRECISE = lax.Precision.HIGHEST
F32 = jnp.float32
BF16 = jnp.bfloat16
MIB = 1 << 20
NO_COST = pl.CostEstimate(flops=0, bytes_accessed=0, transcendentals=0)


def block_call(body, outs, scalars, args, held=0, after=(), limit=16, out_blocks=False, name=None):
    n_args = len(args)
    kept = args[scalars : scalars + held]

    def kernel(*refs):
        refs, sems = (refs[:-1], refs[-1]) if held else (refs, None)
        local = refs[len(refs) - held :] if held else ()
        inputs, results = refs[:n_args], refs[n_args + len(after) : len(refs) - held]
        remote = inputs[scalars : scalars + held]
        copies = [
            pltpu.make_async_copy(src, dst, sems.at[k]) for k, (src, dst) in enumerate(zip(remote, local))
        ]
        for copy in copies:
            copy.start()
        for copy in copies:
            copy.wait()
        body(*inputs[:scalars], *local, *inputs[scalars + held :], *results)

    scratch = [pltpu.VMEM(v.shape, v.dtype) for v in kept]
    if held:
        scratch.append(pltpu.SemaphoreType.DMA((held,)))
    return pl.pallas_call(
        kernel,
        name=name or getattr(body, "func", body).__name__,
        out_shape=outs,
        in_specs=[pl.BlockSpec(memory_space=pltpu.SMEM)] * scalars
        + [pl.BlockSpec(memory_space=pltpu.HBM)] * held
        + [pl.BlockSpec(memory_space=pltpu.VMEM)] * (n_args - scalars - held)
        + [pl.BlockSpec(memory_space=pl.ANY)] * len(after),
        out_specs=[pl.BlockSpec() if out_blocks else pl.BlockSpec(memory_space=pltpu.VMEM)] * len(outs),
        scratch_shapes=scratch,
        compiler_params=pltpu.CompilerParams(vmem_limit_bytes=limit * MIB),
        cost_estimate=NO_COST,
    )(*args, *after)


def iota(shape, dim):
    return lax.broadcasted_iota(jnp.int32, shape, dim)


def dot(a, b, precision=None):
    return jnp.dot(a, b, precision=precision, preferred_element_type=F32)


def head_spread(heads, channels):
    shape = (heads, channels)
    return (iota(shape, 1) // (channels // heads) == iota(shape, 0)).astype(F32)


def running_logs(dt_t_ref, rate_ref):
    logs = -rate_ref[...] * dt_t_ref[...].T
    tokens = logs.shape[0]
    tri = (iota((tokens, tokens), 0) >= iota((tokens, tokens), 1)).astype(F32)
    return dot(tri, logs, PRECISE)


def pack_kernel(ids_t_ref, residual_ref, out_ref):
    parts, rows, wide = out_ref.shape
    part = wide - 128
    ids = ids_t_ref[...].astype(F32).T
    lane = iota((rows, 128), 1)
    named = jnp.where(lane == 0, ids[:, 0:1], jnp.where(lane == 1, ids[:, 1:2], 0.0)).astype(BF16)
    for k in range(parts):
        out_ref[k, :, 0:part] = residual_ref[:, k * part : (k + 1) * part]
        out_ref[k, :, part:wide] = named


def state_kernel(place, x_ref, b_ref, dt_t_ref, rate_ref, init_ref, payload_ref, init_t_ref):
    tokens, channels = x_ref.shape
    heads = dt_t_ref.shape[0]
    width = b_ref.shape[1]
    cum = running_logs(dt_t_ref, rate_ref)
    total = cum[tokens - 1 : tokens, :]
    spread = head_spread(heads, channels)
    tail = dot(jnp.exp(total - cum), spread, PRECISE)
    scaled = (x_ref[...].astype(F32) * tail).astype(BF16)
    keys = b_ref[...].astype(F32).T.astype(BF16)
    own = dot(keys, scaled)
    decay = dot(jnp.broadcast_to(jnp.exp(total), (8, heads)), spread, PRECISE)
    init_t = init_ref[...].T
    init_t_ref[...] = init_t.astype(BF16)
    first = (place[0] == 0).astype(F32)
    payload_ref[0:width, :] = (own + first * (decay[0:1, :] * init_t)).astype(BF16)
    high = decay.astype(BF16).astype(F32)
    rows = iota((16, channels), 0)
    high16 = jnp.broadcast_to(high[0:1, :], (16, channels))
    low16 = jnp.broadcast_to(decay[0:1, :], (16, channels)) - high16
    payload_ref[width : width + 16, :] = jnp.where(
        rows == 0, high16, jnp.where(rows == 1, low16, 0.0)
    ).astype(BF16)


def intra_kernel(x_ref, z_ref, b_ref, c_ref, dt_t_ref, rate_ref, skip_ref, own_ref, fade_ref):
    tokens, channels = x_ref.shape
    heads = dt_t_ref.shape[0]
    width = channels // heads
    shape = (tokens, tokens)
    causal = iota(shape, 0) >= iota(shape, 1)
    cum = running_logs(dt_t_ref, rate_ref)
    cum_t = cum.T
    scores = lax.dot_general(
        c_ref[...], b_ref[...], (((1,), (1,)), ((), ())), preferred_element_type=F32
    )
    spread = head_spread(heads, channels)
    direct = dot(jnp.broadcast_to(skip_ref[...], (8, heads)), spread, PRECISE)[0:1, :]
    fade = dot(jnp.exp(cum), spread, PRECISE)
    per = 128 // width
    lane_head = iota((tokens, 128), 1) // width
    for group in range(heads // per):
        cols = slice(group * 128, (group + 1) * 128)
        x = x_ref[:, cols]
        total = x.astype(F32) * direct[:, cols]
        for k in range(per):
            h = group * per + k
            gap = jnp.where(causal, cum[:, h : h + 1] - cum_t[h : h + 1, :], -1e30)
            weights = (jnp.exp(gap) * scores).astype(BF16)
            part = dot(weights, x)
            total = total + jnp.where(lane_head == k, part, 0.0)
        z = z_ref[:, cols].astype(F32)
        gate = z / (1.0 + jnp.exp(-z))
        own_ref[:, cols] = total * gate
        fade_ref[:, cols] = fade[:, cols] * gate


def place_kernel(cap, experts, me, packed_ref, out_ref):
    blocks, rows, wide = packed_ref.shape
    tokens = blocks * rows
    slots = out_ref.shape[1]
    ids = packed_ref[:, :, wide - 128 : wide].astype(F32).reshape(tokens, 128).T
    ids = ids[0:8, :].astype(jnp.int32)
    shape = (tokens, tokens)
    before = (iota(shape, 0) < iota(shape, 1)) & (iota(shape, 0) // rows == iota(shape, 1) // rows)
    named = iota((experts, tokens), 0) ^ me[0]
    hit = (ids[0:1, :] == named) | (ids[1:2, :] == named)
    rank = dot(hit.astype(BF16), before.astype(BF16)).astype(jnp.int32)
    block = (iota((experts, tokens), 1) // rows) ^ named
    whole = cap - 1
    row = jnp.where(rank < whole, block * whole + rank, blocks * whole + block)
    row = jnp.where(hit, row, -1)
    for e in range(experts):
        out_ref[e] = (iota((slots, tokens), 0) == row[e : e + 1, :]).astype(F32).astype(BF16)


def join_kernel(place, own_ref, other_ref, out_ref):
    width = out_ref.shape[0]
    odd = place[0] % 2 == 1
    own, other = own_ref[0:width, :].astype(F32), other_ref[0:width, :].astype(F32)
    own_decay = own_ref[width : width + 16, :].astype(F32)
    other_decay = other_ref[width : width + 16, :].astype(F32)
    own_decay = own_decay[0:1, :] + own_decay[1:2, :]
    other_decay = other_decay[0:1, :] + other_decay[1:2, :]
    early = jnp.where(odd, other, own)
    late = jnp.where(odd, own, other)
    decay = jnp.where(odd, own_decay, other_decay)
    out_ref[...] = (decay * early + late).astype(BF16)


def stream_kernel(
    place, c_ref, own_ref, fade_ref, init_t_ref, pair_ref, early_ref, res_ref, sel_ref, stream_ref, same_ref, other_ref
):
    width = init_t_ref.shape[0]
    at = place[0]
    zero = (at == 0).astype(F32)
    odd = (at % 2 == 1).astype(F32)
    pair = pair_ref[...].astype(F32)
    decay = pair[width : width + 1, :] + pair[width + 1 : width + 2, :]
    factor = jnp.where(at >= 2, jnp.where(at % 2 == 1, decay, 1.0), 0.0)
    entering = zero * init_t_ref[...].astype(F32) + odd * pair[0:width, :] + factor * early_ref[...].astype(F32)
    mixed = own_ref[...] + fade_ref[...] * dot(c_ref[...], entering.astype(BF16))
    mixer = mixed.astype(BF16).astype(F32)
    tokens, channels = mixer.shape
    residual = res_ref[:, :, 0:channels].astype(F32).reshape(tokens, channels)
    stream = (residual + mixer).astype(BF16)
    stream_ref[...] = stream
    for k in range(same_ref.shape[0]):
        same_ref[k] = dot(sel_ref[2 * k], stream).astype(BF16)
        other_ref[k] = dot(sel_ref[2 * k + 1], stream).astype(BF16)


def up_kernel(first, features, me, *refs):
    own, rx, ry, far, gain, wg, wu = refs[:7]
    carry = () if first else refs[7:10]
    rest = refs[7 if first else 10 :]
    sums = rest[1:] if features else rest
    gate, up, square = sums
    step = pl.program_id(0)
    steps = pl.num_programs(0)

    if first or features:

        @pl.when(step == 0)
        def _():
            for i, acc in enumerate(sums):
                acc[...] = jnp.zeros_like(acc) if first else carry[i][...]

    rows = jnp.concatenate([r[0].astype(F32) for r in (own, rx, ry, far)], axis=0)
    square[...] += jnp.broadcast_to(jnp.sum(rows * rows, axis=1, keepdims=True), square.shape)
    scaled = (rows * gain[0]).astype(BF16)
    gate[...] += dot(scaled, wg[0])
    up[...] += dot(scaled, wu[0])

    if features:

        @pl.when(step == steps - 1)
        def _():
            inverse = lax.rsqrt(square[:, 0:1] * (1.0 / features) + 1e-06)
            g = gate[...] * inverse
            active = g / (1.0 + jnp.exp(-g)) * (up[...] * inverse)
            slots, hidden = own.shape[1], active.shape[1]
            main = slots // 9 * 8
            out = rest[0]
            for d in range(4):
                at = d * slots
                out[d * main : (d + 1) * main, :] = active[at : at + main].astype(BF16)
                ninth = [
                    jnp.broadcast_to(active[row : row + 1], (8, hidden))
                    for row in range(at + main, at + slots)
                ]
                at = (4 + d) * main
                out[at : at + main, :] = jnp.concatenate(ninth, axis=0).astype(BF16)


def up_project(group, last, me, pieces, gain, w_gate, w_up, carry):
    two, slots, part = 2, *pieces[0][0].shape[1:]
    cut = 2
    tile = part // cut
    hidden = w_gate.shape[2]
    total = 4 * slots
    source = lambda i, me: me[0] ^ (2 * group + i // cut)
    row = lambda start: pl.BlockSpec(
        (1, slots, tile), lambda i, me: (start + i // cut, 0, i % cut)
    )
    weight = pl.BlockSpec((1, tile, hidden), lambda i, me: (source(i, me), i % cut, 0))
    in_place = pl.BlockSpec(memory_space=pltpu.VMEM)
    specs = [row(start) for _, start in pieces] + [
        pl.BlockSpec((1, 1, tile), lambda i, me: (source(i, me), 0, i % cut)),
        weight,
        weight,
    ]
    sums = [
        jax.ShapeDtypeStruct((total, hidden), F32),
        jax.ShapeDtypeStruct((total, hidden), F32),
        jax.ShapeDtypeStruct((total, 128), F32),
    ]
    aliases = {}
    if carry is not None:
        specs += [in_place] * 3
        if not last:
            aliases = {8 + i: i for i in range(3)}
    outs = [jax.ShapeDtypeStruct((8 * (slots // 9 * 8), hidden), BF16)] if last else sums
    return pl.pallas_call(
        functools.partial(up_kernel, carry is None, gain.shape[0] * part if last else 0),
        name=f"up_{group}",
        out_shape=outs,
        grid_spec=pltpu.PrefetchScalarGridSpec(
            num_scalar_prefetch=1,
            grid=(two * cut,),
            in_specs=specs,
            out_specs=[in_place] * len(outs),
            scratch_shapes=[pltpu.VMEM(s.shape, s.dtype) for s in sums] if last else [],
        ),
        input_output_aliases=aliases,
        compiler_params=pltpu.CompilerParams(vmem_limit_bytes=48 * MIB),
        cost_estimate=NO_COST,
    )(me, *(array for array, _ in pieces), gain, w_gate, w_up, *(carry or ()))


def down_kernel(act_ref, w_ref, *refs):
    outs, spare = refs[:-1], refs[-1]
    step = pl.program_id(0)
    part = dot(act_ref[...], w_ref[...])
    main = part.shape[0] // 2

    def target(place, shard):
        own, sx, sy, kx, ky = outs[place // 2 * 5 : place // 2 * 5 + 5]
        odd = place % 2
        if shard == 0:
            return own.at[odd]
        if shard == 1:
            return kx if odd else sx.at[1]
        if shard == 2:
            return sy.at[1] if odd else ky
        return sy.at[0] if odd else sx.at[0]

    for shard in range(4):
        for place in range(8):
            at = (shard * 8 + place) * 8
            target(place, shard)[step] = part[at : at + 8, :].astype(BF16)
    ninth = part[main:, :]
    spare[...] = jnp.where(iota(ninth.shape, 0) % 8 == step, ninth, spare[...])

    @pl.when(step == pl.num_programs(0) - 1)
    def _():
        for shard in range(4):
            for place in range(8):
                at = (shard * 8 + place) * 8
                target(place, shard)[8] = spare[at : at + 8, :].astype(BF16)


def down_project(active, w_down):
    total, hidden = active.shape
    features = w_down.shape[1]
    tile = features // 8
    piece = (9, 8, tile)
    outs = []
    for _ in range(4):
        outs += [jax.ShapeDtypeStruct((2,) + piece, BF16)] * 3 + [jax.ShapeDtypeStruct(piece, BF16)] * 2
    return pl.pallas_call(
        down_kernel,
        name="down",
        grid=(8,),
        out_shape=outs,
        in_specs=[
            pl.BlockSpec(memory_space=pltpu.VMEM),
            pl.BlockSpec((hidden, tile), lambda i: (0, i)),
        ],
        out_specs=[pl.BlockSpec(memory_space=pltpu.VMEM)] * len(outs),
        scratch_shapes=[pltpu.VMEM((total // 2, tile), F32)],
        compiler_params=pltpu.CompilerParams(vmem_limit_bytes=48 * MIB),
        cost_estimate=NO_COST,
    )(active, w_down)


def pair_kernel(same, other, *outs):
    for k, out in enumerate(outs):
        out[0] = same[k]
        out[1] = other[k]


def second_kernel(*refs):
    for k, ref in enumerate(refs[:-1]):
        refs[-1][k] = ref[1]


def hold_kernel(a, out):
    out[...] = a[...]


def join_message_kernel(own, to_x, to_y, out_x, out_y):
    for out, through in ((out_x, to_x), (out_y, to_y)):
        out[0:2] = own[...]
        out[2:4] = through[...]


def last_message_kernel(rx, ry, out_x, out_y):
    out_x[...] = ry[...]
    out_y[...] = rx[0:2]


def relay_kernel(kx, ky, rx, ry, *refs):
    ahead, (out_x, out_y) = refs[:-2], refs[-2:]
    if ahead:
        out_x[0:2], out_y[0:2] = ahead[0][...], ahead[1][...]
        out_x, out_y = out_x.at[2], out_y.at[2]
    out_x[...] = (kx[...].astype(F32) + ry[0].astype(F32)).astype(BF16)
    out_y[...] = (ky[...].astype(F32) + rx[0].astype(F32)).astype(BF16)


def finish_kernel(own, rx, ry, last_x, last_y, *refs):
    count = (len(refs) - 1) // 2
    for source, target in zip(refs[:count], refs[count + 1 :]):
        target[...] = source[...]
    out = refs[count]
    if len(last_x.shape) == 4:
        last_x, last_y = last_x.at[2], last_y.at[2]
    out[0] = (own[0].astype(F32) + rx[1].astype(F32) + last_y[...].astype(F32)).astype(BF16)
    out[1] = (own[1].astype(F32) + ry[1].astype(F32) + last_x[...].astype(F32)).astype(BF16)


def mix_kernel(me, ids_t_ref, weight_t_ref, stream_ref, swap_ref, *refs):
    firsts, out_ref = refs[:-1], refs[-1]
    parts = []
    for k, ref in enumerate(firsts):
        parts += [ref.at[0], swap_ref.at[k]]
    rows = ids_t_ref.shape[1]
    experts = len(parts)
    pieces = parts[0].shape[0] - 1
    tile = parts[0].shape[2]
    ids, weights = ids_t_ref[...].T, weight_t_ref[...].T
    named = iota((rows, experts), 1) ^ me[0]
    first, second = ids[:, 0:1] == named, ids[:, 1:2] == named
    weight = jnp.where(first, weights[:, 0:1], jnp.where(second, weights[:, 1:2], 0.0))
    hit = (first | second).astype(F32)
    before = (iota((rows, rows), 0) > iota((rows, rows), 1)).astype(F32)
    rank = dot(before, hit)
    lanes = 2 * experts * 8
    shape = (experts, lanes)
    spread = ((iota(shape, 1) // 8) % experts == iota(shape, 0)).astype(F32)
    weight = dot(weight, spread, PRECISE)
    rank = dot(rank, spread, PRECISE).astype(jnp.int32)
    lane = iota((rows, lanes), 1)
    main = (lane < experts * 8) & (rank == lane % 8)
    extra = (lane >= experts * 8) & (rank == 8)
    last = [part[pieces].astype(F32) for part in parts]
    for k in range(pieces):
        coef = jnp.where(main | (extra & (lane % 8 == k)), weight, 0.0)
        high = coef.astype(BF16)
        low = (coef - high.astype(F32)).astype(BF16)
        data = jnp.concatenate([part[k].astype(F32) for part in parts] + last, axis=0).astype(BF16)
        cols = slice(k * tile, (k + 1) * tile)
        out_ref[:, cols] = (
            stream_ref[k].astype(F32) + (dot(high, data) + dot(low, data))
        ).astype(BF16)


def on_square(
    x_in,
    z_gate,
    b_in,
    c_out,
    dt_step,
    rate,
    skip,
    init_state,
    residual,
    norm_gain,
    expert_ids,
    gate_weights,
    w_gate,
    w_up,
    w_down,
):
    tokens, channels = x_in.shape
    heads = rate.shape[0]
    state = b_in.shape[1]
    owners = lax.axis_size("exp")
    rows, features = residual.shape
    experts = owners
    cap = max(2, 2 * rows // experts + 1)
    slots = owners * cap
    at = lax.axis_index("seq")
    me = lax.axis_index("exp")
    place = jnp.reshape(at, (1,)).astype(jnp.int32)
    self_id = jnp.reshape(me, (1,)).astype(jnp.int32)

    def over_x(v):
        return lax.ppermute(v, "seq", [(i, i ^ 1) for i in range(4)])

    def over_y(v):
        return lax.ppermute(v, "seq", [(i, i ^ 2) for i in range(4)])

    def along(v, mask):
        return lax.ppermute(v, "exp", [(i, i ^ mask) for i in range(owners)])

    rate_row = rate[None, :]
    dt_t = dt_step.T
    ids_t = expert_ids.T
    packed = block_call(
        pack_kernel,
        [jax.ShapeDtypeStruct((owners, rows, channels + 128), BF16)],
        0,
        (ids_t, residual),
        held=2,
        limit=62,
        out_blocks=True,
    )[0]
    packed = lax.all_to_all(packed, "exp", split_axis=0, concat_axis=0, tiled=True)
    payload, init_t = block_call(
        state_kernel,
        [
            jax.ShapeDtypeStruct((state + 16, channels), BF16),
            jax.ShapeDtypeStruct((state, channels), BF16),
        ],
        1,
        (place, x_in, b_in, dt_t, rate_row, init_state.reshape(channels, state)),
        held=5,
        limit=62,
        out_blocks=True,
    )
    pair = over_x(payload)
    own_part, fade = block_call(
        intra_kernel,
        [jax.ShapeDtypeStruct((tokens, channels), F32)] * 2,
        0,
        (x_in, z_gate, b_in, c_out, dt_t, rate_row, skip[None, :]),
        held=7,
        after=(payload,),
        limit=62,
        out_blocks=True,
    )
    joined = block_call(
        join_kernel,
        [jax.ShapeDtypeStruct((state, channels), BF16)],
        1,
        (place, payload, pair),
        held=2,
        limit=62,
    )[0]
    early = over_y(joined)
    select = block_call(
        functools.partial(place_kernel, cap, experts),
        [jax.ShapeDtypeStruct((experts, slots, tokens), BF16)],
        1,
        (self_id, packed),
        held=1,
        limit=62,
    )[0]
    groups = owners // 2
    lanes = jax.ShapeDtypeStruct((groups, slots, channels), BF16)
    stream_here, same, other = block_call(
        stream_kernel,
        [jax.ShapeDtypeStruct((tokens, channels), BF16), lanes, lanes],
        1,
        (place, c_out, own_part, fade, init_t, pair, early, packed, select),
        held=8,
        limit=60,
    )

    gain = norm_gain.reshape(owners, 1, channels)
    wg = w_gate.reshape(owners, channels, w_gate.shape[2])
    wu = w_up.reshape(owners, channels, w_up.shape[2])
    sets = list(block_call(
        pair_kernel,
        [jax.ShapeDtypeStruct((2, slots, channels), BF16)] * groups,
        0,
        (same, along(other, 1)),
    ))
    def hold(v, after, name):
        return block_call(
            hold_kernel, [jax.ShapeDtypeStruct(v.shape, BF16)], 0, (v,), after=after, name=name
        )[0]

    def project(group, quad, carry):
        return up_project(group, group == groups - 1, self_id, quad, gain, wg, wu, carry)

    def message(count):
        return [jax.ShapeDtypeStruct((count,) + sets[0].shape[1:], BF16)] * 2

    near, far, farthest = along(sets[1], 2), along(sets[2], 4), sets[3]
    rx0, ry0 = over_x(sets[0]), over_y(sets[0])
    farthest_held = hold(farthest, (rx0,), "hold_farthest")
    farthest = along(farthest_held, 6)
    rx1, ry1 = over_x(near), over_y(near)
    to_x, to_y = block_call(
        join_message_kernel, message(4), 0, (far, ry1, rx0), after=(ry0, rx1, farthest_held)
    )
    rx2, ry2 = over_x(to_x), over_y(to_y)
    carry = project(0, ((sets[0], 0), (rx0, 0), (ry0, 0), (ry2, 2)), None)
    rx3, ry3 = over_x(farthest), over_y(farthest)
    to_x, to_y = block_call(last_message_kernel, message(2), 0, (rx2, ry3), after=(rx3, carry[2]))
    far3, far2 = over_x(to_x), over_y(to_y)
    carry = project(1, ((near, 0), (rx1, 0), (ry1, 0), (rx2, 2)), carry)
    held_stream = hold(
        stream_here.reshape(owners, rows, channels), (carry[2],), "hold_stream"
    )
    stream = lax.all_to_all(held_stream, "exp", split_axis=0, concat_axis=0, tiled=True)
    carry = project(2, ((far, 0), (rx2, 0), (ry2, 0), (far2, 0)), carry)
    active = project(3, ((farthest, 0), (rx3, 0), (ry3, 0), (far3, 0)), carry)[0]

    wd = w_down.reshape(w_down.shape[1], features)
    piece = jax.ShapeDtypeStruct((9, 8, features // 8), BF16)
    many = lambda count: jax.ShapeDtypeStruct((count,) + piece.shape, BF16)
    sent = down_project(active, wd)
    own, sx, sy, kx, ky = ([sent[5 * g + k] for g in range(groups)] for k in range(5))

    def relay(group, rx, ry, ahead=(), after=()):
        outs = [many(3)] * 2 if ahead else [piece] * 2
        return block_call(
            relay_kernel,
            outs,
            0,
            (kx[group], ky[group], rx, ry, *ahead),
            after=after,
            name=f"relay_{group}",
        )

    def finish(group, rx, ry, last_x, last_y, ahead=()):
        return block_call(
            finish_kernel,
            [many(2)] * (1 + len(ahead)),
            0,
            (own[group], rx, ry, last_x, last_y, *ahead),
            name=f"finish_{group}",
        )

    rx3, ry3 = over_x(sx[3]), over_y(sy[3])
    rx2, ry2 = over_x(sx[2]), over_y(sy[2])
    to_x, to_y = relay(3, rx3, ry3)
    last_x3, last_y3 = over_x(to_x), over_y(to_y)
    to_x, to_y = relay(2, rx2, ry2, (sx[1], sy[1]), (to_x,))
    rx1, ry1 = over_x(to_x), over_y(to_y)
    both3, sx0, sy0 = finish(3, rx3, ry3, last_x3, last_y3, (sx[0], sy[0]))
    back3 = along(both3, 6)
    rx0, ry0 = over_x(sx0), over_y(sy0)
    both2 = finish(2, rx2, ry2, rx1, ry1)[0]
    back2 = along(both2, 4)
    to_x, to_y = relay(1, rx1, ry1, after=(stream,))
    last_x1, last_y1 = over_x(to_x), over_y(to_y)
    to_x, to_y = relay(0, rx0, ry0)
    last_x0, last_y0 = over_x(to_x), over_y(to_y)
    both1 = finish(1, rx1, ry1, last_x1, last_y1)[0]
    back1 = along(both1, 2)
    both0 = finish(0, rx0, ry0, last_x0, last_y0)[0]
    back = [both0, back1, back2, back3]
    swap = block_call(second_kernel, [many(groups)], 0, back)[0]
    swap = along(swap, 1)
    return block_call(
        mix_kernel,
        [jax.ShapeDtypeStruct((rows, features), BF16)],
        1,
        (self_id, ids_t, gate_weights.T, stream, swap, *back),
    )[0]


def entering_2(array, axis, combine, identity):
    devices, mine = (lax.axis_size(axis), lax.axis_index(axis))
    everything = jax.tree.map(
        lambda part, kind: lax.all_gather(part.astype(kind), axis),
        array,
        (jnp.bfloat16, jnp.bfloat16),
    )
    start = jax.tree.map(
        lambda part, zero: jnp.broadcast_to(jnp.asarray(zero, part.dtype), part.shape),
        array,
        identity,
    )

    def hop(k, before):
        reached = k < mine
        new = combine(
            before, jax.tree.map(lambda part, own: part[k].astype(own.dtype), everything, array)
        )
        return jax.tree.map(lambda a, b: jnp.where(reached, a, b), new, before)

    return lax.fori_loop(0, devices, hop, start)


def chain_combine(earlier, later):
    return (earlier[0] + later[0], jnp.exp(later[0])[:, None, None] * earlier[1] + later[1])


def on_device(
    x_in,
    z_gate,
    b_in,
    c_out,
    dt_step,
    rate,
    skip,
    init_state,
    residual,
    norm_gain,
    expert_ids,
    gate_weights,
    w_gate,
    w_up,
    w_down,
):
    token_count, channels = x_in.shape
    heads_here = rate.shape[0]
    head_width = channels // heads_here
    state_width = b_in.shape[1]
    blocks = token_count // GROUP
    inputs = x_in.astype(jnp.float32).reshape(blocks, GROUP, heads_here, head_width)
    keys_in = b_in.astype(jnp.float32).reshape(blocks, GROUP, state_width)
    queries = c_out.astype(jnp.float32).reshape(blocks, GROUP, state_width)
    log_steps = (-rate[None, :] * dt_step).reshape(blocks, GROUP, heads_here)
    cumulative = jnp.cumsum(log_steps, axis=1)
    scores = jnp.einsum("ctn,csn->cts", queries, keys_in, precision=PRECISE)
    causal = jnp.arange(GROUP)[:, None] >= jnp.arange(GROUP)[None, :]
    spread = cumulative[:, :, None, :] - cumulative[:, None, :, :]
    weights = jnp.exp(jnp.where(causal[None, :, :, None], spread, -jnp.inf)) * scores[..., None]
    intra_out = jnp.einsum("ctsh,cshp->cthp", weights, inputs, precision=PRECISE)
    tail_decay = jnp.exp(cumulative[:, -1:, :] - cumulative)
    block_state = jnp.einsum("csh,cshp,csn->chpn", tail_decay, inputs, keys_in, precision=PRECISE)
    block_log = cumulative[:, -1, :]

    def advance(carried, element):
        total_log, total_state = carried
        step_log, step_state = element
        updated = (
            total_log + step_log,
            jnp.exp(step_log)[:, None, None] * total_state + step_state,
        )
        return (updated, (total_log, total_state))

    zero_state = jnp.zeros((heads_here, head_width, state_width), jnp.float32)
    zero_log = jnp.zeros((heads_here,), jnp.float32)
    (device_log, device_state), (enter_log, enter_state) = lax.scan(
        advance, (zero_log, zero_state), (block_log, block_state)
    )
    prior_log, prior_state = entering_2(
        (device_log, device_state), "seq", chain_combine, (zero_log, zero_state)
    )
    incoming = prior_state + jnp.exp(prior_log)[:, None, None] * init_state
    entering = enter_state + jnp.exp(enter_log)[:, :, None, None] * incoming[None]
    inter_out = jnp.exp(cumulative)[..., None] * jnp.einsum(
        "chpn,ctn->cthp", entering, queries, precision=PRECISE
    )
    mixed_out = (intra_out + inter_out + skip[None, None, :, None] * inputs).reshape(
        token_count, channels
    )
    mixer = (mixed_out * jax.nn.silu(z_gate.astype(jnp.float32))).astype(jnp.bfloat16)
    token_mix = lax.all_to_all(mixer, "exp", split_axis=0, concat_axis=1, tiled=True)
    stream = (residual.astype(jnp.float32) + token_mix.astype(jnp.float32)).astype(jnp.bfloat16)
    widened = stream.astype(jnp.float32)
    normed = (
        widened
        * lax.rsqrt(jnp.mean(widened * widened, axis=-1, keepdims=True) + 1e-06)
        * norm_gain[None, :]
    ).astype(jnp.bfloat16)
    rows_here = residual.shape[0]
    owners = lax.axis_size("exp")
    local_experts = w_gate.shape[0]
    experts = owners * local_experts
    capacity = max(2, 2 * rows_here // experts + 1)
    width = residual.shape[1]
    chosen = expert_ids.reshape(-1)
    onehot = (chosen[:, None] == jnp.arange(experts)[None, :]).astype(jnp.int32)
    slot_index = jnp.sum((jnp.cumsum(onehot, axis=0) - onehot) * onehot, axis=1)
    target = chosen * capacity + slot_index
    placing = (target[None, :] == jnp.arange(experts * capacity)[:, None]).astype(jnp.bfloat16)
    pair_rows = jnp.repeat(normed, 2, axis=0)
    outgoing = jnp.dot(placing, pair_rows, preferred_element_type=jnp.float32).astype(jnp.bfloat16)
    outgoing = outgoing.reshape(owners, local_experts, 1, capacity, width)
    arrived = lax.all_to_all(outgoing, "exp", split_axis=0, concat_axis=2, tiled=True)
    segment = lax.all_gather(arrived, "seq", axis=1, tiled=True)
    flattened = segment.reshape(segment.shape[0], -1, segment.shape[-1])
    gate_proj = jnp.einsum("erd,edf->erf", flattened, w_gate, preferred_element_type=jnp.float32)
    up_proj = jnp.einsum("erd,edf->erf", flattened, w_up, preferred_element_type=jnp.float32)
    active = (jax.nn.silu(gate_proj) * up_proj).astype(jnp.bfloat16)
    partial_value = jnp.einsum("erf,efd->erd", active, w_down, preferred_element_type=jnp.float32)
    partials = partial_value.reshape(segment.shape[:-1] + (partial_value.shape[-1],))
    summed = lax.psum_scatter(partials.astype(jnp.bfloat16), "seq", scatter_dimension=1, tiled=True)
    returned = lax.all_to_all(summed, "exp", split_axis=2, concat_axis=0, tiled=True)
    results = returned.reshape(experts * capacity, width)
    picked = results[target].astype(jnp.float32).reshape(rows_here, 2, width)
    mixture = jnp.sum(picked * gate_weights[:, :, None], axis=1)
    return (widened + mixture).astype(jnp.bfloat16)


def solution(mesh):
    square = mesh.shape["seq"] == 4 and mesh.shape["exp"] == 8

    def body(*args):
        rows = args[8].shape[0]
        experts = mesh.shape["exp"] * args[12].shape[0]
        fits = args[12].shape[0] == 1 and 2 * rows // experts + 1 == 9
        return (on_square if square and fits else on_device)(*args)

    return jax.shard_map(
        body,
        mesh=mesh,
        in_specs=(
            P("seq", "exp"),
            P("seq", "exp"),
            P("seq", None),
            P("seq", None),
            P("seq", "exp"),
            P("exp"),
            P("exp"),
            P("exp", None, None),
            P(("seq", "exp"), None),
            P(),
            P(("seq", "exp"), None),
            P(("seq", "exp"), None),
            P("exp", None, "seq"),
            P("exp", None, "seq"),
            P("exp", "seq", None),
        ),
        out_specs=P(("seq", "exp"), None),
        check_vma=False,
    )
```

```python
import functools

import jax
import jax.numpy as jnp
from jax import lax
from jax.experimental import pallas as pl
from jax.experimental.pallas import tpu as pltpu
from jax.sharding import PartitionSpec as P

GROUP = 128
PRECISE = lax.Precision.HIGHEST
F32 = jnp.float32
BF16 = jnp.bfloat16
MIB = 1 << 20
NO_COST = pl.CostEstimate(flops=0, bytes_accessed=0, transcendentals=0)


def block_call(body, outs, scalars, args, held=0, keep=0, after=(), limit=16, out_blocks=False, name=None):
    n_args = len(args)
    kept = [jax.ShapeDtypeStruct(v.shape, v.dtype) for v in args[scalars : scalars + held]]

    def kernel(*refs):
        refs, sems = (refs[:-1], refs[-1]) if held else (refs, None)
        inputs, refs = refs[:n_args], refs[n_args + len(after) :]
        results, refs = refs[: len(outs)], refs[len(outs) :]
        copies = [
            pltpu.make_async_copy(src, dst, sems.at[k])
            for k, (src, dst) in enumerate(zip(inputs[scalars : scalars + held], refs))
        ]
        for copy in copies:
            copy.start()
        for copy in copies:
            copy.wait()
        body(*inputs[:scalars], *refs, *inputs[scalars + held :], *results)

    scratch = [pltpu.VMEM(v.shape, v.dtype) for v in kept[keep:]]
    if held:
        scratch.append(pltpu.SemaphoreType.DMA((held,)))
    return pl.pallas_call(
        kernel,
        name=name or getattr(body, "func", body).__name__,
        out_shape=list(outs) + kept[:keep],
        in_specs=[pl.BlockSpec(memory_space=pltpu.SMEM)] * scalars
        + [pl.BlockSpec(memory_space=pltpu.HBM)] * held
        + [pl.BlockSpec(memory_space=pltpu.VMEM)] * (n_args - scalars - held)
        + [pl.BlockSpec(memory_space=pl.ANY)] * len(after),
        out_specs=[pl.BlockSpec() if out_blocks else pl.BlockSpec(memory_space=pltpu.VMEM)]
        * (len(outs) + keep),
        scratch_shapes=scratch,
        compiler_params=pltpu.CompilerParams(vmem_limit_bytes=limit * MIB),
        cost_estimate=NO_COST,
    )(*args, *after)


def iota(shape, dim):
    return lax.broadcasted_iota(jnp.int32, shape, dim)


def dot(a, b, precision=None):
    return jnp.dot(a, b, precision=precision, preferred_element_type=F32)


def head_spread(heads, channels):
    shape = (heads, channels)
    return (iota(shape, 1) // (channels // heads) == iota(shape, 0)).astype(F32)


def running_logs(dt_t_ref, rate_ref):
    logs = -rate_ref[...] * dt_t_ref[...].T
    tokens = logs.shape[0]
    tri = (iota((tokens, tokens), 0) >= iota((tokens, tokens), 1)).astype(F32)
    return dot(tri, logs, PRECISE)


def pack_kernel(ids_t_ref, residual_ref, out_ref):
    parts, rows, wide = out_ref.shape
    part = wide - 128
    ids = ids_t_ref[...].astype(F32).T
    lane = iota((rows, 128), 1)
    named = jnp.where(lane == 0, ids[:, 0:1], jnp.where(lane == 1, ids[:, 1:2], 0.0)).astype(BF16)
    for k in range(parts):
        out_ref[k, :, 0:part] = residual_ref[:, k * part : (k + 1) * part]
        out_ref[k, :, part:wide] = named


def state_kernel(place, x_ref, z_ref, b_ref, c_ref, dt_t_ref, rate_ref, skip_ref, init_ref, payload_ref, init_t_ref):
    tokens, channels = x_ref.shape
    heads = dt_t_ref.shape[0]
    width = b_ref.shape[1]
    cum = running_logs(dt_t_ref, rate_ref)
    total = cum[tokens - 1 : tokens, :]
    spread = head_spread(heads, channels)
    tail = dot(jnp.exp(total - cum), spread, PRECISE)
    scaled = (x_ref[...].astype(F32) * tail).astype(BF16)
    keys = b_ref[...].astype(F32).T.astype(BF16)
    own = dot(keys, scaled)
    decay = dot(jnp.broadcast_to(jnp.exp(total), (8, heads)), spread, PRECISE)
    init_t = init_ref[...].T
    init_t_ref[...] = init_t.astype(BF16)
    first = (place[0] == 0).astype(F32)
    payload_ref[0:width, :] = (own + first * (decay[0:1, :] * init_t)).astype(BF16)
    high = decay.astype(BF16).astype(F32)
    rows = iota((16, channels), 0)
    high16 = jnp.broadcast_to(high[0:1, :], (16, channels))
    low16 = jnp.broadcast_to(decay[0:1, :], (16, channels)) - high16
    payload_ref[width : width + 16, :] = jnp.where(
        rows == 0, high16, jnp.where(rows == 1, low16, 0.0)
    ).astype(BF16)


def intra_kernel(x_ref, z_ref, b_ref, c_ref, dt_t_ref, rate_ref, skip_ref, init_t_ref, own_ref, fade_ref, c_out_ref, init_out_ref):
    tokens, channels = x_ref.shape
    heads = dt_t_ref.shape[0]
    width = channels // heads
    c_out_ref[...] = c_ref[...]
    init_out_ref[...] = init_t_ref[...]
    shape = (tokens, tokens)
    causal = iota(shape, 0) >= iota(shape, 1)
    cum = running_logs(dt_t_ref, rate_ref)
    cum_t = cum.T
    scores = lax.dot_general(
        c_ref[...], b_ref[...], (((1,), (1,)), ((), ())), preferred_element_type=F32
    )
    spread = head_spread(heads, channels)
    direct = dot(jnp.broadcast_to(skip_ref[...], (8, heads)), spread, PRECISE)[0:1, :]
    fade = dot(jnp.exp(cum), spread, PRECISE)
    per = 128 // width
    lane_head = iota((tokens, 128), 1) // width
    for group in range(heads // per):
        cols = slice(group * 128, (group + 1) * 128)
        x = x_ref[:, cols]
        total = x.astype(F32) * direct[:, cols]
        for k in range(per):
            h = group * per + k
            gap = jnp.where(causal, cum[:, h : h + 1] - cum_t[h : h + 1, :], -1e30)
            weights = (jnp.exp(gap) * scores).astype(BF16)
            part = dot(weights, x)
            total = total + jnp.where(lane_head == k, part, 0.0)
        z = z_ref[:, cols].astype(F32)
        gate = z / (1.0 + jnp.exp(-z))
        own_ref[:, cols] = total * gate
        fade_ref[:, cols] = fade[:, cols] * gate


def place_kernel(cap, experts, me, packed_ref, out_ref):
    blocks, rows, wide = packed_ref.shape
    tokens = blocks * rows
    slots = out_ref.shape[1]
    ids = packed_ref[:, :, wide - 128 : wide].astype(F32).reshape(tokens, 128).T
    ids = ids[0:8, :].astype(jnp.int32)
    shape = (tokens, tokens)
    before = (iota(shape, 0) < iota(shape, 1)) & (iota(shape, 0) // rows == iota(shape, 1) // rows)
    named = iota((experts, tokens), 0) ^ me[0]
    hit = (ids[0:1, :] == named) | (ids[1:2, :] == named)
    rank = dot(hit.astype(BF16), before.astype(BF16)).astype(jnp.int32)
    block = (iota((experts, tokens), 1) // rows) ^ named
    whole = cap - 1
    row = jnp.where(rank < whole, block * whole + rank, blocks * whole + block)
    row = jnp.where(hit, row, -1)
    for e in range(experts):
        out_ref[e] = (iota((slots, tokens), 0) == row[e : e + 1, :]).astype(F32).astype(BF16)


def join_kernel(place, own_ref, other_ref, token_ref, out_ref):
    width = out_ref.shape[0]
    odd = place[0] % 2 == 1
    own, other = own_ref[0:width, :].astype(F32), other_ref[0:width, :].astype(F32)
    own_decay = own_ref[width : width + 16, :].astype(F32)
    other_decay = other_ref[width : width + 16, :].astype(F32)
    own_decay = own_decay[0:1, :] + own_decay[1:2, :]
    other_decay = other_decay[0:1, :] + other_decay[1:2, :]
    early = jnp.where(odd, other, own)
    late = jnp.where(odd, own, other)
    decay = jnp.where(odd, own_decay, other_decay)
    out_ref[...] = (decay * early + late).astype(BF16)


def stream_kernel(
    place, c_ref, own_ref, fade_ref, init_t_ref, pair_ref, early_ref, res_ref, sel_ref, stream_ref, same_ref, other_ref
):
    width = init_t_ref.shape[0]
    at = place[0]
    zero = (at == 0).astype(F32)
    odd = (at % 2 == 1).astype(F32)
    pair = pair_ref[...].astype(F32)
    decay = pair[width : width + 1, :] + pair[width + 1 : width + 2, :]
    factor = jnp.where(at >= 2, jnp.where(at % 2 == 1, decay, 1.0), 0.0)
    entering = zero * init_t_ref[...].astype(F32) + odd * pair[0:width, :] + factor * early_ref[...].astype(F32)
    mixed = own_ref[...] + fade_ref[...] * dot(c_ref[...], entering.astype(BF16))
    mixer = mixed.astype(BF16).astype(F32)
    tokens, channels = mixer.shape
    residual = res_ref[:, :, 0:channels].astype(F32).reshape(tokens, channels)
    stream = (residual + mixer).astype(BF16)
    stream_ref[...] = stream
    for k in range(same_ref.shape[0]):
        same_ref[k] = dot(sel_ref[2 * k], stream).astype(BF16)
        other_ref[k] = dot(sel_ref[2 * k + 1], stream).astype(BF16)


def up_kernel(first, features, near, far, me, *refs):
    count = 3 * near + 2 * far
    parts, (gain, wg, wu) = refs[:count], refs[count : count + 3]
    carry = () if first else refs[count + 3 : count + 6]
    rest = refs[count + 3 if first else count + 6 :]
    sums = rest[1:4] if features else rest
    step = pl.program_id(0)
    steps = pl.num_programs(0)

    if first or features:

        @pl.when(step == 0)
        def _():
            for i, acc in enumerate(sums):
                acc[...] = jnp.zeros_like(acc) if first else carry[i][...]

    gate, up, square = sums
    slots = parts[0].shape[1]
    start, stop = 0 if near else 3 * slots, 4 * slots if far else 3 * slots
    span = slice(start, stop)
    rows = [r[0].astype(F32) for r in parts[: 3 * near]]
    if far:
        even, odd = parts[-2:]
        rows.append(jnp.where(step % 2 == 0, even[0].astype(F32), odd[0].astype(F32)))
    rows = jnp.concatenate(rows, axis=0) if len(rows) > 1 else rows[0]
    square[span, :] += jnp.broadcast_to(
        jnp.sum(rows * rows, axis=1, keepdims=True), (stop - start, square.shape[1])
    )
    scaled = (rows * gain[0]).astype(BF16)
    gate[span, :] += dot(scaled, wg[0])
    up[span, :] += dot(scaled, wu[0])

    if features:
        out, stage = rest[0], rest[4]

        @pl.when(step == steps - 1)
        def _():
            inverse = lax.rsqrt(square[:, 0:1] * (1.0 / features) + 1e-06)
            g = gate[...] * inverse
            active = g / (1.0 + jnp.exp(-g)) * (up[...] * inverse)
            main, ninths = slots // 9 * 8, slots // 9
            for d in range(4):
                at = d * slots
                stage[d * main : (d + 1) * main, :] = active[at : at + main]
                low = 4 * main + d * ninths
                stage[low : low + ninths, :] = active[at + main : at + slots]
            out[...] = stage[...].astype(BF16)


def up_project(name, masks, me, near, far, gain, w_gate, w_up, carry, last=False):
    given = near + far
    slots, part = given[0][0].shape[1:]
    hidden = w_gate.shape[2]
    total = 4 * slots
    source = lambda i, me: me[0] ^ (masks[0] + i)
    rows = [
        pl.BlockSpec((1, slots, part), lambda i, me, start=start: (start + i, 0, 0))
        for _, start in near
    ] + [
        pl.BlockSpec((1, slots, part), lambda i, me, start=start: (start + i // 2, 0, 0))
        for _, start in far
    ]
    weight = pl.BlockSpec((1, part, hidden), lambda i, me: (source(i, me), 0, 0))
    in_place = pl.BlockSpec(memory_space=pltpu.VMEM)
    specs = rows + [pl.BlockSpec((1, 1, part), lambda i, me: (source(i, me), 0, 0)), weight, weight]
    sums = [
        jax.ShapeDtypeStruct((total, hidden), F32),
        jax.ShapeDtypeStruct((total, hidden), F32),
        jax.ShapeDtypeStruct((total, 128), F32),
    ]
    aliases = {}
    if carry is not None:
        specs += [in_place] * 3
        if not last:
            aliases = {1 + len(rows) + 3 + i: i for i in range(3)}
    outs = [jax.ShapeDtypeStruct((total, hidden), BF16)] if last else sums
    scratch = [pltpu.VMEM(s.shape, s.dtype) for s in sums]
    scratch.append(pltpu.VMEM((total, hidden), F32))
    features = gain.shape[0] * part if last else 0
    return pl.pallas_call(
        functools.partial(up_kernel, carry is None, features, bool(near), bool(far)),
        name=name,
        out_shape=outs,
        grid_spec=pltpu.PrefetchScalarGridSpec(
            num_scalar_prefetch=1,
            grid=(len(masks),),
            in_specs=specs,
            out_specs=[in_place] * len(outs),
            scratch_shapes=scratch if last else [],
        ),
        input_output_aliases=aliases,
        compiler_params=pltpu.CompilerParams(vmem_limit_bytes=48 * MIB),
        cost_estimate=NO_COST,
    )(me, *(array for array, _ in given), gain, w_gate, w_up, *(carry or ()))


def down_kernel(act_ref, w_ref, *refs):
    outs, spare = refs[:-1], refs[-1]
    step = pl.program_id(0)
    part = dot(act_ref[...], w_ref[...])
    ninths = part.shape[0] // 9
    main = part.shape[0] - ninths
    places = ninths // 4
    groups = places // 2

    def target(place, shard):
        group, odd = place // 2, place % 2
        if shard == 3:
            return outs[2 * (group // 2) + odd].at[group % 2]
        own, direct_x, direct_y, wait_x, wait_y = outs[groups + 5 * group :][:5]
        if shard == 0:
            return own.at[odd]
        if shard == 1:
            return wait_x if odd else direct_x
        return direct_y if odd else wait_y

    for shard in range(4):
        for place in range(places):
            at = (shard * places + place) * 8
            target(place, shard)[step] = part[at : at + 8, :].astype(BF16)
    for lanes in range(spare.shape[0]):
        spare[lanes, pl.ds(pl.multiple_of(step * ninths, 8), ninths), :] = part[
            main:, lanes * 128 : (lanes + 1) * 128
        ]

    @pl.when(step == pl.num_programs(0) - 1)
    def _():
        for shard in range(4):
            for place in range(places):
                row = pl.ds(shard * places + place, 8, stride=ninths)
                ninth = [spare[lanes, row, :] for lanes in range(spare.shape[0])]
                target(place, shard)[8] = jnp.concatenate(ninth, axis=1).astype(BF16)


def down_project(active, w_down):
    total, hidden = active.shape
    features = w_down.shape[1]
    tile = features // 8
    piece = jax.ShapeDtypeStruct((9, 8, tile), BF16)
    two = jax.ShapeDtypeStruct((2, 9, 8, tile), BF16)
    outs = [two] * 4 + ([two] + [piece] * 4) * 4
    return pl.pallas_call(
        down_kernel,
        name="down",
        grid=(8,),
        out_shape=outs,
        in_specs=[
            pl.BlockSpec(memory_space=pltpu.VMEM),
            pl.BlockSpec((hidden, tile), lambda i: (0, i)),
        ],
        out_specs=[pl.BlockSpec(memory_space=pltpu.VMEM)] * len(outs),
        scratch_shapes=[pltpu.VMEM((tile // 128, 8 * total // 9, 128), F32)],
        compiler_params=pltpu.CompilerParams(vmem_limit_bytes=48 * MIB),
        cost_estimate=NO_COST,
    )(active, w_down)


def pair_kernel(same, other, *outs):
    for k, out in enumerate(outs):
        out[0] = same[k]
        out[1] = other[k]


def second_kernel(*refs):
    for k, ref in enumerate(refs[:-1]):
        refs[-1][k] = ref[1]


def hold_kernel(a, out):
    out[...] = a[...]


def half_message_kernel(rx, ry, out_x, out_y):
    out_x[0], out_y[0] = ry[1], rx[0]


def join_message_kernel(own, rx, ry, out_x, out_y):
    out_x[0:2], out_y[0:2] = own[...], own[...]
    out_x[2], out_y[2] = ry[1], rx[0]


def last_message_kernel(rx2, ry2, rx3, ry3, out_x, out_y):
    out_x[0], out_y[0] = ry2[1], rx2[0]
    out_x[1], out_y[1] = ry3[1], rx3[0]


def relay_kernel(through_x, through_y, *refs):
    ahead = refs[8 : 8 + (len(refs) - 12) // 2]
    outs, copies = refs[8 + len(ahead) :][:4], refs[12 + len(ahead) :]
    for k in range(2):
        direct_x, direct_y, wait_x, wait_y = refs[4 * k : 4 * k + 4]
        out_x, out_y = outs[2 * k : 2 * k + 2]
        out_x[0], out_y[0] = direct_x[...], direct_y[...]
        out_x[1] = (wait_x[...].astype(F32) + through_y[k].astype(F32)).astype(BF16)
        out_y[1] = (wait_y[...].astype(F32) + through_x[k].astype(F32)).astype(BF16)
    for source, copy in zip(ahead, copies):
        copy[...] = source[...]


def finish_kernel(own, rx, ry, *refs):
    ahead = refs[: (len(refs) - 1) // 2]
    out, copies = refs[len(ahead)], refs[len(ahead) + 1 :]
    out[0] = (own[0].astype(F32) + rx[0].astype(F32) + ry[1].astype(F32)).astype(BF16)
    out[1] = (own[1].astype(F32) + ry[0].astype(F32) + rx[1].astype(F32)).astype(BF16)
    for source, copy in zip(ahead, copies):
        copy[...] = source[...]


def mix_kernel(me, ids_t_ref, weight_t_ref, stream_ref, swap_ref, *refs):
    firsts, out_ref = refs[:-1], refs[-1]
    parts = []
    for k, ref in enumerate(firsts):
        parts += [ref.at[0], swap_ref.at[k]]
    rows = ids_t_ref.shape[1]
    experts = len(parts)
    pieces = parts[0].shape[0] - 1
    tile = parts[0].shape[2]
    ids, weights = ids_t_ref[...].T, weight_t_ref[...].T
    named = iota((rows, experts), 1) ^ me[0]
    first, second = ids[:, 0:1] == named, ids[:, 1:2] == named
    weight = jnp.where(first, weights[:, 0:1], jnp.where(second, weights[:, 1:2], 0.0))
    hit = (first | second).astype(F32)
    before = (iota((rows, rows), 0) > iota((rows, rows), 1)).astype(F32)
    rank = dot(before, hit)
    lanes = 2 * experts * 8
    shape = (experts, lanes)
    spread = ((iota(shape, 1) // 8) % experts == iota(shape, 0)).astype(F32)
    weight = dot(weight, spread, PRECISE)
    rank = dot(rank, spread, PRECISE).astype(jnp.int32)
    lane = iota((rows, lanes), 1)
    main = (lane < experts * 8) & (rank == lane % 8)
    extra = (lane >= experts * 8) & (rank == 8)
    last = [part[pieces].astype(F32) for part in parts]
    for k in range(pieces):
        coef = jnp.where(main | (extra & (lane % 8 == k)), weight, 0.0)
        high = coef.astype(BF16)
        low = (coef - high.astype(F32)).astype(BF16)
        data = jnp.concatenate([part[k].astype(F32) for part in parts] + last, axis=0).astype(BF16)
        cols = slice(k * tile, (k + 1) * tile)
        out_ref[:, cols] = (
            stream_ref[k].astype(F32) + (dot(high, data) + dot(low, data))
        ).astype(BF16)


def on_square(
    x_in,
    z_gate,
    b_in,
    c_out,
    dt_step,
    rate,
    skip,
    init_state,
    residual,
    norm_gain,
    expert_ids,
    gate_weights,
    w_gate,
    w_up,
    w_down,
):
    tokens, channels = x_in.shape
    heads = rate.shape[0]
    state = b_in.shape[1]
    owners = lax.axis_size("exp")
    rows, features = residual.shape
    experts = owners
    cap = max(2, 2 * rows // experts + 1)
    slots = owners * cap
    at = lax.axis_index("seq")
    me = lax.axis_index("exp")
    place = jnp.reshape(at, (1,)).astype(jnp.int32)
    self_id = jnp.reshape(me, (1,)).astype(jnp.int32)

    def over_x(v):
        return lax.ppermute(v, "seq", [(i, i ^ 1) for i in range(4)])

    def over_y(v):
        return lax.ppermute(v, "seq", [(i, i ^ 2) for i in range(4)])

    def along(v, mask):
        return lax.ppermute(v, "exp", [(i, i ^ mask) for i in range(owners)])

    rate_row = rate[None, :]
    dt_t = dt_step.T
    ids_t = expert_ids.T
    packed = block_call(
        pack_kernel,
        [jax.ShapeDtypeStruct((owners, rows, channels + 128), BF16)],
        0,
        (ids_t, residual),
        held=2,
        limit=48,
    )[0]
    packed = lax.all_to_all(packed, "exp", split_axis=0, concat_axis=0, tiled=True)
    payload, init_t, x, z, b, c, dt, rates, skips = block_call(
        state_kernel,
        [
            jax.ShapeDtypeStruct((state + 16, channels), BF16),
            jax.ShapeDtypeStruct((state, channels), BF16),
        ],
        1,
        (
            place,
            x_in,
            z_gate,
            b_in,
            c_out,
            dt_t,
            rate_row,
            skip[None, :],
            init_state.reshape(channels, state),
        ),
        held=8,
        keep=7,
        limit=61,
    )
    pair = over_x(payload)
    own_part, fade, c, init_t = block_call(
        intra_kernel,
        [
            jax.ShapeDtypeStruct((tokens, channels), F32),
            jax.ShapeDtypeStruct((tokens, channels), F32),
            jax.ShapeDtypeStruct(c.shape, BF16),
            jax.ShapeDtypeStruct(init_t.shape, BF16),
        ],
        0,
        (x, z, b, c, dt, rates, skips, init_t),
    )
    joined = block_call(
        join_kernel,
        [jax.ShapeDtypeStruct((state, channels), BF16)],
        1,
        (place, payload, pair, c),
    )[0]
    early = over_y(joined)
    select = block_call(
        functools.partial(place_kernel, cap, experts),
        [jax.ShapeDtypeStruct((experts, slots, tokens), BF16)],
        1,
        (self_id, packed),
    )[0]
    groups = owners // 2
    lanes = jax.ShapeDtypeStruct((groups, slots, channels), BF16)
    stream_here, same, other = block_call(
        stream_kernel,
        [jax.ShapeDtypeStruct((tokens, channels), BF16), lanes, lanes],
        1,
        (place, c, own_part, fade, init_t, pair, early, packed, select),
    )

    gain = norm_gain.reshape(owners, 1, channels)
    wg = w_gate.reshape(owners, channels, w_gate.shape[2])
    wu = w_up.reshape(owners, channels, w_up.shape[2])
    sets = list(block_call(
        pair_kernel,
        [jax.ShapeDtypeStruct((2, slots, channels), BF16)] * groups,
        0,
        (same, along(other, 1)),
    ))
    def hold(v, after, name):
        return block_call(
            hold_kernel, [jax.ShapeDtypeStruct(v.shape, BF16)], 0, (v,), after=after, name=name
        )[0]

    def project(name, masks, near, far, carry, last=False):
        return up_project(name, masks, self_id, near, far, gain, wg, wu, carry, last)

    def message(count):
        return [jax.ShapeDtypeStruct((count,) + sets[0].shape[1:], BF16)] * 2

    near, far, farthest = along(sets[1], 2), along(sets[2], 4), sets[3]
    rx0, ry0 = over_x(sets[0]), over_y(sets[0])
    to_x, to_y = block_call(half_message_kernel, message(1), 0, (rx0, ry0))
    fx0, fy0 = over_x(to_x), over_y(to_y)
    rx1, ry1 = over_x(near), over_y(near)
    farthest_held = hold(farthest, (to_x,), "hold_farthest")
    farthest = along(farthest_held, 6)
    carry = project(
        "up_0", (0, 1), [(sets[0], 0), (rx0, 0), (ry0, 0)], [(fy0, 0), (fx0, 0)], None
    )
    to_x, to_y = block_call(
        join_message_kernel, message(3), 0, (far, rx1, ry1), after=(farthest_held, carry[2])
    )
    rx2, ry2 = over_x(to_x), over_y(to_y)
    rx3, ry3 = over_x(farthest), over_y(farthest)
    carry = project(
        "up_1", (2, 3), [(near, 0), (rx1, 0), (ry1, 0)], [(ry2, 2), (rx2, 2)], carry
    )
    to_x, to_y = block_call(
        last_message_kernel, message(2), 0, (rx2, ry2, rx3, ry3), after=(carry[2],)
    )
    fx, fy = over_x(to_x), over_y(to_y)
    carry = project("up_2", (4, 5), [(far, 0), (rx2, 0), (ry2, 0)], [], carry)
    held_stream = hold(
        stream_here.reshape(owners, rows, channels), (carry[2],), "hold_stream"
    )
    stream = lax.all_to_all(held_stream, "exp", split_axis=0, concat_axis=0, tiled=True)
    carry = project("up_3", (6, 7), [(farthest, 0), (rx3, 0), (ry3, 0)], [], carry)
    active = project("up_last", (4, 5, 6, 7), [], [(fy, 0), (fx, 0)], carry, True)[0]

    wd = w_down.reshape(w_down.shape[1], features)
    many = lambda count: jax.ShapeDtypeStruct((count, 9, 8, features // 8), BF16)
    sent = down_project(active, wd)
    own = [sent[4 + 5 * g] for g in range(groups)]
    shares = [sent[5 + 5 * g : 9 + 5 * g] for g in range(groups)]

    def relay(name, through_x, through_y, low, ahead=(), after=()):
        return block_call(
            relay_kernel,
            [many(2)] * (4 + len(ahead)),
            0,
            (through_x, through_y, *shares[low], *shares[low + 1], *ahead),
            after=after,
            name=name,
        )

    def finish(group, rx, ry, ahead=()):
        return block_call(
            finish_kernel,
            [many(2)] * (1 + len(ahead)),
            0,
            (own[group], rx, ry, *ahead),
            name=f"finish_{group}",
        )

    through_x, through_y = over_x(sent[2]), over_y(sent[3])
    x2, y2, x3, y3, next_x, next_y = relay(
        "relay_far", through_x, through_y, 2, (sent[0], sent[1])
    )
    rx3, ry3 = over_x(x3), over_y(y3)
    through_x, through_y = over_x(next_x), over_y(next_y)
    both3, x2, y2 = finish(3, rx3, ry3, (x2, y2))
    back3 = along(both3, 6)
    rx2, ry2 = over_x(x2), over_y(y2)
    x0, y0, x1, y1 = relay("relay_near", through_x, through_y, 0, after=(both3,))
    rx1, ry1 = over_x(x1), over_y(y1)
    both2, x0, y0 = finish(2, rx2, ry2, (x0, y0))
    back2 = along(both2, 4)
    rx0, ry0 = over_x(x0), over_y(y0)
    back1 = along(finish(1, rx1, ry1)[0], 2)
    back = [finish(0, rx0, ry0)[0], back1, back2, back3]
    swap = block_call(second_kernel, [many(groups)], 0, back)[0]
    swap = along(swap, 1)
    return block_call(
        mix_kernel,
        [jax.ShapeDtypeStruct((rows, features), BF16)],
        1,
        (self_id, ids_t, gate_weights.T, stream, swap, *back),
    )[0]


def entering_2(array, axis, combine, identity):
    devices, mine = (lax.axis_size(axis), lax.axis_index(axis))
    everything = jax.tree.map(
        lambda part, kind: lax.all_gather(part.astype(kind), axis),
        array,
        (jnp.bfloat16, jnp.bfloat16),
    )
    start = jax.tree.map(
        lambda part, zero: jnp.broadcast_to(jnp.asarray(zero, part.dtype), part.shape),
        array,
        identity,
    )

    def hop(k, before):
        reached = k < mine
        new = combine(
            before, jax.tree.map(lambda part, own: part[k].astype(own.dtype), everything, array)
        )
        return jax.tree.map(lambda a, b: jnp.where(reached, a, b), new, before)

    return lax.fori_loop(0, devices, hop, start)


def chain_combine(earlier, later):
    return (earlier[0] + later[0], jnp.exp(later[0])[:, None, None] * earlier[1] + later[1])


def on_device(
    x_in,
    z_gate,
    b_in,
    c_out,
    dt_step,
    rate,
    skip,
    init_state,
    residual,
    norm_gain,
    expert_ids,
    gate_weights,
    w_gate,
    w_up,
    w_down,
):
    token_count, channels = x_in.shape
    heads_here = rate.shape[0]
    head_width = channels // heads_here
    state_width = b_in.shape[1]
    blocks = token_count // GROUP
    inputs = x_in.astype(jnp.float32).reshape(blocks, GROUP, heads_here, head_width)
    keys_in = b_in.astype(jnp.float32).reshape(blocks, GROUP, state_width)
    queries = c_out.astype(jnp.float32).reshape(blocks, GROUP, state_width)
    log_steps = (-rate[None, :] * dt_step).reshape(blocks, GROUP, heads_here)
    cumulative = jnp.cumsum(log_steps, axis=1)
    scores = jnp.einsum("ctn,csn->cts", queries, keys_in, precision=PRECISE)
    causal = jnp.arange(GROUP)[:, None] >= jnp.arange(GROUP)[None, :]
    spread = cumulative[:, :, None, :] - cumulative[:, None, :, :]
    weights = jnp.exp(jnp.where(causal[None, :, :, None], spread, -jnp.inf)) * scores[..., None]
    intra_out = jnp.einsum("ctsh,cshp->cthp", weights, inputs, precision=PRECISE)
    tail_decay = jnp.exp(cumulative[:, -1:, :] - cumulative)
    block_state = jnp.einsum("csh,cshp,csn->chpn", tail_decay, inputs, keys_in, precision=PRECISE)
    block_log = cumulative[:, -1, :]

    def advance(carried, element):
        total_log, total_state = carried
        step_log, step_state = element
        updated = (
            total_log + step_log,
            jnp.exp(step_log)[:, None, None] * total_state + step_state,
        )
        return (updated, (total_log, total_state))

    zero_state = jnp.zeros((heads_here, head_width, state_width), jnp.float32)
    zero_log = jnp.zeros((heads_here,), jnp.float32)
    (device_log, device_state), (enter_log, enter_state) = lax.scan(
        advance, (zero_log, zero_state), (block_log, block_state)
    )
    prior_log, prior_state = entering_2(
        (device_log, device_state), "seq", chain_combine, (zero_log, zero_state)
    )
    incoming = prior_state + jnp.exp(prior_log)[:, None, None] * init_state
    entering = enter_state + jnp.exp(enter_log)[:, :, None, None] * incoming[None]
    inter_out = jnp.exp(cumulative)[..., None] * jnp.einsum(
        "chpn,ctn->cthp", entering, queries, precision=PRECISE
    )
    mixed_out = (intra_out + inter_out + skip[None, None, :, None] * inputs).reshape(
        token_count, channels
    )
    mixer = (mixed_out * jax.nn.silu(z_gate.astype(jnp.float32))).astype(jnp.bfloat16)
    token_mix = lax.all_to_all(mixer, "exp", split_axis=0, concat_axis=1, tiled=True)
    stream = (residual.astype(jnp.float32) + token_mix.astype(jnp.float32)).astype(jnp.bfloat16)
    widened = stream.astype(jnp.float32)
    normed = (
        widened
        * lax.rsqrt(jnp.mean(widened * widened, axis=-1, keepdims=True) + 1e-06)
        * norm_gain[None, :]
    ).astype(jnp.bfloat16)
    rows_here = residual.shape[0]
    owners = lax.axis_size("exp")
    local_experts = w_gate.shape[0]
    experts = owners * local_experts
    capacity = max(2, 2 * rows_here // experts + 1)
    width = residual.shape[1]
    chosen = expert_ids.reshape(-1)
    onehot = (chosen[:, None] == jnp.arange(experts)[None, :]).astype(jnp.int32)
    slot_index = jnp.sum((jnp.cumsum(onehot, axis=0) - onehot) * onehot, axis=1)
    target = chosen * capacity + slot_index
    placing = (target[None, :] == jnp.arange(experts * capacity)[:, None]).astype(jnp.bfloat16)
    pair_rows = jnp.repeat(normed, 2, axis=0)
    outgoing = jnp.dot(placing, pair_rows, preferred_element_type=jnp.float32).astype(jnp.bfloat16)
    outgoing = outgoing.reshape(owners, local_experts, 1, capacity, width)
    arrived = lax.all_to_all(outgoing, "exp", split_axis=0, concat_axis=2, tiled=True)
    segment = lax.all_gather(arrived, "seq", axis=1, tiled=True)
    flattened = segment.reshape(segment.shape[0], -1, segment.shape[-1])
    gate_proj = jnp.einsum("erd,edf->erf", flattened, w_gate, preferred_element_type=jnp.float32)
    up_proj = jnp.einsum("erd,edf->erf", flattened, w_up, preferred_element_type=jnp.float32)
    active = (jax.nn.silu(gate_proj) * up_proj).astype(jnp.bfloat16)
    partial_value = jnp.einsum("erf,efd->erd", active, w_down, preferred_element_type=jnp.float32)
    partials = partial_value.reshape(segment.shape[:-1] + (partial_value.shape[-1],))
    summed = lax.psum_scatter(partials.astype(jnp.bfloat16), "seq", scatter_dimension=1, tiled=True)
    returned = lax.all_to_all(summed, "exp", split_axis=2, concat_axis=0, tiled=True)
    results = returned.reshape(experts * capacity, width)
    picked = results[target].astype(jnp.float32).reshape(rows_here, 2, width)
    mixture = jnp.sum(picked * gate_weights[:, :, None], axis=1)
    return (widened + mixture).astype(jnp.bfloat16)


def solution(mesh):
    square = mesh.shape["seq"] == 4 and mesh.shape["exp"] == 8

    def body(*args):
        rows = args[8].shape[0]
        experts = mesh.shape["exp"] * args[12].shape[0]
        fits = args[12].shape[0] == 1 and 2 * rows // experts + 1 == 9
        return (on_square if square and fits else on_device)(*args)

    return jax.shard_map(
        body,
        mesh=mesh,
        in_specs=(
            P("seq", "exp"),
            P("seq", "exp"),
            P("seq", None),
            P("seq", None),
            P("seq", "exp"),
            P("exp"),
            P("exp"),
            P("exp", None, None),
            P(("seq", "exp"), None),
            P(),
            P(("seq", "exp"), None),
            P(("seq", "exp"), None),
            P("exp", None, "seq"),
            P("exp", None, "seq"),
            P("exp", "seq", None),
        ),
        out_specs=P(("seq", "exp"), None),
        check_vma=False,
    )
```

```python
import functools

import jax
import jax.numpy as jnp
from jax import lax
from jax.experimental import pallas as pl
from jax.experimental.pallas import tpu as pltpu
from jax.sharding import PartitionSpec as P

GROUP = 128
PRECISE = lax.Precision.HIGHEST
F32 = jnp.float32
BF16 = jnp.bfloat16
MIB = 1 << 20
NO_COST = pl.CostEstimate(flops=0, bytes_accessed=0, transcendentals=0)


def block_call(body, outs, scalars, args, held=0, keep=0, after=(), limit=16, out_blocks=False, name=None):
    n_args = len(args)
    kept = [jax.ShapeDtypeStruct(v.shape, v.dtype) for v in args[scalars : scalars + held]]

    def kernel(*refs):
        refs, sems = (refs[:-1], refs[-1]) if held else (refs, None)
        inputs, refs = refs[:n_args], refs[n_args + len(after) :]
        results, refs = refs[: len(outs)], refs[len(outs) :]
        copies = [
            pltpu.make_async_copy(src, dst, sems.at[k])
            for k, (src, dst) in enumerate(zip(inputs[scalars : scalars + held], refs))
        ]
        for copy in copies:
            copy.start()
        for copy in copies:
            copy.wait()
        body(*inputs[:scalars], *refs, *inputs[scalars + held :], *results)

    scratch = [pltpu.VMEM(v.shape, v.dtype) for v in kept[keep:]]
    if held:
        scratch.append(pltpu.SemaphoreType.DMA((held,)))
    return pl.pallas_call(
        kernel,
        name=name or getattr(body, "func", body).__name__,
        out_shape=list(outs) + kept[:keep],
        in_specs=[pl.BlockSpec(memory_space=pltpu.SMEM)] * scalars
        + [pl.BlockSpec(memory_space=pltpu.HBM)] * held
        + [pl.BlockSpec(memory_space=pltpu.VMEM)] * (n_args - scalars - held)
        + [pl.BlockSpec(memory_space=pl.ANY)] * len(after),
        out_specs=[pl.BlockSpec() if out_blocks else pl.BlockSpec(memory_space=pltpu.VMEM)]
        * (len(outs) + keep),
        scratch_shapes=scratch,
        compiler_params=pltpu.CompilerParams(vmem_limit_bytes=limit * MIB),
        cost_estimate=NO_COST,
    )(*args, *after)


def iota(shape, dim):
    return lax.broadcasted_iota(jnp.int32, shape, dim)


def dot(a, b, precision=None):
    return jnp.dot(a, b, precision=precision, preferred_element_type=F32)


def head_spread(heads, channels):
    shape = (heads, channels)
    return (iota(shape, 1) // (channels // heads) == iota(shape, 0)).astype(F32)


def running_logs(dt_t_ref, rate_ref):
    logs = -rate_ref[...] * dt_t_ref[...].T
    tokens = logs.shape[0]
    tri = (iota((tokens, tokens), 0) >= iota((tokens, tokens), 1)).astype(F32)
    return dot(tri, logs, PRECISE)


def pack_kernel(ids_t_ref, residual_ref, out_ref):
    parts, rows, wide = out_ref.shape
    part = wide - 128
    ids = ids_t_ref[...].astype(F32).T
    lane = iota((rows, 128), 1)
    named = jnp.where(lane == 0, ids[:, 0:1], jnp.where(lane == 1, ids[:, 1:2], 0.0)).astype(BF16)
    for k in range(parts):
        out_ref[k, :, 0:part] = residual_ref[:, k * part : (k + 1) * part]
        out_ref[k, :, part:wide] = named


def state_kernel(place, x_ref, z_ref, b_ref, c_ref, dt_t_ref, rate_ref, skip_ref, init_ref, payload_ref, init_t_ref):
    tokens, channels = x_ref.shape
    heads = dt_t_ref.shape[0]
    width = b_ref.shape[1]
    cum = running_logs(dt_t_ref, rate_ref)
    total = cum[tokens - 1 : tokens, :]
    spread = head_spread(heads, channels)
    tail = dot(jnp.exp(total - cum), spread, PRECISE)
    scaled = (x_ref[...].astype(F32) * tail).astype(BF16)
    keys = b_ref[...].astype(F32).T.astype(BF16)
    own = dot(keys, scaled)
    decay = dot(jnp.broadcast_to(jnp.exp(total), (8, heads)), spread, PRECISE)
    init_t = init_ref[...].T
    init_t_ref[...] = init_t.astype(BF16)
    first = (place[0] == 0).astype(F32)
    payload_ref[0:width, :] = (own + first * (decay[0:1, :] * init_t)).astype(BF16)
    high = decay.astype(BF16).astype(F32)
    rows = iota((16, channels), 0)
    high16 = jnp.broadcast_to(high[0:1, :], (16, channels))
    low16 = jnp.broadcast_to(decay[0:1, :], (16, channels)) - high16
    payload_ref[width : width + 16, :] = jnp.where(
        rows == 0, high16, jnp.where(rows == 1, low16, 0.0)
    ).astype(BF16)


def intra_kernel(x_ref, z_ref, b_ref, c_ref, dt_t_ref, rate_ref, skip_ref, init_t_ref, own_ref, fade_ref, c_out_ref, init_out_ref):
    tokens, channels = x_ref.shape
    heads = dt_t_ref.shape[0]
    width = channels // heads
    c_out_ref[...] = c_ref[...]
    init_out_ref[...] = init_t_ref[...]
    shape = (tokens, tokens)
    causal = iota(shape, 0) >= iota(shape, 1)
    cum = running_logs(dt_t_ref, rate_ref)
    cum_t = cum.T
    scores = lax.dot_general(
        c_ref[...], b_ref[...], (((1,), (1,)), ((), ())), preferred_element_type=F32
    )
    spread = head_spread(heads, channels)
    direct = dot(jnp.broadcast_to(skip_ref[...], (8, heads)), spread, PRECISE)[0:1, :]
    fade = dot(jnp.exp(cum), spread, PRECISE)
    per = 128 // width
    lane_head = iota((tokens, 128), 1) // width
    for group in range(heads // per):
        cols = slice(group * 128, (group + 1) * 128)
        x = x_ref[:, cols]
        total = x.astype(F32) * direct[:, cols]
        for k in range(per):
            h = group * per + k
            gap = jnp.where(causal, cum[:, h : h + 1] - cum_t[h : h + 1, :], -1e30)
            weights = (jnp.exp(gap) * scores).astype(BF16)
            part = dot(weights, x)
            total = total + jnp.where(lane_head == k, part, 0.0)
        z = z_ref[:, cols].astype(F32)
        gate = z / (1.0 + jnp.exp(-z))
        own_ref[:, cols] = total * gate
        fade_ref[:, cols] = fade[:, cols] * gate


def place_kernel(cap, experts, me, packed_ref, out_ref):
    blocks, rows, wide = packed_ref.shape
    tokens = blocks * rows
    slots = out_ref.shape[1] - rows
    ids = packed_ref[:, :, wide - 128 : wide].astype(F32).reshape(tokens, 128).T
    ids = ids[0:8, :].astype(jnp.int32)
    shape = (tokens, tokens)
    before = (iota(shape, 0) < iota(shape, 1)) & (iota(shape, 0) // rows == iota(shape, 1) // rows)
    named = iota((experts, tokens), 0) ^ me[0]
    hit = (ids[0:1, :] == named) | (ids[1:2, :] == named)
    rank = dot(hit.astype(BF16), before.astype(BF16)).astype(jnp.int32)
    block = (iota((experts, tokens), 1) // rows) ^ named
    whole = cap - 1
    row = jnp.where(rank < whole, block * whole + rank, blocks * whole + block)
    row = jnp.where(hit, row, -1)
    shape = (rows + slots, tokens)
    for e in range(experts):
        owned = ((me[0] ^ e) * rows + iota(shape, 0) == iota(shape, 1)) & (iota(shape, 0) < rows)
        placed = (iota(shape, 0) - rows == row[e : e + 1, :]) & (iota(shape, 0) >= rows)
        out_ref[e] = (owned | placed).astype(F32).astype(BF16)


def join_kernel(place, own_ref, other_ref, token_ref, out_ref):
    width = out_ref.shape[0]
    odd = place[0] % 2 == 1
    own, other = own_ref[0:width, :].astype(F32), other_ref[0:width, :].astype(F32)
    own_decay = own_ref[width : width + 16, :].astype(F32)
    other_decay = other_ref[width : width + 16, :].astype(F32)
    own_decay = own_decay[0:1, :] + own_decay[1:2, :]
    other_decay = other_decay[0:1, :] + other_decay[1:2, :]
    early = jnp.where(odd, other, own)
    late = jnp.where(odd, own, other)
    decay = jnp.where(odd, own_decay, other_decay)
    out_ref[...] = (decay * early + late).astype(BF16)


def stream_kernel(
    place, c_ref, own_ref, fade_ref, init_t_ref, pair_ref, early_ref, res_ref, sel_ref, same_ref, other_ref
):
    width = init_t_ref.shape[0]
    at = place[0]
    zero = (at == 0).astype(F32)
    odd = (at % 2 == 1).astype(F32)
    pair = pair_ref[...].astype(F32)
    decay = pair[width : width + 1, :] + pair[width + 1 : width + 2, :]
    factor = jnp.where(at >= 2, jnp.where(at % 2 == 1, decay, 1.0), 0.0)
    entering = zero * init_t_ref[...].astype(F32) + odd * pair[0:width, :] + factor * early_ref[...].astype(F32)
    mixed = own_ref[...] + fade_ref[...] * dot(c_ref[...], entering.astype(BF16))
    mixer = mixed.astype(BF16).astype(F32)
    tokens, channels = mixer.shape
    residual = res_ref[:, :, 0:channels].astype(F32).reshape(tokens, channels)
    stream = (residual + mixer).astype(BF16)
    for k in range(same_ref.shape[0]):
        same_ref[k] = dot(sel_ref[2 * k], stream).astype(BF16)
        other_ref[k] = dot(sel_ref[2 * k + 1], stream).astype(BF16)


def up_kernel(first, features, after, me, *refs):
    own, rx, ry, even, odd, gain, wg, wu = refs[:8]
    carry = () if first else refs[8:11]
    rest = refs[(8 if first else 11) + after :]
    sums = rest[1:4] if features else rest
    step = pl.program_id(0)
    steps = pl.num_programs(0)

    if first or features:

        @pl.when(step == 0)
        def _():
            for i, acc in enumerate(sums):
                acc[...] = jnp.zeros_like(acc) if first else carry[i][...]

    gate, up, square = sums
    slots = own.shape[1]
    rows = [r[0].astype(F32) for r in (own, rx, ry)]
    rows.append(jnp.where(step == 0, even[0].astype(F32), odd[0].astype(F32)))
    rows = jnp.concatenate(rows, axis=0)
    square[...] += jnp.broadcast_to(jnp.sum(rows * rows, axis=1, keepdims=True), square.shape)
    scaled = (rows * gain[0]).astype(BF16)
    gate[...] += dot(scaled, wg[0])
    up[...] += dot(scaled, wu[0])

    if features:
        out, stage = rest[0], rest[4]

        @pl.when(step == steps - 1)
        def _():
            inverse = lax.rsqrt(square[:, 0:1] * (1.0 / features) + 1e-06)
            g = gate[...] * inverse
            active = g / (1.0 + jnp.exp(-g)) * (up[...] * inverse)
            main, ninths = slots // 9 * 8, slots // 9
            for d in range(4):
                at = d * slots
                stage[d * main : (d + 1) * main, :] = active[at : at + main]
                low = 4 * main + d * ninths
                stage[low : low + ninths, :] = active[at + main : at + slots]
            out[...] = stage[...].astype(BF16)


def up_project(group, last, me, near, far, gain, w_gate, w_up, carry, after=()):
    slots, part = near[0][0].shape[1:]
    hidden = w_gate.shape[2]
    total = 4 * slots
    source = lambda i, me: me[0] ^ (2 * group + i)
    rows = [
        pl.BlockSpec((1, slots, part), lambda i, me, start=start: (start + i, 0, 0))
        for _, start in near
    ] + [
        pl.BlockSpec((1, slots, part), lambda i, me, start=start: (start, 0, 0)) for _, start in far
    ]
    weight = pl.BlockSpec((1, part, hidden), lambda i, me: (source(i, me), 0, 0))
    in_place = pl.BlockSpec(memory_space=pltpu.VMEM)
    specs = rows + [pl.BlockSpec((1, 1, part), lambda i, me: (source(i, me), 0, 0)), weight, weight]
    sums = [
        jax.ShapeDtypeStruct((total, hidden), F32),
        jax.ShapeDtypeStruct((total, hidden), F32),
        jax.ShapeDtypeStruct((total, 128), F32),
    ]
    aliases = {}
    if carry is not None:
        specs += [in_place] * 3
        if not last:
            aliases = {9 + i: i for i in range(3)}
    specs += [pl.BlockSpec(memory_space=pl.ANY)] * len(after)
    outs = [jax.ShapeDtypeStruct((total, hidden), BF16)] if last else sums
    scratch = [pltpu.VMEM(s.shape, s.dtype) for s in sums]
    scratch.append(pltpu.VMEM((total, hidden), F32))
    features = gain.shape[0] * part if last else 0
    return pl.pallas_call(
        functools.partial(up_kernel, carry is None, features, len(after)),
        name=f"up_{group}",
        out_shape=outs,
        grid_spec=pltpu.PrefetchScalarGridSpec(
            num_scalar_prefetch=1,
            grid=(2,),
            in_specs=specs,
            out_specs=[in_place] * len(outs),
            scratch_shapes=scratch if last else [],
        ),
        input_output_aliases=aliases,
        compiler_params=pltpu.CompilerParams(vmem_limit_bytes=48 * MIB),
        cost_estimate=NO_COST,
    )(me, *(array for array, _ in near + far), gain, w_gate, w_up, *(carry or ()), *after)


def cut_of(group):
    return 5 if group % 2 else 4


def down_kernel(act_ref, w_ref, *refs):
    outs, spare = refs[:-1], refs[-1]
    step = pl.program_id(0)
    part = dot(act_ref[...], w_ref[...])
    ninths = part.shape[0] // 9
    main = part.shape[0] - ninths
    groups = ninths // 8

    def through(group, tile):
        to_x, to_y = outs[2 * (group // 2) : 2 * (group // 2) + 2]
        cut = cut_of(group)
        return to_x, tile + (0 if group % 2 else 5), to_y, tile - cut + (0 if group % 2 else 4)

    for shard in range(4):
        for group in range(groups):
            at = (shard * groups + group) * 16
            rows = part[at : at + 16, :].astype(BF16)
            if shard < 3:
                outs[groups + 3 * group + shard][step] = rows
                continue
            to_x, place_x, to_y, place_y = through(group, step)

            @pl.when(step < cut_of(group))
            def _():
                to_x[place_x] = rows

            @pl.when(step >= cut_of(group))
            def _():
                to_y[place_y] = rows

    for lanes in range(spare.shape[0]):
        spare[lanes, pl.ds(pl.multiple_of(step * ninths, 8), ninths), :] = part[
            main:, lanes * 128 : (lanes + 1) * 128
        ]

    @pl.when(step == pl.num_programs(0) - 1)
    def _():
        for shard in range(4):
            for group in range(groups):
                pair = []
                for side in range(2):
                    row = pl.ds((shard * groups + group) * 2 + side, 8, stride=ninths)
                    ninth = [spare[lanes, row, :] for lanes in range(spare.shape[0])]
                    pair.append(jnp.concatenate(ninth, axis=1))
                pair = jnp.concatenate(pair, axis=0).astype(BF16)
                if shard < 3:
                    outs[groups + 3 * group + shard][8] = pair
                else:
                    _, _, to_y, place_y = through(group, 8)
                    to_y[place_y] = pair


def down_project(active, w_down):
    total, hidden = active.shape
    features = w_down.shape[1]
    tile = features // 8
    outs = [jax.ShapeDtypeStruct((9, 16, tile), BF16)] * 16
    return pl.pallas_call(
        down_kernel,
        name="down",
        grid=(8,),
        out_shape=outs,
        in_specs=[
            pl.BlockSpec(memory_space=pltpu.VMEM),
            pl.BlockSpec((hidden, tile), lambda i: (0, i)),
        ],
        out_specs=[pl.BlockSpec(memory_space=pltpu.VMEM)] * len(outs),
        scratch_shapes=[pltpu.VMEM((tile // 128, 8 * total // 9, 128), F32)],
        compiler_params=pltpu.CompilerParams(vmem_limit_bytes=48 * MIB),
        cost_estimate=NO_COST,
    )(active, w_down)


def pair_kernel(same, other, *outs):
    groups = len(outs) // 2
    owned = outs[groups].shape[1]
    for k in range(groups):
        for side, rows in enumerate((same, other)):
            outs[k][side] = rows[k, owned:, :]
            outs[groups + k][side] = rows[k, 0:owned, :]


def second_kernel(*refs):
    parts, out = refs[:-1], refs[-1]
    for h in range(out.shape[0]):
        for k in range(out.shape[1]):
            pair = [ref[k].astype(F32)[8:16] for ref in parts[2 * h : 2 * h + 2]]
            out[h, k] = jnp.concatenate(pair, axis=0).astype(BF16)


def holds_kernel(*refs):
    for source, target in zip(refs[: len(refs) // 2], refs[len(refs) // 2 :]):
        target[...] = source[...]


def hold_kernel(a, out):
    out[...] = a[...]


def half_message_kernel(rx, ry, out_x, out_y):
    out_x[0], out_y[0] = ry[1], rx[0]


def join_message_kernel(own, rx, ry, out_x, out_y):
    out_x[0:2], out_y[0:2] = own[...], own[...]
    out_x[2], out_y[2] = ry[1], rx[0]


def relay_kernel(through_x, through_y, *refs):
    ahead = refs[4 : 4 + (len(refs) - 8) // 2]
    outs, copies = refs[4 + len(ahead) :][:4], refs[8 + len(ahead) :]
    for group in range(2):
        cut = cut_of(group)
        at_x, at_y = (0, -cut) if group else (5, 0)
        for own, out, through, tiles, at in (
            (refs[2 * group], outs[2 * group], through_y, range(cut, 9), at_y),
            (refs[2 * group + 1], outs[2 * group + 1], through_x, range(cut), at_x),
        ):
            for k in range(9):
                if k in tiles:
                    out[k] = (own[k].astype(F32) + through[k + at].astype(F32)).astype(BF16)
                else:
                    out[k] = own[k]
    for source, copy in zip(ahead, copies):
        copy[...] = source[...]


def finish_kernel(own, rx, ry, *refs):
    ahead = refs[: (len(refs) - 1) // 2]
    out, copies = refs[len(ahead)], refs[len(ahead) + 1 :]
    for k in range(9):
        out[k] = (own[k].astype(F32) + rx[k].astype(F32) + ry[k].astype(F32)).astype(BF16)
    for source, copy in zip(ahead, copies):
        copy[...] = source[...]


def mix_kernel(me, ids_t_ref, weight_t_ref, swap_ref, *refs):
    groups = (len(refs) - 1) // 2
    firsts, streams, out_ref = refs[:groups], refs[groups:-1], refs[-1]
    rows = ids_t_ref.shape[1]
    experts = 2 * groups
    pieces = firsts[0].shape[0] - 1
    tile = firsts[0].shape[2]
    ids, weights = ids_t_ref[...].T, weight_t_ref[...].T
    named = iota((rows, experts), 1) ^ me[0]
    first, second = ids[:, 0:1] == named, ids[:, 1:2] == named
    weight = jnp.where(first, weights[:, 0:1], jnp.where(second, weights[:, 1:2], 0.0))
    hit = (first | second).astype(F32)
    before = (iota((rows, rows), 0) > iota((rows, rows), 1)).astype(F32)
    rank = dot(before, hit)
    lanes = 2 * experts * 8
    shape = (experts, lanes)
    spread = ((iota(shape, 1) // 8) % experts == iota(shape, 0)).astype(F32)
    weight = dot(weight, spread, PRECISE)
    rank = dot(rank, spread, PRECISE).astype(jnp.int32)
    lane = iota((rows, lanes), 1)
    main = (lane < experts * 8) & (rank == lane % 8)
    extra = (lane >= experts * 8) & (rank == 8)

    def rows_of(k):
        data = []
        for g in range(groups):
            data.append(firsts[g][k].astype(F32)[0:8])
            data.append(swap_ref[g // 2, k].astype(F32)[g % 2 * 8 : g % 2 * 8 + 8])
        return data

    last = rows_of(pieces)
    for m in range(experts):
        k = me[0] ^ m
        coef = jnp.where(main | (extra & (lane % 8 == k)), weight, 0.0)
        high = coef.astype(BF16)
        low = (coef - high.astype(F32)).astype(BF16)
        data = jnp.concatenate(rows_of(k) + last, axis=0).astype(BF16)
        stream = streams[m // 2][m % 2].astype(F32)
        out_ref[:, pl.ds(pl.multiple_of(k * tile, 128), tile)] = (
            stream + (dot(high, data) + dot(low, data))
        ).astype(BF16)


def on_square(
    x_in,
    z_gate,
    b_in,
    c_out,
    dt_step,
    rate,
    skip,
    init_state,
    residual,
    norm_gain,
    expert_ids,
    gate_weights,
    w_gate,
    w_up,
    w_down,
):
    tokens, channels = x_in.shape
    heads = rate.shape[0]
    state = b_in.shape[1]
    owners = lax.axis_size("exp")
    rows, features = residual.shape
    experts = owners
    cap = max(2, 2 * rows // experts + 1)
    slots = owners * cap
    at = lax.axis_index("seq")
    me = lax.axis_index("exp")
    place = jnp.reshape(at, (1,)).astype(jnp.int32)
    self_id = jnp.reshape(me, (1,)).astype(jnp.int32)

    def over_x(v):
        return lax.ppermute(v, "seq", [(i, i ^ 1) for i in range(4)])

    def over_y(v):
        return lax.ppermute(v, "seq", [(i, i ^ 2) for i in range(4)])

    def along(v, mask):
        return lax.ppermute(v, "exp", [(i, i ^ mask) for i in range(owners)])

    rate_row = rate[None, :]
    dt_t = dt_step.T
    ids_t = expert_ids.T
    packed = block_call(
        pack_kernel,
        [jax.ShapeDtypeStruct((owners, rows, channels + 128), BF16)],
        0,
        (ids_t, residual),
        held=2,
        limit=48,
    )[0]
    packed = lax.all_to_all(packed, "exp", split_axis=0, concat_axis=0, tiled=True)
    payload, init_t, x, z, b, c, dt, rates, skips = block_call(
        state_kernel,
        [
            jax.ShapeDtypeStruct((state + 16, channels), BF16),
            jax.ShapeDtypeStruct((state, channels), BF16),
        ],
        1,
        (
            place,
            x_in,
            z_gate,
            b_in,
            c_out,
            dt_t,
            rate_row,
            skip[None, :],
            init_state.reshape(channels, state),
        ),
        held=8,
        keep=7,
        limit=61,
    )
    pair = over_x(payload)
    own_part, fade, c, init_t = block_call(
        intra_kernel,
        [
            jax.ShapeDtypeStruct((tokens, channels), F32),
            jax.ShapeDtypeStruct((tokens, channels), F32),
            jax.ShapeDtypeStruct(c.shape, BF16),
            jax.ShapeDtypeStruct(init_t.shape, BF16),
        ],
        0,
        (x, z, b, c, dt, rates, skips, init_t),
    )
    joined = block_call(
        join_kernel,
        [jax.ShapeDtypeStruct((state, channels), BF16)],
        1,
        (place, payload, pair, c),
    )[0]
    early = over_y(joined)
    select = block_call(
        functools.partial(place_kernel, cap, experts),
        [jax.ShapeDtypeStruct((experts, rows + slots, tokens), BF16)],
        1,
        (self_id, packed),
    )[0]
    groups = owners // 2
    lanes = jax.ShapeDtypeStruct((groups, rows + slots, channels), BF16)
    same, other = block_call(
        stream_kernel,
        [lanes, lanes],
        1,
        (place, c, own_part, fade, init_t, pair, early, packed, select),
    )

    gain = norm_gain.reshape(owners, 1, channels)
    wg = w_gate.reshape(owners, channels, w_gate.shape[2])
    wu = w_up.reshape(owners, channels, w_up.shape[2])
    sets = list(block_call(
        pair_kernel,
        [jax.ShapeDtypeStruct((2, slots, channels), BF16)] * groups
        + [jax.ShapeDtypeStruct((2, rows, channels), BF16)] * groups,
        0,
        (same, along(other, 1)),
    ))
    sets, streams = sets[:groups], sets[groups:]
    def hold(v, after, name):
        return block_call(
            hold_kernel, [jax.ShapeDtypeStruct(v.shape, BF16)], 0, (v,), after=after, name=name
        )[0]

    def project(group, near, far, carry, after=()):
        last = group == groups - 1
        return up_project(group, last, self_id, near, far, gain, wg, wu, carry, after)

    def message(count):
        return [jax.ShapeDtypeStruct((count,) + sets[0].shape[1:], BF16)] * 2

    near, far, farthest = along(sets[1], 2), along(sets[2], 4), sets[3]
    rx0, ry0 = over_x(sets[0]), over_y(sets[0])
    to_x, to_y = block_call(half_message_kernel, message(1), 0, (rx0, ry0), name="half_0")
    fx0, fy0 = over_x(to_x), over_y(to_y)
    near = hold(near, (fx0, fy0), "hold_near")
    farthest_held = hold(farthest, (to_x,), "hold_farthest")
    farthest = along(farthest_held, 6)
    rx1, ry1 = over_x(near), over_y(near)
    to_x, to_y = block_call(
        join_message_kernel, message(3), 0, (far, rx1, ry1), after=(farthest_held,), name="join_2"
    )
    rx2, ry2 = over_x(to_x), over_y(to_y)
    carry = project(0, [(sets[0], 0), (rx0, 0), (ry0, 0)], [(fy0, 0), (fx0, 0)], None)
    to_x, to_y = block_call(
        join_message_kernel, message(3), 0, (farthest, rx2, ry2), after=(carry[2],), name="join_3"
    )
    rx3, ry3 = over_x(to_x), over_y(to_y)
    held = block_call(
        holds_kernel,
        [jax.ShapeDtypeStruct(v.shape, BF16) for v in streams[1:]],
        0,
        streams[1:],
        after=(to_x,),
    )
    streams[1:] = [along(held[g - 1], 2 * g) for g in range(1, groups)]
    carry = project(1, [(near, 0), (rx1, 0), (ry1, 0)], [(ry2, 2), (rx2, 2)], carry, held[:1])
    to_x, to_y = block_call(
        half_message_kernel, message(1), 0, (rx3, ry3), after=(carry[2], *streams[1:]), name="half_3"
    )
    fx3, fy3 = over_x(to_x), over_y(to_y)
    carry = project(2, [(far, 0), (rx2, 0), (ry2, 0)], [(ry3, 2), (rx3, 2)], carry)
    active = project(3, [(farthest, 0), (rx3, 0), (ry3, 0)], [(fy3, 0), (fx3, 0)], carry)[0]

    wd = w_down.reshape(w_down.shape[1], features)
    tiles = jax.ShapeDtypeStruct((9, 16, features // 8), BF16)
    sent = down_project(active, wd)
    own, own_x, own_y = ([sent[4 + 3 * g + k] for g in range(groups)] for k in range(3))

    def relay(name, through_x, through_y, low, ahead=(), after=()):
        shares = (own_x[low], own_y[low], own_x[low + 1], own_y[low + 1])
        return block_call(
            relay_kernel,
            [tiles] * (4 + len(ahead)),
            0,
            (through_x, through_y, *shares, *ahead),
            after=after,
            name=name,
        )

    def finish(group, rx, ry, ahead=()):
        return block_call(
            finish_kernel,
            [tiles] * (1 + len(ahead)),
            0,
            (own[group], rx, ry, *ahead),
            name=f"finish_{group}",
        )

    through_x, through_y = over_x(sent[2]), over_y(sent[3])
    x2, y2, x3, y3, next_x, next_y = relay(
        "relay_far", through_x, through_y, 2, (sent[0], sent[1])
    )
    rx3, ry3 = over_x(x3), over_y(y3)
    through_x, through_y = over_x(next_x), over_y(next_y)
    both3, x2, y2 = finish(3, rx3, ry3, (x2, y2))
    back3 = along(both3, 6)
    rx2, ry2 = over_x(x2), over_y(y2)
    x0, y0, x1, y1 = relay("relay_near", through_x, through_y, 0, after=(both3,))
    rx1, ry1 = over_x(x1), over_y(y1)
    both2, x0, y0 = finish(2, rx2, ry2, (x0, y0))
    back2 = along(both2, 4)
    rx0, ry0 = over_x(x0), over_y(y0)
    back1 = along(finish(1, rx1, ry1)[0], 2)
    back = [finish(0, rx0, ry0)[0], back1, back2, back3]
    swap = block_call(second_kernel, [jax.ShapeDtypeStruct((2,) + tiles.shape, BF16)], 0, back)[0]
    swap = along(swap, 1)
    return block_call(
        mix_kernel,
        [jax.ShapeDtypeStruct((rows, features), BF16)],
        1,
        (self_id, ids_t, gate_weights.T, swap, *back, *streams),
    )[0]


def entering_2(array, axis, combine, identity):
    devices, mine = (lax.axis_size(axis), lax.axis_index(axis))
    everything = jax.tree.map(
        lambda part, kind: lax.all_gather(part.astype(kind), axis),
        array,
        (jnp.bfloat16, jnp.bfloat16),
    )
    start = jax.tree.map(
        lambda part, zero: jnp.broadcast_to(jnp.asarray(zero, part.dtype), part.shape),
        array,
        identity,
    )

    def hop(k, before):
        reached = k < mine
        new = combine(
            before, jax.tree.map(lambda part, own: part[k].astype(own.dtype), everything, array)
        )
        return jax.tree.map(lambda a, b: jnp.where(reached, a, b), new, before)

    return lax.fori_loop(0, devices, hop, start)


def chain_combine(earlier, later):
    return (earlier[0] + later[0], jnp.exp(later[0])[:, None, None] * earlier[1] + later[1])


def on_device(
    x_in,
    z_gate,
    b_in,
    c_out,
    dt_step,
    rate,
    skip,
    init_state,
    residual,
    norm_gain,
    expert_ids,
    gate_weights,
    w_gate,
    w_up,
    w_down,
):
    token_count, channels = x_in.shape
    heads_here = rate.shape[0]
    head_width = channels // heads_here
    state_width = b_in.shape[1]
    blocks = token_count // GROUP
    inputs = x_in.astype(jnp.float32).reshape(blocks, GROUP, heads_here, head_width)
    keys_in = b_in.astype(jnp.float32).reshape(blocks, GROUP, state_width)
    queries = c_out.astype(jnp.float32).reshape(blocks, GROUP, state_width)
    log_steps = (-rate[None, :] * dt_step).reshape(blocks, GROUP, heads_here)
    cumulative = jnp.cumsum(log_steps, axis=1)
    scores = jnp.einsum("ctn,csn->cts", queries, keys_in, precision=PRECISE)
    causal = jnp.arange(GROUP)[:, None] >= jnp.arange(GROUP)[None, :]
    spread = cumulative[:, :, None, :] - cumulative[:, None, :, :]
    weights = jnp.exp(jnp.where(causal[None, :, :, None], spread, -jnp.inf)) * scores[..., None]
    intra_out = jnp.einsum("ctsh,cshp->cthp", weights, inputs, precision=PRECISE)
    tail_decay = jnp.exp(cumulative[:, -1:, :] - cumulative)
    block_state = jnp.einsum("csh,cshp,csn->chpn", tail_decay, inputs, keys_in, precision=PRECISE)
    block_log = cumulative[:, -1, :]

    def advance(carried, element):
        total_log, total_state = carried
        step_log, step_state = element
        updated = (
            total_log + step_log,
            jnp.exp(step_log)[:, None, None] * total_state + step_state,
        )
        return (updated, (total_log, total_state))

    zero_state = jnp.zeros((heads_here, head_width, state_width), jnp.float32)
    zero_log = jnp.zeros((heads_here,), jnp.float32)
    (device_log, device_state), (enter_log, enter_state) = lax.scan(
        advance, (zero_log, zero_state), (block_log, block_state)
    )
    prior_log, prior_state = entering_2(
        (device_log, device_state), "seq", chain_combine, (zero_log, zero_state)
    )
    incoming = prior_state + jnp.exp(prior_log)[:, None, None] * init_state
    entering = enter_state + jnp.exp(enter_log)[:, :, None, None] * incoming[None]
    inter_out = jnp.exp(cumulative)[..., None] * jnp.einsum(
        "chpn,ctn->cthp", entering, queries, precision=PRECISE
    )
    mixed_out = (intra_out + inter_out + skip[None, None, :, None] * inputs).reshape(
        token_count, channels
    )
    mixer = (mixed_out * jax.nn.silu(z_gate.astype(jnp.float32))).astype(jnp.bfloat16)
    token_mix = lax.all_to_all(mixer, "exp", split_axis=0, concat_axis=1, tiled=True)
    stream = (residual.astype(jnp.float32) + token_mix.astype(jnp.float32)).astype(jnp.bfloat16)
    widened = stream.astype(jnp.float32)
    normed = (
        widened
        * lax.rsqrt(jnp.mean(widened * widened, axis=-1, keepdims=True) + 1e-06)
        * norm_gain[None, :]
    ).astype(jnp.bfloat16)
    rows_here = residual.shape[0]
    owners = lax.axis_size("exp")
    local_experts = w_gate.shape[0]
    experts = owners * local_experts
    capacity = max(2, 2 * rows_here // experts + 1)
    width = residual.shape[1]
    chosen = expert_ids.reshape(-1)
    onehot = (chosen[:, None] == jnp.arange(experts)[None, :]).astype(jnp.int32)
    slot_index = jnp.sum((jnp.cumsum(onehot, axis=0) - onehot) * onehot, axis=1)
    target = chosen * capacity + slot_index
    placing = (target[None, :] == jnp.arange(experts * capacity)[:, None]).astype(jnp.bfloat16)
    pair_rows = jnp.repeat(normed, 2, axis=0)
    outgoing = jnp.dot(placing, pair_rows, preferred_element_type=jnp.float32).astype(jnp.bfloat16)
    outgoing = outgoing.reshape(owners, local_experts, 1, capacity, width)
    arrived = lax.all_to_all(outgoing, "exp", split_axis=0, concat_axis=2, tiled=True)
    segment = lax.all_gather(arrived, "seq", axis=1, tiled=True)
    flattened = segment.reshape(segment.shape[0], -1, segment.shape[-1])
    gate_proj = jnp.einsum("erd,edf->erf", flattened, w_gate, preferred_element_type=jnp.float32)
    up_proj = jnp.einsum("erd,edf->erf", flattened, w_up, preferred_element_type=jnp.float32)
    active = (jax.nn.silu(gate_proj) * up_proj).astype(jnp.bfloat16)
    partial_value = jnp.einsum("erf,efd->erd", active, w_down, preferred_element_type=jnp.float32)
    partials = partial_value.reshape(segment.shape[:-1] + (partial_value.shape[-1],))
    summed = lax.psum_scatter(partials.astype(jnp.bfloat16), "seq", scatter_dimension=1, tiled=True)
    returned = lax.all_to_all(summed, "exp", split_axis=2, concat_axis=0, tiled=True)
    results = returned.reshape(experts * capacity, width)
    picked = results[target].astype(jnp.float32).reshape(rows_here, 2, width)
    mixture = jnp.sum(picked * gate_weights[:, :, None], axis=1)
    return (widened + mixture).astype(jnp.bfloat16)


def solution(mesh):
    square = mesh.shape["seq"] == 4 and mesh.shape["exp"] == 8

    def body(*args):
        rows = args[8].shape[0]
        experts = mesh.shape["exp"] * args[12].shape[0]
        fits = args[12].shape[0] == 1 and 2 * rows // experts + 1 == 9
        return (on_square if square and fits else on_device)(*args)

    return jax.shard_map(
        body,
        mesh=mesh,
        in_specs=(
            P("seq", "exp"),
            P("seq", "exp"),
            P("seq", None),
            P("seq", None),
            P("seq", "exp"),
            P("exp"),
            P("exp"),
            P("exp", None, None),
            P(("seq", "exp"), None),
            P(),
            P(("seq", "exp"), None),
            P(("seq", "exp"), None),
            P("exp", None, "seq"),
            P("exp", None, "seq"),
            P("exp", "seq", None),
        ),
        out_specs=P(("seq", "exp"), None),
        check_vma=False,
    )
```

```python
import functools

import jax
import jax.numpy as jnp
from jax import lax
from jax.experimental import pallas as pl
from jax.experimental.pallas import tpu as pltpu
from jax.sharding import PartitionSpec as P

GROUP = 128
PRECISE = lax.Precision.HIGHEST
F32 = jnp.float32
BF16 = jnp.bfloat16
MIB = 1 << 20
NO_COST = pl.CostEstimate(flops=0, bytes_accessed=0, transcendentals=0)


def block_call(body, outs, scalars, args, held=0, keep=0, after=(), limit=16, out_blocks=False, name=None):
    n_args = len(args)
    kept = [jax.ShapeDtypeStruct(v.shape, v.dtype) for v in args[scalars : scalars + held]]

    def kernel(*refs):
        refs, sems = (refs[:-1], refs[-1]) if held else (refs, None)
        inputs, refs = refs[:n_args], refs[n_args + len(after) :]
        results, refs = refs[: len(outs)], refs[len(outs) :]
        copies = [
            pltpu.make_async_copy(src, dst, sems.at[k])
            for k, (src, dst) in enumerate(zip(inputs[scalars : scalars + held], refs))
        ]
        for copy in copies:
            copy.start()
        for copy in copies:
            copy.wait()
        body(*inputs[:scalars], *refs, *inputs[scalars + held :], *results)

    scratch = [pltpu.VMEM(v.shape, v.dtype) for v in kept[keep:]]
    if held:
        scratch.append(pltpu.SemaphoreType.DMA((held,)))
    return pl.pallas_call(
        kernel,
        name=name or getattr(body, "func", body).__name__,
        out_shape=list(outs) + kept[:keep],
        in_specs=[pl.BlockSpec(memory_space=pltpu.SMEM)] * scalars
        + [pl.BlockSpec(memory_space=pltpu.HBM)] * held
        + [pl.BlockSpec(memory_space=pltpu.VMEM)] * (n_args - scalars - held)
        + [pl.BlockSpec(memory_space=pl.ANY)] * len(after),
        out_specs=[pl.BlockSpec() if out_blocks else pl.BlockSpec(memory_space=pltpu.VMEM)]
        * (len(outs) + keep),
        scratch_shapes=scratch,
        compiler_params=pltpu.CompilerParams(vmem_limit_bytes=limit * MIB),
        cost_estimate=NO_COST,
    )(*args, *after)


def iota(shape, dim):
    return lax.broadcasted_iota(jnp.int32, shape, dim)


def dot(a, b, precision=None):
    return jnp.dot(a, b, precision=precision, preferred_element_type=F32)


def head_spread(heads, channels):
    shape = (heads, channels)
    return (iota(shape, 1) // (channels // heads) == iota(shape, 0)).astype(F32)


def running_logs(dt_t_ref, rate_ref):
    logs = -rate_ref[...] * dt_t_ref[...].T
    tokens = logs.shape[0]
    tri = (iota((tokens, tokens), 0) >= iota((tokens, tokens), 1)).astype(F32)
    return dot(tri, logs, PRECISE)


def pack_kernel(ids_t_ref, residual_ref, out_ref):
    parts, rows, wide = out_ref.shape
    part = wide - 128
    ids = ids_t_ref[...].astype(F32).T
    lane = iota((rows, 128), 1)
    named = jnp.where(lane == 0, ids[:, 0:1], jnp.where(lane == 1, ids[:, 1:2], 0.0)).astype(BF16)
    for k in range(parts):
        out_ref[k, :, 0:part] = residual_ref[:, k * part : (k + 1) * part]
        out_ref[k, :, part:wide] = named


def state_kernel(place, x_ref, b_ref, dt_t_ref, rate_ref, init_ref, payload_ref, init_t_ref):
    tokens, channels = x_ref.shape
    heads = dt_t_ref.shape[0]
    width = b_ref.shape[1]
    cum = running_logs(dt_t_ref, rate_ref)
    total = cum[tokens - 1 : tokens, :]
    spread = head_spread(heads, channels)
    tail = dot(jnp.exp(total - cum), spread, PRECISE)
    scaled = (x_ref[...].astype(F32) * tail).astype(BF16)
    keys = b_ref[...].astype(F32).T.astype(BF16)
    own = dot(keys, scaled)
    decay = dot(jnp.broadcast_to(jnp.exp(total), (8, heads)), spread, PRECISE)
    init_t = init_ref[...].T
    init_t_ref[...] = init_t.astype(BF16)
    first = (place[0] == 0).astype(F32)
    payload_ref[0:width, :] = (own + first * (decay[0:1, :] * init_t)).astype(BF16)
    high = decay.astype(BF16).astype(F32)
    rows = iota((16, channels), 0)
    high16 = jnp.broadcast_to(high[0:1, :], (16, channels))
    low16 = jnp.broadcast_to(decay[0:1, :], (16, channels)) - high16
    payload_ref[width : width + 16, :] = jnp.where(
        rows == 0, high16, jnp.where(rows == 1, low16, 0.0)
    ).astype(BF16)


def intra_kernel(x_ref, z_ref, b_ref, c_ref, dt_t_ref, rate_ref, skip_ref, own_ref, fade_ref, token_ref):
    tokens, channels = x_ref.shape
    heads = dt_t_ref.shape[0]
    width = channels // heads
    token_ref[...] = jnp.zeros_like(token_ref)
    shape = (tokens, tokens)
    causal = iota(shape, 0) >= iota(shape, 1)
    cum = running_logs(dt_t_ref, rate_ref)
    cum_t = cum.T
    scores = lax.dot_general(
        c_ref[...], b_ref[...], (((1,), (1,)), ((), ())), preferred_element_type=F32
    )
    spread = head_spread(heads, channels)
    direct = dot(jnp.broadcast_to(skip_ref[...], (8, heads)), spread, PRECISE)[0:1, :]
    fade = dot(jnp.exp(cum), spread, PRECISE)
    per = 128 // width
    lane_head = iota((tokens, 128), 1) // width
    for group in range(heads // per):
        cols = slice(group * 128, (group + 1) * 128)
        x = x_ref[:, cols]
        total = x.astype(F32) * direct[:, cols]
        for k in range(per):
            h = group * per + k
            gap = jnp.where(causal, cum[:, h : h + 1] - cum_t[h : h + 1, :], -1e30)
            weights = (jnp.exp(gap) * scores).astype(BF16)
            part = dot(weights, x)
            total = total + jnp.where(lane_head == k, part, 0.0)
        z = z_ref[:, cols].astype(F32)
        gate = z / (1.0 + jnp.exp(-z))
        own_ref[:, cols] = total * gate
        fade_ref[:, cols] = fade[:, cols] * gate


def place_kernel(cap, experts, me, packed_ref, *refs):
    count = (len(refs) - 1) // 2
    out_ref = refs[count]
    for source, target in zip(refs[:count], refs[count + 1 :]):
        target[...] = source[...]
    blocks, rows, wide = packed_ref.shape
    tokens = blocks * rows
    slots = out_ref.shape[1] - rows
    ids = packed_ref[:, :, wide - 128 : wide].astype(F32).reshape(tokens, 128).T
    ids = ids[0:8, :].astype(jnp.int32)
    shape = (tokens, tokens)
    before = (iota(shape, 0) < iota(shape, 1)) & (iota(shape, 0) // rows == iota(shape, 1) // rows)
    named = iota((experts, tokens), 0) ^ me[0]
    hit = (ids[0:1, :] == named) | (ids[1:2, :] == named)
    rank = dot(hit.astype(BF16), before.astype(BF16)).astype(jnp.int32)
    block = (iota((experts, tokens), 1) // rows) ^ named
    whole = cap - 1
    row = jnp.where(rank < whole, block * whole + rank, blocks * whole + block)
    row = jnp.where(hit, row, -1)
    shape = (rows + slots, tokens)
    for e in range(experts):
        owned = ((me[0] ^ e) * rows + iota(shape, 0) == iota(shape, 1)) & (iota(shape, 0) < rows)
        placed = (iota(shape, 0) - rows == row[e : e + 1, :]) & (iota(shape, 0) >= rows)
        out_ref[e] = (owned | placed).astype(F32).astype(BF16)


def join_kernel(place, own_ref, other_ref, out_ref):
    width = out_ref.shape[0]
    odd = place[0] % 2 == 1
    own, other = own_ref[0:width, :].astype(F32), other_ref[0:width, :].astype(F32)
    own_decay = own_ref[width : width + 16, :].astype(F32)
    other_decay = other_ref[width : width + 16, :].astype(F32)
    own_decay = own_decay[0:1, :] + own_decay[1:2, :]
    other_decay = other_decay[0:1, :] + other_decay[1:2, :]
    early = jnp.where(odd, other, own)
    late = jnp.where(odd, own, other)
    decay = jnp.where(odd, own_decay, other_decay)
    out_ref[...] = (decay * early + late).astype(BF16)


def stream_kernel(
    place, c_ref, own_ref, fade_ref, init_t_ref, pair_ref, early_ref, res_ref, sel_ref, same_ref, other_ref
):
    width = init_t_ref.shape[0]
    at = place[0]
    zero = (at == 0).astype(F32)
    odd = (at % 2 == 1).astype(F32)
    pair = pair_ref[...].astype(F32)
    decay = pair[width : width + 1, :] + pair[width + 1 : width + 2, :]
    factor = jnp.where(at >= 2, jnp.where(at % 2 == 1, decay, 1.0), 0.0)
    entering = zero * init_t_ref[...].astype(F32) + odd * pair[0:width, :] + factor * early_ref[...].astype(F32)
    mixed = own_ref[...] + fade_ref[...] * dot(c_ref[...], entering.astype(BF16))
    mixer = mixed.astype(BF16).astype(F32)
    tokens, channels = mixer.shape
    residual = res_ref[:, :, 0:channels].astype(F32).reshape(tokens, channels)
    stream = (residual + mixer).astype(BF16)
    for k in range(same_ref.shape[0]):
        same_ref[k] = dot(sel_ref[2 * k], stream).astype(BF16)
        other_ref[k] = dot(sel_ref[2 * k + 1], stream).astype(BF16)


def up_kernel(first, features, after, me, *refs):
    own, rx, ry, even, odd, gain, wg, wu = refs[:8]
    carry = () if first else refs[8:11]
    rest = refs[(8 if first else 11) + after :]
    sums = rest[2:5] if features else rest
    step = pl.program_id(0)
    steps = pl.num_programs(0)

    if first or features:

        @pl.when(step == 0)
        def _():
            for i, acc in enumerate(sums):
                acc[...] = jnp.zeros_like(acc) if first else carry[i][...]

    gate, up, square = sums
    slots = own.shape[1]
    rows = [r[0].astype(F32) for r in (own, rx, ry)]
    rows.append(jnp.where(step == 0, even[0].astype(F32), odd[0].astype(F32)))
    rows = jnp.concatenate(rows, axis=0)
    square[...] += jnp.broadcast_to(jnp.sum(rows * rows, axis=1, keepdims=True), square.shape)
    scaled = (rows * gain[0]).astype(BF16)
    gate[...] += dot(scaled, wg[0])
    up[...] += dot(scaled, wu[0])

    if features:
        outs, stages = rest[:2], rest[5:]

        @pl.when(step == steps - 1)
        def _():
            inverse = lax.rsqrt(square[:, 0:1] * (1.0 / features) + 1e-06)
            g = gate[...] * inverse
            active = g / (1.0 + jnp.exp(-g)) * (up[...] * inverse)
            main, ninths = slots // 9 * 8, slots // 9
            for d in range(4):
                at = d * slots
                stage, d, shards = (stages[0], 0, 1) if d == 3 else (stages[1], d, 3)
                stage[d * main : (d + 1) * main, :] = active[at : at + main]
                low = shards * main + d * ninths
                stage[low : low + ninths, :] = active[at + main : at + slots]
            for out, stage in zip(outs, stages):
                out[...] = stage[...].astype(BF16)


def up_project(group, last, me, near, far, gain, w_gate, w_up, carry, after=()):
    slots, part = near[0][0].shape[1:]
    hidden = w_gate.shape[2]
    total = 4 * slots
    source = lambda i, me: me[0] ^ (2 * group + i)
    rows = [
        pl.BlockSpec((1, slots, part), lambda i, me, start=start: (start + i, 0, 0))
        for _, start in near
    ] + [
        pl.BlockSpec((1, slots, part), lambda i, me, start=start: (start, 0, 0)) for _, start in far
    ]
    weight = pl.BlockSpec((1, part, hidden), lambda i, me: (source(i, me), 0, 0))
    in_place = pl.BlockSpec(memory_space=pltpu.VMEM)
    specs = rows + [pl.BlockSpec((1, 1, part), lambda i, me: (source(i, me), 0, 0)), weight, weight]
    sums = [
        jax.ShapeDtypeStruct((total, hidden), F32),
        jax.ShapeDtypeStruct((total, hidden), F32),
        jax.ShapeDtypeStruct((total, 128), F32),
    ]
    aliases = {}
    if carry is not None:
        specs += [in_place] * 3
        if not last:
            aliases = {9 + i: i for i in range(3)}
    specs += [pl.BlockSpec(memory_space=pl.ANY)] * len(after)
    sizes = (slots, 3 * slots)
    outs = [jax.ShapeDtypeStruct((n, hidden), BF16) for n in sizes] if last else sums
    scratch = [pltpu.VMEM(s.shape, s.dtype) for s in sums]
    scratch += [pltpu.VMEM((n, hidden), F32) for n in sizes]
    features = gain.shape[0] * part if last else 0
    return pl.pallas_call(
        functools.partial(up_kernel, carry is None, features, len(after)),
        name=f"up_{group}",
        out_shape=outs,
        grid_spec=pltpu.PrefetchScalarGridSpec(
            num_scalar_prefetch=1,
            grid=(2,),
            in_specs=specs,
            out_specs=[in_place] * len(outs),
            scratch_shapes=scratch if last else [],
        ),
        input_output_aliases=aliases,
        compiler_params=pltpu.CompilerParams(vmem_limit_bytes=48 * MIB),
        cost_estimate=NO_COST,
    )(me, *(array for array, _ in near + far), gain, w_gate, w_up, *(carry or ()), *after)


def cut_of(group):
    return 5 if group % 2 else 4


def down_kernel(groups, act_ref, w_ref, *refs):
    outs, spare = refs[:-1], refs[-1]
    step = pl.program_id(0)
    part = dot(act_ref[...], w_ref[...])
    ninths = part.shape[0] // 9
    main = part.shape[0] - ninths
    shards = ninths // (2 * groups)

    def through(group, tile):
        to_x, to_y = outs[2 * (group // 2) : 2 * (group // 2) + 2]
        cut = cut_of(group)
        return to_x, tile + (0 if group % 2 else 5), to_y, tile - cut + (0 if group % 2 else 4)

    for shard in range(shards):
        for group in range(groups):
            at = (shard * groups + group) * 16
            rows = part[at : at + 16, :].astype(BF16)
            if shards > 1:
                outs[shards * group + shard][step] = rows
                continue
            to_x, place_x, to_y, place_y = through(group, step)

            @pl.when(step < cut_of(group))
            def _():
                to_x[place_x] = rows

            @pl.when(step >= cut_of(group))
            def _():
                to_y[place_y] = rows

    for lanes in range(spare.shape[0]):
        spare[lanes, pl.ds(pl.multiple_of(step * ninths, 8), ninths), :] = part[
            main:, lanes * 128 : (lanes + 1) * 128
        ]

    @pl.when(step == pl.num_programs(0) - 1)
    def _():
        for shard in range(shards):
            for group in range(groups):
                pair = []
                for side in range(2):
                    row = pl.ds((shard * groups + group) * 2 + side, 8, stride=ninths)
                    ninth = [spare[lanes, row, :] for lanes in range(spare.shape[0])]
                    pair.append(jnp.concatenate(ninth, axis=1))
                pair = jnp.concatenate(pair, axis=0).astype(BF16)
                if shards > 1:
                    outs[shards * group + shard][8] = pair
                else:
                    _, _, to_y, place_y = through(group, 8)
                    to_y[place_y] = pair


def down_project(name, groups, active, w_down):
    total, hidden = active.shape
    features = w_down.shape[1]
    tile = features // 8
    outs = [jax.ShapeDtypeStruct((9, 16, tile), BF16)] * (total // 18)
    return pl.pallas_call(
        functools.partial(down_kernel, groups),
        name=name,
        grid=(8,),
        out_shape=outs,
        in_specs=[
            pl.BlockSpec(memory_space=pltpu.VMEM),
            pl.BlockSpec((hidden, tile), lambda i: (0, i)),
        ],
        out_specs=[pl.BlockSpec(memory_space=pltpu.VMEM)] * len(outs),
        scratch_shapes=[pltpu.VMEM((tile // 128, 8 * total // 9, 128), F32)],
        compiler_params=pltpu.CompilerParams(vmem_limit_bytes=48 * MIB),
        cost_estimate=NO_COST,
    )(active, w_down)


def pair_kernel(same, other, *outs):
    groups = len(outs) // 2
    owned = outs[groups].shape[1]
    for k in range(groups):
        for side, rows in enumerate((same, other)):
            outs[k][side] = rows[k, owned:, :]
            outs[groups + k][side] = rows[k, 0:owned, :]


def second_kernel(*refs):
    parts, out = refs[:-1], refs[-1]
    for h in range(out.shape[0]):
        for k in range(out.shape[1]):
            pair = [ref[k].astype(F32)[8:16] for ref in parts[2 * h : 2 * h + 2]]
            out[h, k] = jnp.concatenate(pair, axis=0).astype(BF16)


def holds_kernel(*refs):
    for source, target in zip(refs[: len(refs) // 2], refs[len(refs) // 2 :]):
        target[...] = source[...]


def hold_kernel(a, out):
    out[...] = a[...]


def half_message_kernel(rx, ry, out_x, out_y):
    out_x[0], out_y[0] = ry[1], rx[0]


def join_message_kernel(own, rx, ry, out_x, out_y):
    out_x[0:2], out_y[0:2] = own[...], own[...]
    out_x[2], out_y[2] = ry[1], rx[0]


def relay_kernel(through_x, through_y, *refs):
    ahead = refs[4 : 4 + (len(refs) - 8) // 2]
    outs, copies = refs[4 + len(ahead) :][:4], refs[8 + len(ahead) :]
    for group in range(2):
        cut = cut_of(group)
        at_x, at_y = (0, -cut) if group else (5, 0)
        for own, out, through, tiles, at in (
            (refs[2 * group], outs[2 * group], through_y, range(cut, 9), at_y),
            (refs[2 * group + 1], outs[2 * group + 1], through_x, range(cut), at_x),
        ):
            for k in range(9):
                if k in tiles:
                    out[k] = (own[k].astype(F32) + through[k + at].astype(F32)).astype(BF16)
                else:
                    out[k] = own[k]
    for source, copy in zip(ahead, copies):
        copy[...] = source[...]


def finish_kernel(own, rx, ry, *refs):
    ahead = refs[: (len(refs) - 1) // 2]
    out, copies = refs[len(ahead)], refs[len(ahead) + 1 :]
    for k in range(9):
        out[k] = (own[k].astype(F32) + rx[k].astype(F32) + ry[k].astype(F32)).astype(BF16)
    for source, copy in zip(ahead, copies):
        copy[...] = source[...]


def mix_kernel(me, ids_t_ref, weight_t_ref, swap_ref, *refs):
    groups = (len(refs) - 1) // 2
    firsts, streams, out_ref = refs[:groups], refs[groups:-1], refs[-1]
    rows = ids_t_ref.shape[1]
    experts = 2 * groups
    pieces = firsts[0].shape[0] - 1
    tile = firsts[0].shape[2]
    ids, weights = ids_t_ref[...].T, weight_t_ref[...].T
    named = iota((rows, experts), 1) ^ me[0]
    first, second = ids[:, 0:1] == named, ids[:, 1:2] == named
    weight = jnp.where(first, weights[:, 0:1], jnp.where(second, weights[:, 1:2], 0.0))
    hit = (first | second).astype(F32)
    before = (iota((rows, rows), 0) > iota((rows, rows), 1)).astype(F32)
    rank = dot(before, hit)
    lanes = 2 * experts * 8
    shape = (experts, lanes)
    spread = ((iota(shape, 1) // 8) % experts == iota(shape, 0)).astype(F32)
    weight = dot(weight, spread, PRECISE)
    rank = dot(rank, spread, PRECISE).astype(jnp.int32)
    lane = iota((rows, lanes), 1)
    main = (lane < experts * 8) & (rank == lane % 8)
    extra = (lane >= experts * 8) & (rank == 8)

    def rows_of(k):
        data = []
        for g in range(groups):
            data.append(firsts[g][k].astype(F32)[0:8])
            data.append(swap_ref[g // 2, k].astype(F32)[g % 2 * 8 : g % 2 * 8 + 8])
        return data

    last = rows_of(pieces)
    for m in range(experts):
        k = me[0] ^ m
        coef = jnp.where(main | (extra & (lane % 8 == k)), weight, 0.0)
        high = coef.astype(BF16)
        low = (coef - high.astype(F32)).astype(BF16)
        data = jnp.concatenate(rows_of(k) + last, axis=0).astype(BF16)
        stream = streams[m // 2][m % 2].astype(F32)
        out_ref[:, pl.ds(pl.multiple_of(k * tile, 128), tile)] = (
            stream + (dot(high, data) + dot(low, data))
        ).astype(BF16)


def on_square(
    x_in,
    z_gate,
    b_in,
    c_out,
    dt_step,
    rate,
    skip,
    init_state,
    residual,
    norm_gain,
    expert_ids,
    gate_weights,
    w_gate,
    w_up,
    w_down,
):
    tokens, channels = x_in.shape
    heads = rate.shape[0]
    state = b_in.shape[1]
    owners = lax.axis_size("exp")
    rows, features = residual.shape
    experts = owners
    cap = max(2, 2 * rows // experts + 1)
    slots = owners * cap
    at = lax.axis_index("seq")
    me = lax.axis_index("exp")
    place = jnp.reshape(at, (1,)).astype(jnp.int32)
    self_id = jnp.reshape(me, (1,)).astype(jnp.int32)

    def over_x(v):
        return lax.ppermute(v, "seq", [(i, i ^ 1) for i in range(4)])

    def over_y(v):
        return lax.ppermute(v, "seq", [(i, i ^ 2) for i in range(4)])

    def along(v, mask):
        return lax.ppermute(v, "exp", [(i, i ^ mask) for i in range(owners)])

    rate_row = rate[None, :]
    dt_t = dt_step.T
    ids_t = expert_ids.T
    packed = block_call(
        pack_kernel,
        [jax.ShapeDtypeStruct((owners, rows, channels + 128), BF16)],
        0,
        (ids_t, residual),
        held=2,
        limit=48,
    )[0]
    packed = lax.all_to_all(packed, "exp", split_axis=0, concat_axis=0, tiled=True)
    payload, init_t = block_call(
        state_kernel,
        [
            jax.ShapeDtypeStruct((state + 16, channels), BF16),
            jax.ShapeDtypeStruct((state, channels), BF16),
        ],
        1,
        (place, x_in, b_in, dt_t, rate_row, init_state.reshape(channels, state)),
        held=5,
        limit=62,
    )
    pair = over_x(payload)
    own_part, fade, token = block_call(
        intra_kernel,
        [
            jax.ShapeDtypeStruct((tokens, channels), F32),
            jax.ShapeDtypeStruct((tokens, channels), F32),
            jax.ShapeDtypeStruct((8, 128), F32),
        ],
        0,
        (x_in, z_gate, b_in, c_out, dt_t, rate_row, skip[None, :]),
        held=7,
        limit=61,
    )
    joined = block_call(
        join_kernel,
        [jax.ShapeDtypeStruct((state, channels), BF16)],
        1,
        (place, payload, pair),
        after=(token,),
    )[0]
    early = over_y(joined)
    handed = (own_part, fade, c_out, init_t)
    select, own_part, fade, c, init_t = block_call(
        functools.partial(place_kernel, cap, experts),
        [jax.ShapeDtypeStruct((experts, rows + slots, tokens), BF16)]
        + [jax.ShapeDtypeStruct(v.shape, v.dtype) for v in handed],
        1,
        (self_id, packed, *handed),
        after=(joined,),
    )
    groups = owners // 2
    lanes = jax.ShapeDtypeStruct((groups, rows + slots, channels), BF16)
    same, other = block_call(
        stream_kernel,
        [lanes, lanes],
        1,
        (place, c, own_part, fade, init_t, pair, early, packed, select),
    )

    gain = norm_gain.reshape(owners, 1, channels)
    wg = w_gate.reshape(owners, channels, w_gate.shape[2])
    wu = w_up.reshape(owners, channels, w_up.shape[2])
    sets = list(block_call(
        pair_kernel,
        [jax.ShapeDtypeStruct((2, slots, channels), BF16)] * groups
        + [jax.ShapeDtypeStruct((2, rows, channels), BF16)] * groups,
        0,
        (same, along(other, 1)),
    ))
    sets, streams = sets[:groups], sets[groups:]
    def hold(v, after, name):
        return block_call(
            hold_kernel, [jax.ShapeDtypeStruct(v.shape, BF16)], 0, (v,), after=after, name=name
        )[0]

    def project(group, near, far, carry, after=()):
        last = group == groups - 1
        return up_project(group, last, self_id, near, far, gain, wg, wu, carry, after)

    def message(count):
        return [jax.ShapeDtypeStruct((count,) + sets[0].shape[1:], BF16)] * 2

    near, far, farthest = along(sets[1], 2), along(sets[2], 4), sets[3]
    rx0, ry0 = over_x(sets[0]), over_y(sets[0])
    to_x, to_y = block_call(half_message_kernel, message(1), 0, (rx0, ry0), name="half_0")
    fx0, fy0 = over_x(to_x), over_y(to_y)
    near = hold(near, (to_x,), "hold_near")
    farthest_held = hold(farthest, (far,), "hold_farthest")
    farthest = along(farthest_held, 6)
    rx1, ry1 = over_x(near), over_y(near)
    to_x, to_y = block_call(
        join_message_kernel, message(3), 0, (far, rx1, ry1), after=(fx0, fy0, farthest_held), name="join_2"
    )
    rx2, ry2 = over_x(to_x), over_y(to_y)
    carry = project(
        0, [(sets[0], 0), (rx0, 0), (ry0, 0)], [(fy0, 0), (fx0, 0)], None
    )
    to_x, to_y = block_call(
        join_message_kernel, message(3), 0, (farthest, rx2, ry2), after=(carry[2],), name="join_3"
    )
    rx3, ry3 = over_x(to_x), over_y(to_y)
    carry = project(1, [(near, 0), (rx1, 0), (ry1, 0)], [(ry2, 2), (rx2, 2)], carry)
    to_x, to_y = block_call(
        half_message_kernel, message(1), 0, (rx3, ry3), after=(carry[2],), name="half_3"
    )
    fx3, fy3 = over_x(to_x), over_y(to_y)
    held = block_call(
        holds_kernel,
        [jax.ShapeDtypeStruct(v.shape, BF16) for v in streams[1:]],
        0,
        streams[1:],
        after=(to_x,),
        name="hold_streams",
    )
    streams[1:] = [along(held[g - 1], 2 * g) for g in range(1, groups)]
    carry = project(2, [(far, 0), (rx2, 0), (ry2, 0)], [(ry3, 2), (rx3, 2)], carry, held[:1])
    active_far, active = project(
        3, [(farthest, 0), (rx3, 0), (ry3, 0)], [(fy3, 0), (fx3, 0)], carry
    )

    wd = w_down.reshape(w_down.shape[1], features)
    tiles = jax.ShapeDtypeStruct((9, 16, features // 8), BF16)
    sent = down_project("down_through", groups, active_far, wd)
    rest = down_project("down_rest", groups, active, wd)
    own, own_x, own_y = ([rest[3 * g + k] for g in range(groups)] for k in range(3))

    def relay(name, through_x, through_y, low, ahead=(), after=()):
        shares = (own_x[low], own_y[low], own_x[low + 1], own_y[low + 1])
        return block_call(
            relay_kernel,
            [tiles] * (4 + len(ahead)),
            0,
            (through_x, through_y, *shares, *ahead),
            after=after,
            name=name,
        )

    def finish(group, rx, ry, ahead=(), after=()):
        return block_call(
            finish_kernel,
            [tiles] * (1 + len(ahead)),
            0,
            (own[group], rx, ry, *ahead),
            after=after,
            name=f"finish_{group}",
        )

    through_x, through_y = over_x(sent[2]), over_y(sent[3])
    x2, y2, x3, y3, next_x, next_y = relay(
        "relay_far", through_x, through_y, 2, (sent[0], sent[1]), streams[1:]
    )
    rx3, ry3 = over_x(x3), over_y(y3)
    through_x, through_y = over_x(next_x), over_y(next_y)
    both3, x2, y2 = finish(3, rx3, ry3, (x2, y2))
    back3 = along(both3, 6)
    rx2, ry2 = over_x(x2), over_y(y2)
    x0, y0, x1, y1 = relay("relay_near", through_x, through_y, 0, after=(both3,))
    rx1, ry1 = over_x(x1), over_y(y1)
    both2, x0, y0 = finish(2, rx2, ry2, (x0, y0))
    back2 = along(both2, 4)
    rx0, ry0 = over_x(x0), over_y(y0)
    back1 = along(finish(1, rx1, ry1, after=(back3,))[0], 2)
    back = [finish(0, rx0, ry0)[0], back1, back2, back3]
    swap = block_call(second_kernel, [jax.ShapeDtypeStruct((2,) + tiles.shape, BF16)], 0, back)[0]
    swap = along(swap, 1)
    return block_call(
        mix_kernel,
        [jax.ShapeDtypeStruct((rows, features), BF16)],
        1,
        (self_id, ids_t, gate_weights.T, swap, *back, *streams),
    )[0]


def entering_2(array, axis, combine, identity):
    devices, mine = (lax.axis_size(axis), lax.axis_index(axis))
    everything = jax.tree.map(
        lambda part, kind: lax.all_gather(part.astype(kind), axis),
        array,
        (jnp.bfloat16, jnp.bfloat16),
    )
    start = jax.tree.map(
        lambda part, zero: jnp.broadcast_to(jnp.asarray(zero, part.dtype), part.shape),
        array,
        identity,
    )

    def hop(k, before):
        reached = k < mine
        new = combine(
            before, jax.tree.map(lambda part, own: part[k].astype(own.dtype), everything, array)
        )
        return jax.tree.map(lambda a, b: jnp.where(reached, a, b), new, before)

    return lax.fori_loop(0, devices, hop, start)


def chain_combine(earlier, later):
    return (earlier[0] + later[0], jnp.exp(later[0])[:, None, None] * earlier[1] + later[1])


def on_device(
    x_in,
    z_gate,
    b_in,
    c_out,
    dt_step,
    rate,
    skip,
    init_state,
    residual,
    norm_gain,
    expert_ids,
    gate_weights,
    w_gate,
    w_up,
    w_down,
):
    token_count, channels = x_in.shape
    heads_here = rate.shape[0]
    head_width = channels // heads_here
    state_width = b_in.shape[1]
    blocks = token_count // GROUP
    inputs = x_in.astype(jnp.float32).reshape(blocks, GROUP, heads_here, head_width)
    keys_in = b_in.astype(jnp.float32).reshape(blocks, GROUP, state_width)
    queries = c_out.astype(jnp.float32).reshape(blocks, GROUP, state_width)
    log_steps = (-rate[None, :] * dt_step).reshape(blocks, GROUP, heads_here)
    cumulative = jnp.cumsum(log_steps, axis=1)
    scores = jnp.einsum("ctn,csn->cts", queries, keys_in, precision=PRECISE)
    causal = jnp.arange(GROUP)[:, None] >= jnp.arange(GROUP)[None, :]
    spread = cumulative[:, :, None, :] - cumulative[:, None, :, :]
    weights = jnp.exp(jnp.where(causal[None, :, :, None], spread, -jnp.inf)) * scores[..., None]
    intra_out = jnp.einsum("ctsh,cshp->cthp", weights, inputs, precision=PRECISE)
    tail_decay = jnp.exp(cumulative[:, -1:, :] - cumulative)
    block_state = jnp.einsum("csh,cshp,csn->chpn", tail_decay, inputs, keys_in, precision=PRECISE)
    block_log = cumulative[:, -1, :]

    def advance(carried, element):
        total_log, total_state = carried
        step_log, step_state = element
        updated = (
            total_log + step_log,
            jnp.exp(step_log)[:, None, None] * total_state + step_state,
        )
        return (updated, (total_log, total_state))

    zero_state = jnp.zeros((heads_here, head_width, state_width), jnp.float32)
    zero_log = jnp.zeros((heads_here,), jnp.float32)
    (device_log, device_state), (enter_log, enter_state) = lax.scan(
        advance, (zero_log, zero_state), (block_log, block_state)
    )
    prior_log, prior_state = entering_2(
        (device_log, device_state), "seq", chain_combine, (zero_log, zero_state)
    )
    incoming = prior_state + jnp.exp(prior_log)[:, None, None] * init_state
    entering = enter_state + jnp.exp(enter_log)[:, :, None, None] * incoming[None]
    inter_out = jnp.exp(cumulative)[..., None] * jnp.einsum(
        "chpn,ctn->cthp", entering, queries, precision=PRECISE
    )
    mixed_out = (intra_out + inter_out + skip[None, None, :, None] * inputs).reshape(
        token_count, channels
    )
    mixer = (mixed_out * jax.nn.silu(z_gate.astype(jnp.float32))).astype(jnp.bfloat16)
    token_mix = lax.all_to_all(mixer, "exp", split_axis=0, concat_axis=1, tiled=True)
    stream = (residual.astype(jnp.float32) + token_mix.astype(jnp.float32)).astype(jnp.bfloat16)
    widened = stream.astype(jnp.float32)
    normed = (
        widened
        * lax.rsqrt(jnp.mean(widened * widened, axis=-1, keepdims=True) + 1e-06)
        * norm_gain[None, :]
    ).astype(jnp.bfloat16)
    rows_here = residual.shape[0]
    owners = lax.axis_size("exp")
    local_experts = w_gate.shape[0]
    experts = owners * local_experts
    capacity = max(2, 2 * rows_here // experts + 1)
    width = residual.shape[1]
    chosen = expert_ids.reshape(-1)
    onehot = (chosen[:, None] == jnp.arange(experts)[None, :]).astype(jnp.int32)
    slot_index = jnp.sum((jnp.cumsum(onehot, axis=0) - onehot) * onehot, axis=1)
    target = chosen * capacity + slot_index
    placing = (target[None, :] == jnp.arange(experts * capacity)[:, None]).astype(jnp.bfloat16)
    pair_rows = jnp.repeat(normed, 2, axis=0)
    outgoing = jnp.dot(placing, pair_rows, preferred_element_type=jnp.float32).astype(jnp.bfloat16)
    outgoing = outgoing.reshape(owners, local_experts, 1, capacity, width)
    arrived = lax.all_to_all(outgoing, "exp", split_axis=0, concat_axis=2, tiled=True)
    segment = lax.all_gather(arrived, "seq", axis=1, tiled=True)
    flattened = segment.reshape(segment.shape[0], -1, segment.shape[-1])
    gate_proj = jnp.einsum("erd,edf->erf", flattened, w_gate, preferred_element_type=jnp.float32)
    up_proj = jnp.einsum("erd,edf->erf", flattened, w_up, preferred_element_type=jnp.float32)
    active = (jax.nn.silu(gate_proj) * up_proj).astype(jnp.bfloat16)
    partial_value = jnp.einsum("erf,efd->erd", active, w_down, preferred_element_type=jnp.float32)
    partials = partial_value.reshape(segment.shape[:-1] + (partial_value.shape[-1],))
    summed = lax.psum_scatter(partials.astype(jnp.bfloat16), "seq", scatter_dimension=1, tiled=True)
    returned = lax.all_to_all(summed, "exp", split_axis=2, concat_axis=0, tiled=True)
    results = returned.reshape(experts * capacity, width)
    picked = results[target].astype(jnp.float32).reshape(rows_here, 2, width)
    mixture = jnp.sum(picked * gate_weights[:, :, None], axis=1)
    return (widened + mixture).astype(jnp.bfloat16)


def solution(mesh):
    square = mesh.shape["seq"] == 4 and mesh.shape["exp"] == 8

    def body(*args):
        rows = args[8].shape[0]
        experts = mesh.shape["exp"] * args[12].shape[0]
        fits = args[12].shape[0] == 1 and 2 * rows // experts + 1 == 9
        return (on_square if square and fits else on_device)(*args)

    return jax.shard_map(
        body,
        mesh=mesh,
        in_specs=(
            P("seq", "exp"),
            P("seq", "exp"),
            P("seq", None),
            P("seq", None),
            P("seq", "exp"),
            P("exp"),
            P("exp"),
            P("exp", None, None),
            P(("seq", "exp"), None),
            P(),
            P(("seq", "exp"), None),
            P(("seq", "exp"), None),
            P("exp", None, "seq"),
            P("exp", None, "seq"),
            P("exp", "seq", None),
        ),
        out_specs=P(("seq", "exp"), None),
        check_vma=False,
    )
```

```python
import functools

import jax
import jax.numpy as jnp
from jax import lax
from jax.experimental import pallas as pl
from jax.experimental.pallas import tpu as pltpu
from jax.sharding import PartitionSpec as P

GROUP = 128
PRECISE = lax.Precision.HIGHEST
F32 = jnp.float32
BF16 = jnp.bfloat16
MIB = 1 << 20
NO_COST = pl.CostEstimate(flops=0, bytes_accessed=0, transcendentals=0)


def block_call(body, outs, scalars, args, held=0, keep=0, after=(), limit=16, out_blocks=False, name=None):
    n_args = len(args)
    kept = [jax.ShapeDtypeStruct(v.shape, v.dtype) for v in args[scalars : scalars + held]]

    def kernel(*refs):
        refs, sems = (refs[:-1], refs[-1]) if held else (refs, None)
        inputs, refs = refs[:n_args], refs[n_args + len(after) :]
        results, refs = refs[: len(outs)], refs[len(outs) :]
        copies = [
            pltpu.make_async_copy(src, dst, sems.at[k])
            for k, (src, dst) in enumerate(zip(inputs[scalars : scalars + held], refs))
        ]
        for copy in copies:
            copy.start()
        for copy in copies:
            copy.wait()
        body(*inputs[:scalars], *refs, *inputs[scalars + held :], *results)

    scratch = [pltpu.VMEM(v.shape, v.dtype) for v in kept[keep:]]
    if held:
        scratch.append(pltpu.SemaphoreType.DMA((held,)))
    return pl.pallas_call(
        kernel,
        name=name or getattr(body, "func", body).__name__,
        out_shape=list(outs) + kept[:keep],
        in_specs=[pl.BlockSpec(memory_space=pltpu.SMEM)] * scalars
        + [pl.BlockSpec(memory_space=pltpu.HBM)] * held
        + [pl.BlockSpec(memory_space=pltpu.VMEM)] * (n_args - scalars - held)
        + [pl.BlockSpec(memory_space=pl.ANY)] * len(after),
        out_specs=[pl.BlockSpec() if out_blocks else pl.BlockSpec(memory_space=pltpu.VMEM)]
        * (len(outs) + keep),
        scratch_shapes=scratch,
        compiler_params=pltpu.CompilerParams(vmem_limit_bytes=limit * MIB),
        cost_estimate=NO_COST,
    )(*args, *after)


def iota(shape, dim):
    return lax.broadcasted_iota(jnp.int32, shape, dim)


def dot(a, b, precision=None):
    return jnp.dot(a, b, precision=precision, preferred_element_type=F32)


def head_spread(heads, channels):
    shape = (heads, channels)
    return (iota(shape, 1) // (channels // heads) == iota(shape, 0)).astype(F32)


def running_logs(dt_t_ref, rate_ref):
    logs = -rate_ref[...] * dt_t_ref[...].T
    tokens = logs.shape[0]
    tri = (iota((tokens, tokens), 0) >= iota((tokens, tokens), 1)).astype(F32)
    return dot(tri, logs, PRECISE)


def pack_kernel(ids_t_ref, residual_ref, out_ref):
    parts, rows, wide = out_ref.shape
    part = wide - 128
    ids = ids_t_ref[...].astype(F32).T
    lane = iota((rows, 128), 1)
    named = jnp.where(lane == 0, ids[:, 0:1], jnp.where(lane == 1, ids[:, 1:2], 0.0)).astype(BF16)
    for k in range(parts):
        out_ref[k, :, 0:part] = residual_ref[:, k * part : (k + 1) * part]
        out_ref[k, :, part:wide] = named


def state_kernel(place, x_ref, b_ref, dt_t_ref, rate_ref, init_ref, payload_ref, init_t_ref):
    tokens, channels = x_ref.shape
    heads = dt_t_ref.shape[0]
    width = b_ref.shape[1]
    cum = running_logs(dt_t_ref, rate_ref)
    total = cum[tokens - 1 : tokens, :]
    spread = head_spread(heads, channels)
    tail = dot(jnp.exp(total - cum), spread, PRECISE)
    scaled = (x_ref[...].astype(F32) * tail).astype(BF16)
    keys = b_ref[...].astype(F32).T.astype(BF16)
    own = dot(keys, scaled)
    decay = dot(jnp.broadcast_to(jnp.exp(total), (8, heads)), spread, PRECISE)
    init_t = init_ref[...].T
    init_t_ref[...] = init_t.astype(BF16)
    first = (place[0] == 0).astype(F32)
    payload_ref[0:width, :] = (own + first * (decay[0:1, :] * init_t)).astype(BF16)
    high = decay.astype(BF16).astype(F32)
    rows = iota((16, channels), 0)
    high16 = jnp.broadcast_to(high[0:1, :], (16, channels))
    low16 = jnp.broadcast_to(decay[0:1, :], (16, channels)) - high16
    payload_ref[width : width + 16, :] = jnp.where(
        rows == 0, high16, jnp.where(rows == 1, low16, 0.0)
    ).astype(BF16)


def intra_kernel(x_ref, z_ref, b_ref, c_ref, dt_t_ref, rate_ref, skip_ref, own_ref, fade_ref, token_ref):
    tokens, channels = x_ref.shape
    heads = dt_t_ref.shape[0]
    width = channels // heads
    token_ref[...] = jnp.zeros_like(token_ref)
    shape = (tokens, tokens)
    causal = iota(shape, 0) >= iota(shape, 1)
    cum = running_logs(dt_t_ref, rate_ref)
    cum_t = cum.T
    scores = lax.dot_general(
        c_ref[...], b_ref[...], (((1,), (1,)), ((), ())), preferred_element_type=F32
    )
    spread = head_spread(heads, channels)
    direct = dot(jnp.broadcast_to(skip_ref[...], (8, heads)), spread, PRECISE)[0:1, :]
    fade = dot(jnp.exp(cum), spread, PRECISE)
    per = 128 // width
    lane_head = iota((tokens, 128), 1) // width
    for group in range(heads // per):
        cols = slice(group * 128, (group + 1) * 128)
        x = x_ref[:, cols]
        total = x.astype(F32) * direct[:, cols]
        for k in range(per):
            h = group * per + k
            gap = jnp.where(causal, cum[:, h : h + 1] - cum_t[h : h + 1, :], -1e30)
            weights = (jnp.exp(gap) * scores).astype(BF16)
            part = dot(weights, x)
            total = total + jnp.where(lane_head == k, part, 0.0)
        z = z_ref[:, cols].astype(F32)
        gate = z / (1.0 + jnp.exp(-z))
        own_ref[:, cols] = total * gate
        fade_ref[:, cols] = fade[:, cols] * gate


def place_kernel(cap, experts, me, packed_ref, *refs):
    count = (len(refs) - 1) // 2
    out_ref = refs[count]
    for source, target in zip(refs[:count], refs[count + 1 :]):
        target[...] = source[...]
    blocks, rows, wide = packed_ref.shape
    tokens = blocks * rows
    slots = out_ref.shape[1] - rows
    ids = packed_ref[:, :, wide - 128 : wide].astype(F32).reshape(tokens, 128).T
    ids = ids[0:8, :].astype(jnp.int32)
    shape = (tokens, tokens)
    before = (iota(shape, 0) < iota(shape, 1)) & (iota(shape, 0) // rows == iota(shape, 1) // rows)
    named = iota((experts, tokens), 0) ^ me[0]
    hit = (ids[0:1, :] == named) | (ids[1:2, :] == named)
    rank = dot(hit.astype(BF16), before.astype(BF16)).astype(jnp.int32)
    block = (iota((experts, tokens), 1) // rows) ^ named
    whole = cap - 1
    row = jnp.where(rank < whole, block * whole + rank, blocks * whole + block)
    row = jnp.where(hit, row, -1)
    shape = (rows + slots, tokens)
    for e in range(experts):
        owned = ((me[0] ^ e) * rows + iota(shape, 0) == iota(shape, 1)) & (iota(shape, 0) < rows)
        placed = (iota(shape, 0) - rows == row[e : e + 1, :]) & (iota(shape, 0) >= rows)
        out_ref[e] = (owned | placed).astype(F32).astype(BF16)


def join_kernel(place, own_ref, other_ref, out_ref):
    width = out_ref.shape[0]
    odd = place[0] % 2 == 1
    own, other = own_ref[0:width, :].astype(F32), other_ref[0:width, :].astype(F32)
    own_decay = own_ref[width : width + 16, :].astype(F32)
    other_decay = other_ref[width : width + 16, :].astype(F32)
    own_decay = own_decay[0:1, :] + own_decay[1:2, :]
    other_decay = other_decay[0:1, :] + other_decay[1:2, :]
    early = jnp.where(odd, other, own)
    late = jnp.where(odd, own, other)
    decay = jnp.where(odd, own_decay, other_decay)
    out_ref[...] = (decay * early + late).astype(BF16)


def stream_kernel(
    place, c_ref, own_ref, fade_ref, init_t_ref, pair_ref, early_ref, res_ref, sel_ref, same_ref, other_ref
):
    width = init_t_ref.shape[0]
    at = place[0]
    zero = (at == 0).astype(F32)
    odd = (at % 2 == 1).astype(F32)
    pair = pair_ref[...].astype(F32)
    decay = pair[width : width + 1, :] + pair[width + 1 : width + 2, :]
    factor = jnp.where(at >= 2, jnp.where(at % 2 == 1, decay, 1.0), 0.0)
    entering = zero * init_t_ref[...].astype(F32) + odd * pair[0:width, :] + factor * early_ref[...].astype(F32)
    mixed = own_ref[...] + fade_ref[...] * dot(c_ref[...], entering.astype(BF16))
    mixer = mixed.astype(BF16).astype(F32)
    tokens, channels = mixer.shape
    residual = res_ref[:, :, 0:channels].astype(F32).reshape(tokens, channels)
    stream = (residual + mixer).astype(BF16)
    for k in range(same_ref.shape[0]):
        same_ref[k] = dot(sel_ref[2 * k], stream).astype(BF16)
        other_ref[k] = dot(sel_ref[2 * k + 1], stream).astype(BF16)


def up_kernel(first, features, after, group, me, *refs):
    own, rx, ry, even, odd, gain, w_gate, w_up = refs[:8]
    carry = () if first else refs[8:11]
    rest, (held_gate, held_up, sems) = refs[(8 if first else 11) + after : -3], refs[-3:]
    sums = rest[2:5] if features else rest
    step = pl.program_id(0)
    steps = held_gate.shape[0]
    tile = held_gate.shape[1]

    def loads(k):
        source = me[0] ^ (2 * group + k // (steps // 2))
        part = pl.ds(pl.multiple_of(k % (steps // 2) * tile, tile), tile)
        return [
            pltpu.make_async_copy(w.at[source, part, :], held.at[k], sems.at[side, k])
            for side, (w, held) in enumerate(((w_gate, held_gate), (w_up, held_up)))
        ]

    @pl.when(step == 0)
    def _():
        for k in range(steps):
            for load in loads(k):
                load.start()

    if first or features:

        @pl.when(step == 0)
        def _():
            for i, acc in enumerate(sums):
                acc[...] = jnp.zeros_like(acc) if first else carry[i][...]

    gate, up, square = sums
    slots = own.shape[1]
    rows = [r[0].astype(F32) for r in (own, rx, ry)]
    rows.append(jnp.where(step < steps // 2, even[0].astype(F32), odd[0].astype(F32)))
    rows = jnp.concatenate(rows, axis=0)
    square[...] += jnp.broadcast_to(jnp.sum(rows * rows, axis=1, keepdims=True), square.shape)
    scaled = (rows * gain[0]).astype(BF16)
    for load in loads(step):
        load.wait()
    gate[...] += dot(scaled, held_gate[step])
    up[...] += dot(scaled, held_up[step])

    if features:
        outs, stages = rest[:2], rest[5:]

        @pl.when(step == steps - 1)
        def _():
            inverse = lax.rsqrt(square[:, 0:1] * (1.0 / features) + 1e-06)
            g = gate[...] * inverse
            active = g / (1.0 + jnp.exp(-g)) * (up[...] * inverse)
            main, ninths = slots // 9 * 8, slots // 9
            for d in range(4):
                at = d * slots
                stage, d, shards = (stages[0], 0, 1) if d == 3 else (stages[1], d, 3)
                stage[d * main : (d + 1) * main, :] = active[at : at + main]
                low = shards * main + d * ninths
                stage[low : low + ninths, :] = active[at + main : at + slots]
            for out, stage in zip(outs, stages):
                out[...] = stage[...].astype(BF16)


def up_project(group, last, me, near, far, gain, w_gate, w_up, carry, after=()):
    slots, part = near[0][0].shape[1:]
    cut = 2
    tile = part // cut
    hidden = w_gate.shape[2]
    total = 4 * slots
    source = lambda i, me: me[0] ^ (2 * group + i // cut)
    rows = [
        pl.BlockSpec((1, slots, tile), lambda i, me, start=start: (start + i // cut, 0, i % cut))
        for _, start in near
    ] + [
        pl.BlockSpec((1, slots, tile), lambda i, me, start=start: (start, 0, i % cut))
        for _, start in far
    ]
    weight = pl.BlockSpec(memory_space=pltpu.HBM)
    in_place = pl.BlockSpec(memory_space=pltpu.VMEM)
    specs = rows + [
        pl.BlockSpec((1, 1, tile), lambda i, me: (source(i, me), 0, i % cut)),
        weight,
        weight,
    ]
    sums = [
        jax.ShapeDtypeStruct((total, hidden), F32),
        jax.ShapeDtypeStruct((total, hidden), F32),
        jax.ShapeDtypeStruct((total, 128), F32),
    ]
    aliases = {}
    if carry is not None:
        specs += [in_place] * 3
        if not last:
            aliases = {9 + i: i for i in range(3)}
    specs += [pl.BlockSpec(memory_space=pl.ANY)] * len(after)
    sizes = (slots, 3 * slots)
    outs = [jax.ShapeDtypeStruct((n, hidden), BF16) for n in sizes] if last else sums
    scratch = [pltpu.VMEM(s.shape, s.dtype) for s in sums]
    scratch += [pltpu.VMEM((n, hidden), F32) for n in sizes]
    features = gain.shape[0] * part if last else 0
    return pl.pallas_call(
        functools.partial(up_kernel, carry is None, features, len(after), group),
        name=f"up_{group}",
        out_shape=outs,
        grid_spec=pltpu.PrefetchScalarGridSpec(
            num_scalar_prefetch=1,
            grid=(2 * cut,),
            in_specs=specs,
            out_specs=[in_place] * len(outs),
            scratch_shapes=(scratch if last else [])
            + [pltpu.VMEM((2 * cut, tile, hidden), BF16)] * 2
            + [pltpu.SemaphoreType.DMA((2, 2 * cut))],
        ),
        input_output_aliases=aliases,
        compiler_params=pltpu.CompilerParams(vmem_limit_bytes=48 * MIB),
        cost_estimate=NO_COST,
    )(me, *(array for array, _ in near + far), gain, w_gate, w_up, *(carry or ()), *after)


def cut_of(group):
    return 5 if group % 2 else 4


def down_kernel(groups, act_ref, w_ref, *refs):
    outs, (spare, held, sems) = refs[:-3], refs[-3:]
    step = pl.program_id(0)
    steps, _, tile = held.shape

    def load(k):
        columns = pl.ds(pl.multiple_of(k * tile, tile), tile)
        return pltpu.make_async_copy(w_ref.at[:, columns], held.at[k], sems.at[k])

    @pl.when(step == 0)
    def _():
        for k in range(steps):
            load(k).start()

    load(step).wait()
    part = dot(act_ref[...], held[step])
    ninths = part.shape[0] // 9
    main = part.shape[0] - ninths
    shards = ninths // (2 * groups)

    def through(group, tile):
        to_x, to_y = outs[2 * (group // 2) : 2 * (group // 2) + 2]
        cut = cut_of(group)
        return to_x, tile + (0 if group % 2 else 5), to_y, tile - cut + (0 if group % 2 else 4)

    for shard in range(shards):
        for group in range(groups):
            at = (shard * groups + group) * 16
            rows = part[at : at + 16, :].astype(BF16)
            if shards > 1:
                outs[shards * group + shard][step] = rows
                continue
            to_x, place_x, to_y, place_y = through(group, step)

            @pl.when(step < cut_of(group))
            def _():
                to_x[place_x] = rows

            @pl.when(step >= cut_of(group))
            def _():
                to_y[place_y] = rows

    for lanes in range(spare.shape[0]):
        spare[lanes, pl.ds(pl.multiple_of(step * ninths, 8), ninths), :] = part[
            main:, lanes * 128 : (lanes + 1) * 128
        ]

    @pl.when(step == steps - 1)
    def _():
        for shard in range(shards):
            for group in range(groups):
                pair = []
                for side in range(2):
                    row = pl.ds((shard * groups + group) * 2 + side, 8, stride=ninths)
                    ninth = [spare[lanes, row, :] for lanes in range(spare.shape[0])]
                    pair.append(jnp.concatenate(ninth, axis=1))
                pair = jnp.concatenate(pair, axis=0).astype(BF16)
                if shards > 1:
                    outs[shards * group + shard][8] = pair
                else:
                    _, _, to_y, place_y = through(group, 8)
                    to_y[place_y] = pair


def down_project(name, groups, active, w_down):
    total, hidden = active.shape
    features = w_down.shape[1]
    tile = features // 8
    outs = [jax.ShapeDtypeStruct((9, 16, tile), BF16)] * (total // 18)
    return pl.pallas_call(
        functools.partial(down_kernel, groups),
        name=name,
        grid=(8,),
        out_shape=outs,
        in_specs=[
            pl.BlockSpec(memory_space=pltpu.VMEM),
            pl.BlockSpec(memory_space=pltpu.HBM),
        ],
        out_specs=[pl.BlockSpec(memory_space=pltpu.VMEM)] * len(outs),
        scratch_shapes=[
            pltpu.VMEM((tile // 128, 8 * total // 9, 128), F32),
            pltpu.VMEM((8, hidden, tile), BF16),
            pltpu.SemaphoreType.DMA((8,)),
        ],
        compiler_params=pltpu.CompilerParams(vmem_limit_bytes=48 * MIB),
        cost_estimate=NO_COST,
    )(active, w_down)


def pair_kernel(same, other, own, own_stream, near, far, last, last_stream):
    owned = own_stream.shape[1]
    for side, rows in enumerate((same, other)):
        own_stream[side], own[side] = rows[0, 0:owned, :], rows[0, owned:, :]
        near[side], far[side] = rows[1], rows[2]
        last_stream[side], last[side] = rows[3, 0:owned, :], rows[3, owned:, :]


def near_kernel(arrived, far, rows, stream, far_out):
    owned = stream.shape[1]
    for side in range(2):
        stream[side], rows[side] = arrived[side, 0:owned, :], arrived[side, owned:, :]
        far_out[side] = far[side]


def second_kernel(*refs):
    parts, out = refs[:-1], refs[-1]
    for h in range(out.shape[0]):
        for k in range(out.shape[1]):
            pair = [ref[k].astype(F32)[8:16] for ref in parts[2 * h : 2 * h + 2]]
            out[h, k] = jnp.concatenate(pair, axis=0).astype(BF16)


def hold_kernel(a, out):
    out[...] = a[...]


def half_message_kernel(rx, ry, out_x, out_y):
    out_x[0], out_y[0] = ry[1], rx[0]


def join_message_kernel(own, rx, ry, out_x, out_y, *parts):
    owned = own.shape[1] - out_x.shape[1]
    for side in range(2):
        rows = own[side, owned:, :]
        out_x[side], out_y[side] = rows, rows
        if parts:
            parts[0][side], parts[1][side] = rows, own[side, 0:owned, :]
    out_x[2], out_y[2] = ry[1], rx[0]


def relay_kernel(through_x, through_y, *refs):
    ahead = refs[4 : 4 + (len(refs) - 8) // 2]
    outs, copies = refs[4 + len(ahead) :][:4], refs[8 + len(ahead) :]
    for group in range(2):
        cut = cut_of(group)
        at_x, at_y = (0, -cut) if group else (5, 0)
        for own, out, through, tiles, at in (
            (refs[2 * group], outs[2 * group], through_y, range(cut, 9), at_y),
            (refs[2 * group + 1], outs[2 * group + 1], through_x, range(cut), at_x),
        ):
            for k in range(9):
                if k in tiles:
                    out[k] = (own[k].astype(F32) + through[k + at].astype(F32)).astype(BF16)
                else:
                    out[k] = own[k]
    for source, copy in zip(ahead, copies):
        copy[...] = source[...]


def finish_kernel(own, rx, ry, *refs):
    ahead = refs[: (len(refs) - 1) // 2]
    out, copies = refs[len(ahead)], refs[len(ahead) + 1 :]
    for k in range(9):
        out[k] = (own[k].astype(F32) + rx[k].astype(F32) + ry[k].astype(F32)).astype(BF16)
    for source, copy in zip(ahead, copies):
        copy[...] = source[...]


def mix_kernel(me, ids_t_ref, weight_t_ref, swap_ref, *refs):
    groups = (len(refs) - 1) // 2
    firsts, streams, out_ref = refs[:groups], refs[groups:-1], refs[-1]
    rows = ids_t_ref.shape[1]
    experts = 2 * groups
    pieces = firsts[0].shape[0] - 1
    tile = firsts[0].shape[2]
    ids, weights = ids_t_ref[...].T, weight_t_ref[...].T
    named = iota((rows, experts), 1) ^ me[0]
    first, second = ids[:, 0:1] == named, ids[:, 1:2] == named
    weight = jnp.where(first, weights[:, 0:1], jnp.where(second, weights[:, 1:2], 0.0))
    hit = (first | second).astype(F32)
    before = (iota((rows, rows), 0) > iota((rows, rows), 1)).astype(F32)
    rank = dot(before, hit)
    lanes = 2 * experts * 8
    shape = (experts, lanes)
    spread = ((iota(shape, 1) // 8) % experts == iota(shape, 0)).astype(F32)
    weight = dot(weight, spread, PRECISE)
    rank = dot(rank, spread, PRECISE).astype(jnp.int32)
    lane = iota((rows, lanes), 1)
    main = (lane < experts * 8) & (rank == lane % 8)
    extra = (lane >= experts * 8) & (rank == 8)

    def rows_of(k):
        data = []
        for g in range(groups):
            data.append(firsts[g][k].astype(F32)[0:8])
            data.append(swap_ref[g // 2, k].astype(F32)[g % 2 * 8 : g % 2 * 8 + 8])
        return data

    last = rows_of(pieces)
    for m in range(experts):
        k = me[0] ^ m
        coef = jnp.where(main | (extra & (lane % 8 == k)), weight, 0.0)
        high = coef.astype(BF16)
        low = (coef - high.astype(F32)).astype(BF16)
        data = jnp.concatenate(rows_of(k) + last, axis=0).astype(BF16)
        stream = streams[m // 2][m % 2].astype(F32)
        out_ref[:, pl.ds(pl.multiple_of(k * tile, 128), tile)] = (
            stream + (dot(high, data) + dot(low, data))
        ).astype(BF16)


def on_square(
    x_in,
    z_gate,
    b_in,
    c_out,
    dt_step,
    rate,
    skip,
    init_state,
    residual,
    norm_gain,
    expert_ids,
    gate_weights,
    w_gate,
    w_up,
    w_down,
):
    tokens, channels = x_in.shape
    heads = rate.shape[0]
    state = b_in.shape[1]
    owners = lax.axis_size("exp")
    rows, features = residual.shape
    experts = owners
    cap = max(2, 2 * rows // experts + 1)
    slots = owners * cap
    at = lax.axis_index("seq")
    me = lax.axis_index("exp")
    place = jnp.reshape(at, (1,)).astype(jnp.int32)
    self_id = jnp.reshape(me, (1,)).astype(jnp.int32)

    def over_x(v):
        return lax.ppermute(v, "seq", [(i, i ^ 1) for i in range(4)])

    def over_y(v):
        return lax.ppermute(v, "seq", [(i, i ^ 2) for i in range(4)])

    def along(v, mask):
        return lax.ppermute(v, "exp", [(i, i ^ mask) for i in range(owners)])

    rate_row = rate[None, :]
    dt_t = dt_step.T
    ids_t = expert_ids.T
    packed = block_call(
        pack_kernel,
        [jax.ShapeDtypeStruct((owners, rows, channels + 128), BF16)],
        0,
        (ids_t, residual),
        held=2,
        limit=48,
    )[0]
    packed = lax.all_to_all(packed, "exp", split_axis=0, concat_axis=0, tiled=True)
    payload, init_t = block_call(
        state_kernel,
        [
            jax.ShapeDtypeStruct((state + 16, channels), BF16),
            jax.ShapeDtypeStruct((state, channels), BF16),
        ],
        1,
        (place, x_in, b_in, dt_t, rate_row, init_state.reshape(channels, state)),
        held=5,
        limit=62,
    )
    pair = over_x(payload)
    own_part, fade, token = block_call(
        intra_kernel,
        [
            jax.ShapeDtypeStruct((tokens, channels), F32),
            jax.ShapeDtypeStruct((tokens, channels), F32),
            jax.ShapeDtypeStruct((8, 128), F32),
        ],
        0,
        (x_in, z_gate, b_in, c_out, dt_t, rate_row, skip[None, :]),
        held=7,
        limit=61,
    )
    joined = block_call(
        join_kernel,
        [jax.ShapeDtypeStruct((state, channels), BF16)],
        1,
        (place, payload, pair),
        after=(token,),
    )[0]
    early = over_y(joined)
    handed = (own_part, fade, c_out, init_t)
    select, own_part, fade, c, init_t = block_call(
        functools.partial(place_kernel, cap, experts),
        [jax.ShapeDtypeStruct((experts, rows + slots, tokens), BF16)]
        + [jax.ShapeDtypeStruct(v.shape, v.dtype) for v in handed],
        1,
        (self_id, packed, *handed),
        after=(joined,),
    )
    groups = owners // 2
    lanes = jax.ShapeDtypeStruct((groups, rows + slots, channels), BF16)
    same, other = block_call(
        stream_kernel,
        [lanes, lanes],
        1,
        (place, c, own_part, fade, init_t, pair, early, packed, select),
    )

    gain = norm_gain.reshape(owners, 1, channels)
    wg = w_gate.reshape(owners, channels, w_gate.shape[2])
    wu = w_up.reshape(owners, channels, w_up.shape[2])
    expert_rows = jax.ShapeDtypeStruct((2, slots, channels), BF16)
    stream_rows = jax.ShapeDtypeStruct((2, rows, channels), BF16)
    both_rows = jax.ShapeDtypeStruct((2, rows + slots, channels), BF16)
    first, stream0, near, far, farthest, stream3 = block_call(
        pair_kernel,
        [expert_rows, stream_rows, both_rows, both_rows, expert_rows, stream_rows],
        0,
        (same, along(other, 1)),
    )
    gain = norm_gain.reshape(owners, 1, channels)
    wg = w_gate.reshape(owners, channels, w_gate.shape[2])
    wu = w_up.reshape(owners, channels, w_up.shape[2])

    def hold(v, after, name):
        return block_call(
            hold_kernel, [jax.ShapeDtypeStruct(v.shape, BF16)], 0, (v,), after=after, name=name
        )[0]

    def project(group, near, far, carry, after=()):
        last = group == groups - 1
        return up_project(group, last, self_id, near, far, gain, wg, wu, carry, after)

    def message(count):
        return [jax.ShapeDtypeStruct((count, slots, channels), BF16)] * 2

    near = along(near, 2)
    rx0, ry0 = over_x(first), over_y(first)
    to_x, to_y = block_call(half_message_kernel, message(1), 0, (rx0, ry0), name="half_0")
    fx0, fy0 = over_x(to_x), over_y(to_y)
    near, stream1, far = block_call(
        near_kernel, [expert_rows, stream_rows, both_rows], 0, (near, far), after=(to_x,)
    )
    far = along(far, 4)
    rx1, ry1 = over_x(near), over_y(near)
    farthest_held = hold(farthest, (far,), "hold_farthest")
    farthest = along(farthest_held, 6)
    to_x, to_y, far, stream2 = block_call(
        join_message_kernel,
        message(3) + [expert_rows, stream_rows],
        0,
        (far, rx1, ry1),
        after=(fx0, fy0, farthest_held),
        name="join_2",
    )
    rx2, ry2 = over_x(to_x), over_y(to_y)
    carry = project(0, [(first, 0), (rx0, 0), (ry0, 0)], [(fy0, 0), (fx0, 0)], None)
    to_x, to_y = block_call(
        join_message_kernel, message(3), 0, (farthest, rx2, ry2), after=(carry[2],), name="join_3"
    )
    rx3, ry3 = over_x(to_x), over_y(to_y)
    carry = project(1, [(near, 0), (rx1, 0), (ry1, 0)], [(ry2, 2), (rx2, 2)], carry)
    to_x, to_y = block_call(
        half_message_kernel, message(1), 0, (rx3, ry3), after=(carry[2],), name="half_3"
    )
    fx3, fy3 = over_x(to_x), over_y(to_y)
    held = hold(stream3, (to_x,), "hold_stream")
    streams = [stream0, stream1, stream2, along(held, 6)]
    carry = project(2, [(far, 0), (rx2, 0), (ry2, 0)], [(ry3, 2), (rx3, 2)], carry, (held,))
    active_far, active = project(
        3, [(farthest, 0), (rx3, 0), (ry3, 0)], [(fy3, 0), (fx3, 0)], carry
    )

    wd = w_down.reshape(w_down.shape[1], features)
    tiles = jax.ShapeDtypeStruct((9, 16, features // 8), BF16)
    sent = down_project("down_through", groups, active_far, wd)
    rest = down_project("down_rest", groups, active, wd)
    own, own_x, own_y = ([rest[3 * g + k] for g in range(groups)] for k in range(3))

    def relay(name, through_x, through_y, low, ahead=(), after=()):
        shares = (own_x[low], own_y[low], own_x[low + 1], own_y[low + 1])
        return block_call(
            relay_kernel,
            [tiles] * (4 + len(ahead)),
            0,
            (through_x, through_y, *shares, *ahead),
            after=after,
            name=name,
        )

    def finish(group, rx, ry, ahead=(), after=()):
        return block_call(
            finish_kernel,
            [tiles] * (1 + len(ahead)),
            0,
            (own[group], rx, ry, *ahead),
            after=after,
            name=f"finish_{group}",
        )

    through_x, through_y = over_x(sent[2]), over_y(sent[3])
    x2, y2, x3, y3, next_x, next_y = relay(
        "relay_far", through_x, through_y, 2, (sent[0], sent[1]), streams[3:]
    )
    rx3, ry3 = over_x(x3), over_y(y3)
    through_x, through_y = over_x(next_x), over_y(next_y)
    both3, x2, y2 = finish(3, rx3, ry3, (x2, y2))
    back3 = along(both3, 6)
    rx2, ry2 = over_x(x2), over_y(y2)
    x0, y0, x1, y1 = relay("relay_near", through_x, through_y, 0, after=(both3,))
    rx1, ry1 = over_x(x1), over_y(y1)
    both2, x0, y0 = finish(2, rx2, ry2, (x0, y0))
    back2 = along(both2, 4)
    rx0, ry0 = over_x(x0), over_y(y0)
    back1 = along(finish(1, rx1, ry1, after=(back3,))[0], 2)
    back = [finish(0, rx0, ry0)[0], back1, back2, back3]
    swap = block_call(second_kernel, [jax.ShapeDtypeStruct((2,) + tiles.shape, BF16)], 0, back)[0]
    swap = along(swap, 1)
    return block_call(
        mix_kernel,
        [jax.ShapeDtypeStruct((rows, features), BF16)],
        1,
        (self_id, ids_t, gate_weights.T, swap, *back, *streams),
    )[0]


def entering_2(array, axis, combine, identity):
    devices, mine = (lax.axis_size(axis), lax.axis_index(axis))
    everything = jax.tree.map(
        lambda part, kind: lax.all_gather(part.astype(kind), axis),
        array,
        (jnp.bfloat16, jnp.bfloat16),
    )
    start = jax.tree.map(
        lambda part, zero: jnp.broadcast_to(jnp.asarray(zero, part.dtype), part.shape),
        array,
        identity,
    )

    def hop(k, before):
        reached = k < mine
        new = combine(
            before, jax.tree.map(lambda part, own: part[k].astype(own.dtype), everything, array)
        )
        return jax.tree.map(lambda a, b: jnp.where(reached, a, b), new, before)

    return lax.fori_loop(0, devices, hop, start)


def chain_combine(earlier, later):
    return (earlier[0] + later[0], jnp.exp(later[0])[:, None, None] * earlier[1] + later[1])


def on_device(
    x_in,
    z_gate,
    b_in,
    c_out,
    dt_step,
    rate,
    skip,
    init_state,
    residual,
    norm_gain,
    expert_ids,
    gate_weights,
    w_gate,
    w_up,
    w_down,
):
    token_count, channels = x_in.shape
    heads_here = rate.shape[0]
    head_width = channels // heads_here
    state_width = b_in.shape[1]
    blocks = token_count // GROUP
    inputs = x_in.astype(jnp.float32).reshape(blocks, GROUP, heads_here, head_width)
    keys_in = b_in.astype(jnp.float32).reshape(blocks, GROUP, state_width)
    queries = c_out.astype(jnp.float32).reshape(blocks, GROUP, state_width)
    log_steps = (-rate[None, :] * dt_step).reshape(blocks, GROUP, heads_here)
    cumulative = jnp.cumsum(log_steps, axis=1)
    scores = jnp.einsum("ctn,csn->cts", queries, keys_in, precision=PRECISE)
    causal = jnp.arange(GROUP)[:, None] >= jnp.arange(GROUP)[None, :]
    spread = cumulative[:, :, None, :] - cumulative[:, None, :, :]
    weights = jnp.exp(jnp.where(causal[None, :, :, None], spread, -jnp.inf)) * scores[..., None]
    intra_out = jnp.einsum("ctsh,cshp->cthp", weights, inputs, precision=PRECISE)
    tail_decay = jnp.exp(cumulative[:, -1:, :] - cumulative)
    block_state = jnp.einsum("csh,cshp,csn->chpn", tail_decay, inputs, keys_in, precision=PRECISE)
    block_log = cumulative[:, -1, :]

    def advance(carried, element):
        total_log, total_state = carried
        step_log, step_state = element
        updated = (
            total_log + step_log,
            jnp.exp(step_log)[:, None, None] * total_state + step_state,
        )
        return (updated, (total_log, total_state))

    zero_state = jnp.zeros((heads_here, head_width, state_width), jnp.float32)
    zero_log = jnp.zeros((heads_here,), jnp.float32)
    (device_log, device_state), (enter_log, enter_state) = lax.scan(
        advance, (zero_log, zero_state), (block_log, block_state)
    )
    prior_log, prior_state = entering_2(
        (device_log, device_state), "seq", chain_combine, (zero_log, zero_state)
    )
    incoming = prior_state + jnp.exp(prior_log)[:, None, None] * init_state
    entering = enter_state + jnp.exp(enter_log)[:, :, None, None] * incoming[None]
    inter_out = jnp.exp(cumulative)[..., None] * jnp.einsum(
        "chpn,ctn->cthp", entering, queries, precision=PRECISE
    )
    mixed_out = (intra_out + inter_out + skip[None, None, :, None] * inputs).reshape(
        token_count, channels
    )
    mixer = (mixed_out * jax.nn.silu(z_gate.astype(jnp.float32))).astype(jnp.bfloat16)
    token_mix = lax.all_to_all(mixer, "exp", split_axis=0, concat_axis=1, tiled=True)
    stream = (residual.astype(jnp.float32) + token_mix.astype(jnp.float32)).astype(jnp.bfloat16)
    widened = stream.astype(jnp.float32)
    normed = (
        widened
        * lax.rsqrt(jnp.mean(widened * widened, axis=-1, keepdims=True) + 1e-06)
        * norm_gain[None, :]
    ).astype(jnp.bfloat16)
    rows_here = residual.shape[0]
    owners = lax.axis_size("exp")
    local_experts = w_gate.shape[0]
    experts = owners * local_experts
    capacity = max(2, 2 * rows_here // experts + 1)
    width = residual.shape[1]
    chosen = expert_ids.reshape(-1)
    onehot = (chosen[:, None] == jnp.arange(experts)[None, :]).astype(jnp.int32)
    slot_index = jnp.sum((jnp.cumsum(onehot, axis=0) - onehot) * onehot, axis=1)
    target = chosen * capacity + slot_index
    placing = (target[None, :] == jnp.arange(experts * capacity)[:, None]).astype(jnp.bfloat16)
    pair_rows = jnp.repeat(normed, 2, axis=0)
    outgoing = jnp.dot(placing, pair_rows, preferred_element_type=jnp.float32).astype(jnp.bfloat16)
    outgoing = outgoing.reshape(owners, local_experts, 1, capacity, width)
    arrived = lax.all_to_all(outgoing, "exp", split_axis=0, concat_axis=2, tiled=True)
    segment = lax.all_gather(arrived, "seq", axis=1, tiled=True)
    flattened = segment.reshape(segment.shape[0], -1, segment.shape[-1])
    gate_proj = jnp.einsum("erd,edf->erf", flattened, w_gate, preferred_element_type=jnp.float32)
    up_proj = jnp.einsum("erd,edf->erf", flattened, w_up, preferred_element_type=jnp.float32)
    active = (jax.nn.silu(gate_proj) * up_proj).astype(jnp.bfloat16)
    partial_value = jnp.einsum("erf,efd->erd", active, w_down, preferred_element_type=jnp.float32)
    partials = partial_value.reshape(segment.shape[:-1] + (partial_value.shape[-1],))
    summed = lax.psum_scatter(partials.astype(jnp.bfloat16), "seq", scatter_dimension=1, tiled=True)
    returned = lax.all_to_all(summed, "exp", split_axis=2, concat_axis=0, tiled=True)
    results = returned.reshape(experts * capacity, width)
    picked = results[target].astype(jnp.float32).reshape(rows_here, 2, width)
    mixture = jnp.sum(picked * gate_weights[:, :, None], axis=1)
    return (widened + mixture).astype(jnp.bfloat16)


def solution(mesh):
    square = mesh.shape["seq"] == 4 and mesh.shape["exp"] == 8

    def body(*args):
        rows = args[8].shape[0]
        experts = mesh.shape["exp"] * args[12].shape[0]
        fits = args[12].shape[0] == 1 and 2 * rows // experts + 1 == 9
        return (on_square if square and fits else on_device)(*args)

    return jax.shard_map(
        body,
        mesh=mesh,
        in_specs=(
            P("seq", "exp"),
            P("seq", "exp"),
            P("seq", None),
            P("seq", None),
            P("seq", "exp"),
            P("exp"),
            P("exp"),
            P("exp", None, None),
            P(("seq", "exp"), None),
            P(),
            P(("seq", "exp"), None),
            P(("seq", "exp"), None),
            P("exp", None, "seq"),
            P("exp", None, "seq"),
            P("exp", "seq", None),
        ),
        out_specs=P(("seq", "exp"), None),
        check_vma=False,
    )
```

```python
import functools

import jax
import jax.numpy as jnp
from jax import lax
from jax.experimental import pallas as pl
from jax.experimental.pallas import tpu as pltpu
from jax.sharding import PartitionSpec as P

GROUP = 128
PRECISE = lax.Precision.HIGHEST
F32 = jnp.float32
BF16 = jnp.bfloat16
MIB = 1 << 20
NO_COST = pl.CostEstimate(flops=0, bytes_accessed=0, transcendentals=0)


def block_call(body, outs, scalars, args, held=0, keep=0, after=(), limit=16, out_blocks=False, name=None):
    n_args = len(args)
    kept = [jax.ShapeDtypeStruct(v.shape, v.dtype) for v in args[scalars : scalars + held]]

    def kernel(*refs):
        refs, sems = (refs[:-1], refs[-1]) if held else (refs, None)
        inputs, refs = refs[:n_args], refs[n_args + len(after) :]
        results, refs = refs[: len(outs)], refs[len(outs) :]
        copies = [
            pltpu.make_async_copy(src, dst, sems.at[k])
            for k, (src, dst) in enumerate(zip(inputs[scalars : scalars + held], refs))
        ]
        for copy in copies:
            copy.start()
        for copy in copies:
            copy.wait()
        body(*inputs[:scalars], *refs, *inputs[scalars + held :], *results)

    scratch = [pltpu.VMEM(v.shape, v.dtype) for v in kept[keep:]]
    if held:
        scratch.append(pltpu.SemaphoreType.DMA((held,)))
    return pl.pallas_call(
        kernel,
        name=name or getattr(body, "func", body).__name__,
        out_shape=list(outs) + kept[:keep],
        in_specs=[pl.BlockSpec(memory_space=pltpu.SMEM)] * scalars
        + [pl.BlockSpec(memory_space=pltpu.HBM)] * held
        + [pl.BlockSpec(memory_space=pltpu.VMEM)] * (n_args - scalars - held)
        + [pl.BlockSpec(memory_space=pl.ANY)] * len(after),
        out_specs=[pl.BlockSpec() if out_blocks else pl.BlockSpec(memory_space=pltpu.VMEM)]
        * (len(outs) + keep),
        scratch_shapes=scratch,
        compiler_params=pltpu.CompilerParams(vmem_limit_bytes=limit * MIB),
        cost_estimate=NO_COST,
    )(*args, *after)


def iota(shape, dim):
    return lax.broadcasted_iota(jnp.int32, shape, dim)


def dot(a, b, precision=None):
    return jnp.dot(a, b, precision=precision, preferred_element_type=F32)


def head_spread(heads, channels):
    shape = (heads, channels)
    return (iota(shape, 1) // (channels // heads) == iota(shape, 0)).astype(F32)


def running_logs(dt_t_ref, rate_ref):
    logs = -rate_ref[...] * dt_t_ref[...].T
    tokens = logs.shape[0]
    tri = (iota((tokens, tokens), 0) >= iota((tokens, tokens), 1)).astype(F32)
    return dot(tri, logs, PRECISE)


def pack_kernel(ids_t_ref, residual_ref, out_ref):
    parts, rows, wide = out_ref.shape
    part = wide - 128
    ids = ids_t_ref[...].astype(F32).T
    lane = iota((rows, 128), 1)
    named = jnp.where(lane == 0, ids[:, 0:1], jnp.where(lane == 1, ids[:, 1:2], 0.0)).astype(BF16)
    for k in range(parts):
        out_ref[k, :, 0:part] = residual_ref[:, k * part : (k + 1) * part]
        out_ref[k, :, part:wide] = named


def state_kernel(place, x_ref, b_ref, dt_t_ref, rate_ref, init_ref, payload_ref, init_t_ref):
    tokens, channels = x_ref.shape
    heads = dt_t_ref.shape[0]
    width = b_ref.shape[1]
    cum = running_logs(dt_t_ref, rate_ref)
    total = cum[tokens - 1 : tokens, :]
    spread = head_spread(heads, channels)
    tail = dot(jnp.exp(total - cum), spread, PRECISE)
    scaled = (x_ref[...].astype(F32) * tail).astype(BF16)
    keys = b_ref[...].astype(F32).T.astype(BF16)
    own = dot(keys, scaled)
    decay = dot(jnp.broadcast_to(jnp.exp(total), (8, heads)), spread, PRECISE)
    init_t = init_ref[...].T
    init_t_ref[...] = init_t.astype(BF16)
    first = (place[0] == 0).astype(F32)
    payload_ref[0:width, :] = (own + first * (decay[0:1, :] * init_t)).astype(BF16)
    high = decay.astype(BF16).astype(F32)
    rows = iota((16, channels), 0)
    high16 = jnp.broadcast_to(high[0:1, :], (16, channels))
    low16 = jnp.broadcast_to(decay[0:1, :], (16, channels)) - high16
    payload_ref[width : width + 16, :] = jnp.where(
        rows == 0, high16, jnp.where(rows == 1, low16, 0.0)
    ).astype(BF16)


def intra_kernel(x_ref, z_ref, b_ref, c_ref, dt_t_ref, rate_ref, skip_ref, own_ref, fade_ref, token_ref):
    tokens, channels = x_ref.shape
    heads = dt_t_ref.shape[0]
    width = channels // heads
    token_ref[...] = jnp.zeros_like(token_ref)
    shape = (tokens, tokens)
    causal = iota(shape, 0) >= iota(shape, 1)
    cum = running_logs(dt_t_ref, rate_ref)
    cum_t = cum.T
    scores = lax.dot_general(
        c_ref[...], b_ref[...], (((1,), (1,)), ((), ())), preferred_element_type=F32
    )
    spread = head_spread(heads, channels)
    direct = dot(jnp.broadcast_to(skip_ref[...], (8, heads)), spread, PRECISE)[0:1, :]
    fade = dot(jnp.exp(cum), spread, PRECISE)
    per = 128 // width
    lane_head = iota((tokens, 128), 1) // width
    for group in range(heads // per):
        cols = slice(group * 128, (group + 1) * 128)
        x = x_ref[:, cols]
        total = x.astype(F32) * direct[:, cols]
        for k in range(per):
            h = group * per + k
            gap = jnp.where(causal, cum[:, h : h + 1] - cum_t[h : h + 1, :], -1e30)
            weights = (jnp.exp(gap) * scores).astype(BF16)
            part = dot(weights, x)
            total = total + jnp.where(lane_head == k, part, 0.0)
        z = z_ref[:, cols].astype(F32)
        gate = z / (1.0 + jnp.exp(-z))
        own_ref[:, cols] = total * gate
        fade_ref[:, cols] = fade[:, cols] * gate


def place_kernel(cap, experts, me, packed_ref, *refs):
    count = (len(refs) - 1) // 2
    out_ref = refs[count]
    for source, target in zip(refs[:count], refs[count + 1 :]):
        target[...] = source[...]
    blocks, rows, wide = packed_ref.shape
    tokens = blocks * rows
    slots = out_ref.shape[1] - rows
    ids = packed_ref[:, :, wide - 128 : wide].astype(F32).reshape(tokens, 128).T
    ids = ids[0:8, :].astype(jnp.int32)
    shape = (tokens, tokens)
    before = (iota(shape, 0) < iota(shape, 1)) & (iota(shape, 0) // rows == iota(shape, 1) // rows)
    named = iota((experts, tokens), 0) ^ me[0]
    hit = (ids[0:1, :] == named) | (ids[1:2, :] == named)
    rank = dot(hit.astype(BF16), before.astype(BF16)).astype(jnp.int32)
    block = (iota((experts, tokens), 1) // rows) ^ named
    whole = cap - 1
    row = jnp.where(rank < whole, block * whole + rank, blocks * whole + block)
    row = jnp.where(hit, row, -1)
    shape = (rows + slots, tokens)
    for e in range(experts):
        owned = ((me[0] ^ e) * rows + iota(shape, 0) == iota(shape, 1)) & (iota(shape, 0) < rows)
        placed = (iota(shape, 0) - rows == row[e : e + 1, :]) & (iota(shape, 0) >= rows)
        out_ref[e] = (owned | placed).astype(F32).astype(BF16)


def join_kernel(place, own_ref, other_ref, out_ref):
    width = out_ref.shape[0]
    odd = place[0] % 2 == 1
    own, other = own_ref[0:width, :].astype(F32), other_ref[0:width, :].astype(F32)
    own_decay = own_ref[width : width + 16, :].astype(F32)
    other_decay = other_ref[width : width + 16, :].astype(F32)
    own_decay = own_decay[0:1, :] + own_decay[1:2, :]
    other_decay = other_decay[0:1, :] + other_decay[1:2, :]
    early = jnp.where(odd, other, own)
    late = jnp.where(odd, own, other)
    decay = jnp.where(odd, own_decay, other_decay)
    out_ref[...] = (decay * early + late).astype(BF16)


def stream_kernel(
    place, c_ref, own_ref, fade_ref, init_t_ref, pair_ref, early_ref, res_ref, sel_ref, same_ref, other_ref
):
    width = init_t_ref.shape[0]
    at = place[0]
    zero = (at == 0).astype(F32)
    odd = (at % 2 == 1).astype(F32)
    pair = pair_ref[...].astype(F32)
    decay = pair[width : width + 1, :] + pair[width + 1 : width + 2, :]
    factor = jnp.where(at >= 2, jnp.where(at % 2 == 1, decay, 1.0), 0.0)
    entering = zero * init_t_ref[...].astype(F32) + odd * pair[0:width, :] + factor * early_ref[...].astype(F32)
    mixed = own_ref[...] + fade_ref[...] * dot(c_ref[...], entering.astype(BF16))
    mixer = mixed.astype(BF16).astype(F32)
    tokens, channels = mixer.shape
    residual = res_ref[:, :, 0:channels].astype(F32).reshape(tokens, channels)
    stream = (residual + mixer).astype(BF16)
    for k in range(same_ref.shape[0]):
        same_ref[k] = dot(sel_ref[2 * k], stream).astype(BF16)
        other_ref[k] = dot(sel_ref[2 * k + 1], stream).astype(BF16)


def up_kernel(first, features, after, group, me, *refs):
    own, rx, ry, even, odd, gain, w_gate, w_up = refs[:8]
    carry = () if first else refs[8:11]
    rest, (held_gate, held_up, sems) = refs[(8 if first else 11) + after : -3], refs[-3:]
    sums = rest[2:5] if features else rest
    step = pl.program_id(0)
    steps = held_gate.shape[0]
    tile = held_gate.shape[1]

    def loads(k):
        source = me[0] ^ (2 * group + k // (steps // 2))
        part = pl.ds(pl.multiple_of(k % (steps // 2) * tile, tile), tile)
        return [
            pltpu.make_async_copy(w.at[source, part, :], held.at[k], sems.at[side, k])
            for side, (w, held) in enumerate(((w_gate, held_gate), (w_up, held_up)))
        ]

    @pl.when(step == 0)
    def _():
        for k in range(steps):
            for load in loads(k):
                load.start()

    if first or features:

        @pl.when(step == 0)
        def _():
            for i, acc in enumerate(sums):
                acc[...] = jnp.zeros_like(acc) if first else carry[i][...]

    gate, up, square = sums
    slots = own.shape[1]
    rows = [r[0].astype(F32) for r in (own, rx, ry)]
    rows.append(jnp.where(step < steps // 2, even[0].astype(F32), odd[0].astype(F32)))
    rows = jnp.concatenate(rows, axis=0)
    square[...] += jnp.broadcast_to(jnp.sum(rows * rows, axis=1, keepdims=True), square.shape)
    scaled = (rows * gain[0]).astype(BF16)
    load_gate, load_up = loads(step)
    load_gate.wait()
    gate[...] += dot(scaled, held_gate[step])
    load_up.wait()
    up[...] += dot(scaled, held_up[step])

    if features:
        outs, stages = rest[:2], rest[5:]

        @pl.when(step == steps - 1)
        def _():
            inverse = lax.rsqrt(square[:, 0:1] * (1.0 / features) + 1e-06)
            g = gate[...] * inverse
            active = g / (1.0 + jnp.exp(-g)) * (up[...] * inverse)
            main, ninths = slots // 9 * 8, slots // 9
            for d in range(4):
                at = d * slots
                stage, d, shards = (stages[0], 0, 1) if d == 3 else (stages[1], d, 3)
                stage[d * main : (d + 1) * main, :] = active[at : at + main]
                low = shards * main + d * ninths
                stage[low : low + ninths, :] = active[at + main : at + slots]
            for out, stage in zip(outs, stages):
                out[...] = stage[...].astype(BF16)


def up_project(group, last, me, near, far, gain, w_gate, w_up, carry, after=()):
    slots, part = near[0][0].shape[1:]
    cut = 1
    tile = part // cut
    hidden = w_gate.shape[2]
    total = 4 * slots
    source = lambda i, me: me[0] ^ (2 * group + i // cut)
    rows = [
        pl.BlockSpec((1, slots, tile), lambda i, me, start=start: (start + i // cut, 0, i % cut))
        for _, start in near
    ] + [
        pl.BlockSpec((1, slots, tile), lambda i, me, start=start: (start, 0, i % cut))
        for _, start in far
    ]
    weight = pl.BlockSpec(memory_space=pltpu.HBM)
    in_place = pl.BlockSpec(memory_space=pltpu.VMEM)
    specs = rows + [
        pl.BlockSpec((1, 1, tile), lambda i, me: (source(i, me), 0, i % cut)),
        weight,
        weight,
    ]
    sums = [
        jax.ShapeDtypeStruct((total, hidden), F32),
        jax.ShapeDtypeStruct((total, hidden), F32),
        jax.ShapeDtypeStruct((total, 128), F32),
    ]
    aliases = {}
    if carry is not None:
        specs += [in_place] * 3
        if not last:
            aliases = {9 + i: i for i in range(3)}
    specs += [pl.BlockSpec(memory_space=pl.ANY)] * len(after)
    sizes = (slots, 3 * slots)
    outs = [jax.ShapeDtypeStruct((n, hidden), BF16) for n in sizes] if last else sums
    scratch = [pltpu.VMEM(s.shape, s.dtype) for s in sums]
    scratch += [pltpu.VMEM((n, hidden), F32) for n in sizes]
    features = gain.shape[0] * part if last else 0
    return pl.pallas_call(
        functools.partial(up_kernel, carry is None, features, len(after), group),
        name=f"up_{group}",
        out_shape=outs,
        grid_spec=pltpu.PrefetchScalarGridSpec(
            num_scalar_prefetch=1,
            grid=(2 * cut,),
            in_specs=specs,
            out_specs=[in_place] * len(outs),
            scratch_shapes=(scratch if last else [])
            + [pltpu.VMEM((2 * cut, tile, hidden), BF16)] * 2
            + [pltpu.SemaphoreType.DMA((2, 2 * cut))],
        ),
        input_output_aliases=aliases,
        compiler_params=pltpu.CompilerParams(vmem_limit_bytes=48 * MIB),
        cost_estimate=NO_COST,
    )(me, *(array for array, _ in near + far), gain, w_gate, w_up, *(carry or ()), *after)


def cut_of(group):
    return 5 if group % 2 else 4


def down_kernel(groups, act_ref, w_ref, *refs):
    outs, (spare, held, sems) = refs[:-3], refs[-3:]
    step = pl.program_id(0)
    steps, _, tile = held.shape

    def load(k):
        columns = pl.ds(pl.multiple_of(k * tile, tile), tile)
        return pltpu.make_async_copy(w_ref.at[:, columns], held.at[k], sems.at[k])

    @pl.when(step == 0)
    def _():
        for k in range(steps):
            load(k).start()

    load(step).wait()
    part = dot(act_ref[...], held[step])
    ninths = part.shape[0] // 9
    main = part.shape[0] - ninths
    shards = ninths // (2 * groups)

    def through(group, tile):
        to_x, to_y = outs[2 * (group // 2) : 2 * (group // 2) + 2]
        cut = cut_of(group)
        return to_x, tile + (0 if group % 2 else 5), to_y, tile - cut + (0 if group % 2 else 4)

    for shard in range(shards):
        for group in range(groups):
            at = (shard * groups + group) * 16
            rows = part[at : at + 16, :].astype(BF16)
            if shards > 1:
                outs[shards * group + shard][step] = rows
                continue
            to_x, place_x, to_y, place_y = through(group, step)

            @pl.when(step < cut_of(group))
            def _():
                to_x[place_x] = rows

            @pl.when(step >= cut_of(group))
            def _():
                to_y[place_y] = rows

    for lanes in range(spare.shape[0]):
        spare[lanes, pl.ds(pl.multiple_of(step * ninths, 8), ninths), :] = part[
            main:, lanes * 128 : (lanes + 1) * 128
        ]

    @pl.when(step == steps - 1)
    def _():
        for shard in range(shards):
            for group in range(groups):
                pair = []
                for side in range(2):
                    row = pl.ds((shard * groups + group) * 2 + side, 8, stride=ninths)
                    ninth = [spare[lanes, row, :] for lanes in range(spare.shape[0])]
                    pair.append(jnp.concatenate(ninth, axis=1))
                pair = jnp.concatenate(pair, axis=0).astype(BF16)
                if shards > 1:
                    outs[shards * group + shard][8] = pair
                else:
                    _, _, to_y, place_y = through(group, 8)
                    to_y[place_y] = pair


def down_project(name, groups, active, w_down):
    total, hidden = active.shape
    features = w_down.shape[1]
    tile = features // 8
    outs = [jax.ShapeDtypeStruct((9, 16, tile), BF16)] * (total // 18)
    return pl.pallas_call(
        functools.partial(down_kernel, groups),
        name=name,
        grid=(8,),
        out_shape=outs,
        in_specs=[
            pl.BlockSpec(memory_space=pltpu.VMEM),
            pl.BlockSpec(memory_space=pltpu.HBM),
        ],
        out_specs=[pl.BlockSpec(memory_space=pltpu.VMEM)] * len(outs),
        scratch_shapes=[
            pltpu.VMEM((tile // 128, 8 * total // 9, 128), F32),
            pltpu.VMEM((8, hidden, tile), BF16),
            pltpu.SemaphoreType.DMA((8,)),
        ],
        compiler_params=pltpu.CompilerParams(vmem_limit_bytes=48 * MIB),
        cost_estimate=NO_COST,
    )(active, w_down)


def pair_kernel(same, other, *outs):
    owned = outs[0].shape[1]
    for side, rows in enumerate((same, other)):
        for group, part in enumerate((outs[0:2], outs[2:4], outs[4:5], outs[5:7])):
            if len(part) == 1:
                part[0][side] = rows[group]
            else:
                part[0][side], part[1][side] = rows[group, 0:owned, :], rows[group, owned:, :]


def second_kernel(*refs):
    parts, out = refs[:-1], refs[-1]
    for h in range(out.shape[0]):
        for k in range(out.shape[1]):
            pair = [ref[k].astype(F32)[8:16] for ref in parts[2 * h : 2 * h + 2]]
            out[h, k] = jnp.concatenate(pair, axis=0).astype(BF16)


def hold_kernel(*refs):
    for source, target in zip(refs[: len(refs) // 2], refs[len(refs) // 2 :]):
        target[...] = source[...]


def half_message_kernel(rx, ry, out_x, out_y):
    out_x[0], out_y[0] = ry[1], rx[0]


def join_message_kernel(own, rx, ry, out_x, out_y, *parts):
    owned = own.shape[1] - out_x.shape[1]
    for side in range(2):
        rows = own[side, owned:, :]
        out_x[side], out_y[side] = rows, rows
        if parts:
            parts[0][side], parts[1][side] = rows, own[side, 0:owned, :]
    out_x[2], out_y[2] = ry[1], rx[0]


def relay_kernel(through_x, through_y, *refs):
    start = through_x.shape[0] - 9
    for group in range(2):
        cut = cut_of(group)
        at_x, at_y = (0, -cut) if group else (5, 0)
        for own, out, through, tiles, at in (
            (refs[2 * group], refs[4 + 2 * group], through_y, range(cut, 9), at_y),
            (refs[2 * group + 1], refs[5 + 2 * group], through_x, range(cut), at_x),
        ):
            for k in range(9):
                if k in tiles:
                    passed = through[start + k + at].astype(F32)
                    out[k] = (own[k].astype(F32) + passed).astype(BF16)
                else:
                    out[k] = own[k]


def finish_kernel(own, rx, ry, *refs):
    count = len(refs) if len(refs) == 1 else len(refs) - 2
    ahead, out, messages = refs[: count - 1], refs[count - 1], refs[count:]
    for k in range(9):
        out[k] = (own[k].astype(F32) + rx[k].astype(F32) + ry[k].astype(F32)).astype(BF16)
    for at, source in enumerate(ahead):
        messages[at % 2][at // 2 * 9 : at // 2 * 9 + 9] = source[...]


def mix_kernel(me, ids_t_ref, weight_t_ref, swap_ref, *refs):
    groups = (len(refs) - 1) // 2
    firsts, streams, out_ref = refs[:groups], refs[groups:-1], refs[-1]
    rows = ids_t_ref.shape[1]
    experts = 2 * groups
    pieces = firsts[0].shape[0] - 1
    tile = firsts[0].shape[2]
    ids, weights = ids_t_ref[...].T, weight_t_ref[...].T
    named = iota((rows, experts), 1) ^ me[0]
    first, second = ids[:, 0:1] == named, ids[:, 1:2] == named
    weight = jnp.where(first, weights[:, 0:1], jnp.where(second, weights[:, 1:2], 0.0))
    hit = (first | second).astype(F32)
    before = (iota((rows, rows), 0) > iota((rows, rows), 1)).astype(F32)
    rank = dot(before, hit)
    lanes = 2 * experts * 8
    shape = (experts, lanes)
    spread = ((iota(shape, 1) // 8) % experts == iota(shape, 0)).astype(F32)
    weight = dot(weight, spread, PRECISE)
    rank = dot(rank, spread, PRECISE).astype(jnp.int32)
    lane = iota((rows, lanes), 1)
    main = (lane < experts * 8) & (rank == lane % 8)
    extra = (lane >= experts * 8) & (rank == 8)

    def rows_of(k):
        data = []
        for g in range(groups):
            data.append(firsts[g][k].astype(F32)[0:8])
            data.append(swap_ref[g // 2, k].astype(F32)[g % 2 * 8 : g % 2 * 8 + 8])
        return data

    last = rows_of(pieces)
    for m in range(experts):
        k = me[0] ^ m
        coef = jnp.where(main | (extra & (lane % 8 == k)), weight, 0.0)
        high = coef.astype(BF16)
        low = (coef - high.astype(F32)).astype(BF16)
        data = jnp.concatenate(rows_of(k) + last, axis=0).astype(BF16)
        stream = streams[m // 2][m % 2].astype(F32)
        out_ref[:, pl.ds(pl.multiple_of(k * tile, 128), tile)] = (
            stream + (dot(high, data) + dot(low, data))
        ).astype(BF16)


def on_square(
    x_in,
    z_gate,
    b_in,
    c_out,
    dt_step,
    rate,
    skip,
    init_state,
    residual,
    norm_gain,
    expert_ids,
    gate_weights,
    w_gate,
    w_up,
    w_down,
):
    tokens, channels = x_in.shape
    heads = rate.shape[0]
    state = b_in.shape[1]
    owners = lax.axis_size("exp")
    rows, features = residual.shape
    experts = owners
    cap = max(2, 2 * rows // experts + 1)
    slots = owners * cap
    at = lax.axis_index("seq")
    me = lax.axis_index("exp")
    place = jnp.reshape(at, (1,)).astype(jnp.int32)
    self_id = jnp.reshape(me, (1,)).astype(jnp.int32)

    def over_x(v):
        return lax.ppermute(v, "seq", [(i, i ^ 1) for i in range(4)])

    def over_y(v):
        return lax.ppermute(v, "seq", [(i, i ^ 2) for i in range(4)])

    def along(v, mask):
        return lax.ppermute(v, "exp", [(i, i ^ mask) for i in range(owners)])

    rate_row = rate[None, :]
    dt_t = dt_step.T
    ids_t = expert_ids.T
    packed = block_call(
        pack_kernel,
        [jax.ShapeDtypeStruct((owners, rows, channels + 128), BF16)],
        0,
        (ids_t, residual),
        held=2,
        limit=48,
    )[0]
    packed = lax.all_to_all(packed, "exp", split_axis=0, concat_axis=0, tiled=True)
    payload, init_t = block_call(
        state_kernel,
        [
            jax.ShapeDtypeStruct((state + 16, channels), BF16),
            jax.ShapeDtypeStruct((state, channels), BF16),
        ],
        1,
        (place, x_in, b_in, dt_t, rate_row, init_state.reshape(channels, state)),
        held=5,
        limit=62,
    )
    pair = over_x(payload)
    own_part, fade, token = block_call(
        intra_kernel,
        [
            jax.ShapeDtypeStruct((tokens, channels), F32),
            jax.ShapeDtypeStruct((tokens, channels), F32),
            jax.ShapeDtypeStruct((8, 128), F32),
        ],
        0,
        (x_in, z_gate, b_in, c_out, dt_t, rate_row, skip[None, :]),
        held=7,
        limit=61,
    )
    joined = block_call(
        join_kernel,
        [jax.ShapeDtypeStruct((state, channels), BF16)],
        1,
        (place, payload, pair),
        after=(token,),
    )[0]
    early = over_y(joined)
    handed = (own_part, fade, c_out, init_t)
    select, own_part, fade, c, init_t = block_call(
        functools.partial(place_kernel, cap, experts),
        [jax.ShapeDtypeStruct((experts, rows + slots, tokens), BF16)]
        + [jax.ShapeDtypeStruct(v.shape, v.dtype) for v in handed],
        1,
        (self_id, packed, *handed),
        after=(joined,),
    )
    groups = owners // 2
    lanes = jax.ShapeDtypeStruct((groups, rows + slots, channels), BF16)
    same, other = block_call(
        stream_kernel,
        [lanes, lanes],
        1,
        (place, c, own_part, fade, init_t, pair, early, packed, select),
    )

    gain = norm_gain.reshape(owners, 1, channels)
    wg = w_gate.reshape(owners, channels, w_gate.shape[2])
    wu = w_up.reshape(owners, channels, w_up.shape[2])
    expert_rows = jax.ShapeDtypeStruct((2, slots, channels), BF16)
    stream_rows = jax.ShapeDtypeStruct((2, rows, channels), BF16)
    both_rows = jax.ShapeDtypeStruct((2, rows + slots, channels), BF16)
    stream0, first, stream1, near, far, stream3, farthest = block_call(
        pair_kernel,
        [stream_rows, expert_rows, stream_rows, expert_rows, both_rows, stream_rows, expert_rows],
        0,
        (same, along(other, 1)),
    )
    gain = norm_gain.reshape(owners, 1, channels)
    wg = w_gate.reshape(owners, channels, w_gate.shape[2])
    wu = w_up.reshape(owners, channels, w_up.shape[2])
    gain = norm_gain.reshape(owners, 1, channels)
    wg = w_gate.reshape(owners, channels, w_gate.shape[2])
    wu = w_up.reshape(owners, channels, w_up.shape[2])

    def hold(values, after, name):
        outs = [jax.ShapeDtypeStruct(v.shape, BF16) for v in values]
        return block_call(hold_kernel, outs, 0, values, after=after, name=name)

    def project(group, near, far, carry, after=()):
        last = group == groups - 1
        return up_project(group, last, self_id, near, far, gain, wg, wu, carry, after)

    def message(count):
        return [jax.ShapeDtypeStruct((count, slots, channels), BF16)] * 2

    near, far = along(near, 2), along(far, 4)
    rx0, ry0 = over_x(first), over_y(first)
    to_x, to_y = block_call(half_message_kernel, message(1), 0, (rx0, ry0), name="half_0")
    fx0, fy0 = over_x(to_x), over_y(to_y)
    near, stream1 = hold((near, stream1), (to_x,), "hold_near")
    rx1, ry1 = over_x(near), over_y(near)
    stream1 = along(stream1, 2)
    farthest_held = hold((farthest,), (far,), "hold_farthest")[0]
    farthest = along(farthest_held, 6)
    to_x, to_y, far, stream2 = block_call(
        join_message_kernel,
        message(3) + [expert_rows, stream_rows],
        0,
        (far, rx1, ry1),
        after=(fx0, fy0, farthest_held, stream1),
        name="join_2",
    )
    rx2, ry2 = over_x(to_x), over_y(to_y)
    carry = project(0, [(first, 0), (rx0, 0), (ry0, 0)], [(fy0, 0), (fx0, 0)], None)
    to_x, to_y = block_call(
        join_message_kernel, message(3), 0, (farthest, rx2, ry2), after=(carry[2],), name="join_3"
    )
    rx3, ry3 = over_x(to_x), over_y(to_y)
    held = hold((stream3,), (to_x,), "hold_stream")[0]
    stream3 = along(held, 6)
    carry = project(1, [(near, 0), (rx1, 0), (ry1, 0)], [(ry2, 2), (rx2, 2)], carry, (held,))
    to_x, to_y = block_call(
        half_message_kernel, message(1), 0, (rx3, ry3), after=(carry[2], stream3), name="half_3"
    )
    fx3, fy3 = over_x(to_x), over_y(to_y)
    carry = project(2, [(far, 0), (rx2, 0), (ry2, 0)], [(ry3, 2), (rx3, 2)], carry)
    active_far, active = project(
        3, [(farthest, 0), (rx3, 0), (ry3, 0)], [(fy3, 0), (fx3, 0)], carry
    )

    wd = w_down.reshape(w_down.shape[1], features)
    tiles = jax.ShapeDtypeStruct((9, 16, features // 8), BF16)
    sent = down_project("down_through", groups, active_far, wd)
    rest = down_project("down_rest", groups, active, wd)
    own, own_x, own_y = ([rest[3 * g + k] for g in range(groups)] for k in range(3))

    def relay(name, through_x, through_y, low, after=()):
        shares = (own_x[low], own_y[low], own_x[low + 1], own_y[low + 1])
        return block_call(
            relay_kernel, [tiles] * 4, 0, (through_x, through_y, *shares), after=after, name=name
        )

    def finish(group, rx, ry, ahead=(), after=()):
        ahead_tiles = jax.ShapeDtypeStruct((9 * len(ahead) // 2, *tiles.shape[1:]), BF16)
        return block_call(
            finish_kernel,
            [tiles] + ([ahead_tiles] * 2 if ahead else []),
            0,
            (own[group], rx, ry, *ahead),
            after=after,
            name=f"finish_{group}",
        )

    through_x, through_y = over_x(sent[2]), over_y(sent[3])
    x2, y2, x3, y3 = relay("relay_far", through_x, through_y, 2)
    rx3, ry3 = over_x(x3), over_y(y3)
    both3, to_x, to_y = finish(3, rx3, ry3, (x2, y2, sent[0], sent[1]))
    back3 = along(both3, 6)
    rx2, ry2 = over_x(to_x), over_y(to_y)
    both2 = finish(2, rx2, ry2)[0]
    back2 = along(both2, 4)
    x0, y0, x1, y1 = relay("relay_near", rx2, ry2, 0, (both2,))
    rx1, ry1 = over_x(x1), over_y(y1)
    both1, x0, y0 = finish(1, rx1, ry1, (x0, y0), (back3,))
    back1 = along(both1, 2)
    rx0, ry0 = over_x(x0), over_y(y0)
    back = [finish(0, rx0, ry0)[0], back1, back2, back3]
    swap = block_call(second_kernel, [jax.ShapeDtypeStruct((2,) + tiles.shape, BF16)], 0, back)[0]
    swap = along(swap, 1)
    return block_call(
        mix_kernel,
        [jax.ShapeDtypeStruct((rows, features), BF16)],
        1,
        (self_id, ids_t, gate_weights.T, swap, *back, stream0, stream1, stream2, stream3),
    )[0]


def entering_2(array, axis, combine, identity):
    devices, mine = (lax.axis_size(axis), lax.axis_index(axis))
    everything = jax.tree.map(
        lambda part, kind: lax.all_gather(part.astype(kind), axis),
        array,
        (jnp.bfloat16, jnp.bfloat16),
    )
    start = jax.tree.map(
        lambda part, zero: jnp.broadcast_to(jnp.asarray(zero, part.dtype), part.shape),
        array,
        identity,
    )

    def hop(k, before):
        reached = k < mine
        new = combine(
            before, jax.tree.map(lambda part, own: part[k].astype(own.dtype), everything, array)
        )
        return jax.tree.map(lambda a, b: jnp.where(reached, a, b), new, before)

    return lax.fori_loop(0, devices, hop, start)


def chain_combine(earlier, later):
    return (earlier[0] + later[0], jnp.exp(later[0])[:, None, None] * earlier[1] + later[1])


def on_device(
    x_in,
    z_gate,
    b_in,
    c_out,
    dt_step,
    rate,
    skip,
    init_state,
    residual,
    norm_gain,
    expert_ids,
    gate_weights,
    w_gate,
    w_up,
    w_down,
):
    token_count, channels = x_in.shape
    heads_here = rate.shape[0]
    head_width = channels // heads_here
    state_width = b_in.shape[1]
    blocks = token_count // GROUP
    inputs = x_in.astype(jnp.float32).reshape(blocks, GROUP, heads_here, head_width)
    keys_in = b_in.astype(jnp.float32).reshape(blocks, GROUP, state_width)
    queries = c_out.astype(jnp.float32).reshape(blocks, GROUP, state_width)
    log_steps = (-rate[None, :] * dt_step).reshape(blocks, GROUP, heads_here)
    cumulative = jnp.cumsum(log_steps, axis=1)
    scores = jnp.einsum("ctn,csn->cts", queries, keys_in, precision=PRECISE)
    causal = jnp.arange(GROUP)[:, None] >= jnp.arange(GROUP)[None, :]
    spread = cumulative[:, :, None, :] - cumulative[:, None, :, :]
    weights = jnp.exp(jnp.where(causal[None, :, :, None], spread, -jnp.inf)) * scores[..., None]
    intra_out = jnp.einsum("ctsh,cshp->cthp", weights, inputs, precision=PRECISE)
    tail_decay = jnp.exp(cumulative[:, -1:, :] - cumulative)
    block_state = jnp.einsum("csh,cshp,csn->chpn", tail_decay, inputs, keys_in, precision=PRECISE)
    block_log = cumulative[:, -1, :]

    def advance(carried, element):
        total_log, total_state = carried
        step_log, step_state = element
        updated = (
            total_log + step_log,
            jnp.exp(step_log)[:, None, None] * total_state + step_state,
        )
        return (updated, (total_log, total_state))

    zero_state = jnp.zeros((heads_here, head_width, state_width), jnp.float32)
    zero_log = jnp.zeros((heads_here,), jnp.float32)
    (device_log, device_state), (enter_log, enter_state) = lax.scan(
        advance, (zero_log, zero_state), (block_log, block_state)
    )
    prior_log, prior_state = entering_2(
        (device_log, device_state), "seq", chain_combine, (zero_log, zero_state)
    )
    incoming = prior_state + jnp.exp(prior_log)[:, None, None] * init_state
    entering = enter_state + jnp.exp(enter_log)[:, :, None, None] * incoming[None]
    inter_out = jnp.exp(cumulative)[..., None] * jnp.einsum(
        "chpn,ctn->cthp", entering, queries, precision=PRECISE
    )
    mixed_out = (intra_out + inter_out + skip[None, None, :, None] * inputs).reshape(
        token_count, channels
    )
    mixer = (mixed_out * jax.nn.silu(z_gate.astype(jnp.float32))).astype(jnp.bfloat16)
    token_mix = lax.all_to_all(mixer, "exp", split_axis=0, concat_axis=1, tiled=True)
    stream = (residual.astype(jnp.float32) + token_mix.astype(jnp.float32)).astype(jnp.bfloat16)
    widened = stream.astype(jnp.float32)
    normed = (
        widened
        * lax.rsqrt(jnp.mean(widened * widened, axis=-1, keepdims=True) + 1e-06)
        * norm_gain[None, :]
    ).astype(jnp.bfloat16)
    rows_here = residual.shape[0]
    owners = lax.axis_size("exp")
    local_experts = w_gate.shape[0]
    experts = owners * local_experts
    capacity = max(2, 2 * rows_here // experts + 1)
    width = residual.shape[1]
    chosen = expert_ids.reshape(-1)
    onehot = (chosen[:, None] == jnp.arange(experts)[None, :]).astype(jnp.int32)
    slot_index = jnp.sum((jnp.cumsum(onehot, axis=0) - onehot) * onehot, axis=1)
    target = chosen * capacity + slot_index
    placing = (target[None, :] == jnp.arange(experts * capacity)[:, None]).astype(jnp.bfloat16)
    pair_rows = jnp.repeat(normed, 2, axis=0)
    outgoing = jnp.dot(placing, pair_rows, preferred_element_type=jnp.float32).astype(jnp.bfloat16)
    outgoing = outgoing.reshape(owners, local_experts, 1, capacity, width)
    arrived = lax.all_to_all(outgoing, "exp", split_axis=0, concat_axis=2, tiled=True)
    segment = lax.all_gather(arrived, "seq", axis=1, tiled=True)
    flattened = segment.reshape(segment.shape[0], -1, segment.shape[-1])
    gate_proj = jnp.einsum("erd,edf->erf", flattened, w_gate, preferred_element_type=jnp.float32)
    up_proj = jnp.einsum("erd,edf->erf", flattened, w_up, preferred_element_type=jnp.float32)
    active = (jax.nn.silu(gate_proj) * up_proj).astype(jnp.bfloat16)
    partial_value = jnp.einsum("erf,efd->erd", active, w_down, preferred_element_type=jnp.float32)
    partials = partial_value.reshape(segment.shape[:-1] + (partial_value.shape[-1],))
    summed = lax.psum_scatter(partials.astype(jnp.bfloat16), "seq", scatter_dimension=1, tiled=True)
    returned = lax.all_to_all(summed, "exp", split_axis=2, concat_axis=0, tiled=True)
    results = returned.reshape(experts * capacity, width)
    picked = results[target].astype(jnp.float32).reshape(rows_here, 2, width)
    mixture = jnp.sum(picked * gate_weights[:, :, None], axis=1)
    return (widened + mixture).astype(jnp.bfloat16)


def solution(mesh):
    square = mesh.shape["seq"] == 4 and mesh.shape["exp"] == 8

    def body(*args):
        rows = args[8].shape[0]
        experts = mesh.shape["exp"] * args[12].shape[0]
        fits = args[12].shape[0] == 1 and 2 * rows // experts + 1 == 9
        return (on_square if square and fits else on_device)(*args)

    return jax.shard_map(
        body,
        mesh=mesh,
        in_specs=(
            P("seq", "exp"),
            P("seq", "exp"),
            P("seq", None),
            P("seq", None),
            P("seq", "exp"),
            P("exp"),
            P("exp"),
            P("exp", None, None),
            P(("seq", "exp"), None),
            P(),
            P(("seq", "exp"), None),
            P(("seq", "exp"), None),
            P("exp", None, "seq"),
            P("exp", None, "seq"),
            P("exp", "seq", None),
        ),
        out_specs=P(("seq", "exp"), None),
        check_vma=False,
    )
```

```python
import functools

import jax
import jax.numpy as jnp
from jax import lax
from jax.experimental import pallas as pl
from jax.experimental.pallas import tpu as pltpu
from jax.sharding import PartitionSpec as P

GROUP = 128
PRECISE = lax.Precision.HIGHEST
F32 = jnp.float32
BF16 = jnp.bfloat16
MIB = 1 << 20
NO_COST = pl.CostEstimate(flops=0, bytes_accessed=0, transcendentals=0)


def block_call(body, outs, scalars, args, held=0, keep=0, after=(), limit=16, out_blocks=False, name=None):
    n_args = len(args)
    kept = [jax.ShapeDtypeStruct(v.shape, v.dtype) for v in args[scalars : scalars + held]]

    def kernel(*refs):
        refs, sems = (refs[:-1], refs[-1]) if held else (refs, None)
        inputs, refs = refs[:n_args], refs[n_args + len(after) :]
        results, refs = refs[: len(outs)], refs[len(outs) :]
        copies = [
            pltpu.make_async_copy(src, dst, sems.at[k])
            for k, (src, dst) in enumerate(zip(inputs[scalars : scalars + held], refs))
        ]
        for copy in copies:
            copy.start()
        for copy in copies:
            copy.wait()
        body(*inputs[:scalars], *refs, *inputs[scalars + held :], *results)

    scratch = [pltpu.VMEM(v.shape, v.dtype) for v in kept[keep:]]
    if held:
        scratch.append(pltpu.SemaphoreType.DMA((held,)))
    return pl.pallas_call(
        kernel,
        name=name or getattr(body, "func", body).__name__,
        out_shape=list(outs) + kept[:keep],
        in_specs=[pl.BlockSpec(memory_space=pltpu.SMEM)] * scalars
        + [pl.BlockSpec(memory_space=pltpu.HBM)] * held
        + [pl.BlockSpec(memory_space=pltpu.VMEM)] * (n_args - scalars - held)
        + [pl.BlockSpec(memory_space=pl.ANY)] * len(after),
        out_specs=[pl.BlockSpec() if out_blocks else pl.BlockSpec(memory_space=pltpu.VMEM)]
        * (len(outs) + keep),
        scratch_shapes=scratch,
        compiler_params=pltpu.CompilerParams(vmem_limit_bytes=limit * MIB),
        cost_estimate=NO_COST,
    )(*args, *after)


def iota(shape, dim):
    return lax.broadcasted_iota(jnp.int32, shape, dim)


def dot(a, b, precision=None):
    return jnp.dot(a, b, precision=precision, preferred_element_type=F32)


def head_spread(heads, channels):
    shape = (heads, channels)
    return (iota(shape, 1) // (channels // heads) == iota(shape, 0)).astype(F32)


def running_logs(dt_t_ref, rate_ref):
    logs = -rate_ref[...] * dt_t_ref[...].T
    tokens = logs.shape[0]
    tri = (iota((tokens, tokens), 0) >= iota((tokens, tokens), 1)).astype(F32)
    return dot(tri, logs, PRECISE)


def pack_kernel(ids_t_ref, residual_ref, out_ref):
    parts, rows, wide = out_ref.shape
    part = wide - 128
    ids = ids_t_ref[...].astype(F32).T
    lane = iota((rows, 128), 1)
    named = jnp.where(lane == 0, ids[:, 0:1], jnp.where(lane == 1, ids[:, 1:2], 0.0)).astype(BF16)
    for k in range(parts):
        out_ref[k, :, 0:part] = residual_ref[:, k * part : (k + 1) * part]
        out_ref[k, :, part:wide] = named


def state_kernel(place, x_ref, b_ref, dt_t_ref, rate_ref, init_ref, payload_ref, init_t_ref):
    tokens, channels = x_ref.shape
    heads = dt_t_ref.shape[0]
    width = b_ref.shape[1]
    cum = running_logs(dt_t_ref, rate_ref)
    total = cum[tokens - 1 : tokens, :]
    spread = head_spread(heads, channels)
    tail = dot(jnp.exp(total - cum), spread, PRECISE)
    scaled = (x_ref[...].astype(F32) * tail).astype(BF16)
    keys = b_ref[...].astype(F32).T.astype(BF16)
    own = dot(keys, scaled)
    decay = dot(jnp.broadcast_to(jnp.exp(total), (8, heads)), spread, PRECISE)
    init_t = init_ref[...].T
    init_t_ref[...] = init_t.astype(BF16)
    first = (place[0] == 0).astype(F32)
    payload_ref[0:width, :] = (own + first * (decay[0:1, :] * init_t)).astype(BF16)
    high = decay.astype(BF16).astype(F32)
    rows = iota((16, channels), 0)
    high16 = jnp.broadcast_to(high[0:1, :], (16, channels))
    low16 = jnp.broadcast_to(decay[0:1, :], (16, channels)) - high16
    payload_ref[width : width + 16, :] = jnp.where(
        rows == 0, high16, jnp.where(rows == 1, low16, 0.0)
    ).astype(BF16)


def intra_kernel(x_ref, z_ref, b_ref, c_ref, dt_t_ref, rate_ref, skip_ref, own_ref, fade_ref, token_ref):
    tokens, channels = x_ref.shape
    heads = dt_t_ref.shape[0]
    width = channels // heads
    token_ref[...] = jnp.zeros_like(token_ref)
    shape = (tokens, tokens)
    causal = iota(shape, 0) >= iota(shape, 1)
    cum = running_logs(dt_t_ref, rate_ref)
    cum_t = cum.T
    scores = lax.dot_general(
        c_ref[...], b_ref[...], (((1,), (1,)), ((), ())), preferred_element_type=F32
    )
    spread = head_spread(heads, channels)
    direct = dot(jnp.broadcast_to(skip_ref[...], (8, heads)), spread, PRECISE)[0:1, :]
    fade = dot(jnp.exp(cum), spread, PRECISE)
    per = 128 // width
    lane_head = iota((tokens, 128), 1) // width
    for group in range(heads // per):
        cols = slice(group * 128, (group + 1) * 128)
        x = x_ref[:, cols]
        total = x.astype(F32) * direct[:, cols]
        for k in range(per):
            h = group * per + k
            gap = jnp.where(causal, cum[:, h : h + 1] - cum_t[h : h + 1, :], -1e30)
            weights = (jnp.exp(gap) * scores).astype(BF16)
            part = dot(weights, x)
            total = total + jnp.where(lane_head == k, part, 0.0)
        z = z_ref[:, cols].astype(F32)
        gate = z / (1.0 + jnp.exp(-z))
        own_ref[:, cols] = total * gate
        fade_ref[:, cols] = fade[:, cols] * gate


def place_kernel(cap, experts, me, packed_ref, *refs):
    count = (len(refs) - 1) // 2
    out_ref = refs[count]
    for source, target in zip(refs[:count], refs[count + 1 :]):
        target[...] = source[...]
    blocks, rows, wide = packed_ref.shape
    tokens = blocks * rows
    slots = out_ref.shape[1] - rows
    ids = packed_ref[:, :, wide - 128 : wide].astype(F32).reshape(tokens, 128).T
    ids = ids[0:8, :].astype(jnp.int32)
    shape = (tokens, tokens)
    before = (iota(shape, 0) < iota(shape, 1)) & (iota(shape, 0) // rows == iota(shape, 1) // rows)
    named = iota((experts, tokens), 0) ^ me[0]
    hit = (ids[0:1, :] == named) | (ids[1:2, :] == named)
    rank = dot(hit.astype(BF16), before.astype(BF16)).astype(jnp.int32)
    block = (iota((experts, tokens), 1) // rows) ^ named
    whole = cap - 1
    row = jnp.where(rank < whole, block * whole + rank, blocks * whole + block)
    row = jnp.where(hit, row, -1)
    shape = (rows + slots, tokens)
    for e in range(experts):
        owned = ((me[0] ^ e) * rows + iota(shape, 0) == iota(shape, 1)) & (iota(shape, 0) < rows)
        placed = (iota(shape, 0) - rows == row[e : e + 1, :]) & (iota(shape, 0) >= rows)
        out_ref[e] = (owned | placed).astype(F32).astype(BF16)


def join_kernel(place, own_ref, other_ref, out_ref):
    width = out_ref.shape[0]
    odd = place[0] % 2 == 1
    own, other = own_ref[0:width, :].astype(F32), other_ref[0:width, :].astype(F32)
    own_decay = own_ref[width : width + 16, :].astype(F32)
    other_decay = other_ref[width : width + 16, :].astype(F32)
    own_decay = own_decay[0:1, :] + own_decay[1:2, :]
    other_decay = other_decay[0:1, :] + other_decay[1:2, :]
    early = jnp.where(odd, other, own)
    late = jnp.where(odd, own, other)
    decay = jnp.where(odd, own_decay, other_decay)
    out_ref[...] = (decay * early + late).astype(BF16)


def stream_kernel(
    place, c_ref, own_ref, fade_ref, init_t_ref, pair_ref, early_ref, res_ref, sel_ref, same_ref, other_ref
):
    width = init_t_ref.shape[0]
    at = place[0]
    zero = (at == 0).astype(F32)
    odd = (at % 2 == 1).astype(F32)
    pair = pair_ref[...].astype(F32)
    decay = pair[width : width + 1, :] + pair[width + 1 : width + 2, :]
    factor = jnp.where(at >= 2, jnp.where(at % 2 == 1, decay, 1.0), 0.0)
    entering = zero * init_t_ref[...].astype(F32) + odd * pair[0:width, :] + factor * early_ref[...].astype(F32)
    mixed = own_ref[...] + fade_ref[...] * dot(c_ref[...], entering.astype(BF16))
    mixer = mixed.astype(BF16).astype(F32)
    tokens, channels = mixer.shape
    residual = res_ref[:, :, 0:channels].astype(F32).reshape(tokens, channels)
    stream = (residual + mixer).astype(BF16)
    for k in range(same_ref.shape[0]):
        same_ref[k] = dot(sel_ref[2 * k], stream).astype(BF16)
        other_ref[k] = dot(sel_ref[2 * k + 1], stream).astype(BF16)


def up_kernel(first, features, after, me, *refs):
    own, rx, ry, even, odd, gain, wg, wu = refs[:8]
    carry = () if first else refs[8:11]
    rest = refs[(8 if first else 11) + after :]
    sums = rest[2:5] if features else rest
    step = pl.program_id(0)
    steps = pl.num_programs(0)

    if first or features:

        @pl.when(step == 0)
        def _():
            for i, acc in enumerate(sums):
                acc[...] = jnp.zeros_like(acc) if first else carry[i][...]

    gate, up, square = sums
    slots = own.shape[1]
    rows = [r[0].astype(F32) for r in (own, rx, ry)]
    rows.append(jnp.where(step == 0, even[0].astype(F32), odd[0].astype(F32)))
    rows = jnp.concatenate(rows, axis=0)
    square[...] += jnp.broadcast_to(jnp.sum(rows * rows, axis=1, keepdims=True), square.shape)
    scaled = (rows * gain[0]).astype(BF16)
    gate[...] += dot(scaled, wg[0])
    up[...] += dot(scaled, wu[0])

    if features:
        outs, stages = rest[:2], rest[5:]

        @pl.when(step == steps - 1)
        def _():
            inverse = lax.rsqrt(square[:, 0:1] * (1.0 / features) + 1e-06)
            g = gate[...] * inverse
            active = g / (1.0 + jnp.exp(-g)) * (up[...] * inverse)
            main, ninths = slots // 9 * 8, slots // 9
            for d in range(4):
                at = d * slots
                stage, d, shards = (stages[0], 0, 1) if d == 3 else (stages[1], d, 3)
                stage[d * main : (d + 1) * main, :] = active[at : at + main]
                low = shards * main + d * ninths
                stage[low : low + ninths, :] = active[at + main : at + slots]
            for out, stage in zip(outs, stages):
                out[...] = stage[...].astype(BF16)


def up_project(group, last, me, near, far, gain, w_gate, w_up, carry, after=()):
    slots, part = near[0][0].shape[1:]
    hidden = w_gate.shape[2]
    total = 4 * slots
    source = lambda i, me: me[0] ^ (2 * group + i)
    rows = [
        pl.BlockSpec((1, slots, part), lambda i, me, start=start: (start + i, 0, 0))
        for _, start in near
    ] + [
        pl.BlockSpec((1, slots, part), lambda i, me, start=start: (start, 0, 0)) for _, start in far
    ]
    weight = pl.BlockSpec((1, part, hidden), lambda i, me: (source(i, me), 0, 0))
    in_place = pl.BlockSpec(memory_space=pltpu.VMEM)
    specs = rows + [pl.BlockSpec((1, 1, part), lambda i, me: (source(i, me), 0, 0)), weight, weight]
    sums = [
        jax.ShapeDtypeStruct((total, hidden), F32),
        jax.ShapeDtypeStruct((total, hidden), F32),
        jax.ShapeDtypeStruct((total, 128), F32),
    ]
    aliases = {}
    if carry is not None:
        specs += [in_place] * 3
        if not last:
            aliases = {9 + i: i for i in range(3)}
    specs += [pl.BlockSpec(memory_space=pl.ANY)] * len(after)
    sizes = (slots, 3 * slots)
    outs = [jax.ShapeDtypeStruct((n, hidden), BF16) for n in sizes] if last else sums
    scratch = [pltpu.VMEM(s.shape, s.dtype) for s in sums]
    scratch += [pltpu.VMEM((n, hidden), F32) for n in sizes]
    features = gain.shape[0] * part if last else 0
    return pl.pallas_call(
        functools.partial(up_kernel, carry is None, features, len(after)),
        name=f"up_{group}",
        out_shape=outs,
        grid_spec=pltpu.PrefetchScalarGridSpec(
            num_scalar_prefetch=1,
            grid=(2,),
            in_specs=specs,
            out_specs=[in_place] * len(outs),
            scratch_shapes=scratch if last else [],
        ),
        input_output_aliases=aliases,
        compiler_params=pltpu.CompilerParams(vmem_limit_bytes=48 * MIB),
        cost_estimate=NO_COST,
    )(me, *(array for array, _ in near + far), gain, w_gate, w_up, *(carry or ()), *after)


def cut_of(group):
    return 5 if group % 2 else 4


def down_kernel(groups, act_ref, w_ref, *refs):
    outs, (spare, held, sems) = refs[:-3], refs[-3:]
    step = pl.program_id(0)
    steps, _, tile = held.shape

    def load(k):
        columns = pl.ds(pl.multiple_of(k * tile, tile), tile)
        return pltpu.make_async_copy(w_ref.at[:, columns], held.at[k], sems.at[k])

    @pl.when(step == 0)
    def _():
        for k in range(steps):
            load(k).start()

    load(step).wait()
    part = dot(act_ref[...], held[step])
    ninths = part.shape[0] // 9
    main = part.shape[0] - ninths
    shards = ninths // (2 * groups)

    def through(group, tile):
        to_x, to_y = outs[2 * (group // 2) : 2 * (group // 2) + 2]
        cut = cut_of(group)
        return to_x, tile + (0 if group % 2 else 5), to_y, tile - cut + (0 if group % 2 else 4)

    for shard in range(shards):
        for group in range(groups):
            at = (shard * groups + group) * 16
            rows = part[at : at + 16, :].astype(BF16)
            if shards > 1:
                outs[shards * group + shard][step] = rows
                continue
            to_x, place_x, to_y, place_y = through(group, step)

            @pl.when(step < cut_of(group))
            def _():
                to_x[place_x] = rows

            @pl.when(step >= cut_of(group))
            def _():
                to_y[place_y] = rows

    for lanes in range(spare.shape[0]):
        spare[lanes, pl.ds(pl.multiple_of(step * ninths, 8), ninths), :] = part[
            main:, lanes * 128 : (lanes + 1) * 128
        ]

    @pl.when(step == steps - 1)
    def _():
        for shard in range(shards):
            for group in range(groups):
                pair = []
                for side in range(2):
                    row = pl.ds((shard * groups + group) * 2 + side, 8, stride=ninths)
                    ninth = [spare[lanes, row, :] for lanes in range(spare.shape[0])]
                    pair.append(jnp.concatenate(ninth, axis=1))
                pair = jnp.concatenate(pair, axis=0).astype(BF16)
                if shards > 1:
                    outs[shards * group + shard][8] = pair
                else:
                    _, _, to_y, place_y = through(group, 8)
                    to_y[place_y] = pair


def down_project(name, groups, active, w_down):
    total, hidden = active.shape
    features = w_down.shape[1]
    tile = features // 8
    outs = [jax.ShapeDtypeStruct((9, 16, tile), BF16)] * (total // 18)
    return pl.pallas_call(
        functools.partial(down_kernel, groups),
        name=name,
        grid=(8,),
        out_shape=outs,
        in_specs=[
            pl.BlockSpec(memory_space=pltpu.VMEM),
            pl.BlockSpec(memory_space=pltpu.HBM),
        ],
        out_specs=[pl.BlockSpec(memory_space=pltpu.VMEM)] * len(outs),
        scratch_shapes=[
            pltpu.VMEM((tile // 128, 8 * total // 9, 128), F32),
            pltpu.VMEM((8, hidden, tile), BF16),
            pltpu.SemaphoreType.DMA((8,)),
        ],
        compiler_params=pltpu.CompilerParams(vmem_limit_bytes=48 * MIB),
        cost_estimate=NO_COST,
    )(active, w_down)


def pair_kernel(same, other, *outs):
    owned = outs[0].shape[1]
    for side, rows in enumerate((same, other)):
        for group, part in enumerate((outs[0:2], outs[2:4], outs[4:5], outs[5:7])):
            if len(part) == 1:
                part[0][side] = rows[group]
            else:
                part[0][side], part[1][side] = rows[group, 0:owned, :], rows[group, owned:, :]


def second_kernel(*refs):
    parts, out = refs[:-1], refs[-1]
    for h in range(out.shape[0]):
        for k in range(out.shape[1]):
            pair = [ref[k].astype(F32)[8:16] for ref in parts[2 * h : 2 * h + 2]]
            out[h, k] = jnp.concatenate(pair, axis=0).astype(BF16)


def hold_kernel(*refs):
    for source, target in zip(refs[: len(refs) // 2], refs[len(refs) // 2 :]):
        target[...] = source[...]


def half_message_kernel(rx, ry, out_x, out_y):
    out_x[0], out_y[0] = ry[1], rx[0]


def join_message_kernel(own, rx, ry, out_x, out_y, *parts):
    owned = own.shape[1] - out_x.shape[1]
    for side in range(2):
        rows = own[side, owned:, :]
        out_x[side], out_y[side] = rows, rows
        if parts:
            parts[0][side], parts[1][side] = rows, own[side, 0:owned, :]
    out_x[2], out_y[2] = ry[1], rx[0]


def relay_kernel(through_x, through_y, *refs):
    ahead = refs[4 : 4 + (len(refs) - 8) // 2]
    outs, copies = refs[4 + len(ahead) :][:4], refs[8 + len(ahead) :]
    for group in range(2):
        cut = cut_of(group)
        at_x, at_y = (0, -cut) if group else (5, 0)
        for own, out, through, tiles, at in (
            (refs[2 * group], outs[2 * group], through_y, range(cut, 9), at_y),
            (refs[2 * group + 1], outs[2 * group + 1], through_x, range(cut), at_x),
        ):
            for k in range(9):
                if k in tiles:
                    out[k] = (own[k].astype(F32) + through[k + at].astype(F32)).astype(BF16)
                else:
                    out[k] = own[k]
    for source, copy in zip(ahead, copies):
        copy[...] = source[...]


def finish_kernel(own, rx, ry, *refs):
    ahead = refs[: (len(refs) - 1) // 2]
    out, copies = refs[len(ahead)], refs[len(ahead) + 1 :]
    for k in range(9):
        out[k] = (own[k].astype(F32) + rx[k].astype(F32) + ry[k].astype(F32)).astype(BF16)
    for source, copy in zip(ahead, copies):
        copy[...] = source[...]


def mix_kernel(me, ids_t_ref, weight_t_ref, swap_ref, *refs):
    groups = (len(refs) - 1) // 2
    firsts, streams, out_ref = refs[:groups], refs[groups:-1], refs[-1]
    rows = ids_t_ref.shape[1]
    experts = 2 * groups
    pieces = firsts[0].shape[0] - 1
    tile = firsts[0].shape[2]
    ids, weights = ids_t_ref[...].T, weight_t_ref[...].T
    named = iota((rows, experts), 1) ^ me[0]
    first, second = ids[:, 0:1] == named, ids[:, 1:2] == named
    weight = jnp.where(first, weights[:, 0:1], jnp.where(second, weights[:, 1:2], 0.0))
    hit = (first | second).astype(F32)
    before = (iota((rows, rows), 0) > iota((rows, rows), 1)).astype(F32)
    rank = dot(before, hit)
    lanes = 2 * experts * 8
    shape = (experts, lanes)
    spread = ((iota(shape, 1) // 8) % experts == iota(shape, 0)).astype(F32)
    weight = dot(weight, spread, PRECISE)
    rank = dot(rank, spread, PRECISE).astype(jnp.int32)
    lane = iota((rows, lanes), 1)
    main = (lane < experts * 8) & (rank == lane % 8)
    extra = (lane >= experts * 8) & (rank == 8)

    def rows_of(k):
        data = []
        for g in range(groups):
            data.append(firsts[g][k].astype(F32)[0:8])
            data.append(swap_ref[g // 2, k].astype(F32)[g % 2 * 8 : g % 2 * 8 + 8])
        return data

    last = rows_of(pieces)
    for m in range(experts):
        k = me[0] ^ m
        coef = jnp.where(main | (extra & (lane % 8 == k)), weight, 0.0)
        high = coef.astype(BF16)
        low = (coef - high.astype(F32)).astype(BF16)
        data = jnp.concatenate(rows_of(k) + last, axis=0).astype(BF16)
        stream = streams[m // 2][m % 2].astype(F32)
        out_ref[:, pl.ds(pl.multiple_of(k * tile, 128), tile)] = (
            stream + (dot(high, data) + dot(low, data))
        ).astype(BF16)


def on_square(
    x_in,
    z_gate,
    b_in,
    c_out,
    dt_step,
    rate,
    skip,
    init_state,
    residual,
    norm_gain,
    expert_ids,
    gate_weights,
    w_gate,
    w_up,
    w_down,
):
    tokens, channels = x_in.shape
    heads = rate.shape[0]
    state = b_in.shape[1]
    owners = lax.axis_size("exp")
    rows, features = residual.shape
    experts = owners
    cap = max(2, 2 * rows // experts + 1)
    slots = owners * cap
    at = lax.axis_index("seq")
    me = lax.axis_index("exp")
    place = jnp.reshape(at, (1,)).astype(jnp.int32)
    self_id = jnp.reshape(me, (1,)).astype(jnp.int32)

    def over_x(v):
        return lax.ppermute(v, "seq", [(i, i ^ 1) for i in range(4)])

    def over_y(v):
        return lax.ppermute(v, "seq", [(i, i ^ 2) for i in range(4)])

    def along(v, mask):
        return lax.ppermute(v, "exp", [(i, i ^ mask) for i in range(owners)])

    rate_row = rate[None, :]
    dt_t = dt_step.T
    ids_t = expert_ids.T
    packed = block_call(
        pack_kernel,
        [jax.ShapeDtypeStruct((owners, rows, channels + 128), BF16)],
        0,
        (ids_t, residual),
        held=2,
        limit=48,
    )[0]
    packed = lax.all_to_all(packed, "exp", split_axis=0, concat_axis=0, tiled=True)
    payload, init_t = block_call(
        state_kernel,
        [
            jax.ShapeDtypeStruct((state + 16, channels), BF16),
            jax.ShapeDtypeStruct((state, channels), BF16),
        ],
        1,
        (place, x_in, b_in, dt_t, rate_row, init_state.reshape(channels, state)),
        held=5,
        limit=62,
    )
    pair = over_x(payload)
    own_part, fade, token = block_call(
        intra_kernel,
        [
            jax.ShapeDtypeStruct((tokens, channels), F32),
            jax.ShapeDtypeStruct((tokens, channels), F32),
            jax.ShapeDtypeStruct((8, 128), F32),
        ],
        0,
        (x_in, z_gate, b_in, c_out, dt_t, rate_row, skip[None, :]),
        held=7,
        limit=61,
    )
    joined = block_call(
        join_kernel,
        [jax.ShapeDtypeStruct((state, channels), BF16)],
        1,
        (place, payload, pair),
        after=(token,),
    )[0]
    early = over_y(joined)
    handed = (own_part, fade, c_out, init_t)
    select, own_part, fade, c, init_t = block_call(
        functools.partial(place_kernel, cap, experts),
        [jax.ShapeDtypeStruct((experts, rows + slots, tokens), BF16)]
        + [jax.ShapeDtypeStruct(v.shape, v.dtype) for v in handed],
        1,
        (self_id, packed, *handed),
        after=(joined,),
    )
    groups = owners // 2
    lanes = jax.ShapeDtypeStruct((groups, rows + slots, channels), BF16)
    same, other = block_call(
        stream_kernel,
        [lanes, lanes],
        1,
        (place, c, own_part, fade, init_t, pair, early, packed, select),
    )

    gain = norm_gain.reshape(owners, 1, channels)
    wg = w_gate.reshape(owners, channels, w_gate.shape[2])
    wu = w_up.reshape(owners, channels, w_up.shape[2])
    expert_rows = jax.ShapeDtypeStruct((2, slots, channels), BF16)
    stream_rows = jax.ShapeDtypeStruct((2, rows, channels), BF16)
    both_rows = jax.ShapeDtypeStruct((2, rows + slots, channels), BF16)
    stream0, first, stream1, near, far, stream3, farthest = block_call(
        pair_kernel,
        [stream_rows, expert_rows, stream_rows, expert_rows, both_rows, stream_rows, expert_rows],
        0,
        (same, along(other, 1)),
    )
    gain = norm_gain.reshape(owners, 1, channels)
    wg = w_gate.reshape(owners, channels, w_gate.shape[2])
    wu = w_up.reshape(owners, channels, w_up.shape[2])
    gain = norm_gain.reshape(owners, 1, channels)
    wg = w_gate.reshape(owners, channels, w_gate.shape[2])
    wu = w_up.reshape(owners, channels, w_up.shape[2])

    def hold(values, after, name):
        outs = [jax.ShapeDtypeStruct(v.shape, BF16) for v in values]
        return block_call(hold_kernel, outs, 0, values, after=after, name=name)

    def project(group, near, far, carry, after=()):
        last = group == groups - 1
        return up_project(group, last, self_id, near, far, gain, wg, wu, carry, after)

    def message(count):
        return [jax.ShapeDtypeStruct((count, slots, channels), BF16)] * 2

    near, far = along(near, 2), along(far, 4)
    rx0, ry0 = over_x(first), over_y(first)
    to_x, to_y = block_call(half_message_kernel, message(1), 0, (rx0, ry0), name="half_0")
    fx0, fy0 = over_x(to_x), over_y(to_y)
    near, stream1 = hold((near, stream1), (to_x,), "hold_near")
    rx1, ry1 = over_x(near), over_y(near)
    stream1 = along(stream1, 2)
    farthest_held = hold((farthest,), (far,), "hold_farthest")[0]
    farthest = along(farthest_held, 6)
    to_x, to_y, far, stream2 = block_call(
        join_message_kernel,
        message(3) + [expert_rows, stream_rows],
        0,
        (far, rx1, ry1),
        after=(fx0, fy0, farthest_held, stream1),
        name="join_2",
    )
    rx2, ry2 = over_x(to_x), over_y(to_y)
    carry = project(0, [(first, 0), (rx0, 0), (ry0, 0)], [(fy0, 0), (fx0, 0)], None)
    to_x, to_y = block_call(
        join_message_kernel, message(3), 0, (farthest, rx2, ry2), after=(carry[2],), name="join_3"
    )
    rx3, ry3 = over_x(to_x), over_y(to_y)
    held = hold((stream3,), (to_x,), "hold_stream")[0]
    stream3 = along(held, 6)
    carry = project(1, [(near, 0), (rx1, 0), (ry1, 0)], [(ry2, 2), (rx2, 2)], carry, (held,))
    to_x, to_y = block_call(
        half_message_kernel, message(1), 0, (rx3, ry3), after=(carry[2], stream3), name="half_3"
    )
    fx3, fy3 = over_x(to_x), over_y(to_y)
    carry = project(2, [(far, 0), (rx2, 0), (ry2, 0)], [(ry3, 2), (rx3, 2)], carry)
    active_far, active = project(
        3, [(farthest, 0), (rx3, 0), (ry3, 0)], [(fy3, 0), (fx3, 0)], carry
    )

    wd = w_down.reshape(w_down.shape[1], features)
    tiles = jax.ShapeDtypeStruct((9, 16, features // 8), BF16)
    sent = down_project("down_through", groups, active_far, wd)
    rest = down_project("down_rest", groups, active, wd)
    own, own_x, own_y = ([rest[3 * g + k] for g in range(groups)] for k in range(3))

    def relay(name, through_x, through_y, low, ahead=(), after=()):
        shares = (own_x[low], own_y[low], own_x[low + 1], own_y[low + 1])
        return block_call(
            relay_kernel,
            [tiles] * (4 + len(ahead)),
            0,
            (through_x, through_y, *shares, *ahead),
            after=after,
            name=name,
        )

    def finish(group, rx, ry, ahead=(), after=()):
        return block_call(
            finish_kernel,
            [tiles] * (1 + len(ahead)),
            0,
            (own[group], rx, ry, *ahead),
            after=after,
            name=f"finish_{group}",
        )

    through_x, through_y = over_x(sent[2]), over_y(sent[3])
    x2, y2, x3, y3, next_x, next_y = relay(
        "relay_far", through_x, through_y, 2, (sent[0], sent[1])
    )
    rx3, ry3 = over_x(x3), over_y(y3)
    through_x, through_y = over_x(next_x), over_y(next_y)
    both3, x2, y2 = finish(3, rx3, ry3, (x2, y2))
    back3 = along(both3, 6)
    rx2, ry2 = over_x(x2), over_y(y2)
    x0, y0, x1, y1 = relay("relay_near", through_x, through_y, 0, after=(both3,))
    rx1, ry1 = over_x(x1), over_y(y1)
    both2, x0, y0 = finish(2, rx2, ry2, (x0, y0))
    back2 = along(both2, 4)
    rx0, ry0 = over_x(x0), over_y(y0)
    back1 = along(finish(1, rx1, ry1, after=(back3,))[0], 2)
    back = [finish(0, rx0, ry0)[0], back1, back2, back3]
    swap = block_call(second_kernel, [jax.ShapeDtypeStruct((2,) + tiles.shape, BF16)], 0, back)[0]
    swap = along(swap, 1)
    return block_call(
        mix_kernel,
        [jax.ShapeDtypeStruct((rows, features), BF16)],
        1,
        (self_id, ids_t, gate_weights.T, swap, *back, stream0, stream1, stream2, stream3),
    )[0]


def entering_2(array, axis, combine, identity):
    devices, mine = (lax.axis_size(axis), lax.axis_index(axis))
    everything = jax.tree.map(
        lambda part, kind: lax.all_gather(part.astype(kind), axis),
        array,
        (jnp.bfloat16, jnp.bfloat16),
    )
    start = jax.tree.map(
        lambda part, zero: jnp.broadcast_to(jnp.asarray(zero, part.dtype), part.shape),
        array,
        identity,
    )

    def hop(k, before):
        reached = k < mine
        new = combine(
            before, jax.tree.map(lambda part, own: part[k].astype(own.dtype), everything, array)
        )
        return jax.tree.map(lambda a, b: jnp.where(reached, a, b), new, before)

    return lax.fori_loop(0, devices, hop, start)


def chain_combine(earlier, later):
    return (earlier[0] + later[0], jnp.exp(later[0])[:, None, None] * earlier[1] + later[1])


def on_device(
    x_in,
    z_gate,
    b_in,
    c_out,
    dt_step,
    rate,
    skip,
    init_state,
    residual,
    norm_gain,
    expert_ids,
    gate_weights,
    w_gate,
    w_up,
    w_down,
):
    token_count, channels = x_in.shape
    heads_here = rate.shape[0]
    head_width = channels // heads_here
    state_width = b_in.shape[1]
    blocks = token_count // GROUP
    inputs = x_in.astype(jnp.float32).reshape(blocks, GROUP, heads_here, head_width)
    keys_in = b_in.astype(jnp.float32).reshape(blocks, GROUP, state_width)
    queries = c_out.astype(jnp.float32).reshape(blocks, GROUP, state_width)
    log_steps = (-rate[None, :] * dt_step).reshape(blocks, GROUP, heads_here)
    cumulative = jnp.cumsum(log_steps, axis=1)
    scores = jnp.einsum("ctn,csn->cts", queries, keys_in, precision=PRECISE)
    causal = jnp.arange(GROUP)[:, None] >= jnp.arange(GROUP)[None, :]
    spread = cumulative[:, :, None, :] - cumulative[:, None, :, :]
    weights = jnp.exp(jnp.where(causal[None, :, :, None], spread, -jnp.inf)) * scores[..., None]
    intra_out = jnp.einsum("ctsh,cshp->cthp", weights, inputs, precision=PRECISE)
    tail_decay = jnp.exp(cumulative[:, -1:, :] - cumulative)
    block_state = jnp.einsum("csh,cshp,csn->chpn", tail_decay, inputs, keys_in, precision=PRECISE)
    block_log = cumulative[:, -1, :]

    def advance(carried, element):
        total_log, total_state = carried
        step_log, step_state = element
        updated = (
            total_log + step_log,
            jnp.exp(step_log)[:, None, None] * total_state + step_state,
        )
        return (updated, (total_log, total_state))

    zero_state = jnp.zeros((heads_here, head_width, state_width), jnp.float32)
    zero_log = jnp.zeros((heads_here,), jnp.float32)
    (device_log, device_state), (enter_log, enter_state) = lax.scan(
        advance, (zero_log, zero_state), (block_log, block_state)
    )
    prior_log, prior_state = entering_2(
        (device_log, device_state), "seq", chain_combine, (zero_log, zero_state)
    )
    incoming = prior_state + jnp.exp(prior_log)[:, None, None] * init_state
    entering = enter_state + jnp.exp(enter_log)[:, :, None, None] * incoming[None]
    inter_out = jnp.exp(cumulative)[..., None] * jnp.einsum(
        "chpn,ctn->cthp", entering, queries, precision=PRECISE
    )
    mixed_out = (intra_out + inter_out + skip[None, None, :, None] * inputs).reshape(
        token_count, channels
    )
    mixer = (mixed_out * jax.nn.silu(z_gate.astype(jnp.float32))).astype(jnp.bfloat16)
    token_mix = lax.all_to_all(mixer, "exp", split_axis=0, concat_axis=1, tiled=True)
    stream = (residual.astype(jnp.float32) + token_mix.astype(jnp.float32)).astype(jnp.bfloat16)
    widened = stream.astype(jnp.float32)
    normed = (
        widened
        * lax.rsqrt(jnp.mean(widened * widened, axis=-1, keepdims=True) + 1e-06)
        * norm_gain[None, :]
    ).astype(jnp.bfloat16)
    rows_here = residual.shape[0]
    owners = lax.axis_size("exp")
    local_experts = w_gate.shape[0]
    experts = owners * local_experts
    capacity = max(2, 2 * rows_here // experts + 1)
    width = residual.shape[1]
    chosen = expert_ids.reshape(-1)
    onehot = (chosen[:, None] == jnp.arange(experts)[None, :]).astype(jnp.int32)
    slot_index = jnp.sum((jnp.cumsum(onehot, axis=0) - onehot) * onehot, axis=1)
    target = chosen * capacity + slot_index
    placing = (target[None, :] == jnp.arange(experts * capacity)[:, None]).astype(jnp.bfloat16)
    pair_rows = jnp.repeat(normed, 2, axis=0)
    outgoing = jnp.dot(placing, pair_rows, preferred_element_type=jnp.float32).astype(jnp.bfloat16)
    outgoing = outgoing.reshape(owners, local_experts, 1, capacity, width)
    arrived = lax.all_to_all(outgoing, "exp", split_axis=0, concat_axis=2, tiled=True)
    segment = lax.all_gather(arrived, "seq", axis=1, tiled=True)
    flattened = segment.reshape(segment.shape[0], -1, segment.shape[-1])
    gate_proj = jnp.einsum("erd,edf->erf", flattened, w_gate, preferred_element_type=jnp.float32)
    up_proj = jnp.einsum("erd,edf->erf", flattened, w_up, preferred_element_type=jnp.float32)
    active = (jax.nn.silu(gate_proj) * up_proj).astype(jnp.bfloat16)
    partial_value = jnp.einsum("erf,efd->erd", active, w_down, preferred_element_type=jnp.float32)
    partials = partial_value.reshape(segment.shape[:-1] + (partial_value.shape[-1],))
    summed = lax.psum_scatter(partials.astype(jnp.bfloat16), "seq", scatter_dimension=1, tiled=True)
    returned = lax.all_to_all(summed, "exp", split_axis=2, concat_axis=0, tiled=True)
    results = returned.reshape(experts * capacity, width)
    picked = results[target].astype(jnp.float32).reshape(rows_here, 2, width)
    mixture = jnp.sum(picked * gate_weights[:, :, None], axis=1)
    return (widened + mixture).astype(jnp.bfloat16)


def solution(mesh):
    square = mesh.shape["seq"] == 4 and mesh.shape["exp"] == 8

    def body(*args):
        rows = args[8].shape[0]
        experts = mesh.shape["exp"] * args[12].shape[0]
        fits = args[12].shape[0] == 1 and 2 * rows // experts + 1 == 9
        return (on_square if square and fits else on_device)(*args)

    return jax.shard_map(
        body,
        mesh=mesh,
        in_specs=(
            P("seq", "exp"),
            P("seq", "exp"),
            P("seq", None),
            P("seq", None),
            P("seq", "exp"),
            P("exp"),
            P("exp"),
            P("exp", None, None),
            P(("seq", "exp"), None),
            P(),
            P(("seq", "exp"), None),
            P(("seq", "exp"), None),
            P("exp", None, "seq"),
            P("exp", None, "seq"),
            P("exp", "seq", None),
        ),
        out_specs=P(("seq", "exp"), None),
        check_vma=False,
    )
```

```python
import functools

import jax
import jax.numpy as jnp
from jax import lax
from jax.experimental import pallas as pl
from jax.experimental.pallas import tpu as pltpu
from jax.sharding import PartitionSpec as P

GROUP = 128
PRECISE = lax.Precision.HIGHEST
F32 = jnp.float32
BF16 = jnp.bfloat16
MIB = 1 << 20
NO_COST = pl.CostEstimate(flops=0, bytes_accessed=0, transcendentals=0)


def block_call(body, outs, scalars, args, held=0, keep=0, after=(), limit=16, out_blocks=False, name=None):
    n_args = len(args)
    kept = [jax.ShapeDtypeStruct(v.shape, v.dtype) for v in args[scalars : scalars + held]]

    def kernel(*refs):
        refs, sems = (refs[:-1], refs[-1]) if held else (refs, None)
        inputs, refs = refs[:n_args], refs[n_args + len(after) :]
        results, refs = refs[: len(outs)], refs[len(outs) :]
        copies = [
            pltpu.make_async_copy(src, dst, sems.at[k])
            for k, (src, dst) in enumerate(zip(inputs[scalars : scalars + held], refs))
        ]
        for copy in copies:
            copy.start()
        for copy in copies:
            copy.wait()
        body(*inputs[:scalars], *refs, *inputs[scalars + held :], *results)

    scratch = [pltpu.VMEM(v.shape, v.dtype) for v in kept[keep:]]
    if held:
        scratch.append(pltpu.SemaphoreType.DMA((held,)))
    return pl.pallas_call(
        kernel,
        name=name or getattr(body, "func", body).__name__,
        out_shape=list(outs) + kept[:keep],
        in_specs=[pl.BlockSpec(memory_space=pltpu.SMEM)] * scalars
        + [pl.BlockSpec(memory_space=pltpu.HBM)] * held
        + [pl.BlockSpec(memory_space=pltpu.VMEM)] * (n_args - scalars - held)
        + [pl.BlockSpec(memory_space=pl.ANY)] * len(after),
        out_specs=[pl.BlockSpec() if out_blocks else pl.BlockSpec(memory_space=pltpu.VMEM)]
        * (len(outs) + keep),
        scratch_shapes=scratch,
        compiler_params=pltpu.CompilerParams(vmem_limit_bytes=limit * MIB),
        cost_estimate=NO_COST,
    )(*args, *after)


def iota(shape, dim):
    return lax.broadcasted_iota(jnp.int32, shape, dim)


def dot(a, b, precision=None):
    return jnp.dot(a, b, precision=precision, preferred_element_type=F32)


def head_spread(heads, channels):
    shape = (heads, channels)
    return (iota(shape, 1) // (channels // heads) == iota(shape, 0)).astype(F32)


def running_logs(dt_t_ref, rate_ref):
    logs = -rate_ref[...] * dt_t_ref[...].T
    tokens = logs.shape[0]
    tri = (iota((tokens, tokens), 0) >= iota((tokens, tokens), 1)).astype(F32)
    return dot(tri, logs, PRECISE)


def pack_kernel(ids_t_ref, residual_ref, out_ref):
    parts, rows, wide = out_ref.shape
    part = wide - 128
    ids = ids_t_ref[...].astype(F32).T
    lane = iota((rows, 128), 1)
    named = jnp.where(lane == 0, ids[:, 0:1], jnp.where(lane == 1, ids[:, 1:2], 0.0)).astype(BF16)
    for k in range(parts):
        out_ref[k, :, 0:part] = residual_ref[:, k * part : (k + 1) * part]
        out_ref[k, :, part:wide] = named


def state_kernel(place, x_ref, b_ref, dt_t_ref, rate_ref, init_ref, payload_ref, init_t_ref):
    tokens, channels = x_ref.shape
    heads = dt_t_ref.shape[0]
    width = b_ref.shape[1]
    cum = running_logs(dt_t_ref, rate_ref)
    total = cum[tokens - 1 : tokens, :]
    spread = head_spread(heads, channels)
    tail = dot(jnp.exp(total - cum), spread, PRECISE)
    scaled = (x_ref[...].astype(F32) * tail).astype(BF16)
    keys = b_ref[...].astype(F32).T.astype(BF16)
    own = dot(keys, scaled)
    decay = dot(jnp.broadcast_to(jnp.exp(total), (8, heads)), spread, PRECISE)
    init_t = init_ref[...].T
    init_t_ref[...] = init_t.astype(BF16)
    first = (place[0] == 0).astype(F32)
    payload_ref[0:width, :] = (own + first * (decay[0:1, :] * init_t)).astype(BF16)
    high = decay.astype(BF16).astype(F32)
    rows = iota((16, channels), 0)
    high16 = jnp.broadcast_to(high[0:1, :], (16, channels))
    low16 = jnp.broadcast_to(decay[0:1, :], (16, channels)) - high16
    payload_ref[width : width + 16, :] = jnp.where(
        rows == 0, high16, jnp.where(rows == 1, low16, 0.0)
    ).astype(BF16)


def intra_kernel(x_ref, z_ref, b_ref, c_ref, dt_t_ref, rate_ref, skip_ref, own_ref, fade_ref, token_ref):
    tokens, channels = x_ref.shape
    heads = dt_t_ref.shape[0]
    width = channels // heads
    token_ref[...] = jnp.zeros_like(token_ref)
    shape = (tokens, tokens)
    causal = iota(shape, 0) >= iota(shape, 1)
    cum = running_logs(dt_t_ref, rate_ref)
    cum_t = cum.T
    scores = lax.dot_general(
        c_ref[...], b_ref[...], (((1,), (1,)), ((), ())), preferred_element_type=F32
    )
    spread = head_spread(heads, channels)
    direct = dot(jnp.broadcast_to(skip_ref[...], (8, heads)), spread, PRECISE)[0:1, :]
    fade = dot(jnp.exp(cum), spread, PRECISE)
    per = 128 // width
    lane_head = iota((tokens, 128), 1) // width
    for group in range(heads // per):
        cols = slice(group * 128, (group + 1) * 128)
        x = x_ref[:, cols]
        total = x.astype(F32) * direct[:, cols]
        for k in range(per):
            h = group * per + k
            gap = jnp.where(causal, cum[:, h : h + 1] - cum_t[h : h + 1, :], -1e30)
            weights = (jnp.exp(gap) * scores).astype(BF16)
            part = dot(weights, x)
            total = total + jnp.where(lane_head == k, part, 0.0)
        z = z_ref[:, cols].astype(F32)
        gate = z / (1.0 + jnp.exp(-z))
        own_ref[:, cols] = total * gate
        fade_ref[:, cols] = fade[:, cols] * gate


def place_kernel(cap, experts, me, packed_ref, *refs):
    count = (len(refs) - 1) // 2
    out_ref = refs[count]
    for source, target in zip(refs[:count], refs[count + 1 :]):
        target[...] = source[...]
    blocks, rows, wide = packed_ref.shape
    tokens = blocks * rows
    slots = out_ref.shape[1] - rows
    ids = packed_ref[:, :, wide - 128 : wide].astype(F32).reshape(tokens, 128).T
    ids = ids[0:8, :].astype(jnp.int32)
    shape = (tokens, tokens)
    before = (iota(shape, 0) < iota(shape, 1)) & (iota(shape, 0) // rows == iota(shape, 1) // rows)
    named = iota((experts, tokens), 0) ^ me[0]
    hit = (ids[0:1, :] == named) | (ids[1:2, :] == named)
    rank = dot(hit.astype(BF16), before.astype(BF16)).astype(jnp.int32)
    block = (iota((experts, tokens), 1) // rows) ^ named
    whole = cap - 1
    row = jnp.where(rank < whole, block * whole + rank, blocks * whole + block)
    row = jnp.where(hit, row, -1)
    shape = (rows + slots, tokens)
    for e in range(experts):
        owned = ((me[0] ^ e) * rows + iota(shape, 0) == iota(shape, 1)) & (iota(shape, 0) < rows)
        placed = (iota(shape, 0) - rows == row[e : e + 1, :]) & (iota(shape, 0) >= rows)
        out_ref[e] = (owned | placed).astype(F32).astype(BF16)


def join_kernel(place, own_ref, other_ref, out_ref):
    width = out_ref.shape[0]
    odd = place[0] % 2 == 1
    own, other = own_ref[0:width, :].astype(F32), other_ref[0:width, :].astype(F32)
    own_decay = own_ref[width : width + 16, :].astype(F32)
    other_decay = other_ref[width : width + 16, :].astype(F32)
    own_decay = own_decay[0:1, :] + own_decay[1:2, :]
    other_decay = other_decay[0:1, :] + other_decay[1:2, :]
    early = jnp.where(odd, other, own)
    late = jnp.where(odd, own, other)
    decay = jnp.where(odd, own_decay, other_decay)
    out_ref[...] = (decay * early + late).astype(BF16)


def stream_kernel(
    place, c_ref, own_ref, fade_ref, init_t_ref, pair_ref, early_ref, res_ref, sel_ref, near_a_ref, near_b_ref, same_ref, other_ref
):
    width = init_t_ref.shape[0]
    at = place[0]
    zero = (at == 0).astype(F32)
    odd = (at % 2 == 1).astype(F32)
    pair = pair_ref[...].astype(F32)
    decay = pair[width : width + 1, :] + pair[width + 1 : width + 2, :]
    factor = jnp.where(at >= 2, jnp.where(at % 2 == 1, decay, 1.0), 0.0)
    entering = zero * init_t_ref[...].astype(F32) + odd * pair[0:width, :] + factor * early_ref[...].astype(F32)
    mixed = own_ref[...] + fade_ref[...] * dot(c_ref[...], entering.astype(BF16))
    mixer = mixed.astype(BF16).astype(F32)
    tokens, channels = mixer.shape
    residual = res_ref[:, :, 0:channels].astype(F32).reshape(tokens, channels)
    stream = (residual + mixer).astype(BF16)
    near_a_ref[...] = dot(sel_ref[2], stream).astype(BF16)
    near_b_ref[...] = dot(sel_ref[3], stream).astype(BF16)
    for at, k in enumerate((0, 2, 3)):
        same_ref[at] = dot(sel_ref[2 * k], stream).astype(BF16)
        other_ref[at] = dot(sel_ref[2 * k + 1], stream).astype(BF16)


def up_kernel(first, features, after, me, *refs):
    own, rx, ry, even, odd, gain, wg, wu = refs[:8]
    carry = () if first else refs[8:11]
    rest = refs[(8 if first else 11) + after :]
    sums = rest[2:5] if features else rest
    step = pl.program_id(0)
    steps = pl.num_programs(0)

    if first or features:

        @pl.when(step == 0)
        def _():
            for i, acc in enumerate(sums):
                acc[...] = jnp.zeros_like(acc) if first else carry[i][...]

    gate, up, square = sums
    slots = own.shape[1]
    rows = [r[0].astype(F32) for r in (own, rx, ry)]
    rows.append(jnp.where(step == 0, even[0].astype(F32), odd[0].astype(F32)))
    rows = jnp.concatenate(rows, axis=0)
    square[...] += jnp.broadcast_to(jnp.sum(rows * rows, axis=1, keepdims=True), square.shape)
    scaled = (rows * gain[0]).astype(BF16)
    gate[...] += dot(scaled, wg[0])
    up[...] += dot(scaled, wu[0])

    if features:
        outs, stages = rest[:2], rest[5:]

        @pl.when(step == steps - 1)
        def _():
            inverse = lax.rsqrt(square[:, 0:1] * (1.0 / features) + 1e-06)
            g = gate[...] * inverse
            active = g / (1.0 + jnp.exp(-g)) * (up[...] * inverse)
            main, ninths = slots // 9 * 8, slots // 9
            for d in range(4):
                at = d * slots
                stage, d, shards = (stages[0], 0, 1) if d == 3 else (stages[1], d, 3)
                stage[d * main : (d + 1) * main, :] = active[at : at + main]
                low = shards * main + d * ninths
                stage[low : low + ninths, :] = active[at + main : at + slots]
            for out, stage in zip(outs, stages):
                out[...] = stage[...].astype(BF16)


def up_project(group, last, me, near, far, gain, w_gate, w_up, carry, after=()):
    slots, part = near[0][0].shape[1:]
    hidden = w_gate.shape[2]
    total = 4 * slots
    source = lambda i, me: me[0] ^ (2 * group + i)
    rows = [
        pl.BlockSpec((1, slots, part), lambda i, me, start=start: (start + i, 0, 0))
        for _, start in near
    ] + [
        pl.BlockSpec((1, slots, part), lambda i, me, start=start: (start, 0, 0)) for _, start in far
    ]
    weight = pl.BlockSpec((1, part, hidden), lambda i, me: (source(i, me), 0, 0))
    in_place = pl.BlockSpec(memory_space=pltpu.VMEM)
    specs = rows + [pl.BlockSpec((1, 1, part), lambda i, me: (source(i, me), 0, 0)), weight, weight]
    sums = [
        jax.ShapeDtypeStruct((total, hidden), F32),
        jax.ShapeDtypeStruct((total, hidden), F32),
        jax.ShapeDtypeStruct((total, 128), F32),
    ]
    aliases = {}
    if carry is not None:
        specs += [in_place] * 3
        if not last:
            aliases = {9 + i: i for i in range(3)}
    specs += [pl.BlockSpec(memory_space=pl.ANY)] * len(after)
    sizes = (slots, 3 * slots)
    outs = [jax.ShapeDtypeStruct((n, hidden), BF16) for n in sizes] if last else sums
    scratch = [pltpu.VMEM(s.shape, s.dtype) for s in sums]
    scratch += [pltpu.VMEM((n, hidden), F32) for n in sizes]
    features = gain.shape[0] * part if last else 0
    return pl.pallas_call(
        functools.partial(up_kernel, carry is None, features, len(after)),
        name=f"up_{group}",
        out_shape=outs,
        grid_spec=pltpu.PrefetchScalarGridSpec(
            num_scalar_prefetch=1,
            grid=(2,),
            in_specs=specs,
            out_specs=[in_place] * len(outs),
            scratch_shapes=scratch if last else [],
        ),
        input_output_aliases=aliases,
        compiler_params=pltpu.CompilerParams(vmem_limit_bytes=48 * MIB),
        cost_estimate=NO_COST,
    )(me, *(array for array, _ in near + far), gain, w_gate, w_up, *(carry or ()), *after)


def cut_of(group):
    return 5 if group % 2 else 4


def down_kernel(groups, act_ref, w_ref, *refs):
    outs, (spare, held, sems) = refs[:-3], refs[-3:]
    step = pl.program_id(0)
    steps, _, tile = held.shape

    def load(k):
        columns = pl.ds(pl.multiple_of(k * tile, tile), tile)
        return pltpu.make_async_copy(w_ref.at[:, columns], held.at[k], sems.at[k])

    @pl.when(step == 0)
    def _():
        for k in range(steps):
            load(k).start()

    load(step).wait()
    part = dot(act_ref[...], held[step])
    ninths = part.shape[0] // 9
    main = part.shape[0] - ninths
    shards = ninths // (2 * groups)

    def through(group, tile):
        to_x, to_y = outs[2 * (group // 2) : 2 * (group // 2) + 2]
        cut = cut_of(group)
        return to_x, tile + (0 if group % 2 else 5), to_y, tile - cut + (0 if group % 2 else 4)

    for shard in range(shards):
        for group in range(groups):
            at = (shard * groups + group) * 16
            rows = part[at : at + 16, :].astype(BF16)
            if shards > 1:
                outs[shards * group + shard][step] = rows
                continue
            to_x, place_x, to_y, place_y = through(group, step)

            @pl.when(step < cut_of(group))
            def _():
                to_x[place_x] = rows

            @pl.when(step >= cut_of(group))
            def _():
                to_y[place_y] = rows

    for lanes in range(spare.shape[0]):
        spare[lanes, pl.ds(pl.multiple_of(step * ninths, 8), ninths), :] = part[
            main:, lanes * 128 : (lanes + 1) * 128
        ]

    @pl.when(step == steps - 1)
    def _():
        for shard in range(shards):
            for group in range(groups):
                pair = []
                for side in range(2):
                    row = pl.ds((shard * groups + group) * 2 + side, 8, stride=ninths)
                    ninth = [spare[lanes, row, :] for lanes in range(spare.shape[0])]
                    pair.append(jnp.concatenate(ninth, axis=1))
                pair = jnp.concatenate(pair, axis=0).astype(BF16)
                if shards > 1:
                    outs[shards * group + shard][8] = pair
                else:
                    _, _, to_y, place_y = through(group, 8)
                    to_y[place_y] = pair


def down_project(name, groups, active, w_down):
    total, hidden = active.shape
    features = w_down.shape[1]
    tile = features // 8
    outs = [jax.ShapeDtypeStruct((9, 16, tile), BF16)] * (total // 18)
    return pl.pallas_call(
        functools.partial(down_kernel, groups),
        name=name,
        grid=(8,),
        out_shape=outs,
        in_specs=[
            pl.BlockSpec(memory_space=pltpu.VMEM),
            pl.BlockSpec(memory_space=pltpu.HBM),
        ],
        out_specs=[pl.BlockSpec(memory_space=pltpu.VMEM)] * len(outs),
        scratch_shapes=[
            pltpu.VMEM((tile // 128, 8 * total // 9, 128), F32),
            pltpu.VMEM((8, hidden, tile), BF16),
            pltpu.SemaphoreType.DMA((8,)),
        ],
        compiler_params=pltpu.CompilerParams(vmem_limit_bytes=48 * MIB),
        cost_estimate=NO_COST,
    )(active, w_down)


def pair_kernel(same, other, own_stream, own, far, last_stream, last):
    owned = own_stream.shape[1]
    for side, rows in enumerate((same, other)):
        own_stream[side], own[side] = rows[0, 0:owned, :], rows[0, owned:, :]
        far[side] = rows[1]
        last_stream[side], last[side] = rows[2, 0:owned, :], rows[2, owned:, :]


def near_kernel(same, other, stream, rows):
    owned = stream.shape[1]
    for side, came in enumerate((same, other)):
        stream[side], rows[side] = came[0:owned, :], came[owned:, :]


def second_kernel(*refs):
    parts, out = refs[:-1], refs[-1]
    for h in range(out.shape[0]):
        for k in range(out.shape[1]):
            pair = [ref[k].astype(F32)[8:16] for ref in parts[2 * h : 2 * h + 2]]
            out[h, k] = jnp.concatenate(pair, axis=0).astype(BF16)


def hold_kernel(*refs):
    for source, target in zip(refs[: len(refs) // 2], refs[len(refs) // 2 :]):
        target[...] = source[...]


def half_message_kernel(rx, ry, out_x, out_y):
    out_x[0], out_y[0] = ry[1], rx[0]


def join_message_kernel(own, rx, ry, out_x, out_y, *parts):
    owned = own.shape[1] - out_x.shape[1]
    for side in range(2):
        rows = own[side, owned:, :]
        out_x[side], out_y[side] = rows, rows
        if parts:
            parts[0][side], parts[1][side] = rows, own[side, 0:owned, :]
    out_x[2], out_y[2] = ry[1], rx[0]


def relay_kernel(through_x, through_y, *refs):
    ahead = refs[4 : 4 + (len(refs) - 8) // 2]
    outs, copies = refs[4 + len(ahead) :][:4], refs[8 + len(ahead) :]
    for group in range(2):
        cut = cut_of(group)
        at_x, at_y = (0, -cut) if group else (5, 0)
        for own, out, through, tiles, at in (
            (refs[2 * group], outs[2 * group], through_y, range(cut, 9), at_y),
            (refs[2 * group + 1], outs[2 * group + 1], through_x, range(cut), at_x),
        ):
            for k in range(9):
                if k in tiles:
                    out[k] = (own[k].astype(F32) + through[k + at].astype(F32)).astype(BF16)
                else:
                    out[k] = own[k]
    for source, copy in zip(ahead, copies):
        copy[...] = source[...]


def finish_kernel(own, rx, ry, *refs):
    ahead = refs[: (len(refs) - 1) // 2]
    out, copies = refs[len(ahead)], refs[len(ahead) + 1 :]
    for k in range(9):
        out[k] = (own[k].astype(F32) + rx[k].astype(F32) + ry[k].astype(F32)).astype(BF16)
    for source, copy in zip(ahead, copies):
        copy[...] = source[...]


def mix_kernel(me, ids_t_ref, weight_t_ref, swap_ref, *refs):
    groups = (len(refs) - 1) // 2
    firsts, streams, out_ref = refs[:groups], refs[groups:-1], refs[-1]
    rows = ids_t_ref.shape[1]
    experts = 2 * groups
    pieces = firsts[0].shape[0] - 1
    tile = firsts[0].shape[2]
    ids, weights = ids_t_ref[...].T, weight_t_ref[...].T
    named = iota((rows, experts), 1) ^ me[0]
    first, second = ids[:, 0:1] == named, ids[:, 1:2] == named
    weight = jnp.where(first, weights[:, 0:1], jnp.where(second, weights[:, 1:2], 0.0))
    hit = (first | second).astype(F32)
    before = (iota((rows, rows), 0) > iota((rows, rows), 1)).astype(F32)
    rank = dot(before, hit)
    lanes = 2 * experts * 8
    shape = (experts, lanes)
    spread = ((iota(shape, 1) // 8) % experts == iota(shape, 0)).astype(F32)
    weight = dot(weight, spread, PRECISE)
    rank = dot(rank, spread, PRECISE).astype(jnp.int32)
    lane = iota((rows, lanes), 1)
    main = (lane < experts * 8) & (rank == lane % 8)
    extra = (lane >= experts * 8) & (rank == 8)

    def rows_of(k):
        data = []
        for g in range(groups):
            data.append(firsts[g][k].astype(F32)[0:8])
            data.append(swap_ref[g // 2, k].astype(F32)[g % 2 * 8 : g % 2 * 8 + 8])
        return data

    last = rows_of(pieces)
    for m in range(experts):
        k = me[0] ^ m
        coef = jnp.where(main | (extra & (lane % 8 == k)), weight, 0.0)
        high = coef.astype(BF16)
        low = (coef - high.astype(F32)).astype(BF16)
        data = jnp.concatenate(rows_of(k) + last, axis=0).astype(BF16)
        stream = streams[m // 2][m % 2].astype(F32)
        out_ref[:, pl.ds(pl.multiple_of(k * tile, 128), tile)] = (
            stream + (dot(high, data) + dot(low, data))
        ).astype(BF16)


def on_square(
    x_in,
    z_gate,
    b_in,
    c_out,
    dt_step,
    rate,
    skip,
    init_state,
    residual,
    norm_gain,
    expert_ids,
    gate_weights,
    w_gate,
    w_up,
    w_down,
):
    tokens, channels = x_in.shape
    heads = rate.shape[0]
    state = b_in.shape[1]
    owners = lax.axis_size("exp")
    rows, features = residual.shape
    experts = owners
    cap = max(2, 2 * rows // experts + 1)
    slots = owners * cap
    at = lax.axis_index("seq")
    me = lax.axis_index("exp")
    place = jnp.reshape(at, (1,)).astype(jnp.int32)
    self_id = jnp.reshape(me, (1,)).astype(jnp.int32)

    def over_x(v):
        return lax.ppermute(v, "seq", [(i, i ^ 1) for i in range(4)])

    def over_y(v):
        return lax.ppermute(v, "seq", [(i, i ^ 2) for i in range(4)])

    def along(v, mask):
        return lax.ppermute(v, "exp", [(i, i ^ mask) for i in range(owners)])

    rate_row = rate[None, :]
    dt_t = dt_step.T
    ids_t = expert_ids.T
    packed = block_call(
        pack_kernel,
        [jax.ShapeDtypeStruct((owners, rows, channels + 128), BF16)],
        0,
        (ids_t, residual),
        held=2,
        limit=48,
    )[0]
    packed = lax.all_to_all(packed, "exp", split_axis=0, concat_axis=0, tiled=True)
    payload, init_t = block_call(
        state_kernel,
        [
            jax.ShapeDtypeStruct((state + 16, channels), BF16),
            jax.ShapeDtypeStruct((state, channels), BF16),
        ],
        1,
        (place, x_in, b_in, dt_t, rate_row, init_state.reshape(channels, state)),
        held=5,
        limit=62,
    )
    pair = over_x(payload)
    own_part, fade, token = block_call(
        intra_kernel,
        [
            jax.ShapeDtypeStruct((tokens, channels), F32),
            jax.ShapeDtypeStruct((tokens, channels), F32),
            jax.ShapeDtypeStruct((8, 128), F32),
        ],
        0,
        (x_in, z_gate, b_in, c_out, dt_t, rate_row, skip[None, :]),
        held=7,
        limit=61,
    )
    joined = block_call(
        join_kernel,
        [jax.ShapeDtypeStruct((state, channels), BF16)],
        1,
        (place, payload, pair),
        after=(token,),
    )[0]
    early = over_y(joined)
    handed = (own_part, fade, c_out, init_t)
    select, own_part, fade, c, init_t = block_call(
        functools.partial(place_kernel, cap, experts),
        [jax.ShapeDtypeStruct((experts, rows + slots, tokens), BF16)]
        + [jax.ShapeDtypeStruct(v.shape, v.dtype) for v in handed],
        1,
        (self_id, packed, *handed),
        after=(joined,),
    )
    groups = owners // 2
    lanes = jax.ShapeDtypeStruct((groups - 1, rows + slots, channels), BF16)
    one = jax.ShapeDtypeStruct(lanes.shape[1:], BF16)
    near_a, near_b, same, other = block_call(
        stream_kernel,
        [one, one, lanes, lanes],
        1,
        (place, c, own_part, fade, init_t, pair, early, packed, select),
    )

    gain = norm_gain.reshape(owners, 1, channels)
    wg = w_gate.reshape(owners, channels, w_gate.shape[2])
    wu = w_up.reshape(owners, channels, w_up.shape[2])
    expert_rows = jax.ShapeDtypeStruct((2, slots, channels), BF16)
    stream_rows = jax.ShapeDtypeStruct((2, rows, channels), BF16)
    both_rows = jax.ShapeDtypeStruct((2, rows + slots, channels), BF16)
    near_a, near_b = along(near_a, 2), along(near_b, 3)
    stream0, first, far, stream3, farthest = block_call(
        pair_kernel,
        [stream_rows, expert_rows, both_rows, stream_rows, expert_rows],
        0,
        (same, along(other, 1)),
    )
    gain = norm_gain.reshape(owners, 1, channels)
    wg = w_gate.reshape(owners, channels, w_gate.shape[2])
    wu = w_up.reshape(owners, channels, w_up.shape[2])
    gain = norm_gain.reshape(owners, 1, channels)
    wg = w_gate.reshape(owners, channels, w_gate.shape[2])
    wu = w_up.reshape(owners, channels, w_up.shape[2])

    def hold(values, after, name):
        outs = [jax.ShapeDtypeStruct(v.shape, BF16) for v in values]
        return block_call(hold_kernel, outs, 0, values, after=after, name=name)

    def project(group, near, far, carry, after=()):
        last = group == groups - 1
        return up_project(group, last, self_id, near, far, gain, wg, wu, carry, after)

    def message(count):
        return [jax.ShapeDtypeStruct((count, slots, channels), BF16)] * 2

    far = along(far, 4)
    rx0, ry0 = over_x(first), over_y(first)
    stream1, near = block_call(near_kernel, [stream_rows, expert_rows], 0, (near_a, near_b))
    rx1, ry1 = over_x(near), over_y(near)
    to_x, to_y = block_call(
        half_message_kernel, message(1), 0, (rx0, ry0), after=(near,), name="half_0"
    )
    fx0, fy0 = over_x(to_x), over_y(to_y)
    farthest_held = hold((farthest,), (far,), "hold_farthest")[0]
    farthest = along(farthest_held, 6)
    to_x, to_y, far, stream2 = block_call(
        join_message_kernel,
        message(3) + [expert_rows, stream_rows],
        0,
        (far, rx1, ry1),
        after=(fx0, fy0, farthest_held),
        name="join_2",
    )
    rx2, ry2 = over_x(to_x), over_y(to_y)
    carry = project(0, [(first, 0), (rx0, 0), (ry0, 0)], [(fy0, 0), (fx0, 0)], None)
    to_x, to_y = block_call(
        join_message_kernel, message(3), 0, (farthest, rx2, ry2), after=(carry[2],), name="join_3"
    )
    rx3, ry3 = over_x(to_x), over_y(to_y)
    held = hold((stream3,), (to_x,), "hold_stream")[0]
    stream3 = along(held, 6)
    carry = project(1, [(near, 0), (rx1, 0), (ry1, 0)], [(ry2, 2), (rx2, 2)], carry, (held,))
    to_x, to_y = block_call(
        half_message_kernel, message(1), 0, (rx3, ry3), after=(carry[2], stream3), name="half_3"
    )
    fx3, fy3 = over_x(to_x), over_y(to_y)
    carry = project(2, [(far, 0), (rx2, 0), (ry2, 0)], [(ry3, 2), (rx3, 2)], carry)
    active_far, active = project(
        3, [(farthest, 0), (rx3, 0), (ry3, 0)], [(fy3, 0), (fx3, 0)], carry
    )

    wd = w_down.reshape(w_down.shape[1], features)
    tiles = jax.ShapeDtypeStruct((9, 16, features // 8), BF16)
    sent = down_project("down_through", groups, active_far, wd)
    rest = down_project("down_rest", groups, active, wd)
    own, own_x, own_y = ([rest[3 * g + k] for g in range(groups)] for k in range(3))

    def relay(name, through_x, through_y, low, ahead=(), after=()):
        shares = (own_x[low], own_y[low], own_x[low + 1], own_y[low + 1])
        return block_call(
            relay_kernel,
            [tiles] * (4 + len(ahead)),
            0,
            (through_x, through_y, *shares, *ahead),
            after=after,
            name=name,
        )

    def finish(group, rx, ry, ahead=(), after=()):
        return block_call(
            finish_kernel,
            [tiles] * (1 + len(ahead)),
            0,
            (own[group], rx, ry, *ahead),
            after=after,
            name=f"finish_{group}",
        )

    through_x, through_y = over_x(sent[2]), over_y(sent[3])
    x2, y2, x3, y3, next_x, next_y = relay(
        "relay_far", through_x, through_y, 2, (sent[0], sent[1])
    )
    rx3, ry3 = over_x(x3), over_y(y3)
    through_x, through_y = over_x(next_x), over_y(next_y)
    both3, x2, y2 = finish(3, rx3, ry3, (x2, y2))
    back3 = along(both3, 6)
    rx2, ry2 = over_x(x2), over_y(y2)
    x0, y0, x1, y1 = relay("relay_near", through_x, through_y, 0, after=(both3,))
    rx1, ry1 = over_x(x1), over_y(y1)
    both2, x0, y0 = finish(2, rx2, ry2, (x0, y0))
    back2 = along(both2, 4)
    rx0, ry0 = over_x(x0), over_y(y0)
    back1 = along(finish(1, rx1, ry1, after=(back3,))[0], 2)
    back = [finish(0, rx0, ry0)[0], back1, back2, back3]
    swap = block_call(second_kernel, [jax.ShapeDtypeStruct((2,) + tiles.shape, BF16)], 0, back)[0]
    swap = along(swap, 1)
    return block_call(
        mix_kernel,
        [jax.ShapeDtypeStruct((rows, features), BF16)],
        1,
        (self_id, ids_t, gate_weights.T, swap, *back, stream0, stream1, stream2, stream3),
    )[0]


def entering_2(array, axis, combine, identity):
    devices, mine = (lax.axis_size(axis), lax.axis_index(axis))
    everything = jax.tree.map(
        lambda part, kind: lax.all_gather(part.astype(kind), axis),
        array,
        (jnp.bfloat16, jnp.bfloat16),
    )
    start = jax.tree.map(
        lambda part, zero: jnp.broadcast_to(jnp.asarray(zero, part.dtype), part.shape),
        array,
        identity,
    )

    def hop(k, before):
        reached = k < mine
        new = combine(
            before, jax.tree.map(lambda part, own: part[k].astype(own.dtype), everything, array)
        )
        return jax.tree.map(lambda a, b: jnp.where(reached, a, b), new, before)

    return lax.fori_loop(0, devices, hop, start)


def chain_combine(earlier, later):
    return (earlier[0] + later[0], jnp.exp(later[0])[:, None, None] * earlier[1] + later[1])


def on_device(
    x_in,
    z_gate,
    b_in,
    c_out,
    dt_step,
    rate,
    skip,
    init_state,
    residual,
    norm_gain,
    expert_ids,
    gate_weights,
    w_gate,
    w_up,
    w_down,
):
    token_count, channels = x_in.shape
    heads_here = rate.shape[0]
    head_width = channels // heads_here
    state_width = b_in.shape[1]
    blocks = token_count // GROUP
    inputs = x_in.astype(jnp.float32).reshape(blocks, GROUP, heads_here, head_width)
    keys_in = b_in.astype(jnp.float32).reshape(blocks, GROUP, state_width)
    queries = c_out.astype(jnp.float32).reshape(blocks, GROUP, state_width)
    log_steps = (-rate[None, :] * dt_step).reshape(blocks, GROUP, heads_here)
    cumulative = jnp.cumsum(log_steps, axis=1)
    scores = jnp.einsum("ctn,csn->cts", queries, keys_in, precision=PRECISE)
    causal = jnp.arange(GROUP)[:, None] >= jnp.arange(GROUP)[None, :]
    spread = cumulative[:, :, None, :] - cumulative[:, None, :, :]
    weights = jnp.exp(jnp.where(causal[None, :, :, None], spread, -jnp.inf)) * scores[..., None]
    intra_out = jnp.einsum("ctsh,cshp->cthp", weights, inputs, precision=PRECISE)
    tail_decay = jnp.exp(cumulative[:, -1:, :] - cumulative)
    block_state = jnp.einsum("csh,cshp,csn->chpn", tail_decay, inputs, keys_in, precision=PRECISE)
    block_log = cumulative[:, -1, :]

    def advance(carried, element):
        total_log, total_state = carried
        step_log, step_state = element
        updated = (
            total_log + step_log,
            jnp.exp(step_log)[:, None, None] * total_state + step_state,
        )
        return (updated, (total_log, total_state))

    zero_state = jnp.zeros((heads_here, head_width, state_width), jnp.float32)
    zero_log = jnp.zeros((heads_here,), jnp.float32)
    (device_log, device_state), (enter_log, enter_state) = lax.scan(
        advance, (zero_log, zero_state), (block_log, block_state)
    )
    prior_log, prior_state = entering_2(
        (device_log, device_state), "seq", chain_combine, (zero_log, zero_state)
    )
    incoming = prior_state + jnp.exp(prior_log)[:, None, None] * init_state
    entering = enter_state + jnp.exp(enter_log)[:, :, None, None] * incoming[None]
    inter_out = jnp.exp(cumulative)[..., None] * jnp.einsum(
        "chpn,ctn->cthp", entering, queries, precision=PRECISE
    )
    mixed_out = (intra_out + inter_out + skip[None, None, :, None] * inputs).reshape(
        token_count, channels
    )
    mixer = (mixed_out * jax.nn.silu(z_gate.astype(jnp.float32))).astype(jnp.bfloat16)
    token_mix = lax.all_to_all(mixer, "exp", split_axis=0, concat_axis=1, tiled=True)
    stream = (residual.astype(jnp.float32) + token_mix.astype(jnp.float32)).astype(jnp.bfloat16)
    widened = stream.astype(jnp.float32)
    normed = (
        widened
        * lax.rsqrt(jnp.mean(widened * widened, axis=-1, keepdims=True) + 1e-06)
        * norm_gain[None, :]
    ).astype(jnp.bfloat16)
    rows_here = residual.shape[0]
    owners = lax.axis_size("exp")
    local_experts = w_gate.shape[0]
    experts = owners * local_experts
    capacity = max(2, 2 * rows_here // experts + 1)
    width = residual.shape[1]
    chosen = expert_ids.reshape(-1)
    onehot = (chosen[:, None] == jnp.arange(experts)[None, :]).astype(jnp.int32)
    slot_index = jnp.sum((jnp.cumsum(onehot, axis=0) - onehot) * onehot, axis=1)
    target = chosen * capacity + slot_index
    placing = (target[None, :] == jnp.arange(experts * capacity)[:, None]).astype(jnp.bfloat16)
    pair_rows = jnp.repeat(normed, 2, axis=0)
    outgoing = jnp.dot(placing, pair_rows, preferred_element_type=jnp.float32).astype(jnp.bfloat16)
    outgoing = outgoing.reshape(owners, local_experts, 1, capacity, width)
    arrived = lax.all_to_all(outgoing, "exp", split_axis=0, concat_axis=2, tiled=True)
    segment = lax.all_gather(arrived, "seq", axis=1, tiled=True)
    flattened = segment.reshape(segment.shape[0], -1, segment.shape[-1])
    gate_proj = jnp.einsum("erd,edf->erf", flattened, w_gate, preferred_element_type=jnp.float32)
    up_proj = jnp.einsum("erd,edf->erf", flattened, w_up, preferred_element_type=jnp.float32)
    active = (jax.nn.silu(gate_proj) * up_proj).astype(jnp.bfloat16)
    partial_value = jnp.einsum("erf,efd->erd", active, w_down, preferred_element_type=jnp.float32)
    partials = partial_value.reshape(segment.shape[:-1] + (partial_value.shape[-1],))
    summed = lax.psum_scatter(partials.astype(jnp.bfloat16), "seq", scatter_dimension=1, tiled=True)
    returned = lax.all_to_all(summed, "exp", split_axis=2, concat_axis=0, tiled=True)
    results = returned.reshape(experts * capacity, width)
    picked = results[target].astype(jnp.float32).reshape(rows_here, 2, width)
    mixture = jnp.sum(picked * gate_weights[:, :, None], axis=1)
    return (widened + mixture).astype(jnp.bfloat16)


def solution(mesh):
    square = mesh.shape["seq"] == 4 and mesh.shape["exp"] == 8

    def body(*args):
        rows = args[8].shape[0]
        experts = mesh.shape["exp"] * args[12].shape[0]
        fits = args[12].shape[0] == 1 and 2 * rows // experts + 1 == 9
        return (on_square if square and fits else on_device)(*args)

    return jax.shard_map(
        body,
        mesh=mesh,
        in_specs=(
            P("seq", "exp"),
            P("seq", "exp"),
            P("seq", None),
            P("seq", None),
            P("seq", "exp"),
            P("exp"),
            P("exp"),
            P("exp", None, None),
            P(("seq", "exp"), None),
            P(),
            P(("seq", "exp"), None),
            P(("seq", "exp"), None),
            P("exp", None, "seq"),
            P("exp", None, "seq"),
            P("exp", "seq", None),
        ),
        out_specs=P(("seq", "exp"), None),
        check_vma=False,
    )
```

```python
import functools

import jax
import jax.numpy as jnp
from jax import lax
from jax.experimental import pallas as pl
from jax.experimental.pallas import tpu as pltpu
from jax.sharding import PartitionSpec as P

GROUP = 128
PRECISE = lax.Precision.HIGHEST
F32 = jnp.float32
BF16 = jnp.bfloat16
MIB = 1 << 20
NO_COST = pl.CostEstimate(flops=0, bytes_accessed=0, transcendentals=0)


def block_call(body, outs, scalars, args, held=0, keep=0, after=(), limit=16, out_blocks=False, name=None):
    n_args = len(args)
    kept = [jax.ShapeDtypeStruct(v.shape, v.dtype) for v in args[scalars : scalars + held]]

    def kernel(*refs):
        refs, sems = (refs[:-1], refs[-1]) if held else (refs, None)
        inputs, refs = refs[:n_args], refs[n_args + len(after) :]
        results, refs = refs[: len(outs)], refs[len(outs) :]
        copies = [
            pltpu.make_async_copy(src, dst, sems.at[k])
            for k, (src, dst) in enumerate(zip(inputs[scalars : scalars + held], refs))
        ]
        for copy in copies:
            copy.start()
        for copy in copies:
            copy.wait()
        body(*inputs[:scalars], *refs, *inputs[scalars + held :], *results)

    scratch = [pltpu.VMEM(v.shape, v.dtype) for v in kept[keep:]]
    if held:
        scratch.append(pltpu.SemaphoreType.DMA((held,)))
    return pl.pallas_call(
        kernel,
        name=name or getattr(body, "func", body).__name__,
        out_shape=list(outs) + kept[:keep],
        in_specs=[pl.BlockSpec(memory_space=pltpu.SMEM)] * scalars
        + [pl.BlockSpec(memory_space=pltpu.HBM)] * held
        + [pl.BlockSpec(memory_space=pltpu.VMEM)] * (n_args - scalars - held)
        + [pl.BlockSpec(memory_space=pl.ANY)] * len(after),
        out_specs=[pl.BlockSpec() if out_blocks else pl.BlockSpec(memory_space=pltpu.VMEM)]
        * (len(outs) + keep),
        scratch_shapes=scratch,
        compiler_params=pltpu.CompilerParams(vmem_limit_bytes=limit * MIB),
        cost_estimate=NO_COST,
    )(*args, *after)


def iota(shape, dim):
    return lax.broadcasted_iota(jnp.int32, shape, dim)


def dot(a, b, precision=None):
    return jnp.dot(a, b, precision=precision, preferred_element_type=F32)


def head_spread(heads, channels):
    shape = (heads, channels)
    return (iota(shape, 1) // (channels // heads) == iota(shape, 0)).astype(F32)


def running_logs(dt_t_ref, rate_ref):
    logs = -rate_ref[...] * dt_t_ref[...].T
    tokens = logs.shape[0]
    tri = (iota((tokens, tokens), 0) >= iota((tokens, tokens), 1)).astype(F32)
    return dot(tri, logs, PRECISE)


def pack_kernel(ids_t_ref, residual_ref, out_ref):
    parts, rows, wide = out_ref.shape
    part = wide - 128
    ids = ids_t_ref[...].astype(F32).T
    lane = iota((rows, 128), 1)
    named = jnp.where(lane == 0, ids[:, 0:1], jnp.where(lane == 1, ids[:, 1:2], 0.0)).astype(BF16)
    for k in range(parts):
        out_ref[k, :, 0:part] = residual_ref[:, k * part : (k + 1) * part]
        out_ref[k, :, part:wide] = named


def state_kernel(place, x_ref, b_ref, dt_t_ref, rate_ref, init_ref, payload_ref, init_t_ref):
    tokens, channels = x_ref.shape
    heads = dt_t_ref.shape[0]
    width = b_ref.shape[1]
    cum = running_logs(dt_t_ref, rate_ref)
    total = cum[tokens - 1 : tokens, :]
    spread = head_spread(heads, channels)
    tail = dot(jnp.exp(total - cum), spread, PRECISE)
    scaled = (x_ref[...].astype(F32) * tail).astype(BF16)
    keys = b_ref[...].astype(F32).T.astype(BF16)
    own = dot(keys, scaled)
    decay = dot(jnp.broadcast_to(jnp.exp(total), (8, heads)), spread, PRECISE)
    init_t = init_ref[...].T
    init_t_ref[...] = init_t.astype(BF16)
    first = (place[0] == 0).astype(F32)
    payload_ref[0:width, :] = (own + first * (decay[0:1, :] * init_t)).astype(BF16)
    high = decay.astype(BF16).astype(F32)
    rows = iota((16, channels), 0)
    high16 = jnp.broadcast_to(high[0:1, :], (16, channels))
    low16 = jnp.broadcast_to(decay[0:1, :], (16, channels)) - high16
    payload_ref[width : width + 16, :] = jnp.where(
        rows == 0, high16, jnp.where(rows == 1, low16, 0.0)
    ).astype(BF16)


def intra_kernel(x_ref, z_ref, b_ref, c_ref, dt_t_ref, rate_ref, skip_ref, own_ref, fade_ref, token_ref):
    tokens, channels = x_ref.shape
    heads = dt_t_ref.shape[0]
    width = channels // heads
    token_ref[...] = jnp.zeros_like(token_ref)
    shape = (tokens, tokens)
    causal = iota(shape, 0) >= iota(shape, 1)
    cum = running_logs(dt_t_ref, rate_ref)
    cum_t = cum.T
    scores = lax.dot_general(
        c_ref[...], b_ref[...], (((1,), (1,)), ((), ())), preferred_element_type=F32
    )
    spread = head_spread(heads, channels)
    direct = dot(jnp.broadcast_to(skip_ref[...], (8, heads)), spread, PRECISE)[0:1, :]
    fade = dot(jnp.exp(cum), spread, PRECISE)
    per = 128 // width
    lane_head = iota((tokens, 128), 1) // width
    for group in range(heads // per):
        cols = slice(group * 128, (group + 1) * 128)
        x = x_ref[:, cols]
        total = x.astype(F32) * direct[:, cols]
        for k in range(per):
            h = group * per + k
            gap = jnp.where(causal, cum[:, h : h + 1] - cum_t[h : h + 1, :], -1e30)
            weights = (jnp.exp(gap) * scores).astype(BF16)
            part = dot(weights, x)
            total = total + jnp.where(lane_head == k, part, 0.0)
        z = z_ref[:, cols].astype(F32)
        gate = z / (1.0 + jnp.exp(-z))
        own_ref[:, cols] = total * gate
        fade_ref[:, cols] = fade[:, cols] * gate


def place_kernel(cap, experts, me, packed_ref, *refs):
    count = (len(refs) - 1) // 2
    out_ref = refs[count]
    for source, target in zip(refs[:count], refs[count + 1 :]):
        target[...] = source[...]
    blocks, rows, wide = packed_ref.shape
    tokens = blocks * rows
    slots = out_ref.shape[1] - rows
    ids = packed_ref[:, :, wide - 128 : wide].astype(F32).reshape(tokens, 128).T
    ids = ids[0:8, :].astype(jnp.int32)
    shape = (tokens, tokens)
    before = (iota(shape, 0) < iota(shape, 1)) & (iota(shape, 0) // rows == iota(shape, 1) // rows)
    named = iota((experts, tokens), 0) ^ me[0]
    hit = (ids[0:1, :] == named) | (ids[1:2, :] == named)
    rank = dot(hit.astype(BF16), before.astype(BF16)).astype(jnp.int32)
    block = (iota((experts, tokens), 1) // rows) ^ named
    whole = cap - 1
    row = jnp.where(rank < whole, block * whole + rank, blocks * whole + block)
    row = jnp.where(hit, row, -1)
    shape = (rows + slots, tokens)
    for e in range(experts):
        owned = ((me[0] ^ e) * rows + iota(shape, 0) == iota(shape, 1)) & (iota(shape, 0) < rows)
        placed = (iota(shape, 0) - rows == row[e : e + 1, :]) & (iota(shape, 0) >= rows)
        out_ref[e] = (owned | placed).astype(F32).astype(BF16)


def join_kernel(place, own_ref, other_ref, out_ref):
    width = out_ref.shape[0]
    odd = place[0] % 2 == 1
    own, other = own_ref[0:width, :].astype(F32), other_ref[0:width, :].astype(F32)
    own_decay = own_ref[width : width + 16, :].astype(F32)
    other_decay = other_ref[width : width + 16, :].astype(F32)
    own_decay = own_decay[0:1, :] + own_decay[1:2, :]
    other_decay = other_decay[0:1, :] + other_decay[1:2, :]
    early = jnp.where(odd, other, own)
    late = jnp.where(odd, own, other)
    decay = jnp.where(odd, own_decay, other_decay)
    out_ref[...] = (decay * early + late).astype(BF16)


def stream_kernel(
    place, c_ref, own_ref, fade_ref, init_t_ref, pair_ref, early_ref, res_ref, sel_ref, near_a_ref, near_b_ref, same_ref, other_ref
):
    width = init_t_ref.shape[0]
    at = place[0]
    zero = (at == 0).astype(F32)
    odd = (at % 2 == 1).astype(F32)
    pair = pair_ref[...].astype(F32)
    decay = pair[width : width + 1, :] + pair[width + 1 : width + 2, :]
    factor = jnp.where(at >= 2, jnp.where(at % 2 == 1, decay, 1.0), 0.0)
    entering = zero * init_t_ref[...].astype(F32) + odd * pair[0:width, :] + factor * early_ref[...].astype(F32)
    mixed = own_ref[...] + fade_ref[...] * dot(c_ref[...], entering.astype(BF16))
    mixer = mixed.astype(BF16).astype(F32)
    tokens, channels = mixer.shape
    residual = res_ref[:, :, 0:channels].astype(F32).reshape(tokens, channels)
    stream = (residual + mixer).astype(BF16)
    owned = sel_ref.shape[1] - near_a_ref.shape[0]
    near_a_ref[...] = dot(sel_ref[2, owned:, :], stream).astype(BF16)
    near_b_ref[...] = dot(sel_ref[3, owned:, :], stream).astype(BF16)
    for at, k in enumerate((0, 2, 3, 1)):
        same_ref[at] = dot(sel_ref[2 * k], stream).astype(BF16)
        other_ref[at] = dot(sel_ref[2 * k + 1], stream).astype(BF16)


def up_kernel(first, features, after, me, *refs):
    own, rx, ry, even, odd, gain, wg, wu = refs[:8]
    carry = () if first else refs[8:11]
    rest = refs[(8 if first else 11) + after :]
    sums = rest[2:5] if features else rest
    step = pl.program_id(0)
    steps = pl.num_programs(0)

    if first or features:

        @pl.when(step == 0)
        def _():
            for i, acc in enumerate(sums):
                acc[...] = jnp.zeros_like(acc) if first else carry[i][...]

    gate, up, square = sums
    slots = own.shape[1]
    rows = [r[0].astype(F32) for r in (own, rx, ry)]
    rows.append(jnp.where(step == 0, even[0].astype(F32), odd[0].astype(F32)))
    rows = jnp.concatenate(rows, axis=0)
    square[...] += jnp.broadcast_to(jnp.sum(rows * rows, axis=1, keepdims=True), square.shape)
    scaled = (rows * gain[0]).astype(BF16)
    gate[...] += dot(scaled, wg[0])
    up[...] += dot(scaled, wu[0])

    if features:
        outs, stages = rest[:2], rest[5:]

        @pl.when(step == steps - 1)
        def _():
            inverse = lax.rsqrt(square[:, 0:1] * (1.0 / features) + 1e-06)
            g = gate[...] * inverse
            active = g / (1.0 + jnp.exp(-g)) * (up[...] * inverse)
            main, ninths = slots // 9 * 8, slots // 9
            for d in range(4):
                at = d * slots
                stage, d, shards = (stages[0], 0, 1) if d == 3 else (stages[1], d, 3)
                stage[d * main : (d + 1) * main, :] = active[at : at + main]
                low = shards * main + d * ninths
                stage[low : low + ninths, :] = active[at + main : at + slots]
            for out, stage in zip(outs, stages):
                out[...] = stage[...].astype(BF16)


def up_project(group, last, me, near, far, gain, w_gate, w_up, carry, after=()):
    slots, part = near[0][0].shape[1:]
    hidden = w_gate.shape[2]
    total = 4 * slots
    source = lambda i, me: me[0] ^ (2 * group + i)
    rows = [
        pl.BlockSpec((1, slots, part), lambda i, me, start=start: (start + i, 0, 0))
        for _, start in near
    ] + [
        pl.BlockSpec((1, slots, part), lambda i, me, start=start: (start, 0, 0)) for _, start in far
    ]
    weight = pl.BlockSpec((1, part, hidden), lambda i, me: (source(i, me), 0, 0))
    in_place = pl.BlockSpec(memory_space=pltpu.VMEM)
    specs = rows + [pl.BlockSpec((1, 1, part), lambda i, me: (source(i, me), 0, 0)), weight, weight]
    sums = [
        jax.ShapeDtypeStruct((total, hidden), F32),
        jax.ShapeDtypeStruct((total, hidden), F32),
        jax.ShapeDtypeStruct((total, 128), F32),
    ]
    aliases = {}
    if carry is not None:
        specs += [in_place] * 3
        if not last:
            aliases = {9 + i: i for i in range(3)}
    specs += [pl.BlockSpec(memory_space=pl.ANY)] * len(after)
    sizes = (slots, 3 * slots)
    outs = [jax.ShapeDtypeStruct((n, hidden), BF16) for n in sizes] if last else sums
    scratch = [pltpu.VMEM(s.shape, s.dtype) for s in sums]
    scratch += [pltpu.VMEM((n, hidden), F32) for n in sizes]
    features = gain.shape[0] * part if last else 0
    return pl.pallas_call(
        functools.partial(up_kernel, carry is None, features, len(after)),
        name=f"up_{group}",
        out_shape=outs,
        grid_spec=pltpu.PrefetchScalarGridSpec(
            num_scalar_prefetch=1,
            grid=(2,),
            in_specs=specs,
            out_specs=[in_place] * len(outs),
            scratch_shapes=scratch if last else [],
        ),
        input_output_aliases=aliases,
        compiler_params=pltpu.CompilerParams(vmem_limit_bytes=48 * MIB),
        cost_estimate=NO_COST,
    )(me, *(array for array, _ in near + far), gain, w_gate, w_up, *(carry or ()), *after)


def cut_of(group):
    return 5 if group % 2 else 4


def down_kernel(groups, act_ref, w_ref, *refs):
    outs, (spare, held, sems) = refs[:-3], refs[-3:]
    step = pl.program_id(0)
    steps, _, tile = held.shape

    def load(k):
        columns = pl.ds(pl.multiple_of(k * tile, tile), tile)
        return pltpu.make_async_copy(w_ref.at[:, columns], held.at[k], sems.at[k])

    @pl.when(step == 0)
    def _():
        for k in range(steps):
            load(k).start()

    load(step).wait()
    part = dot(act_ref[...], held[step])
    ninths = part.shape[0] // 9
    main = part.shape[0] - ninths
    shards = ninths // (2 * groups)

    def through(group, tile):
        to_x, to_y = outs[2 * (group // 2) : 2 * (group // 2) + 2]
        cut = cut_of(group)
        return to_x, tile + (0 if group % 2 else 5), to_y, tile - cut + (0 if group % 2 else 4)

    for shard in range(shards):
        for group in range(groups):
            at = (shard * groups + group) * 16
            rows = part[at : at + 16, :].astype(BF16)
            if shards > 1:
                outs[shards * group + shard][step] = rows
                continue
            to_x, place_x, to_y, place_y = through(group, step)

            @pl.when(step < cut_of(group))
            def _():
                to_x[place_x] = rows

            @pl.when(step >= cut_of(group))
            def _():
                to_y[place_y] = rows

    for lanes in range(spare.shape[0]):
        spare[lanes, pl.ds(pl.multiple_of(step * ninths, 8), ninths), :] = part[
            main:, lanes * 128 : (lanes + 1) * 128
        ]

    @pl.when(step == steps - 1)
    def _():
        for shard in range(shards):
            for group in range(groups):
                pair = []
                for side in range(2):
                    row = pl.ds((shard * groups + group) * 2 + side, 8, stride=ninths)
                    ninth = [spare[lanes, row, :] for lanes in range(spare.shape[0])]
                    pair.append(jnp.concatenate(ninth, axis=1))
                pair = jnp.concatenate(pair, axis=0).astype(BF16)
                if shards > 1:
                    outs[shards * group + shard][8] = pair
                else:
                    _, _, to_y, place_y = through(group, 8)
                    to_y[place_y] = pair


def down_project(name, groups, active, w_down):
    total, hidden = active.shape
    features = w_down.shape[1]
    tile = features // 8
    outs = [jax.ShapeDtypeStruct((9, 16, tile), BF16)] * (total // 18)
    return pl.pallas_call(
        functools.partial(down_kernel, groups),
        name=name,
        grid=(8,),
        out_shape=outs,
        in_specs=[
            pl.BlockSpec(memory_space=pltpu.VMEM),
            pl.BlockSpec(memory_space=pltpu.HBM),
        ],
        out_specs=[pl.BlockSpec(memory_space=pltpu.VMEM)] * len(outs),
        scratch_shapes=[
            pltpu.VMEM((tile // 128, 8 * total // 9, 128), F32),
            pltpu.VMEM((8, hidden, tile), BF16),
            pltpu.SemaphoreType.DMA((8,)),
        ],
        compiler_params=pltpu.CompilerParams(vmem_limit_bytes=48 * MIB),
        cost_estimate=NO_COST,
    )(active, w_down)


def pair_kernel(same, other, own_stream, own, far, last_stream, last, near_stream):
    owned = own_stream.shape[1]
    for side, rows in enumerate((same, other)):
        own_stream[side], own[side] = rows[0, 0:owned, :], rows[0, owned:, :]
        far[side] = rows[1]
        last_stream[side], last[side] = rows[2, 0:owned, :], rows[2, owned:, :]
        near_stream[side] = rows[3, 0:owned, :]


def near_kernel(same, other, rows):
    rows[0], rows[1] = same[...], other[...]


def second_kernel(*refs):
    parts, out = refs[:-1], refs[-1]
    for h in range(out.shape[0]):
        for k in range(out.shape[1]):
            pair = [ref[k].astype(F32)[8:16] for ref in parts[2 * h : 2 * h + 2]]
            out[h, k] = jnp.concatenate(pair, axis=0).astype(BF16)


def hold_kernel(*refs):
    for source, target in zip(refs[: len(refs) // 2], refs[len(refs) // 2 :]):
        target[...] = source[...]


def half_message_kernel(rx, ry, out_x, out_y):
    out_x[0], out_y[0] = ry[1], rx[0]


def join_message_kernel(own, rx, ry, out_x, out_y, *parts):
    owned = own.shape[1] - out_x.shape[1]
    for side in range(2):
        rows = own[side, owned:, :]
        out_x[side], out_y[side] = rows, rows
        if parts:
            parts[0][side], parts[1][side] = rows, own[side, 0:owned, :]
    out_x[2], out_y[2] = ry[1], rx[0]


def relay_kernel(through_x, through_y, *refs):
    ahead = refs[4 : 4 + (len(refs) - 8) // 2]
    outs, copies = refs[4 + len(ahead) :][:4], refs[8 + len(ahead) :]
    for group in range(2):
        cut = cut_of(group)
        at_x, at_y = (0, -cut) if group else (5, 0)
        for own, out, through, tiles, at in (
            (refs[2 * group], outs[2 * group], through_y, range(cut, 9), at_y),
            (refs[2 * group + 1], outs[2 * group + 1], through_x, range(cut), at_x),
        ):
            for k in range(9):
                if k in tiles:
                    out[k] = (own[k].astype(F32) + through[k + at].astype(F32)).astype(BF16)
                else:
                    out[k] = own[k]
    for source, copy in zip(ahead, copies):
        copy[...] = source[...]


def finish_kernel(own, rx, ry, *refs):
    ahead = refs[: (len(refs) - 1) // 2]
    out, copies = refs[len(ahead)], refs[len(ahead) + 1 :]
    for k in range(9):
        out[k] = (own[k].astype(F32) + rx[k].astype(F32) + ry[k].astype(F32)).astype(BF16)
    for source, copy in zip(ahead, copies):
        copy[...] = source[...]


def mix_kernel(me, ids_t_ref, weight_t_ref, swap_ref, *refs):
    groups = (len(refs) - 1) // 2
    firsts, streams, out_ref = refs[:groups], refs[groups:-1], refs[-1]
    rows = ids_t_ref.shape[1]
    experts = 2 * groups
    pieces = firsts[0].shape[0] - 1
    tile = firsts[0].shape[2]
    ids, weights = ids_t_ref[...].T, weight_t_ref[...].T
    named = iota((rows, experts), 1) ^ me[0]
    first, second = ids[:, 0:1] == named, ids[:, 1:2] == named
    weight = jnp.where(first, weights[:, 0:1], jnp.where(second, weights[:, 1:2], 0.0))
    hit = (first | second).astype(F32)
    before = (iota((rows, rows), 0) > iota((rows, rows), 1)).astype(F32)
    rank = dot(before, hit)
    lanes = 2 * experts * 8
    shape = (experts, lanes)
    spread = ((iota(shape, 1) // 8) % experts == iota(shape, 0)).astype(F32)
    weight = dot(weight, spread, PRECISE)
    rank = dot(rank, spread, PRECISE).astype(jnp.int32)
    lane = iota((rows, lanes), 1)
    main = (lane < experts * 8) & (rank == lane % 8)
    extra = (lane >= experts * 8) & (rank == 8)

    def rows_of(k):
        data = []
        for g in range(groups):
            data.append(firsts[g][k].astype(F32)[0:8])
            data.append(swap_ref[g // 2, k].astype(F32)[g % 2 * 8 : g % 2 * 8 + 8])
        return data

    last = rows_of(pieces)
    for m in range(experts):
        k = me[0] ^ m
        coef = jnp.where(main | (extra & (lane % 8 == k)), weight, 0.0)
        high = coef.astype(BF16)
        low = (coef - high.astype(F32)).astype(BF16)
        data = jnp.concatenate(rows_of(k) + last, axis=0).astype(BF16)
        stream = streams[m // 2][m % 2].astype(F32)
        out_ref[:, pl.ds(pl.multiple_of(k * tile, 128), tile)] = (
            stream + (dot(high, data) + dot(low, data))
        ).astype(BF16)


def on_square(
    x_in,
    z_gate,
    b_in,
    c_out,
    dt_step,
    rate,
    skip,
    init_state,
    residual,
    norm_gain,
    expert_ids,
    gate_weights,
    w_gate,
    w_up,
    w_down,
):
    tokens, channels = x_in.shape
    heads = rate.shape[0]
    state = b_in.shape[1]
    owners = lax.axis_size("exp")
    rows, features = residual.shape
    experts = owners
    cap = max(2, 2 * rows // experts + 1)
    slots = owners * cap
    at = lax.axis_index("seq")
    me = lax.axis_index("exp")
    place = jnp.reshape(at, (1,)).astype(jnp.int32)
    self_id = jnp.reshape(me, (1,)).astype(jnp.int32)

    def over_x(v):
        return lax.ppermute(v, "seq", [(i, i ^ 1) for i in range(4)])

    def over_y(v):
        return lax.ppermute(v, "seq", [(i, i ^ 2) for i in range(4)])

    def along(v, mask):
        return lax.ppermute(v, "exp", [(i, i ^ mask) for i in range(owners)])

    rate_row = rate[None, :]
    dt_t = dt_step.T
    ids_t = expert_ids.T
    packed = block_call(
        pack_kernel,
        [jax.ShapeDtypeStruct((owners, rows, channels + 128), BF16)],
        0,
        (ids_t, residual),
        held=2,
        limit=48,
    )[0]
    packed = lax.all_to_all(packed, "exp", split_axis=0, concat_axis=0, tiled=True)
    payload, init_t = block_call(
        state_kernel,
        [
            jax.ShapeDtypeStruct((state + 16, channels), BF16),
            jax.ShapeDtypeStruct((state, channels), BF16),
        ],
        1,
        (place, x_in, b_in, dt_t, rate_row, init_state.reshape(channels, state)),
        held=5,
        limit=62,
    )
    pair = over_x(payload)
    own_part, fade, token = block_call(
        intra_kernel,
        [
            jax.ShapeDtypeStruct((tokens, channels), F32),
            jax.ShapeDtypeStruct((tokens, channels), F32),
            jax.ShapeDtypeStruct((8, 128), F32),
        ],
        0,
        (x_in, z_gate, b_in, c_out, dt_t, rate_row, skip[None, :]),
        held=7,
        limit=61,
    )
    joined = block_call(
        join_kernel,
        [jax.ShapeDtypeStruct((state, channels), BF16)],
        1,
        (place, payload, pair),
        after=(token,),
    )[0]
    early = over_y(joined)
    handed = (own_part, fade, c_out, init_t)
    select, own_part, fade, c, init_t = block_call(
        functools.partial(place_kernel, cap, experts),
        [jax.ShapeDtypeStruct((experts, rows + slots, tokens), BF16)]
        + [jax.ShapeDtypeStruct(v.shape, v.dtype) for v in handed],
        1,
        (self_id, packed, *handed),
        after=(joined,),
    )
    groups = owners // 2
    lanes = jax.ShapeDtypeStruct((groups, rows + slots, channels), BF16)
    one = jax.ShapeDtypeStruct((slots, channels), BF16)
    near_a, near_b, same, other = block_call(
        stream_kernel,
        [one, one, lanes, lanes],
        1,
        (place, c, own_part, fade, init_t, pair, early, packed, select),
    )

    gain = norm_gain.reshape(owners, 1, channels)
    wg = w_gate.reshape(owners, channels, w_gate.shape[2])
    wu = w_up.reshape(owners, channels, w_up.shape[2])
    expert_rows = jax.ShapeDtypeStruct((2, slots, channels), BF16)
    stream_rows = jax.ShapeDtypeStruct((2, rows, channels), BF16)
    both_rows = jax.ShapeDtypeStruct((2, rows + slots, channels), BF16)
    near_a, near_b = along(near_a, 2), along(near_b, 3)
    stream0, first, far, stream3, farthest, stream1 = block_call(
        pair_kernel,
        [stream_rows, expert_rows, both_rows, stream_rows, expert_rows, stream_rows],
        0,
        (same, along(other, 1)),
    )
    gain = norm_gain.reshape(owners, 1, channels)
    wg = w_gate.reshape(owners, channels, w_gate.shape[2])
    wu = w_up.reshape(owners, channels, w_up.shape[2])
    gain = norm_gain.reshape(owners, 1, channels)
    wg = w_gate.reshape(owners, channels, w_gate.shape[2])
    wu = w_up.reshape(owners, channels, w_up.shape[2])

    def hold(values, after, name):
        outs = [jax.ShapeDtypeStruct(v.shape, BF16) for v in values]
        return block_call(hold_kernel, outs, 0, values, after=after, name=name)

    def project(group, near, far, carry, after=()):
        last = group == groups - 1
        return up_project(group, last, self_id, near, far, gain, wg, wu, carry, after)

    def message(count):
        return [jax.ShapeDtypeStruct((count, slots, channels), BF16)] * 2

    far = along(far, 4)
    rx0, ry0 = over_x(first), over_y(first)
    near = block_call(near_kernel, [expert_rows], 0, (near_a, near_b))[0]
    rx1, ry1 = over_x(near), over_y(near)
    to_x, to_y = block_call(
        half_message_kernel, message(1), 0, (rx0, ry0), after=(near,), name="half_0"
    )
    fx0, fy0 = over_x(to_x), over_y(to_y)
    farthest_held = hold((farthest,), (far,), "hold_farthest")[0]
    farthest = along(farthest_held, 6)
    to_x, to_y, far, stream2 = block_call(
        join_message_kernel,
        message(3) + [expert_rows, stream_rows],
        0,
        (far, rx1, ry1),
        after=(fx0, fy0, farthest_held),
        name="join_2",
    )
    rx2, ry2 = over_x(to_x), over_y(to_y)
    carry = project(0, [(first, 0), (rx0, 0), (ry0, 0)], [(fy0, 0), (fx0, 0)], None)
    to_x, to_y = block_call(
        join_message_kernel, message(3), 0, (farthest, rx2, ry2), after=(carry[2],), name="join_3"
    )
    rx3, ry3 = over_x(to_x), over_y(to_y)
    held, stream1 = hold((stream3, stream1), (to_x,), "hold_streams")
    stream3, stream1 = along(held, 6), along(stream1, 2)
    carry = project(1, [(near, 0), (rx1, 0), (ry1, 0)], [(ry2, 2), (rx2, 2)], carry, (held,))
    to_x, to_y = block_call(
        half_message_kernel, message(1), 0, (rx3, ry3), after=(carry[2], stream1, stream3), name="half_3"
    )
    fx3, fy3 = over_x(to_x), over_y(to_y)
    carry = project(2, [(far, 0), (rx2, 0), (ry2, 0)], [(ry3, 2), (rx3, 2)], carry)
    active_far, active = project(
        3, [(farthest, 0), (rx3, 0), (ry3, 0)], [(fy3, 0), (fx3, 0)], carry
    )

    wd = w_down.reshape(w_down.shape[1], features)
    tiles = jax.ShapeDtypeStruct((9, 16, features // 8), BF16)
    sent = down_project("down_through", groups, active_far, wd)
    rest = down_project("down_rest", groups, active, wd)
    own, own_x, own_y = ([rest[3 * g + k] for g in range(groups)] for k in range(3))

    def relay(name, through_x, through_y, low, ahead=(), after=()):
        shares = (own_x[low], own_y[low], own_x[low + 1], own_y[low + 1])
        return block_call(
            relay_kernel,
            [tiles] * (4 + len(ahead)),
            0,
            (through_x, through_y, *shares, *ahead),
            after=after,
            name=name,
        )

    def finish(group, rx, ry, ahead=(), after=()):
        return block_call(
            finish_kernel,
            [tiles] * (1 + len(ahead)),
            0,
            (own[group], rx, ry, *ahead),
            after=after,
            name=f"finish_{group}",
        )

    through_x, through_y = over_x(sent[2]), over_y(sent[3])
    x2, y2, x3, y3, next_x, next_y = relay(
        "relay_far", through_x, through_y, 2, (sent[0], sent[1])
    )
    rx3, ry3 = over_x(x3), over_y(y3)
    through_x, through_y = over_x(next_x), over_y(next_y)
    both3, x2, y2 = finish(3, rx3, ry3, (x2, y2))
    back3 = along(both3, 6)
    rx2, ry2 = over_x(x2), over_y(y2)
    x0, y0, x1, y1 = relay("relay_near", through_x, through_y, 0, after=(both3,))
    rx1, ry1 = over_x(x1), over_y(y1)
    both2, x0, y0 = finish(2, rx2, ry2, (x0, y0))
    back2 = along(both2, 4)
    rx0, ry0 = over_x(x0), over_y(y0)
    back1 = along(finish(1, rx1, ry1, after=(back3,))[0], 2)
    back = [finish(0, rx0, ry0)[0], back1, back2, back3]
    swap = block_call(second_kernel, [jax.ShapeDtypeStruct((2,) + tiles.shape, BF16)], 0, back)[0]
    swap = along(swap, 1)
    return block_call(
        mix_kernel,
        [jax.ShapeDtypeStruct((rows, features), BF16)],
        1,
        (self_id, ids_t, gate_weights.T, swap, *back, stream0, stream1, stream2, stream3),
    )[0]


def entering_2(array, axis, combine, identity):
    devices, mine = (lax.axis_size(axis), lax.axis_index(axis))
    everything = jax.tree.map(
        lambda part, kind: lax.all_gather(part.astype(kind), axis),
        array,
        (jnp.bfloat16, jnp.bfloat16),
    )
    start = jax.tree.map(
        lambda part, zero: jnp.broadcast_to(jnp.asarray(zero, part.dtype), part.shape),
        array,
        identity,
    )

    def hop(k, before):
        reached = k < mine
        new = combine(
            before, jax.tree.map(lambda part, own: part[k].astype(own.dtype), everything, array)
        )
        return jax.tree.map(lambda a, b: jnp.where(reached, a, b), new, before)

    return lax.fori_loop(0, devices, hop, start)


def chain_combine(earlier, later):
    return (earlier[0] + later[0], jnp.exp(later[0])[:, None, None] * earlier[1] + later[1])


def on_device(
    x_in,
    z_gate,
    b_in,
    c_out,
    dt_step,
    rate,
    skip,
    init_state,
    residual,
    norm_gain,
    expert_ids,
    gate_weights,
    w_gate,
    w_up,
    w_down,
):
    token_count, channels = x_in.shape
    heads_here = rate.shape[0]
    head_width = channels // heads_here
    state_width = b_in.shape[1]
    blocks = token_count // GROUP
    inputs = x_in.astype(jnp.float32).reshape(blocks, GROUP, heads_here, head_width)
    keys_in = b_in.astype(jnp.float32).reshape(blocks, GROUP, state_width)
    queries = c_out.astype(jnp.float32).reshape(blocks, GROUP, state_width)
    log_steps = (-rate[None, :] * dt_step).reshape(blocks, GROUP, heads_here)
    cumulative = jnp.cumsum(log_steps, axis=1)
    scores = jnp.einsum("ctn,csn->cts", queries, keys_in, precision=PRECISE)
    causal = jnp.arange(GROUP)[:, None] >= jnp.arange(GROUP)[None, :]
    spread = cumulative[:, :, None, :] - cumulative[:, None, :, :]
    weights = jnp.exp(jnp.where(causal[None, :, :, None], spread, -jnp.inf)) * scores[..., None]
    intra_out = jnp.einsum("ctsh,cshp->cthp", weights, inputs, precision=PRECISE)
    tail_decay = jnp.exp(cumulative[:, -1:, :] - cumulative)
    block_state = jnp.einsum("csh,cshp,csn->chpn", tail_decay, inputs, keys_in, precision=PRECISE)
    block_log = cumulative[:, -1, :]

    def advance(carried, element):
        total_log, total_state = carried
        step_log, step_state = element
        updated = (
            total_log + step_log,
            jnp.exp(step_log)[:, None, None] * total_state + step_state,
        )
        return (updated, (total_log, total_state))

    zero_state = jnp.zeros((heads_here, head_width, state_width), jnp.float32)
    zero_log = jnp.zeros((heads_here,), jnp.float32)
    (device_log, device_state), (enter_log, enter_state) = lax.scan(
        advance, (zero_log, zero_state), (block_log, block_state)
    )
    prior_log, prior_state = entering_2(
        (device_log, device_state), "seq", chain_combine, (zero_log, zero_state)
    )
    incoming = prior_state + jnp.exp(prior_log)[:, None, None] * init_state
    entering = enter_state + jnp.exp(enter_log)[:, :, None, None] * incoming[None]
    inter_out = jnp.exp(cumulative)[..., None] * jnp.einsum(
        "chpn,ctn->cthp", entering, queries, precision=PRECISE
    )
    mixed_out = (intra_out + inter_out + skip[None, None, :, None] * inputs).reshape(
        token_count, channels
    )
    mixer = (mixed_out * jax.nn.silu(z_gate.astype(jnp.float32))).astype(jnp.bfloat16)
    token_mix = lax.all_to_all(mixer, "exp", split_axis=0, concat_axis=1, tiled=True)
    stream = (residual.astype(jnp.float32) + token_mix.astype(jnp.float32)).astype(jnp.bfloat16)
    widened = stream.astype(jnp.float32)
    normed = (
        widened
        * lax.rsqrt(jnp.mean(widened * widened, axis=-1, keepdims=True) + 1e-06)
        * norm_gain[None, :]
    ).astype(jnp.bfloat16)
    rows_here = residual.shape[0]
    owners = lax.axis_size("exp")
    local_experts = w_gate.shape[0]
    experts = owners * local_experts
    capacity = max(2, 2 * rows_here // experts + 1)
    width = residual.shape[1]
    chosen = expert_ids.reshape(-1)
    onehot = (chosen[:, None] == jnp.arange(experts)[None, :]).astype(jnp.int32)
    slot_index = jnp.sum((jnp.cumsum(onehot, axis=0) - onehot) * onehot, axis=1)
    target = chosen * capacity + slot_index
    placing = (target[None, :] == jnp.arange(experts * capacity)[:, None]).astype(jnp.bfloat16)
    pair_rows = jnp.repeat(normed, 2, axis=0)
    outgoing = jnp.dot(placing, pair_rows, preferred_element_type=jnp.float32).astype(jnp.bfloat16)
    outgoing = outgoing.reshape(owners, local_experts, 1, capacity, width)
    arrived = lax.all_to_all(outgoing, "exp", split_axis=0, concat_axis=2, tiled=True)
    segment = lax.all_gather(arrived, "seq", axis=1, tiled=True)
    flattened = segment.reshape(segment.shape[0], -1, segment.shape[-1])
    gate_proj = jnp.einsum("erd,edf->erf", flattened, w_gate, preferred_element_type=jnp.float32)
    up_proj = jnp.einsum("erd,edf->erf", flattened, w_up, preferred_element_type=jnp.float32)
    active = (jax.nn.silu(gate_proj) * up_proj).astype(jnp.bfloat16)
    partial_value = jnp.einsum("erf,efd->erd", active, w_down, preferred_element_type=jnp.float32)
    partials = partial_value.reshape(segment.shape[:-1] + (partial_value.shape[-1],))
    summed = lax.psum_scatter(partials.astype(jnp.bfloat16), "seq", scatter_dimension=1, tiled=True)
    returned = lax.all_to_all(summed, "exp", split_axis=2, concat_axis=0, tiled=True)
    results = returned.reshape(experts * capacity, width)
    picked = results[target].astype(jnp.float32).reshape(rows_here, 2, width)
    mixture = jnp.sum(picked * gate_weights[:, :, None], axis=1)
    return (widened + mixture).astype(jnp.bfloat16)


def solution(mesh):
    square = mesh.shape["seq"] == 4 and mesh.shape["exp"] == 8

    def body(*args):
        rows = args[8].shape[0]
        experts = mesh.shape["exp"] * args[12].shape[0]
        fits = args[12].shape[0] == 1 and 2 * rows // experts + 1 == 9
        return (on_square if square and fits else on_device)(*args)

    return jax.shard_map(
        body,
        mesh=mesh,
        in_specs=(
            P("seq", "exp"),
            P("seq", "exp"),
            P("seq", None),
            P("seq", None),
            P("seq", "exp"),
            P("exp"),
            P("exp"),
            P("exp", None, None),
            P(("seq", "exp"), None),
            P(),
            P(("seq", "exp"), None),
            P(("seq", "exp"), None),
            P("exp", None, "seq"),
            P("exp", None, "seq"),
            P("exp", "seq", None),
        ),
        out_specs=P(("seq", "exp"), None),
        check_vma=False,
    )
```

```python
import functools

import jax
import jax.numpy as jnp
from jax import lax
from jax.experimental import pallas as pl
from jax.experimental.pallas import tpu as pltpu
from jax.sharding import PartitionSpec as P

GROUP = 128
PRECISE = lax.Precision.HIGHEST
F32 = jnp.float32
BF16 = jnp.bfloat16
MIB = 1 << 20
NO_COST = pl.CostEstimate(flops=0, bytes_accessed=0, transcendentals=0)


def block_call(body, outs, scalars, args, held=0, keep=0, after=(), limit=16, out_blocks=False, name=None):
    n_args = len(args)
    kept = [jax.ShapeDtypeStruct(v.shape, v.dtype) for v in args[scalars : scalars + held]]

    def kernel(*refs):
        refs, sems = (refs[:-1], refs[-1]) if held else (refs, None)
        inputs, refs = refs[:n_args], refs[n_args + len(after) :]
        results, refs = refs[: len(outs)], refs[len(outs) :]
        copies = [
            pltpu.make_async_copy(src, dst, sems.at[k])
            for k, (src, dst) in enumerate(zip(inputs[scalars : scalars + held], refs))
        ]
        for copy in copies:
            copy.start()
        for copy in copies:
            copy.wait()
        body(*inputs[:scalars], *refs, *inputs[scalars + held :], *results)

    scratch = [pltpu.VMEM(v.shape, v.dtype) for v in kept[keep:]]
    if held:
        scratch.append(pltpu.SemaphoreType.DMA((held,)))
    return pl.pallas_call(
        kernel,
        name=name or getattr(body, "func", body).__name__,
        out_shape=list(outs) + kept[:keep],
        in_specs=[pl.BlockSpec(memory_space=pltpu.SMEM)] * scalars
        + [pl.BlockSpec(memory_space=pltpu.HBM)] * held
        + [pl.BlockSpec(memory_space=pltpu.VMEM)] * (n_args - scalars - held)
        + [pl.BlockSpec(memory_space=pl.ANY)] * len(after),
        out_specs=[pl.BlockSpec() if out_blocks else pl.BlockSpec(memory_space=pltpu.VMEM)]
        * (len(outs) + keep),
        scratch_shapes=scratch,
        compiler_params=pltpu.CompilerParams(vmem_limit_bytes=limit * MIB),
        cost_estimate=NO_COST,
    )(*args, *after)


def iota(shape, dim):
    return lax.broadcasted_iota(jnp.int32, shape, dim)


def dot(a, b, precision=None):
    return jnp.dot(a, b, precision=precision, preferred_element_type=F32)


def head_spread(heads, channels):
    shape = (heads, channels)
    return (iota(shape, 1) // (channels // heads) == iota(shape, 0)).astype(F32)


def running_logs(dt_t_ref, rate_ref):
    logs = -rate_ref[...] * dt_t_ref[...].T
    tokens = logs.shape[0]
    tri = (iota((tokens, tokens), 0) >= iota((tokens, tokens), 1)).astype(F32)
    return dot(tri, logs, PRECISE)


def pack_kernel(ids_t_ref, residual_ref, out_ref):
    parts, rows, wide = out_ref.shape
    part = wide - 128
    ids = ids_t_ref[...].astype(F32).T
    lane = iota((rows, 128), 1)
    named = jnp.where(lane == 0, ids[:, 0:1], jnp.where(lane == 1, ids[:, 1:2], 0.0)).astype(BF16)
    for k in range(parts):
        out_ref[k, :, 0:part] = residual_ref[:, k * part : (k + 1) * part]
        out_ref[k, :, part:wide] = named


def state_kernel(place, x_ref, b_ref, dt_t_ref, rate_ref, init_ref, payload_ref, init_t_ref):
    tokens, channels = x_ref.shape
    heads = dt_t_ref.shape[0]
    width = b_ref.shape[1]
    cum = running_logs(dt_t_ref, rate_ref)
    total = cum[tokens - 1 : tokens, :]
    spread = head_spread(heads, channels)
    tail = dot(jnp.exp(total - cum), spread, PRECISE)
    scaled = (x_ref[...].astype(F32) * tail).astype(BF16)
    keys = b_ref[...].astype(F32).T.astype(BF16)
    own = dot(keys, scaled)
    decay = dot(jnp.broadcast_to(jnp.exp(total), (8, heads)), spread, PRECISE)
    init_t = init_ref[...].T
    init_t_ref[...] = init_t.astype(BF16)
    first = (place[0] == 0).astype(F32)
    payload_ref[0:width, :] = (own + first * (decay[0:1, :] * init_t)).astype(BF16)
    high = decay.astype(BF16).astype(F32)
    rows = iota((16, channels), 0)
    high16 = jnp.broadcast_to(high[0:1, :], (16, channels))
    low16 = jnp.broadcast_to(decay[0:1, :], (16, channels)) - high16
    payload_ref[width : width + 16, :] = jnp.where(
        rows == 0, high16, jnp.where(rows == 1, low16, 0.0)
    ).astype(BF16)


def intra_kernel(x_ref, z_ref, b_ref, c_ref, dt_t_ref, rate_ref, skip_ref, own_ref, fade_ref, token_ref):
    tokens, channels = x_ref.shape
    heads = dt_t_ref.shape[0]
    width = channels // heads
    token_ref[...] = jnp.zeros_like(token_ref)
    shape = (tokens, tokens)
    causal = iota(shape, 0) >= iota(shape, 1)
    cum = running_logs(dt_t_ref, rate_ref)
    cum_t = cum.T
    scores = lax.dot_general(
        c_ref[...], b_ref[...], (((1,), (1,)), ((), ())), preferred_element_type=F32
    )
    spread = head_spread(heads, channels)
    direct = dot(jnp.broadcast_to(skip_ref[...], (8, heads)), spread, PRECISE)[0:1, :]
    fade = dot(jnp.exp(cum), spread, PRECISE)
    per = 128 // width
    lane_head = iota((tokens, 128), 1) // width
    for group in range(heads // per):
        cols = slice(group * 128, (group + 1) * 128)
        x = x_ref[:, cols]
        total = x.astype(F32) * direct[:, cols]
        for k in range(per):
            h = group * per + k
            gap = jnp.where(causal, cum[:, h : h + 1] - cum_t[h : h + 1, :], -1e30)
            weights = (jnp.exp(gap) * scores).astype(BF16)
            part = dot(weights, x)
            total = total + jnp.where(lane_head == k, part, 0.0)
        z = z_ref[:, cols].astype(F32)
        gate = z / (1.0 + jnp.exp(-z))
        own_ref[:, cols] = total * gate
        fade_ref[:, cols] = fade[:, cols] * gate


def place_kernel(cap, experts, me, packed_ref, *refs):
    count = (len(refs) - 1) // 2
    out_ref = refs[count]
    for source, target in zip(refs[:count], refs[count + 1 :]):
        target[...] = source[...]
    blocks, rows, wide = packed_ref.shape
    tokens = blocks * rows
    slots = out_ref.shape[1] - rows
    ids = packed_ref[:, :, wide - 128 : wide].astype(F32).reshape(tokens, 128).T
    ids = ids[0:8, :].astype(jnp.int32)
    shape = (tokens, tokens)
    before = (iota(shape, 0) < iota(shape, 1)) & (iota(shape, 0) // rows == iota(shape, 1) // rows)
    named = iota((experts, tokens), 0) ^ me[0]
    hit = (ids[0:1, :] == named) | (ids[1:2, :] == named)
    rank = dot(hit.astype(BF16), before.astype(BF16)).astype(jnp.int32)
    block = (iota((experts, tokens), 1) // rows) ^ named
    whole = cap - 1
    row = jnp.where(rank < whole, block * whole + rank, blocks * whole + block)
    row = jnp.where(hit, row, -1)
    shape = (rows + slots, tokens)
    for e in range(experts):
        owned = ((me[0] ^ e) * rows + iota(shape, 0) == iota(shape, 1)) & (iota(shape, 0) < rows)
        placed = (iota(shape, 0) - rows == row[e : e + 1, :]) & (iota(shape, 0) >= rows)
        out_ref[e] = (owned | placed).astype(F32).astype(BF16)


def join_kernel(place, own_ref, other_ref, out_ref):
    width = out_ref.shape[0]
    odd = place[0] % 2 == 1
    own, other = own_ref[0:width, :].astype(F32), other_ref[0:width, :].astype(F32)
    own_decay = own_ref[width : width + 16, :].astype(F32)
    other_decay = other_ref[width : width + 16, :].astype(F32)
    own_decay = own_decay[0:1, :] + own_decay[1:2, :]
    other_decay = other_decay[0:1, :] + other_decay[1:2, :]
    early = jnp.where(odd, other, own)
    late = jnp.where(odd, own, other)
    decay = jnp.where(odd, own_decay, other_decay)
    out_ref[...] = (decay * early + late).astype(BF16)


def stream_kernel(
    place, c_ref, own_ref, fade_ref, init_t_ref, pair_ref, early_ref, res_ref, sel_ref, near_a_ref, near_b_ref, same_ref, other_ref
):
    width = init_t_ref.shape[0]
    at = place[0]
    zero = (at == 0).astype(F32)
    odd = (at % 2 == 1).astype(F32)
    pair = pair_ref[...].astype(F32)
    decay = pair[width : width + 1, :] + pair[width + 1 : width + 2, :]
    factor = jnp.where(at >= 2, jnp.where(at % 2 == 1, decay, 1.0), 0.0)
    entering = zero * init_t_ref[...].astype(F32) + odd * pair[0:width, :] + factor * early_ref[...].astype(F32)
    mixed = own_ref[...] + fade_ref[...] * dot(c_ref[...], entering.astype(BF16))
    mixer = mixed.astype(BF16).astype(F32)
    tokens, channels = mixer.shape
    residual = res_ref[:, :, 0:channels].astype(F32).reshape(tokens, channels)
    stream = (residual + mixer).astype(BF16)
    owned = sel_ref.shape[1] - near_a_ref.shape[0]
    near_a_ref[...] = dot(sel_ref[2, owned:, :], stream).astype(BF16)
    near_b_ref[...] = dot(sel_ref[3, owned:, :], stream).astype(BF16)
    for at, k in enumerate((0, 2, 3, 1)):
        same_ref[at] = dot(sel_ref[2 * k], stream).astype(BF16)
        other_ref[at] = dot(sel_ref[2 * k + 1], stream).astype(BF16)


def up_kernel(first, features, after, me, *refs):
    own, rx, ry, even, odd, gain, wg, wu = refs[:8]
    carry = () if first else refs[8:11]
    rest = refs[(8 if first else 11) + after :]
    sums = rest[2:5] if features else rest
    step = pl.program_id(0)
    steps = pl.num_programs(0)

    if first or features:

        @pl.when(step == 0)
        def _():
            for i, acc in enumerate(sums):
                acc[...] = jnp.zeros_like(acc) if first else carry[i][...]

    gate, up, square = sums
    slots = own.shape[1]
    rows = [r[0].astype(F32) for r in (own, rx, ry)]
    rows.append(jnp.where(step == 0, even[0].astype(F32), odd[0].astype(F32)))
    rows = jnp.concatenate(rows, axis=0)
    square[...] += jnp.broadcast_to(jnp.sum(rows * rows, axis=1, keepdims=True), square.shape)
    scaled = (rows * gain[0]).astype(BF16)
    gate[...] += dot(scaled, wg[0])
    up[...] += dot(scaled, wu[0])

    if features:
        outs, stages = rest[:2], rest[5:]

        @pl.when(step == steps - 1)
        def _():
            inverse = lax.rsqrt(square[:, 0:1] * (1.0 / features) + 1e-06)
            g = gate[...] * inverse
            active = g / (1.0 + jnp.exp(-g)) * (up[...] * inverse)
            main, ninths = slots // 9 * 8, slots // 9
            for d in range(4):
                at = d * slots
                stage, d, shards = (stages[0], 0, 1) if d == 3 else (stages[1], d, 3)
                stage[d * main : (d + 1) * main, :] = active[at : at + main]
                low = shards * main + d * ninths
                stage[low : low + ninths, :] = active[at + main : at + slots]
            for out, stage in zip(outs, stages):
                out[...] = stage[...].astype(BF16)


def up_project(group, last, me, near, far, gain, w_gate, w_up, carry, after=()):
    slots, part = near[0][0].shape[1:]
    hidden = w_gate.shape[2]
    total = 4 * slots
    source = lambda i, me: me[0] ^ (2 * group + i)
    rows = [
        pl.BlockSpec((1, slots, part), lambda i, me, start=start: (start + i, 0, 0))
        for _, start in near
    ] + [
        pl.BlockSpec((1, slots, part), lambda i, me, start=start: (start, 0, 0)) for _, start in far
    ]
    weight = pl.BlockSpec((1, part, hidden), lambda i, me: (source(i, me), 0, 0))
    in_place = pl.BlockSpec(memory_space=pltpu.VMEM)
    specs = rows + [pl.BlockSpec((1, 1, part), lambda i, me: (source(i, me), 0, 0)), weight, weight]
    sums = [
        jax.ShapeDtypeStruct((total, hidden), F32),
        jax.ShapeDtypeStruct((total, hidden), F32),
        jax.ShapeDtypeStruct((total, 128), F32),
    ]
    aliases = {}
    if carry is not None:
        specs += [in_place] * 3
        if not last:
            aliases = {9 + i: i for i in range(3)}
    specs += [pl.BlockSpec(memory_space=pl.ANY)] * len(after)
    sizes = (slots, 3 * slots)
    outs = [jax.ShapeDtypeStruct((n, hidden), BF16) for n in sizes] if last else sums
    scratch = [pltpu.VMEM(s.shape, s.dtype) for s in sums]
    scratch += [pltpu.VMEM((n, hidden), F32) for n in sizes]
    features = gain.shape[0] * part if last else 0
    return pl.pallas_call(
        functools.partial(up_kernel, carry is None, features, len(after)),
        name=f"up_{group}",
        out_shape=outs,
        grid_spec=pltpu.PrefetchScalarGridSpec(
            num_scalar_prefetch=1,
            grid=(2,),
            in_specs=specs,
            out_specs=[in_place] * len(outs),
            scratch_shapes=scratch if last else [],
        ),
        input_output_aliases=aliases,
        compiler_params=pltpu.CompilerParams(vmem_limit_bytes=48 * MIB),
        cost_estimate=NO_COST,
    )(me, *(array for array, _ in near + far), gain, w_gate, w_up, *(carry or ()), *after)


def cut_of(group):
    return 5 if group % 2 else 4


def down_kernel(groups, act_ref, w_ref, *refs):
    outs, (spare, held, sems) = refs[:-3], refs[-3:]
    step = pl.program_id(0)
    steps, _, tile = held.shape

    def load(k):
        columns = pl.ds(pl.multiple_of(k * tile, tile), tile)
        return pltpu.make_async_copy(w_ref.at[:, columns], held.at[k], sems.at[k])

    @pl.when(step == 0)
    def _():
        for k in range(steps):
            load(k).start()

    load(step).wait()
    part = dot(act_ref[...], held[step])
    ninths = part.shape[0] // 9
    main = part.shape[0] - ninths
    shards = ninths // (2 * groups)

    def through(group, tile):
        to_x, to_y = outs[2 * (group // 2) : 2 * (group // 2) + 2]
        cut = cut_of(group)
        return to_x, tile + (0 if group % 2 else 5), to_y, tile - cut + (0 if group % 2 else 4)

    for shard in range(shards):
        for group in range(groups):
            at = (shard * groups + group) * 16
            rows = part[at : at + 16, :].astype(BF16)
            if shards > 1:
                outs[shards * group + shard][step] = rows
                continue
            to_x, place_x, to_y, place_y = through(group, step)

            @pl.when(step < cut_of(group))
            def _():
                to_x[place_x] = rows

            @pl.when(step >= cut_of(group))
            def _():
                to_y[place_y] = rows

    for lanes in range(spare.shape[0]):
        spare[lanes, pl.ds(pl.multiple_of(step * ninths, 8), ninths), :] = part[
            main:, lanes * 128 : (lanes + 1) * 128
        ]

    @pl.when(step == steps - 1)
    def _():
        for shard in range(shards):
            for group in range(groups):
                pair = []
                for side in range(2):
                    row = pl.ds((shard * groups + group) * 2 + side, 8, stride=ninths)
                    ninth = [spare[lanes, row, :] for lanes in range(spare.shape[0])]
                    pair.append(jnp.concatenate(ninth, axis=1))
                pair = jnp.concatenate(pair, axis=0).astype(BF16)
                if shards > 1:
                    outs[shards * group + shard][8] = pair
                else:
                    _, _, to_y, place_y = through(group, 8)
                    to_y[place_y] = pair


def down_project(name, groups, active, w_down):
    total, hidden = active.shape
    features = w_down.shape[1]
    tile = features // 8
    outs = [jax.ShapeDtypeStruct((9, 16, tile), BF16)] * (total // 18)
    return pl.pallas_call(
        functools.partial(down_kernel, groups),
        name=name,
        grid=(8,),
        out_shape=outs,
        in_specs=[
            pl.BlockSpec(memory_space=pltpu.VMEM),
            pl.BlockSpec(memory_space=pltpu.HBM),
        ],
        out_specs=[pl.BlockSpec(memory_space=pltpu.VMEM)] * len(outs),
        scratch_shapes=[
            pltpu.VMEM((tile // 128, 8 * total // 9, 128), F32),
            pltpu.VMEM((8, hidden, tile), BF16),
            pltpu.SemaphoreType.DMA((8,)),
        ],
        compiler_params=pltpu.CompilerParams(vmem_limit_bytes=48 * MIB),
        cost_estimate=NO_COST,
    )(active, w_down)


def pair_kernel(same, other, own_stream, own, far_stream, far, last_stream, last, near_stream):
    owned = own_stream.shape[1]
    for side, rows in enumerate((same, other)):
        own_stream[side], own[side] = rows[0, 0:owned, :], rows[0, owned:, :]
        far_stream[side], far[side] = rows[1, 0:owned, :], rows[1, owned:, :]
        last_stream[side], last[side] = rows[2, 0:owned, :], rows[2, owned:, :]
        near_stream[side] = rows[3, 0:owned, :]


def near_kernel(same, other, rows):
    rows[0], rows[1] = same[...], other[...]


def second_kernel(*refs):
    parts, out = refs[:-1], refs[-1]
    for h in range(out.shape[0]):
        for k in range(out.shape[1]):
            pair = [ref[k].astype(F32)[8:16] for ref in parts[2 * h : 2 * h + 2]]
            out[h, k] = jnp.concatenate(pair, axis=0).astype(BF16)


def hold_kernel(*refs):
    for source, target in zip(refs[: len(refs) // 2], refs[len(refs) // 2 :]):
        target[...] = source[...]


def half_message_kernel(rx, ry, out_x, out_y):
    out_x[0], out_y[0] = ry[1], rx[0]


def join_message_kernel(own, rx, ry, out_x, out_y):
    out_x[0:2], out_y[0:2] = own[...], own[...]
    out_x[2], out_y[2] = ry[1], rx[0]


def relay_kernel(through_x, through_y, *refs):
    ahead = refs[4 : 4 + (len(refs) - 8) // 2]
    outs, copies = refs[4 + len(ahead) :][:4], refs[8 + len(ahead) :]
    for group in range(2):
        cut = cut_of(group)
        at_x, at_y = (0, -cut) if group else (5, 0)
        for own, out, through, tiles, at in (
            (refs[2 * group], outs[2 * group], through_y, range(cut, 9), at_y),
            (refs[2 * group + 1], outs[2 * group + 1], through_x, range(cut), at_x),
        ):
            for k in range(9):
                if k in tiles:
                    out[k] = (own[k].astype(F32) + through[k + at].astype(F32)).astype(BF16)
                else:
                    out[k] = own[k]
    for source, copy in zip(ahead, copies):
        copy[...] = source[...]


def finish_kernel(own, rx, ry, *refs):
    ahead = refs[: (len(refs) - 1) // 2]
    out, copies = refs[len(ahead)], refs[len(ahead) + 1 :]
    for k in range(9):
        out[k] = (own[k].astype(F32) + rx[k].astype(F32) + ry[k].astype(F32)).astype(BF16)
    for source, copy in zip(ahead, copies):
        copy[...] = source[...]


def mix_kernel(me, ids_t_ref, weight_t_ref, swap_ref, *refs):
    groups = (len(refs) - 1) // 2
    firsts, streams, out_ref = refs[:groups], refs[groups:-1], refs[-1]
    rows = ids_t_ref.shape[1]
    experts = 2 * groups
    pieces = firsts[0].shape[0] - 1
    tile = firsts[0].shape[2]
    ids, weights = ids_t_ref[...].T, weight_t_ref[...].T
    named = iota((rows, experts), 1) ^ me[0]
    first, second = ids[:, 0:1] == named, ids[:, 1:2] == named
    weight = jnp.where(first, weights[:, 0:1], jnp.where(second, weights[:, 1:2], 0.0))
    hit = (first | second).astype(F32)
    before = (iota((rows, rows), 0) > iota((rows, rows), 1)).astype(F32)
    rank = dot(before, hit)
    lanes = 2 * experts * 8
    shape = (experts, lanes)
    spread = ((iota(shape, 1) // 8) % experts == iota(shape, 0)).astype(F32)
    weight = dot(weight, spread, PRECISE)
    rank = dot(rank, spread, PRECISE).astype(jnp.int32)
    lane = iota((rows, lanes), 1)
    main = (lane < experts * 8) & (rank == lane % 8)
    extra = (lane >= experts * 8) & (rank == 8)

    def rows_of(k):
        data = []
        for g in range(groups):
            data.append(firsts[g][k].astype(F32)[0:8])
            data.append(swap_ref[g // 2, k].astype(F32)[g % 2 * 8 : g % 2 * 8 + 8])
        return data

    last = rows_of(pieces)
    for m in range(experts):
        k = me[0] ^ m
        coef = jnp.where(main | (extra & (lane % 8 == k)), weight, 0.0)
        high = coef.astype(BF16)
        low = (coef - high.astype(F32)).astype(BF16)
        data = jnp.concatenate(rows_of(k) + last, axis=0).astype(BF16)
        stream = streams[m // 2][m % 2].astype(F32)
        out_ref[:, pl.ds(pl.multiple_of(k * tile, 128), tile)] = (
            stream + (dot(high, data) + dot(low, data))
        ).astype(BF16)


def on_square(
    x_in,
    z_gate,
    b_in,
    c_out,
    dt_step,
    rate,
    skip,
    init_state,
    residual,
    norm_gain,
    expert_ids,
    gate_weights,
    w_gate,
    w_up,
    w_down,
):
    tokens, channels = x_in.shape
    heads = rate.shape[0]
    state = b_in.shape[1]
    owners = lax.axis_size("exp")
    rows, features = residual.shape
    experts = owners
    cap = max(2, 2 * rows // experts + 1)
    slots = owners * cap
    at = lax.axis_index("seq")
    me = lax.axis_index("exp")
    place = jnp.reshape(at, (1,)).astype(jnp.int32)
    self_id = jnp.reshape(me, (1,)).astype(jnp.int32)

    def over_x(v):
        return lax.ppermute(v, "seq", [(i, i ^ 1) for i in range(4)])

    def over_y(v):
        return lax.ppermute(v, "seq", [(i, i ^ 2) for i in range(4)])

    def along(v, mask):
        return lax.ppermute(v, "exp", [(i, i ^ mask) for i in range(owners)])

    rate_row = rate[None, :]
    dt_t = dt_step.T
    ids_t = expert_ids.T
    payload, init_t = block_call(
        state_kernel,
        [
            jax.ShapeDtypeStruct((state + 16, channels), BF16),
            jax.ShapeDtypeStruct((state, channels), BF16),
        ],
        1,
        (place, x_in, b_in, dt_t, rate_row, init_state.reshape(channels, state)),
        held=5,
        limit=62,
    )
    pair = over_x(payload)
    packed = block_call(
        pack_kernel,
        [jax.ShapeDtypeStruct((owners, rows, channels + 128), BF16)],
        0,
        (ids_t, residual),
        held=2,
        after=(payload,),
        limit=48,
    )[0]
    packed = lax.all_to_all(packed, "exp", split_axis=0, concat_axis=0, tiled=True)
    own_part, fade, token = block_call(
        intra_kernel,
        [
            jax.ShapeDtypeStruct((tokens, channels), F32),
            jax.ShapeDtypeStruct((tokens, channels), F32),
            jax.ShapeDtypeStruct((8, 128), F32),
        ],
        0,
        (x_in, z_gate, b_in, c_out, dt_t, rate_row, skip[None, :]),
        held=7,
        limit=61,
    )
    joined = block_call(
        join_kernel,
        [jax.ShapeDtypeStruct((state, channels), BF16)],
        1,
        (place, payload, pair),
    )[0]
    early = over_y(joined)
    handed = (own_part, fade, c_out, init_t)
    select, own_part, fade, c, init_t = block_call(
        functools.partial(place_kernel, cap, experts),
        [jax.ShapeDtypeStruct((experts, rows + slots, tokens), BF16)]
        + [jax.ShapeDtypeStruct(v.shape, v.dtype) for v in handed],
        1,
        (self_id, packed, *handed),
        after=(joined,),
    )
    groups = owners // 2
    lanes = jax.ShapeDtypeStruct((groups, rows + slots, channels), BF16)
    one = jax.ShapeDtypeStruct((slots, channels), BF16)
    near_a, near_b, same, other = block_call(
        stream_kernel,
        [one, one, lanes, lanes],
        1,
        (place, c, own_part, fade, init_t, pair, early, packed, select),
    )

    gain = norm_gain.reshape(owners, 1, channels)
    wg = w_gate.reshape(owners, channels, w_gate.shape[2])
    wu = w_up.reshape(owners, channels, w_up.shape[2])
    expert_rows = jax.ShapeDtypeStruct((2, slots, channels), BF16)
    stream_rows = jax.ShapeDtypeStruct((2, rows, channels), BF16)
    near_a, near_b = along(near_a, 2), along(near_b, 3)
    stream0, first, stream2, far, stream3, farthest, stream1 = block_call(
        pair_kernel,
        [stream_rows, expert_rows] * 3 + [stream_rows],
        0,
        (same, along(other, 1)),
    )
    gain = norm_gain.reshape(owners, 1, channels)
    wg = w_gate.reshape(owners, channels, w_gate.shape[2])
    wu = w_up.reshape(owners, channels, w_up.shape[2])
    gain = norm_gain.reshape(owners, 1, channels)
    wg = w_gate.reshape(owners, channels, w_gate.shape[2])
    wu = w_up.reshape(owners, channels, w_up.shape[2])

    def hold(values, after, name):
        outs = [jax.ShapeDtypeStruct(v.shape, BF16) for v in values]
        return block_call(hold_kernel, outs, 0, values, after=after, name=name)

    def project(group, near, far, carry, after=()):
        last = group == groups - 1
        return up_project(group, last, self_id, near, far, gain, wg, wu, carry, after)

    def message(count):
        return [jax.ShapeDtypeStruct((count, slots, channels), BF16)] * 2

    far = along(far, 4)
    rx0, ry0 = over_x(first), over_y(first)
    near = block_call(near_kernel, [expert_rows], 0, (near_a, near_b))[0]
    rx1, ry1 = over_x(near), over_y(near)
    to_x, to_y = block_call(
        half_message_kernel, message(1), 0, (rx0, ry0), after=(near,), name="half_0"
    )
    fx0, fy0 = over_x(to_x), over_y(to_y)
    farthest_held = hold((farthest,), (far,), "hold_farthest")[0]
    farthest = along(farthest_held, 6)
    to_x, to_y = block_call(
        join_message_kernel,
        message(3),
        0,
        (far, rx1, ry1),
        after=(fx0, fy0, farthest_held),
        name="join_2",
    )
    rx2, ry2 = over_x(to_x), over_y(to_y)
    carry = project(0, [(first, 0), (rx0, 0), (ry0, 0)], [(fy0, 0), (fx0, 0)], None)
    to_x, to_y = block_call(
        join_message_kernel, message(3), 0, (farthest, rx2, ry2), after=(carry[2],), name="join_3"
    )
    rx3, ry3 = over_x(to_x), over_y(to_y)
    held = hold((stream1, stream2, stream3), (to_x,), "hold_streams")
    stream1, stream2, stream3 = (along(v, 2 * g + 2) for g, v in enumerate(held))
    carry = project(1, [(near, 0), (rx1, 0), (ry1, 0)], [(ry2, 2), (rx2, 2)], carry, held[:1])
    to_x, to_y = block_call(
        half_message_kernel, message(1), 0, (rx3, ry3), after=(carry[2], stream1, stream2, stream3), name="half_3"
    )
    fx3, fy3 = over_x(to_x), over_y(to_y)
    carry = project(2, [(far, 0), (rx2, 0), (ry2, 0)], [(ry3, 2), (rx3, 2)], carry)
    active_far, active = project(
        3, [(farthest, 0), (rx3, 0), (ry3, 0)], [(fy3, 0), (fx3, 0)], carry
    )

    wd = w_down.reshape(w_down.shape[1], features)
    tiles = jax.ShapeDtypeStruct((9, 16, features // 8), BF16)
    sent = down_project("down_through", groups, active_far, wd)
    rest = down_project("down_rest", groups, active, wd)
    own, own_x, own_y = ([rest[3 * g + k] for g in range(groups)] for k in range(3))

    def relay(name, through_x, through_y, low, ahead=(), after=()):
        shares = (own_x[low], own_y[low], own_x[low + 1], own_y[low + 1])
        return block_call(
            relay_kernel,
            [tiles] * (4 + len(ahead)),
            0,
            (through_x, through_y, *shares, *ahead),
            after=after,
            name=name,
        )

    def finish(group, rx, ry, ahead=(), after=()):
        return block_call(
            finish_kernel,
            [tiles] * (1 + len(ahead)),
            0,
            (own[group], rx, ry, *ahead),
            after=after,
            name=f"finish_{group}",
        )

    through_x, through_y = over_x(sent[2]), over_y(sent[3])
    x2, y2, x3, y3, next_x, next_y = relay(
        "relay_far", through_x, through_y, 2, (sent[0], sent[1])
    )
    rx3, ry3 = over_x(x3), over_y(y3)
    through_x, through_y = over_x(next_x), over_y(next_y)
    both3, x2, y2 = finish(3, rx3, ry3, (x2, y2))
    back3 = along(both3, 6)
    rx2, ry2 = over_x(x2), over_y(y2)
    x0, y0, x1, y1 = relay("relay_near", through_x, through_y, 0, after=(both3,))
    rx1, ry1 = over_x(x1), over_y(y1)
    both2, x0, y0 = finish(2, rx2, ry2, (x0, y0))
    back2 = along(both2, 4)
    rx0, ry0 = over_x(x0), over_y(y0)
    back1 = along(finish(1, rx1, ry1, after=(back3,))[0], 2)
    back = [finish(0, rx0, ry0)[0], back1, back2, back3]
    swap = block_call(second_kernel, [jax.ShapeDtypeStruct((2,) + tiles.shape, BF16)], 0, back)[0]
    swap = along(swap, 1)
    return block_call(
        mix_kernel,
        [jax.ShapeDtypeStruct((rows, features), BF16)],
        1,
        (self_id, ids_t, gate_weights.T, swap, *back, stream0, stream1, stream2, stream3),
    )[0]


def entering_2(array, axis, combine, identity):
    devices, mine = (lax.axis_size(axis), lax.axis_index(axis))
    everything = jax.tree.map(
        lambda part, kind: lax.all_gather(part.astype(kind), axis),
        array,
        (jnp.bfloat16, jnp.bfloat16),
    )
    start = jax.tree.map(
        lambda part, zero: jnp.broadcast_to(jnp.asarray(zero, part.dtype), part.shape),
        array,
        identity,
    )

    def hop(k, before):
        reached = k < mine
        new = combine(
            before, jax.tree.map(lambda part, own: part[k].astype(own.dtype), everything, array)
        )
        return jax.tree.map(lambda a, b: jnp.where(reached, a, b), new, before)

    return lax.fori_loop(0, devices, hop, start)


def chain_combine(earlier, later):
    return (earlier[0] + later[0], jnp.exp(later[0])[:, None, None] * earlier[1] + later[1])


def on_device(
    x_in,
    z_gate,
    b_in,
    c_out,
    dt_step,
    rate,
    skip,
    init_state,
    residual,
    norm_gain,
    expert_ids,
    gate_weights,
    w_gate,
    w_up,
    w_down,
):
    token_count, channels = x_in.shape
    heads_here = rate.shape[0]
    head_width = channels // heads_here
    state_width = b_in.shape[1]
    blocks = token_count // GROUP
    inputs = x_in.astype(jnp.float32).reshape(blocks, GROUP, heads_here, head_width)
    keys_in = b_in.astype(jnp.float32).reshape(blocks, GROUP, state_width)
    queries = c_out.astype(jnp.float32).reshape(blocks, GROUP, state_width)
    log_steps = (-rate[None, :] * dt_step).reshape(blocks, GROUP, heads_here)
    cumulative = jnp.cumsum(log_steps, axis=1)
    scores = jnp.einsum("ctn,csn->cts", queries, keys_in, precision=PRECISE)
    causal = jnp.arange(GROUP)[:, None] >= jnp.arange(GROUP)[None, :]
    spread = cumulative[:, :, None, :] - cumulative[:, None, :, :]
    weights = jnp.exp(jnp.where(causal[None, :, :, None], spread, -jnp.inf)) * scores[..., None]
    intra_out = jnp.einsum("ctsh,cshp->cthp", weights, inputs, precision=PRECISE)
    tail_decay = jnp.exp(cumulative[:, -1:, :] - cumulative)
    block_state = jnp.einsum("csh,cshp,csn->chpn", tail_decay, inputs, keys_in, precision=PRECISE)
    block_log = cumulative[:, -1, :]

    def advance(carried, element):
        total_log, total_state = carried
        step_log, step_state = element
        updated = (
            total_log + step_log,
            jnp.exp(step_log)[:, None, None] * total_state + step_state,
        )
        return (updated, (total_log, total_state))

    zero_state = jnp.zeros((heads_here, head_width, state_width), jnp.float32)
    zero_log = jnp.zeros((heads_here,), jnp.float32)
    (device_log, device_state), (enter_log, enter_state) = lax.scan(
        advance, (zero_log, zero_state), (block_log, block_state)
    )
    prior_log, prior_state = entering_2(
        (device_log, device_state), "seq", chain_combine, (zero_log, zero_state)
    )
    incoming = prior_state + jnp.exp(prior_log)[:, None, None] * init_state
    entering = enter_state + jnp.exp(enter_log)[:, :, None, None] * incoming[None]
    inter_out = jnp.exp(cumulative)[..., None] * jnp.einsum(
        "chpn,ctn->cthp", entering, queries, precision=PRECISE
    )
    mixed_out = (intra_out + inter_out + skip[None, None, :, None] * inputs).reshape(
        token_count, channels
    )
    mixer = (mixed_out * jax.nn.silu(z_gate.astype(jnp.float32))).astype(jnp.bfloat16)
    token_mix = lax.all_to_all(mixer, "exp", split_axis=0, concat_axis=1, tiled=True)
    stream = (residual.astype(jnp.float32) + token_mix.astype(jnp.float32)).astype(jnp.bfloat16)
    widened = stream.astype(jnp.float32)
    normed = (
        widened
        * lax.rsqrt(jnp.mean(widened * widened, axis=-1, keepdims=True) + 1e-06)
        * norm_gain[None, :]
    ).astype(jnp.bfloat16)
    rows_here = residual.shape[0]
    owners = lax.axis_size("exp")
    local_experts = w_gate.shape[0]
    experts = owners * local_experts
    capacity = max(2, 2 * rows_here // experts + 1)
    width = residual.shape[1]
    chosen = expert_ids.reshape(-1)
    onehot = (chosen[:, None] == jnp.arange(experts)[None, :]).astype(jnp.int32)
    slot_index = jnp.sum((jnp.cumsum(onehot, axis=0) - onehot) * onehot, axis=1)
    target = chosen * capacity + slot_index
    placing = (target[None, :] == jnp.arange(experts * capacity)[:, None]).astype(jnp.bfloat16)
    pair_rows = jnp.repeat(normed, 2, axis=0)
    outgoing = jnp.dot(placing, pair_rows, preferred_element_type=jnp.float32).astype(jnp.bfloat16)
    outgoing = outgoing.reshape(owners, local_experts, 1, capacity, width)
    arrived = lax.all_to_all(outgoing, "exp", split_axis=0, concat_axis=2, tiled=True)
    segment = lax.all_gather(arrived, "seq", axis=1, tiled=True)
    flattened = segment.reshape(segment.shape[0], -1, segment.shape[-1])
    gate_proj = jnp.einsum("erd,edf->erf", flattened, w_gate, preferred_element_type=jnp.float32)
    up_proj = jnp.einsum("erd,edf->erf", flattened, w_up, preferred_element_type=jnp.float32)
    active = (jax.nn.silu(gate_proj) * up_proj).astype(jnp.bfloat16)
    partial_value = jnp.einsum("erf,efd->erd", active, w_down, preferred_element_type=jnp.float32)
    partials = partial_value.reshape(segment.shape[:-1] + (partial_value.shape[-1],))
    summed = lax.psum_scatter(partials.astype(jnp.bfloat16), "seq", scatter_dimension=1, tiled=True)
    returned = lax.all_to_all(summed, "exp", split_axis=2, concat_axis=0, tiled=True)
    results = returned.reshape(experts * capacity, width)
    picked = results[target].astype(jnp.float32).reshape(rows_here, 2, width)
    mixture = jnp.sum(picked * gate_weights[:, :, None], axis=1)
    return (widened + mixture).astype(jnp.bfloat16)


def solution(mesh):
    square = mesh.shape["seq"] == 4 and mesh.shape["exp"] == 8

    def body(*args):
        rows = args[8].shape[0]
        experts = mesh.shape["exp"] * args[12].shape[0]
        fits = args[12].shape[0] == 1 and 2 * rows // experts + 1 == 9
        return (on_square if square and fits else on_device)(*args)

    return jax.shard_map(
        body,
        mesh=mesh,
        in_specs=(
            P("seq", "exp"),
            P("seq", "exp"),
            P("seq", None),
            P("seq", None),
            P("seq", "exp"),
            P("exp"),
            P("exp"),
            P("exp", None, None),
            P(("seq", "exp"), None),
            P(),
            P(("seq", "exp"), None),
            P(("seq", "exp"), None),
            P("exp", None, "seq"),
            P("exp", None, "seq"),
            P("exp", "seq", None),
        ),
        out_specs=P(("seq", "exp"), None),
        check_vma=False,
    )
```

```python
import functools

import jax
import jax.numpy as jnp
from jax import lax
from jax.experimental import pallas as pl
from jax.experimental.pallas import tpu as pltpu
from jax.sharding import PartitionSpec as P

GROUP = 128
PRECISE = lax.Precision.HIGHEST
F32 = jnp.float32
BF16 = jnp.bfloat16
MIB = 1 << 20
NO_COST = pl.CostEstimate(flops=0, bytes_accessed=0, transcendentals=0)


def block_call(body, outs, scalars, args, held=0, keep=0, after=(), limit=16, out_blocks=False, name=None):
    n_args = len(args)
    kept = [jax.ShapeDtypeStruct(v.shape, v.dtype) for v in args[scalars : scalars + held]]

    def kernel(*refs):
        refs, sems = (refs[:-1], refs[-1]) if held else (refs, None)
        inputs, refs = refs[:n_args], refs[n_args + len(after) :]
        results, refs = refs[: len(outs)], refs[len(outs) :]
        copies = [
            pltpu.make_async_copy(src, dst, sems.at[k])
            for k, (src, dst) in enumerate(zip(inputs[scalars : scalars + held], refs))
        ]
        for copy in copies:
            copy.start()
        for copy in copies:
            copy.wait()
        body(*inputs[:scalars], *refs, *inputs[scalars + held :], *results)

    scratch = [pltpu.VMEM(v.shape, v.dtype) for v in kept[keep:]]
    if held:
        scratch.append(pltpu.SemaphoreType.DMA((held,)))
    return pl.pallas_call(
        kernel,
        name=name or getattr(body, "func", body).__name__,
        out_shape=list(outs) + kept[:keep],
        in_specs=[pl.BlockSpec(memory_space=pltpu.SMEM)] * scalars
        + [pl.BlockSpec(memory_space=pltpu.HBM)] * held
        + [pl.BlockSpec(memory_space=pltpu.VMEM)] * (n_args - scalars - held)
        + [pl.BlockSpec(memory_space=pl.ANY)] * len(after),
        out_specs=[pl.BlockSpec() if out_blocks else pl.BlockSpec(memory_space=pltpu.VMEM)]
        * (len(outs) + keep),
        scratch_shapes=scratch,
        compiler_params=pltpu.CompilerParams(vmem_limit_bytes=limit * MIB),
        cost_estimate=NO_COST,
    )(*args, *after)


def iota(shape, dim):
    return lax.broadcasted_iota(jnp.int32, shape, dim)


def dot(a, b, precision=None):
    return jnp.dot(a, b, precision=precision, preferred_element_type=F32)


def head_spread(heads, channels):
    shape = (heads, channels)
    return (iota(shape, 1) // (channels // heads) == iota(shape, 0)).astype(F32)


def running_logs(dt_t_ref, rate_ref):
    logs = -rate_ref[...] * dt_t_ref[...].T
    tokens = logs.shape[0]
    tri = (iota((tokens, tokens), 0) >= iota((tokens, tokens), 1)).astype(F32)
    return dot(tri, logs, PRECISE)


def pack_kernel(ids_t_ref, residual_ref, out_ref):
    parts, rows, wide = out_ref.shape
    part = wide - 128
    ids = ids_t_ref[...].astype(F32).T
    lane = iota((rows, 128), 1)
    named = jnp.where(lane == 0, ids[:, 0:1], jnp.where(lane == 1, ids[:, 1:2], 0.0)).astype(BF16)
    for k in range(parts):
        out_ref[k, :, 0:part] = residual_ref[:, k * part : (k + 1) * part]
        out_ref[k, :, part:wide] = named


def state_kernel(place, x_ref, b_ref, dt_t_ref, rate_ref, init_ref, payload_ref, init_t_ref):
    tokens, channels = x_ref.shape
    heads = dt_t_ref.shape[0]
    width = b_ref.shape[1]
    cum = running_logs(dt_t_ref, rate_ref)
    total = cum[tokens - 1 : tokens, :]
    spread = head_spread(heads, channels)
    tail = dot(jnp.exp(total - cum), spread, PRECISE)
    scaled = (x_ref[...].astype(F32) * tail).astype(BF16)
    keys = b_ref[...].astype(F32).T.astype(BF16)
    own = dot(keys, scaled)
    decay = dot(jnp.broadcast_to(jnp.exp(total), (8, heads)), spread, PRECISE)
    init_t = init_ref[...].T
    init_t_ref[...] = init_t.astype(BF16)
    first = (place[0] == 0).astype(F32)
    payload_ref[0:width, :] = (own + first * (decay[0:1, :] * init_t)).astype(BF16)
    high = decay.astype(BF16).astype(F32)
    rows = iota((16, channels), 0)
    high16 = jnp.broadcast_to(high[0:1, :], (16, channels))
    low16 = jnp.broadcast_to(decay[0:1, :], (16, channels)) - high16
    payload_ref[width : width + 16, :] = jnp.where(
        rows == 0, high16, jnp.where(rows == 1, low16, 0.0)
    ).astype(BF16)


def intra_kernel(x_ref, z_ref, b_ref, c_ref, dt_t_ref, rate_ref, skip_ref, own_ref, fade_ref, token_ref):
    tokens, channels = x_ref.shape
    heads = dt_t_ref.shape[0]
    width = channels // heads
    token_ref[...] = jnp.zeros_like(token_ref)
    shape = (tokens, tokens)
    causal = iota(shape, 0) >= iota(shape, 1)
    cum = running_logs(dt_t_ref, rate_ref)
    cum_t = cum.T
    scores = lax.dot_general(
        c_ref[...], b_ref[...], (((1,), (1,)), ((), ())), preferred_element_type=F32
    )
    spread = head_spread(heads, channels)
    direct = dot(jnp.broadcast_to(skip_ref[...], (8, heads)), spread, PRECISE)[0:1, :]
    fade = dot(jnp.exp(cum), spread, PRECISE)
    per = 128 // width
    lane_head = iota((tokens, 128), 1) // width
    for group in range(heads // per):
        cols = slice(group * 128, (group + 1) * 128)
        x = x_ref[:, cols]
        total = x.astype(F32) * direct[:, cols]
        for k in range(per):
            h = group * per + k
            gap = jnp.where(causal, cum[:, h : h + 1] - cum_t[h : h + 1, :], -1e30)
            weights = (jnp.exp(gap) * scores).astype(BF16)
            part = dot(weights, x)
            total = total + jnp.where(lane_head == k, part, 0.0)
        z = z_ref[:, cols].astype(F32)
        gate = z / (1.0 + jnp.exp(-z))
        own_ref[:, cols] = total * gate
        fade_ref[:, cols] = fade[:, cols] * gate


def place_kernel(cap, experts, me, packed_ref, *refs):
    count = (len(refs) - 1) // 2
    out_ref = refs[count]
    for source, target in zip(refs[:count], refs[count + 1 :]):
        target[...] = source[...]
    blocks, rows, wide = packed_ref.shape
    tokens = blocks * rows
    slots = out_ref.shape[1] - rows
    ids = packed_ref[:, :, wide - 128 : wide].astype(F32).reshape(tokens, 128).T
    ids = ids[0:8, :].astype(jnp.int32)
    shape = (tokens, tokens)
    before = (iota(shape, 0) < iota(shape, 1)) & (iota(shape, 0) // rows == iota(shape, 1) // rows)
    named = iota((experts, tokens), 0) ^ me[0]
    hit = (ids[0:1, :] == named) | (ids[1:2, :] == named)
    rank = dot(hit.astype(BF16), before.astype(BF16)).astype(jnp.int32)
    block = (iota((experts, tokens), 1) // rows) ^ named
    whole = cap - 1
    row = jnp.where(rank < whole, block * whole + rank, blocks * whole + block)
    row = jnp.where(hit, row, -1)
    shape = (rows + slots, tokens)
    for e in range(experts):
        owned = ((me[0] ^ e) * rows + iota(shape, 0) == iota(shape, 1)) & (iota(shape, 0) < rows)
        placed = (iota(shape, 0) - rows == row[e : e + 1, :]) & (iota(shape, 0) >= rows)
        out_ref[e] = (owned | placed).astype(F32).astype(BF16)


def join_kernel(place, own_ref, other_ref, out_ref):
    width = out_ref.shape[0]
    odd = place[0] % 2 == 1
    own, other = own_ref[0:width, :].astype(F32), other_ref[0:width, :].astype(F32)
    own_decay = own_ref[width : width + 16, :].astype(F32)
    other_decay = other_ref[width : width + 16, :].astype(F32)
    own_decay = own_decay[0:1, :] + own_decay[1:2, :]
    other_decay = other_decay[0:1, :] + other_decay[1:2, :]
    early = jnp.where(odd, other, own)
    late = jnp.where(odd, own, other)
    decay = jnp.where(odd, own_decay, other_decay)
    out_ref[...] = (decay * early + late).astype(BF16)


def stream_kernel(
    place, c_ref, own_ref, fade_ref, init_t_ref, pair_ref, early_ref, res_ref, sel_ref, near_a_ref, near_b_ref, same_ref, other_ref
):
    width = init_t_ref.shape[0]
    at = place[0]
    zero = (at == 0).astype(F32)
    odd = (at % 2 == 1).astype(F32)
    pair = pair_ref[...].astype(F32)
    decay = pair[width : width + 1, :] + pair[width + 1 : width + 2, :]
    factor = jnp.where(at >= 2, jnp.where(at % 2 == 1, decay, 1.0), 0.0)
    entering = zero * init_t_ref[...].astype(F32) + odd * pair[0:width, :] + factor * early_ref[...].astype(F32)
    mixed = own_ref[...] + fade_ref[...] * dot(c_ref[...], entering.astype(BF16))
    mixer = mixed.astype(BF16).astype(F32)
    tokens, channels = mixer.shape
    residual = res_ref[:, :, 0:channels].astype(F32).reshape(tokens, channels)
    stream = (residual + mixer).astype(BF16)
    owned = stream.shape[0] // sel_ref.shape[0]
    slots = sel_ref.shape[1] - owned
    near_a_ref[0:slots, :] = dot(sel_ref[2, owned:, :], stream).astype(BF16)
    near_b_ref[0:slots, :] = dot(sel_ref[3, owned:, :], stream).astype(BF16)
    for at, k in enumerate((0, 2, 3, 1)):
        same_ref[at] = dot(sel_ref[2 * k], stream).astype(BF16)
        other_ref[at] = dot(sel_ref[2 * k + 1], stream).astype(BF16)


def up_kernel(first, features, after, me, *refs):
    own, rx, ry, even, odd, gain, wg, wu = refs[:8]
    carry = () if first else refs[8:11]
    rest = refs[(8 if first else 11) + after :]
    sums = rest[2:5] if features else rest
    step = pl.program_id(0)
    steps = pl.num_programs(0)

    if first or features:

        @pl.when(step == 0)
        def _():
            for i, acc in enumerate(sums):
                acc[...] = jnp.zeros_like(acc) if first else carry[i][...]

    gate, up, square = sums
    slots = own.shape[1]
    rows = [r[0].astype(F32) for r in (own, rx, ry)]
    rows.append(jnp.where(step == 0, even[0].astype(F32), odd[0].astype(F32)))
    rows = jnp.concatenate(rows, axis=0)
    square[...] += jnp.broadcast_to(jnp.sum(rows * rows, axis=1, keepdims=True), square.shape)
    scaled = (rows * gain[0]).astype(BF16)
    gate[...] += dot(scaled, wg[0])
    up[...] += dot(scaled, wu[0])

    if features:
        outs, stages = rest[:2], rest[5:]

        @pl.when(step == steps - 1)
        def _():
            inverse = lax.rsqrt(square[:, 0:1] * (1.0 / features) + 1e-06)
            g = gate[...] * inverse
            active = g / (1.0 + jnp.exp(-g)) * (up[...] * inverse)
            main, ninths = slots // 9 * 8, slots // 9
            for d in range(4):
                at = d * slots
                stage, d, shards = (stages[0], 0, 1) if d == 3 else (stages[1], d, 3)
                stage[d * main : (d + 1) * main, :] = active[at : at + main]
                low = shards * main + d * ninths
                stage[low : low + ninths, :] = active[at + main : at + slots]
            for out, stage in zip(outs, stages):
                out[...] = stage[...].astype(BF16)


def up_project(group, last, me, near, far, gain, w_gate, w_up, carry, after=()):
    slots, part = near[0][0].shape[1:]
    hidden = w_gate.shape[2]
    total = 4 * slots
    source = lambda i, me: me[0] ^ (2 * group + i)
    rows = [
        pl.BlockSpec((1, slots, part), lambda i, me, start=start: (start + i, 0, 0))
        for _, start in near
    ] + [
        pl.BlockSpec((1, slots, part), lambda i, me, start=start: (start, 0, 0)) for _, start in far
    ]
    weight = pl.BlockSpec((1, part, hidden), lambda i, me: (source(i, me), 0, 0))
    in_place = pl.BlockSpec(memory_space=pltpu.VMEM)
    specs = rows + [pl.BlockSpec((1, 1, part), lambda i, me: (source(i, me), 0, 0)), weight, weight]
    sums = [
        jax.ShapeDtypeStruct((total, hidden), F32),
        jax.ShapeDtypeStruct((total, hidden), F32),
        jax.ShapeDtypeStruct((total, 128), F32),
    ]
    aliases = {}
    if carry is not None:
        specs += [in_place] * 3
        if not last:
            aliases = {9 + i: i for i in range(3)}
    specs += [pl.BlockSpec(memory_space=pl.ANY)] * len(after)
    sizes = (slots, 3 * slots)
    outs = [jax.ShapeDtypeStruct((n, hidden), BF16) for n in sizes] if last else sums
    scratch = [pltpu.VMEM(s.shape, s.dtype) for s in sums]
    scratch += [pltpu.VMEM((n, hidden), F32) for n in sizes]
    features = gain.shape[0] * part if last else 0
    return pl.pallas_call(
        functools.partial(up_kernel, carry is None, features, len(after)),
        name=f"up_{group}",
        out_shape=outs,
        grid_spec=pltpu.PrefetchScalarGridSpec(
            num_scalar_prefetch=1,
            grid=(2,),
            in_specs=specs,
            out_specs=[in_place] * len(outs),
            scratch_shapes=scratch if last else [],
        ),
        input_output_aliases=aliases,
        compiler_params=pltpu.CompilerParams(vmem_limit_bytes=48 * MIB),
        cost_estimate=NO_COST,
    )(me, *(array for array, _ in near + far), gain, w_gate, w_up, *(carry or ()), *after)


def cut_of(group):
    return 5 if group % 2 else 4


def down_kernel(groups, act_ref, w_ref, *refs):
    outs, (spare, held, sems) = refs[:-3], refs[-3:]
    step = pl.program_id(0)
    steps, _, tile = held.shape

    def load(k):
        columns = pl.ds(pl.multiple_of(k * tile, tile), tile)
        return pltpu.make_async_copy(w_ref.at[:, columns], held.at[k], sems.at[k])

    @pl.when(step == 0)
    def _():
        for k in range(steps):
            load(k).start()

    load(step).wait()
    part = dot(act_ref[...], held[step])
    ninths = part.shape[0] // 9
    main = part.shape[0] - ninths
    shards = ninths // (2 * groups)

    def through(group, tile):
        to_x, to_y = outs[2 * (group // 2) : 2 * (group // 2) + 2]
        cut = cut_of(group)
        return to_x, tile + (0 if group % 2 else 5), to_y, tile - cut + (0 if group % 2 else 4)

    for shard in range(shards):
        for group in range(groups):
            at = (shard * groups + group) * 16
            rows = part[at : at + 16, :].astype(BF16)
            if shards > 1:
                outs[shards * group + shard][step] = rows
                continue
            to_x, place_x, to_y, place_y = through(group, step)

            @pl.when(step < cut_of(group))
            def _():
                to_x[place_x] = rows

            @pl.when(step >= cut_of(group))
            def _():
                to_y[place_y] = rows

    for lanes in range(spare.shape[0]):
        spare[lanes, pl.ds(pl.multiple_of(step * ninths, 8), ninths), :] = part[
            main:, lanes * 128 : (lanes + 1) * 128
        ]

    @pl.when(step == steps - 1)
    def _():
        for shard in range(shards):
            for group in range(groups):
                pair = []
                for side in range(2):
                    row = pl.ds((shard * groups + group) * 2 + side, 8, stride=ninths)
                    ninth = [spare[lanes, row, :] for lanes in range(spare.shape[0])]
                    pair.append(jnp.concatenate(ninth, axis=1))
                pair = jnp.concatenate(pair, axis=0).astype(BF16)
                if shards > 1:
                    outs[shards * group + shard][8] = pair
                else:
                    _, _, to_y, place_y = through(group, 8)
                    to_y[place_y] = pair


def down_project(name, groups, active, w_down):
    total, hidden = active.shape
    features = w_down.shape[1]
    tile = features // 8
    outs = [jax.ShapeDtypeStruct((9, 16, tile), BF16)] * (total // 18)
    return pl.pallas_call(
        functools.partial(down_kernel, groups),
        name=name,
        grid=(8,),
        out_shape=outs,
        in_specs=[
            pl.BlockSpec(memory_space=pltpu.VMEM),
            pl.BlockSpec(memory_space=pltpu.HBM),
        ],
        out_specs=[pl.BlockSpec(memory_space=pltpu.VMEM)] * len(outs),
        scratch_shapes=[
            pltpu.VMEM((tile // 128, 8 * total // 9, 128), F32),
            pltpu.VMEM((8, hidden, tile), BF16),
            pltpu.SemaphoreType.DMA((8,)),
        ],
        compiler_params=pltpu.CompilerParams(vmem_limit_bytes=48 * MIB),
        cost_estimate=NO_COST,
    )(active, w_down)


def pair_kernel(same, other, own_stream, own, far_stream, far, last_stream, last, near_stream):
    owned = same.shape[1] - own.shape[1]
    for side, rows in enumerate((same, other)):
        own_stream[side, 0:owned, :], own[side] = rows[0, 0:owned, :], rows[0, owned:, :]
        far_stream[side, 0:owned, :], far[side] = rows[1, 0:owned, :], rows[1, owned:, :]
        last_stream[side, 0:owned, :], last[side] = rows[2, 0:owned, :], rows[2, owned:, :]
        near_stream[side, 0:owned, :] = rows[3, 0:owned, :]


def near_kernel(same, other, rows):
    slots = rows.shape[1]
    rows[0], rows[1] = same[0:slots, :], other[0:slots, :]


def second_kernel(*refs):
    parts, out = refs[:-1], refs[-1]
    for h in range(out.shape[0]):
        for k in range(out.shape[1]):
            pair = [ref[k].astype(F32)[8:16] for ref in parts[2 * h : 2 * h + 2]]
            out[h, k] = jnp.concatenate(pair, axis=0).astype(BF16)


def hold_kernel(*refs):
    for source, target in zip(refs[: len(refs) // 2], refs[len(refs) // 2 :]):
        target[...] = source[...]


def half_message_kernel(rx, ry, out_x, out_y):
    out_x[0], out_y[0] = ry[1], rx[0]


def join_message_kernel(own, rx, ry, out_x, out_y):
    out_x[0:2], out_y[0:2] = own[...], own[...]
    out_x[2], out_y[2] = ry[1], rx[0]


def relay_kernel(through_x, through_y, *refs):
    ahead = refs[4 : 4 + (len(refs) - 8) // 2]
    outs, copies = refs[4 + len(ahead) :][:4], refs[8 + len(ahead) :]
    for group in range(2):
        cut = cut_of(group)
        at_x, at_y = (0, -cut) if group else (5, 0)
        for own, out, through, tiles, at in (
            (refs[2 * group], outs[2 * group], through_y, range(cut, 9), at_y),
            (refs[2 * group + 1], outs[2 * group + 1], through_x, range(cut), at_x),
        ):
            for k in range(9):
                if k in tiles:
                    out[k] = (own[k].astype(F32) + through[k + at].astype(F32)).astype(BF16)
                else:
                    out[k] = own[k]
    for source, copy in zip(ahead, copies):
        copy[...] = source[...]


def finish_kernel(own, rx, ry, *refs):
    ahead = refs[: (len(refs) - 1) // 2]
    out, copies = refs[len(ahead)], refs[len(ahead) + 1 :]
    for k in range(9):
        out[k] = (own[k].astype(F32) + rx[k].astype(F32) + ry[k].astype(F32)).astype(BF16)
    for source, copy in zip(ahead, copies):
        copy[...] = source[...]


def mix_kernel(me, ids_t_ref, weight_t_ref, swap_ref, *refs):
    groups = (len(refs) - 1) // 2
    firsts, streams, out_ref = refs[:groups], refs[groups:-1], refs[-1]
    rows = ids_t_ref.shape[1]
    experts = 2 * groups
    pieces = firsts[0].shape[0] - 1
    tile = firsts[0].shape[2]
    ids, weights = ids_t_ref[...].T, weight_t_ref[...].T
    named = iota((rows, experts), 1) ^ me[0]
    first, second = ids[:, 0:1] == named, ids[:, 1:2] == named
    weight = jnp.where(first, weights[:, 0:1], jnp.where(second, weights[:, 1:2], 0.0))
    hit = (first | second).astype(F32)
    before = (iota((rows, rows), 0) > iota((rows, rows), 1)).astype(F32)
    rank = dot(before, hit)
    lanes = 2 * experts * 8
    shape = (experts, lanes)
    spread = ((iota(shape, 1) // 8) % experts == iota(shape, 0)).astype(F32)
    weight = dot(weight, spread, PRECISE)
    rank = dot(rank, spread, PRECISE).astype(jnp.int32)
    lane = iota((rows, lanes), 1)
    main = (lane < experts * 8) & (rank == lane % 8)
    extra = (lane >= experts * 8) & (rank == 8)

    def rows_of(k):
        data = []
        for g in range(groups):
            data.append(firsts[g][k].astype(F32)[0:8])
            data.append(swap_ref[g // 2, k].astype(F32)[g % 2 * 8 : g % 2 * 8 + 8])
        return data

    last = rows_of(pieces)
    for m in range(experts):
        k = me[0] ^ m
        coef = jnp.where(main | (extra & (lane % 8 == k)), weight, 0.0)
        high = coef.astype(BF16)
        low = (coef - high.astype(F32)).astype(BF16)
        data = jnp.concatenate(rows_of(k) + last, axis=0).astype(BF16)
        stream = streams[m // 2][m % 2, 0:rows, :].astype(F32)
        out_ref[:, pl.ds(pl.multiple_of(k * tile, 128), tile)] = (
            stream + (dot(high, data) + dot(low, data))
        ).astype(BF16)


def on_square(
    x_in,
    z_gate,
    b_in,
    c_out,
    dt_step,
    rate,
    skip,
    init_state,
    residual,
    norm_gain,
    expert_ids,
    gate_weights,
    w_gate,
    w_up,
    w_down,
):
    tokens, channels = x_in.shape
    heads = rate.shape[0]
    state = b_in.shape[1]
    owners = lax.axis_size("exp")
    rows, features = residual.shape
    experts = owners
    cap = max(2, 2 * rows // experts + 1)
    slots = owners * cap
    at = lax.axis_index("seq")
    me = lax.axis_index("exp")
    place = jnp.reshape(at, (1,)).astype(jnp.int32)
    self_id = jnp.reshape(me, (1,)).astype(jnp.int32)

    def over_x(v):
        return lax.ppermute(v, "seq", [(i, i ^ 1) for i in range(4)])

    def over_y(v):
        return lax.ppermute(v, "seq", [(i, i ^ 2) for i in range(4)])

    def along(v, mask):
        return lax.ppermute(v, "exp", [(i, i ^ mask) for i in range(owners)])

    rate_row = rate[None, :]
    dt_t = dt_step.T
    ids_t = expert_ids.T
    packed = block_call(
        pack_kernel,
        [jax.ShapeDtypeStruct((owners, rows, channels + 128), BF16)],
        0,
        (ids_t, residual),
        held=2,
        limit=48,
    )[0]
    packed = lax.all_to_all(packed, "exp", split_axis=0, concat_axis=0, tiled=True)
    payload, init_t = block_call(
        state_kernel,
        [
            jax.ShapeDtypeStruct((state + 16, channels), BF16),
            jax.ShapeDtypeStruct((state, channels), BF16),
        ],
        1,
        (place, x_in, b_in, dt_t, rate_row, init_state.reshape(channels, state)),
        held=5,
        limit=62,
    )
    pair = over_x(payload)
    own_part, fade, token = block_call(
        intra_kernel,
        [
            jax.ShapeDtypeStruct((tokens, channels), F32),
            jax.ShapeDtypeStruct((tokens, channels), F32),
            jax.ShapeDtypeStruct((8, 128), F32),
        ],
        0,
        (x_in, z_gate, b_in, c_out, dt_t, rate_row, skip[None, :]),
        held=7,
        limit=61,
    )
    joined = block_call(
        join_kernel,
        [jax.ShapeDtypeStruct((state, channels), BF16)],
        1,
        (place, payload, pair),
        after=(token,),
    )[0]
    early = over_y(joined)
    handed = (own_part, fade, c_out, init_t)
    select, own_part, fade, c, init_t = block_call(
        functools.partial(place_kernel, cap, experts),
        [jax.ShapeDtypeStruct((experts, rows + slots, tokens), BF16)]
        + [jax.ShapeDtypeStruct(v.shape, v.dtype) for v in handed],
        1,
        (self_id, packed, *handed),
        after=(joined,),
    )
    groups = owners // 2
    lanes = jax.ShapeDtypeStruct((groups, rows + slots, channels), BF16)
    one = jax.ShapeDtypeStruct((slots + 8, channels), BF16)
    near_a, near_b, same, other = block_call(
        stream_kernel,
        [one, one, lanes, lanes],
        1,
        (place, c, own_part, fade, init_t, pair, early, packed, select),
    )

    gain = norm_gain.reshape(owners, 1, channels)
    wg = w_gate.reshape(owners, channels, w_gate.shape[2])
    wu = w_up.reshape(owners, channels, w_up.shape[2])
    expert_rows = jax.ShapeDtypeStruct((2, slots, channels), BF16)
    stream_rows = jax.ShapeDtypeStruct((2, 40, channels), BF16)
    near_a, near_b = along(near_a, 2), along(near_b, 3)
    stream0, first, stream2, far, stream3, farthest, stream1 = block_call(
        pair_kernel,
        [stream_rows, expert_rows] * 3 + [stream_rows],
        0,
        (same, along(other, 1)),
    )
    gain = norm_gain.reshape(owners, 1, channels)
    wg = w_gate.reshape(owners, channels, w_gate.shape[2])
    wu = w_up.reshape(owners, channels, w_up.shape[2])
    gain = norm_gain.reshape(owners, 1, channels)
    wg = w_gate.reshape(owners, channels, w_gate.shape[2])
    wu = w_up.reshape(owners, channels, w_up.shape[2])

    def hold(values, after, name):
        outs = [jax.ShapeDtypeStruct(v.shape, BF16) for v in values]
        return block_call(hold_kernel, outs, 0, values, after=after, name=name)

    def project(group, near, far, carry, after=()):
        last = group == groups - 1
        return up_project(group, last, self_id, near, far, gain, wg, wu, carry, after)

    def message(count):
        return [jax.ShapeDtypeStruct((count, slots, channels), BF16)] * 2

    far = along(far, 4)
    rx0, ry0 = over_x(first), over_y(first)
    near = block_call(near_kernel, [expert_rows], 0, (near_a, near_b))[0]
    rx1, ry1 = over_x(near), over_y(near)
    to_x, to_y = block_call(
        half_message_kernel, message(1), 0, (rx0, ry0), after=(near,), name="half_0"
    )
    fx0, fy0 = over_x(to_x), over_y(to_y)
    farthest_held = hold((farthest,), (far,), "hold_farthest")[0]
    farthest = along(farthest_held, 6)
    to_x, to_y = block_call(
        join_message_kernel,
        message(3),
        0,
        (far, rx1, ry1),
        after=(fx0, fy0, farthest_held),
        name="join_2",
    )
    rx2, ry2 = over_x(to_x), over_y(to_y)
    carry = project(0, [(first, 0), (rx0, 0), (ry0, 0)], [(fy0, 0), (fx0, 0)], None)
    to_x, to_y = block_call(
        join_message_kernel, message(3), 0, (farthest, rx2, ry2), after=(carry[2],), name="join_3"
    )
    rx3, ry3 = over_x(to_x), over_y(to_y)
    held = hold((stream1, stream2, stream3), (to_x,), "hold_streams")
    stream1, stream2, stream3 = (along(v, 2 * g + 2) for g, v in enumerate(held))
    carry = project(1, [(near, 0), (rx1, 0), (ry1, 0)], [(ry2, 2), (rx2, 2)], carry, held[:1])
    to_x, to_y = block_call(
        half_message_kernel, message(1), 0, (rx3, ry3), after=(carry[2],), name="half_3"
    )
    fx3, fy3 = over_x(to_x), over_y(to_y)
    carry = project(2, [(far, 0), (rx2, 0), (ry2, 0)], [(ry3, 2), (rx3, 2)], carry, (stream1, stream2, stream3))
    active_far, active = project(
        3, [(farthest, 0), (rx3, 0), (ry3, 0)], [(fy3, 0), (fx3, 0)], carry
    )

    wd = w_down.reshape(w_down.shape[1], features)
    tiles = jax.ShapeDtypeStruct((9, 16, features // 8), BF16)
    sent = down_project("down_through", groups, active_far, wd)
    rest = down_project("down_rest", groups, active, wd)
    own, own_x, own_y = ([rest[3 * g + k] for g in range(groups)] for k in range(3))

    def relay(name, through_x, through_y, low, ahead=(), after=()):
        shares = (own_x[low], own_y[low], own_x[low + 1], own_y[low + 1])
        return block_call(
            relay_kernel,
            [tiles] * (4 + len(ahead)),
            0,
            (through_x, through_y, *shares, *ahead),
            after=after,
            name=name,
        )

    def finish(group, rx, ry, ahead=(), after=()):
        return block_call(
            finish_kernel,
            [tiles] * (1 + len(ahead)),
            0,
            (own[group], rx, ry, *ahead),
            after=after,
            name=f"finish_{group}",
        )

    through_x, through_y = over_x(sent[2]), over_y(sent[3])
    x2, y2, x3, y3, next_x, next_y = relay(
        "relay_far", through_x, through_y, 2, (sent[0], sent[1])
    )
    rx3, ry3 = over_x(x3), over_y(y3)
    through_x, through_y = over_x(next_x), over_y(next_y)
    both3, x2, y2 = finish(3, rx3, ry3, (x2, y2))
    back3 = along(both3, 6)
    rx2, ry2 = over_x(x2), over_y(y2)
    x0, y0, x1, y1 = relay("relay_near", through_x, through_y, 0, after=(both3,))
    rx1, ry1 = over_x(x1), over_y(y1)
    both2, x0, y0 = finish(2, rx2, ry2, (x0, y0))
    back2 = along(both2, 4)
    rx0, ry0 = over_x(x0), over_y(y0)
    back1 = along(finish(1, rx1, ry1, after=(back3,))[0], 2)
    back = [finish(0, rx0, ry0)[0], back1, back2, back3]
    swap = block_call(second_kernel, [jax.ShapeDtypeStruct((2,) + tiles.shape, BF16)], 0, back)[0]
    swap = along(swap, 1)
    return block_call(
        mix_kernel,
        [jax.ShapeDtypeStruct((rows, features), BF16)],
        1,
        (self_id, ids_t, gate_weights.T, swap, *back, stream0, stream1, stream2, stream3),
    )[0]


def entering_2(array, axis, combine, identity):
    devices, mine = (lax.axis_size(axis), lax.axis_index(axis))
    everything = jax.tree.map(
        lambda part, kind: lax.all_gather(part.astype(kind), axis),
        array,
        (jnp.bfloat16, jnp.bfloat16),
    )
    start = jax.tree.map(
        lambda part, zero: jnp.broadcast_to(jnp.asarray(zero, part.dtype), part.shape),
        array,
        identity,
    )

    def hop(k, before):
        reached = k < mine
        new = combine(
            before, jax.tree.map(lambda part, own: part[k].astype(own.dtype), everything, array)
        )
        return jax.tree.map(lambda a, b: jnp.where(reached, a, b), new, before)

    return lax.fori_loop(0, devices, hop, start)


def chain_combine(earlier, later):
    return (earlier[0] + later[0], jnp.exp(later[0])[:, None, None] * earlier[1] + later[1])


def on_device(
    x_in,
    z_gate,
    b_in,
    c_out,
    dt_step,
    rate,
    skip,
    init_state,
    residual,
    norm_gain,
    expert_ids,
    gate_weights,
    w_gate,
    w_up,
    w_down,
):
    token_count, channels = x_in.shape
    heads_here = rate.shape[0]
    head_width = channels // heads_here
    state_width = b_in.shape[1]
    blocks = token_count // GROUP
    inputs = x_in.astype(jnp.float32).reshape(blocks, GROUP, heads_here, head_width)
    keys_in = b_in.astype(jnp.float32).reshape(blocks, GROUP, state_width)
    queries = c_out.astype(jnp.float32).reshape(blocks, GROUP, state_width)
    log_steps = (-rate[None, :] * dt_step).reshape(blocks, GROUP, heads_here)
    cumulative = jnp.cumsum(log_steps, axis=1)
    scores = jnp.einsum("ctn,csn->cts", queries, keys_in, precision=PRECISE)
    causal = jnp.arange(GROUP)[:, None] >= jnp.arange(GROUP)[None, :]
    spread = cumulative[:, :, None, :] - cumulative[:, None, :, :]
    weights = jnp.exp(jnp.where(causal[None, :, :, None], spread, -jnp.inf)) * scores[..., None]
    intra_out = jnp.einsum("ctsh,cshp->cthp", weights, inputs, precision=PRECISE)
    tail_decay = jnp.exp(cumulative[:, -1:, :] - cumulative)
    block_state = jnp.einsum("csh,cshp,csn->chpn", tail_decay, inputs, keys_in, precision=PRECISE)
    block_log = cumulative[:, -1, :]

    def advance(carried, element):
        total_log, total_state = carried
        step_log, step_state = element
        updated = (
            total_log + step_log,
            jnp.exp(step_log)[:, None, None] * total_state + step_state,
        )
        return (updated, (total_log, total_state))

    zero_state = jnp.zeros((heads_here, head_width, state_width), jnp.float32)
    zero_log = jnp.zeros((heads_here,), jnp.float32)
    (device_log, device_state), (enter_log, enter_state) = lax.scan(
        advance, (zero_log, zero_state), (block_log, block_state)
    )
    prior_log, prior_state = entering_2(
        (device_log, device_state), "seq", chain_combine, (zero_log, zero_state)
    )
    incoming = prior_state + jnp.exp(prior_log)[:, None, None] * init_state
    entering = enter_state + jnp.exp(enter_log)[:, :, None, None] * incoming[None]
    inter_out = jnp.exp(cumulative)[..., None] * jnp.einsum(
        "chpn,ctn->cthp", entering, queries, precision=PRECISE
    )
    mixed_out = (intra_out + inter_out + skip[None, None, :, None] * inputs).reshape(
        token_count, channels
    )
    mixer = (mixed_out * jax.nn.silu(z_gate.astype(jnp.float32))).astype(jnp.bfloat16)
    token_mix = lax.all_to_all(mixer, "exp", split_axis=0, concat_axis=1, tiled=True)
    stream = (residual.astype(jnp.float32) + token_mix.astype(jnp.float32)).astype(jnp.bfloat16)
    widened = stream.astype(jnp.float32)
    normed = (
        widened
        * lax.rsqrt(jnp.mean(widened * widened, axis=-1, keepdims=True) + 1e-06)
        * norm_gain[None, :]
    ).astype(jnp.bfloat16)
    rows_here = residual.shape[0]
    owners = lax.axis_size("exp")
    local_experts = w_gate.shape[0]
    experts = owners * local_experts
    capacity = max(2, 2 * rows_here // experts + 1)
    width = residual.shape[1]
    chosen = expert_ids.reshape(-1)
    onehot = (chosen[:, None] == jnp.arange(experts)[None, :]).astype(jnp.int32)
    slot_index = jnp.sum((jnp.cumsum(onehot, axis=0) - onehot) * onehot, axis=1)
    target = chosen * capacity + slot_index
    placing = (target[None, :] == jnp.arange(experts * capacity)[:, None]).astype(jnp.bfloat16)
    pair_rows = jnp.repeat(normed, 2, axis=0)
    outgoing = jnp.dot(placing, pair_rows, preferred_element_type=jnp.float32).astype(jnp.bfloat16)
    outgoing = outgoing.reshape(owners, local_experts, 1, capacity, width)
    arrived = lax.all_to_all(outgoing, "exp", split_axis=0, concat_axis=2, tiled=True)
    segment = lax.all_gather(arrived, "seq", axis=1, tiled=True)
    flattened = segment.reshape(segment.shape[0], -1, segment.shape[-1])
    gate_proj = jnp.einsum("erd,edf->erf", flattened, w_gate, preferred_element_type=jnp.float32)
    up_proj = jnp.einsum("erd,edf->erf", flattened, w_up, preferred_element_type=jnp.float32)
    active = (jax.nn.silu(gate_proj) * up_proj).astype(jnp.bfloat16)
    partial_value = jnp.einsum("erf,efd->erd", active, w_down, preferred_element_type=jnp.float32)
    partials = partial_value.reshape(segment.shape[:-1] + (partial_value.shape[-1],))
    summed = lax.psum_scatter(partials.astype(jnp.bfloat16), "seq", scatter_dimension=1, tiled=True)
    returned = lax.all_to_all(summed, "exp", split_axis=2, concat_axis=0, tiled=True)
    results = returned.reshape(experts * capacity, width)
    picked = results[target].astype(jnp.float32).reshape(rows_here, 2, width)
    mixture = jnp.sum(picked * gate_weights[:, :, None], axis=1)
    return (widened + mixture).astype(jnp.bfloat16)


def solution(mesh):
    square = mesh.shape["seq"] == 4 and mesh.shape["exp"] == 8

    def body(*args):
        rows = args[8].shape[0]
        experts = mesh.shape["exp"] * args[12].shape[0]
        fits = args[12].shape[0] == 1 and 2 * rows // experts + 1 == 9
        return (on_square if square and fits else on_device)(*args)

    return jax.shard_map(
        body,
        mesh=mesh,
        in_specs=(
            P("seq", "exp"),
            P("seq", "exp"),
            P("seq", None),
            P("seq", None),
            P("seq", "exp"),
            P("exp"),
            P("exp"),
            P("exp", None, None),
            P(("seq", "exp"), None),
            P(),
            P(("seq", "exp"), None),
            P(("seq", "exp"), None),
            P("exp", None, "seq"),
            P("exp", None, "seq"),
            P("exp", "seq", None),
        ),
        out_specs=P(("seq", "exp"), None),
        check_vma=False,
    )
```

```python
import functools

import jax
import jax.numpy as jnp
from jax import lax
from jax.experimental import pallas as pl
from jax.experimental.pallas import tpu as pltpu
from jax.sharding import PartitionSpec as P

GROUP = 128
PRECISE = lax.Precision.HIGHEST
F32 = jnp.float32
BF16 = jnp.bfloat16
MIB = 1 << 20
NO_COST = pl.CostEstimate(flops=0, bytes_accessed=0, transcendentals=0)


def block_call(body, outs, scalars, args, held=0, keep=0, after=(), limit=16, out_blocks=False, name=None):
    n_args = len(args)
    kept = [jax.ShapeDtypeStruct(v.shape, v.dtype) for v in args[scalars : scalars + held]]

    def kernel(*refs):
        refs, sems = (refs[:-1], refs[-1]) if held else (refs, None)
        inputs, refs = refs[:n_args], refs[n_args + len(after) :]
        results, refs = refs[: len(outs)], refs[len(outs) :]
        copies = [
            pltpu.make_async_copy(src, dst, sems.at[k])
            for k, (src, dst) in enumerate(zip(inputs[scalars : scalars + held], refs))
        ]
        for copy in copies:
            copy.start()
        for copy in copies:
            copy.wait()
        body(*inputs[:scalars], *refs, *inputs[scalars + held :], *results)

    scratch = [pltpu.VMEM(v.shape, v.dtype) for v in kept[keep:]]
    if held:
        scratch.append(pltpu.SemaphoreType.DMA((held,)))
    return pl.pallas_call(
        kernel,
        name=name or getattr(body, "func", body).__name__,
        out_shape=list(outs) + kept[:keep],
        in_specs=[pl.BlockSpec(memory_space=pltpu.SMEM)] * scalars
        + [pl.BlockSpec(memory_space=pltpu.HBM)] * held
        + [pl.BlockSpec(memory_space=pltpu.VMEM)] * (n_args - scalars - held)
        + [pl.BlockSpec(memory_space=pl.ANY)] * len(after),
        out_specs=[pl.BlockSpec() if out_blocks else pl.BlockSpec(memory_space=pltpu.VMEM)]
        * (len(outs) + keep),
        scratch_shapes=scratch,
        compiler_params=pltpu.CompilerParams(vmem_limit_bytes=limit * MIB),
        cost_estimate=NO_COST,
    )(*args, *after)


def iota(shape, dim):
    return lax.broadcasted_iota(jnp.int32, shape, dim)


def dot(a, b, precision=None):
    return jnp.dot(a, b, precision=precision, preferred_element_type=F32)


def head_spread(heads, channels):
    shape = (heads, channels)
    return (iota(shape, 1) // (channels // heads) == iota(shape, 0)).astype(F32)


def running_logs(dt_t_ref, rate_ref):
    logs = -rate_ref[...] * dt_t_ref[...].T
    tokens = logs.shape[0]
    tri = (iota((tokens, tokens), 0) >= iota((tokens, tokens), 1)).astype(F32)
    return dot(tri, logs, PRECISE)


def pack_kernel(ids_t_ref, residual_ref, out_ref):
    parts, rows, wide = out_ref.shape
    part = wide - 128
    ids = ids_t_ref[...].astype(F32).T
    lane = iota((rows, 128), 1)
    named = jnp.where(lane == 0, ids[:, 0:1], jnp.where(lane == 1, ids[:, 1:2], 0.0)).astype(BF16)
    for k in range(parts):
        out_ref[k, :, 0:part] = residual_ref[:, k * part : (k + 1) * part]
        out_ref[k, :, part:wide] = named


def state_kernel(place, x_ref, b_ref, dt_t_ref, rate_ref, init_ref, payload_ref, init_t_ref):
    tokens, channels = x_ref.shape
    heads = dt_t_ref.shape[0]
    width = b_ref.shape[1]
    cum = running_logs(dt_t_ref, rate_ref)
    total = cum[tokens - 1 : tokens, :]
    spread = head_spread(heads, channels)
    tail = dot(jnp.exp(total - cum), spread, PRECISE)
    scaled = (x_ref[...].astype(F32) * tail).astype(BF16)
    keys = b_ref[...].astype(F32).T.astype(BF16)
    own = dot(keys, scaled)
    decay = dot(jnp.broadcast_to(jnp.exp(total), (8, heads)), spread, PRECISE)
    init_t = init_ref[...].T
    init_t_ref[...] = init_t.astype(BF16)
    first = (place[0] == 0).astype(F32)
    payload_ref[0:width, :] = (own + first * (decay[0:1, :] * init_t)).astype(BF16)
    high = decay.astype(BF16).astype(F32)
    rows = iota((16, channels), 0)
    high16 = jnp.broadcast_to(high[0:1, :], (16, channels))
    low16 = jnp.broadcast_to(decay[0:1, :], (16, channels)) - high16
    payload_ref[width : width + 16, :] = jnp.where(
        rows == 0, high16, jnp.where(rows == 1, low16, 0.0)
    ).astype(BF16)


def intra_kernel(x_ref, z_ref, b_ref, c_ref, dt_t_ref, rate_ref, skip_ref, own_ref, fade_ref, token_ref):
    tokens, channels = x_ref.shape
    heads = dt_t_ref.shape[0]
    width = channels // heads
    token_ref[...] = jnp.zeros_like(token_ref)
    shape = (tokens, tokens)
    causal = iota(shape, 0) >= iota(shape, 1)
    cum = running_logs(dt_t_ref, rate_ref)
    cum_t = cum.T
    scores = lax.dot_general(
        c_ref[...], b_ref[...], (((1,), (1,)), ((), ())), preferred_element_type=F32
    )
    spread = head_spread(heads, channels)
    direct = dot(jnp.broadcast_to(skip_ref[...], (8, heads)), spread, PRECISE)[0:1, :]
    fade = dot(jnp.exp(cum), spread, PRECISE)
    per = 128 // width
    lane_head = iota((tokens, 128), 1) // width
    for group in range(heads // per):
        cols = slice(group * 128, (group + 1) * 128)
        x = x_ref[:, cols]
        total = x.astype(F32) * direct[:, cols]
        for k in range(per):
            h = group * per + k
            gap = jnp.where(causal, cum[:, h : h + 1] - cum_t[h : h + 1, :], -1e30)
            weights = (jnp.exp(gap) * scores).astype(BF16)
            part = dot(weights, x)
            total = total + jnp.where(lane_head == k, part, 0.0)
        z = z_ref[:, cols].astype(F32)
        gate = z / (1.0 + jnp.exp(-z))
        own_ref[:, cols] = total * gate
        fade_ref[:, cols] = fade[:, cols] * gate


def place_kernel(cap, experts, me, packed_ref, *refs):
    count = (len(refs) - 1) // 2
    out_ref = refs[count]
    for source, target in zip(refs[:count], refs[count + 1 :]):
        target[...] = source[...]
    blocks, rows, wide = packed_ref.shape
    tokens = blocks * rows
    slots = out_ref.shape[1] - rows
    ids = packed_ref[:, :, wide - 128 : wide].astype(F32).reshape(tokens, 128).T
    ids = ids[0:8, :].astype(jnp.int32)
    shape = (tokens, tokens)
    before = (iota(shape, 0) < iota(shape, 1)) & (iota(shape, 0) // rows == iota(shape, 1) // rows)
    named = iota((experts, tokens), 0) ^ me[0]
    hit = (ids[0:1, :] == named) | (ids[1:2, :] == named)
    rank = dot(hit.astype(BF16), before.astype(BF16)).astype(jnp.int32)
    block = (iota((experts, tokens), 1) // rows) ^ named
    whole = cap - 1
    row = jnp.where(rank < whole, block * whole + rank, blocks * whole + block)
    row = jnp.where(hit, row, -1)
    shape = (rows + slots, tokens)
    for e in range(experts):
        owned = ((me[0] ^ e) * rows + iota(shape, 0) == iota(shape, 1)) & (iota(shape, 0) < rows)
        placed = (iota(shape, 0) - rows == row[e : e + 1, :]) & (iota(shape, 0) >= rows)
        out_ref[e] = (owned | placed).astype(F32).astype(BF16)


def join_kernel(place, own_ref, other_ref, out_ref):
    width = out_ref.shape[0]
    odd = place[0] % 2 == 1
    own, other = own_ref[0:width, :].astype(F32), other_ref[0:width, :].astype(F32)
    own_decay = own_ref[width : width + 16, :].astype(F32)
    other_decay = other_ref[width : width + 16, :].astype(F32)
    own_decay = own_decay[0:1, :] + own_decay[1:2, :]
    other_decay = other_decay[0:1, :] + other_decay[1:2, :]
    early = jnp.where(odd, other, own)
    late = jnp.where(odd, own, other)
    decay = jnp.where(odd, own_decay, other_decay)
    out_ref[...] = (decay * early + late).astype(BF16)


def stream_kernel(
    place, c_ref, own_ref, fade_ref, init_t_ref, pair_ref, early_ref, res_ref, sel_ref, near_a_ref, near_b_ref, same_ref, other_ref
):
    width = init_t_ref.shape[0]
    at = place[0]
    zero = (at == 0).astype(F32)
    odd = (at % 2 == 1).astype(F32)
    pair = pair_ref[...].astype(F32)
    decay = pair[width : width + 1, :] + pair[width + 1 : width + 2, :]
    factor = jnp.where(at >= 2, jnp.where(at % 2 == 1, decay, 1.0), 0.0)
    entering = zero * init_t_ref[...].astype(F32) + odd * pair[0:width, :] + factor * early_ref[...].astype(F32)
    mixed = own_ref[...] + fade_ref[...] * dot(c_ref[...], entering.astype(BF16))
    mixer = mixed.astype(BF16).astype(F32)
    tokens, channels = mixer.shape
    residual = res_ref[:, :, 0:channels].astype(F32).reshape(tokens, channels)
    stream = (residual + mixer).astype(BF16)
    owned = sel_ref.shape[1] - near_a_ref.shape[0]
    near_a_ref[...] = dot(sel_ref[2, owned:, :], stream).astype(BF16)
    near_b_ref[...] = dot(sel_ref[3, owned:, :], stream).astype(BF16)
    for at, k in enumerate((0, 2, 3, 1)):
        same_ref[at] = dot(sel_ref[2 * k], stream).astype(BF16)
        other_ref[at] = dot(sel_ref[2 * k + 1], stream).astype(BF16)


def up_kernel(first, features, after, me, *refs):
    own, rx, ry, even, odd, gain, wg, wu = refs[:8]
    carry = () if first else refs[8:11]
    rest = refs[(8 if first else 11) + after :]
    sums = rest[2:5] if features else rest
    step = pl.program_id(0)
    steps = pl.num_programs(0)

    if first or features:

        @pl.when(step == 0)
        def _():
            for i, acc in enumerate(sums):
                acc[...] = jnp.zeros_like(acc) if first else carry[i][...]

    gate, up, square = sums
    slots = own.shape[1]
    rows = [r[0].astype(F32) for r in (own, rx, ry)]
    rows.append(jnp.where(step == 0, even[0].astype(F32), odd[0].astype(F32)))
    rows = jnp.concatenate(rows, axis=0)
    square[...] += jnp.broadcast_to(jnp.sum(rows * rows, axis=1, keepdims=True), square.shape)
    scaled = (rows * gain[0]).astype(BF16)
    gate[...] += dot(scaled, wg[0])
    up[...] += dot(scaled, wu[0])

    if features:
        outs, stages = rest[:2], rest[5:]

        @pl.when(step == steps - 1)
        def _():
            inverse = lax.rsqrt(square[:, 0:1] * (1.0 / features) + 1e-06)
            g = gate[...] * inverse
            active = g / (1.0 + jnp.exp(-g)) * (up[...] * inverse)
            main, ninths = slots // 9 * 8, slots // 9
            for d in range(4):
                at = d * slots
                stage, d, shards = (stages[0], 0, 1) if d == 3 else (stages[1], d, 3)
                stage[d * main : (d + 1) * main, :] = active[at : at + main]
                low = shards * main + d * ninths
                stage[low : low + ninths, :] = active[at + main : at + slots]
            for out, stage in zip(outs, stages):
                out[...] = stage[...].astype(BF16)


def up_project(group, last, me, near, far, gain, w_gate, w_up, carry, after=()):
    slots, part = near[0][0].shape[1:]
    hidden = w_gate.shape[2]
    total = 4 * slots
    source = lambda i, me: me[0] ^ (2 * group + i)
    rows = [
        pl.BlockSpec((1, slots, part), lambda i, me, start=start: (start + i, 0, 0))
        for _, start in near
    ] + [
        pl.BlockSpec((1, slots, part), lambda i, me, start=start: (start, 0, 0)) for _, start in far
    ]
    weight = pl.BlockSpec((1, part, hidden), lambda i, me: (source(i, me), 0, 0))
    in_place = pl.BlockSpec(memory_space=pltpu.VMEM)
    specs = rows + [pl.BlockSpec((1, 1, part), lambda i, me: (source(i, me), 0, 0)), weight, weight]
    sums = [
        jax.ShapeDtypeStruct((total, hidden), F32),
        jax.ShapeDtypeStruct((total, hidden), F32),
        jax.ShapeDtypeStruct((total, 128), F32),
    ]
    aliases = {}
    if carry is not None:
        specs += [in_place] * 3
        if not last:
            aliases = {9 + i: i for i in range(3)}
    specs += [pl.BlockSpec(memory_space=pl.ANY)] * len(after)
    sizes = (slots, 3 * slots)
    outs = [jax.ShapeDtypeStruct((n, hidden), BF16) for n in sizes] if last else sums
    scratch = [pltpu.VMEM(s.shape, s.dtype) for s in sums]
    scratch += [pltpu.VMEM((n, hidden), F32) for n in sizes]
    features = gain.shape[0] * part if last else 0
    return pl.pallas_call(
        functools.partial(up_kernel, carry is None, features, len(after)),
        name=f"up_{group}",
        out_shape=outs,
        grid_spec=pltpu.PrefetchScalarGridSpec(
            num_scalar_prefetch=1,
            grid=(2,),
            in_specs=specs,
            out_specs=[in_place] * len(outs),
            scratch_shapes=scratch if last else [],
        ),
        input_output_aliases=aliases,
        compiler_params=pltpu.CompilerParams(vmem_limit_bytes=48 * MIB),
        cost_estimate=NO_COST,
    )(me, *(array for array, _ in near + far), gain, w_gate, w_up, *(carry or ()), *after)


def cut_of(group):
    return 5 if group % 2 else 4


def down_kernel(groups, act_ref, w_ref, *refs):
    outs, (spare, held, sems) = refs[:-3], refs[-3:]
    step = pl.program_id(0)
    steps, _, tile = held.shape

    def load(k):
        columns = pl.ds(pl.multiple_of(k * tile, tile), tile)
        return pltpu.make_async_copy(w_ref.at[:, columns], held.at[k], sems.at[k])

    @pl.when(step == 0)
    def _():
        for k in range(steps):
            load(k).start()

    load(step).wait()
    part = dot(act_ref[...], held[step])
    ninths = part.shape[0] // 9
    main = part.shape[0] - ninths
    shards = ninths // (2 * groups)

    def through(group, tile):
        to_x, to_y = outs[2 * (group // 2) : 2 * (group // 2) + 2]
        cut = cut_of(group)
        return to_x, tile + (0 if group % 2 else 5), to_y, tile - cut + (0 if group % 2 else 4)

    for shard in range(shards):
        for group in range(groups):
            at = (shard * groups + group) * 16
            rows = part[at : at + 16, :].astype(BF16)
            if shards > 1:
                outs[shards * group + shard][step] = rows
                continue
            to_x, place_x, to_y, place_y = through(group, step)

            @pl.when(step < cut_of(group))
            def _():
                to_x[place_x] = rows

            @pl.when(step >= cut_of(group))
            def _():
                to_y[place_y] = rows

    for lanes in range(spare.shape[0]):
        spare[lanes, pl.ds(pl.multiple_of(step * ninths, 8), ninths), :] = part[
            main:, lanes * 128 : (lanes + 1) * 128
        ]

    @pl.when(step == steps - 1)
    def _():
        for shard in range(shards):
            for group in range(groups):
                pair = []
                for side in range(2):
                    row = pl.ds((shard * groups + group) * 2 + side, 8, stride=ninths)
                    ninth = [spare[lanes, row, :] for lanes in range(spare.shape[0])]
                    pair.append(jnp.concatenate(ninth, axis=1))
                pair = jnp.concatenate(pair, axis=0).astype(BF16)
                if shards > 1:
                    outs[shards * group + shard][8] = pair
                else:
                    _, _, to_y, place_y = through(group, 8)
                    to_y[place_y] = pair


def down_project(name, groups, active, w_down):
    total, hidden = active.shape
    features = w_down.shape[1]
    tile = features // 8
    outs = [jax.ShapeDtypeStruct((9, 16, tile), BF16)] * (total // 18)
    return pl.pallas_call(
        functools.partial(down_kernel, groups),
        name=name,
        grid=(8,),
        out_shape=outs,
        in_specs=[
            pl.BlockSpec(memory_space=pltpu.VMEM),
            pl.BlockSpec(memory_space=pltpu.HBM),
        ],
        out_specs=[pl.BlockSpec(memory_space=pltpu.VMEM)] * len(outs),
        scratch_shapes=[
            pltpu.VMEM((tile // 128, 8 * total // 9, 128), F32),
            pltpu.VMEM((8, hidden, tile), BF16),
            pltpu.SemaphoreType.DMA((8,)),
        ],
        compiler_params=pltpu.CompilerParams(vmem_limit_bytes=48 * MIB),
        cost_estimate=NO_COST,
    )(active, w_down)


def pair_kernel(same, other, own_stream, own, far, last_stream, last, near_stream):
    owned = same.shape[1] - own.shape[1]
    for side, rows in enumerate((same, other)):
        own_stream[side, 0:owned, :], own[side] = rows[0, 0:owned, :], rows[0, owned:, :]
        far[side] = rows[1]
        last_stream[side, 0:owned, :], last[side] = rows[2, 0:owned, :], rows[2, owned:, :]
        near_stream[side, 0:owned, :] = rows[3, 0:owned, :]


def near_kernel(same, other, rows):
    rows[0], rows[1] = same[...], other[...]


def second_kernel(*refs):
    parts, out = refs[:-1], refs[-1]
    for h in range(out.shape[0]):
        for k in range(out.shape[1]):
            pair = [ref[k].astype(F32)[8:16] for ref in parts[2 * h : 2 * h + 2]]
            out[h, k] = jnp.concatenate(pair, axis=0).astype(BF16)


def hold_kernel(*refs):
    for source, target in zip(refs[: len(refs) // 2], refs[len(refs) // 2 :]):
        target[...] = source[...]


def half_message_kernel(rx, ry, out_x, out_y):
    out_x[0], out_y[0] = ry[1], rx[0]


def join_message_kernel(own, rx, ry, out_x, out_y, *parts):
    owned = own.shape[1] - out_x.shape[1]
    for side in range(2):
        rows = own[side, owned:, :]
        out_x[side], out_y[side] = rows, rows
        if parts:
            parts[0][side], parts[1][side, 0:owned, :] = rows, own[side, 0:owned, :]
    out_x[2], out_y[2] = ry[1], rx[0]


def relay_kernel(through_x, through_y, *refs):
    ahead = refs[4 : 4 + (len(refs) - 8) // 2]
    outs, copies = refs[4 + len(ahead) :][:4], refs[8 + len(ahead) :]
    for group in range(2):
        cut = cut_of(group)
        at_x, at_y = (0, -cut) if group else (5, 0)
        for own, out, through, tiles, at in (
            (refs[2 * group], outs[2 * group], through_y, range(cut, 9), at_y),
            (refs[2 * group + 1], outs[2 * group + 1], through_x, range(cut), at_x),
        ):
            for k in range(9):
                if k in tiles:
                    out[k] = (own[k].astype(F32) + through[k + at].astype(F32)).astype(BF16)
                else:
                    out[k] = own[k]
    for source, copy in zip(ahead, copies):
        copy[...] = source[...]


def finish_kernel(own, rx, ry, *refs):
    ahead = refs[: (len(refs) - 1) // 2]
    out, copies = refs[len(ahead)], refs[len(ahead) + 1 :]
    for k in range(9):
        out[k] = (own[k].astype(F32) + rx[k].astype(F32) + ry[k].astype(F32)).astype(BF16)
    for source, copy in zip(ahead, copies):
        copy[...] = source[...]


def mix_kernel(me, ids_t_ref, weight_t_ref, swap_ref, *refs):
    groups = (len(refs) - 1) // 2
    firsts, streams, out_ref = refs[:groups], refs[groups:-1], refs[-1]
    rows = ids_t_ref.shape[1]
    experts = 2 * groups
    pieces = firsts[0].shape[0] - 1
    tile = firsts[0].shape[2]
    ids, weights = ids_t_ref[...].T, weight_t_ref[...].T
    named = iota((rows, experts), 1) ^ me[0]
    first, second = ids[:, 0:1] == named, ids[:, 1:2] == named
    weight = jnp.where(first, weights[:, 0:1], jnp.where(second, weights[:, 1:2], 0.0))
    hit = (first | second).astype(F32)
    before = (iota((rows, rows), 0) > iota((rows, rows), 1)).astype(F32)
    rank = dot(before, hit)
    lanes = 2 * experts * 8
    shape = (experts, lanes)
    spread = ((iota(shape, 1) // 8) % experts == iota(shape, 0)).astype(F32)
    weight = dot(weight, spread, PRECISE)
    rank = dot(rank, spread, PRECISE).astype(jnp.int32)
    lane = iota((rows, lanes), 1)
    main = (lane < experts * 8) & (rank == lane % 8)
    extra = (lane >= experts * 8) & (rank == 8)

    def rows_of(k):
        data = []
        for g in range(groups):
            data.append(firsts[g][k].astype(F32)[0:8])
            data.append(swap_ref[g // 2, k].astype(F32)[g % 2 * 8 : g % 2 * 8 + 8])
        return data

    last = rows_of(pieces)
    for m in range(experts):
        k = me[0] ^ m
        coef = jnp.where(main | (extra & (lane % 8 == k)), weight, 0.0)
        high = coef.astype(BF16)
        low = (coef - high.astype(F32)).astype(BF16)
        data = jnp.concatenate(rows_of(k) + last, axis=0).astype(BF16)
        stream = streams[m // 2][m % 2, 0:rows, :].astype(F32)
        out_ref[:, pl.ds(pl.multiple_of(k * tile, 128), tile)] = (
            stream + (dot(high, data) + dot(low, data))
        ).astype(BF16)


def on_square(
    x_in,
    z_gate,
    b_in,
    c_out,
    dt_step,
    rate,
    skip,
    init_state,
    residual,
    norm_gain,
    expert_ids,
    gate_weights,
    w_gate,
    w_up,
    w_down,
):
    tokens, channels = x_in.shape
    heads = rate.shape[0]
    state = b_in.shape[1]
    owners = lax.axis_size("exp")
    rows, features = residual.shape
    experts = owners
    cap = max(2, 2 * rows // experts + 1)
    slots = owners * cap
    at = lax.axis_index("seq")
    me = lax.axis_index("exp")
    place = jnp.reshape(at, (1,)).astype(jnp.int32)
    self_id = jnp.reshape(me, (1,)).astype(jnp.int32)

    def over_x(v):
        return lax.ppermute(v, "seq", [(i, i ^ 1) for i in range(4)])

    def over_y(v):
        return lax.ppermute(v, "seq", [(i, i ^ 2) for i in range(4)])

    def along(v, mask):
        return lax.ppermute(v, "exp", [(i, i ^ mask) for i in range(owners)])

    rate_row = rate[None, :]
    dt_t = dt_step.T
    ids_t = expert_ids.T
    packed = block_call(
        pack_kernel,
        [jax.ShapeDtypeStruct((owners, rows, channels + 128), BF16)],
        0,
        (ids_t, residual),
        held=2,
        limit=48,
    )[0]
    packed = lax.all_to_all(packed, "exp", split_axis=0, concat_axis=0, tiled=True)
    payload, init_t = block_call(
        state_kernel,
        [
            jax.ShapeDtypeStruct((state + 16, channels), BF16),
            jax.ShapeDtypeStruct((state, channels), BF16),
        ],
        1,
        (place, x_in, b_in, dt_t, rate_row, init_state.reshape(channels, state)),
        held=5,
        limit=62,
    )
    pair = over_x(payload)
    own_part, fade, token = block_call(
        intra_kernel,
        [
            jax.ShapeDtypeStruct((tokens, channels), F32),
            jax.ShapeDtypeStruct((tokens, channels), F32),
            jax.ShapeDtypeStruct((8, 128), F32),
        ],
        0,
        (x_in, z_gate, b_in, c_out, dt_t, rate_row, skip[None, :]),
        held=7,
        limit=61,
    )
    joined = block_call(
        join_kernel,
        [jax.ShapeDtypeStruct((state, channels), BF16)],
        1,
        (place, payload, pair),
        after=(token,),
    )[0]
    early = over_y(joined)
    handed = (own_part, fade, c_out, init_t)
    select, own_part, fade, c, init_t = block_call(
        functools.partial(place_kernel, cap, experts),
        [jax.ShapeDtypeStruct((experts, rows + slots, tokens), BF16)]
        + [jax.ShapeDtypeStruct(v.shape, v.dtype) for v in handed],
        1,
        (self_id, packed, *handed),
        after=(joined,),
    )
    groups = owners // 2
    lanes = jax.ShapeDtypeStruct((groups, rows + slots, channels), BF16)
    one = jax.ShapeDtypeStruct((slots, channels), BF16)
    near_a, near_b, same, other = block_call(
        stream_kernel,
        [one, one, lanes, lanes],
        1,
        (place, c, own_part, fade, init_t, pair, early, packed, select),
    )

    gain = norm_gain.reshape(owners, 1, channels)
    wg = w_gate.reshape(owners, channels, w_gate.shape[2])
    wu = w_up.reshape(owners, channels, w_up.shape[2])
    expert_rows = jax.ShapeDtypeStruct((2, slots, channels), BF16)
    stream_rows = jax.ShapeDtypeStruct((2, rows + 8, channels), BF16)
    both_rows = jax.ShapeDtypeStruct((2, rows + slots, channels), BF16)
    near_a, near_b = along(near_a, 2), along(near_b, 3)
    stream0, first, far, stream3, farthest, stream1 = block_call(
        pair_kernel,
        [stream_rows, expert_rows, both_rows, stream_rows, expert_rows, stream_rows],
        0,
        (same, along(other, 1)),
    )
    gain = norm_gain.reshape(owners, 1, channels)
    wg = w_gate.reshape(owners, channels, w_gate.shape[2])
    wu = w_up.reshape(owners, channels, w_up.shape[2])
    gain = norm_gain.reshape(owners, 1, channels)
    wg = w_gate.reshape(owners, channels, w_gate.shape[2])
    wu = w_up.reshape(owners, channels, w_up.shape[2])

    def hold(values, after, name):
        outs = [jax.ShapeDtypeStruct(v.shape, BF16) for v in values]
        return block_call(hold_kernel, outs, 0, values, after=after, name=name)

    def project(group, near, far, carry, after=()):
        last = group == groups - 1
        return up_project(group, last, self_id, near, far, gain, wg, wu, carry, after)

    def message(count):
        return [jax.ShapeDtypeStruct((count, slots, channels), BF16)] * 2

    far = along(far, 4)
    rx0, ry0 = over_x(first), over_y(first)
    near = block_call(near_kernel, [expert_rows], 0, (near_a, near_b))[0]
    rx1, ry1 = over_x(near), over_y(near)
    to_x, to_y = block_call(
        half_message_kernel, message(1), 0, (rx0, ry0), after=(near,), name="half_0"
    )
    fx0, fy0 = over_x(to_x), over_y(to_y)
    farthest_held = hold((farthest,), (far,), "hold_farthest")[0]
    farthest = along(farthest_held, 6)
    to_x, to_y, far, stream2 = block_call(
        join_message_kernel,
        message(3) + [expert_rows, stream_rows],
        0,
        (far, rx1, ry1),
        after=(fx0, fy0, farthest_held),
        name="join_2",
    )
    rx2, ry2 = over_x(to_x), over_y(to_y)
    carry = project(0, [(first, 0), (rx0, 0), (ry0, 0)], [(fy0, 0), (fx0, 0)], None)
    to_x, to_y = block_call(
        join_message_kernel, message(3), 0, (farthest, rx2, ry2), after=(carry[2],), name="join_3"
    )
    rx3, ry3 = over_x(to_x), over_y(to_y)
    held, stream1 = hold((stream3, stream1), (to_x,), "hold_streams")
    stream3, stream1 = along(held, 6), along(stream1, 2)
    carry = project(1, [(near, 0), (rx1, 0), (ry1, 0)], [(ry2, 2), (rx2, 2)], carry, (held,))
    to_x, to_y = block_call(
        half_message_kernel, message(1), 0, (rx3, ry3), after=(carry[2],), name="half_3"
    )
    fx3, fy3 = over_x(to_x), over_y(to_y)
    carry = project(2, [(far, 0), (rx2, 0), (ry2, 0)], [(ry3, 2), (rx3, 2)], carry, (stream1, stream3))
    active_far, active = project(
        3, [(farthest, 0), (rx3, 0), (ry3, 0)], [(fy3, 0), (fx3, 0)], carry
    )

    wd = w_down.reshape(w_down.shape[1], features)
    tiles = jax.ShapeDtypeStruct((9, 16, features // 8), BF16)
    sent = down_project("down_through", groups, active_far, wd)
    rest = down_project("down_rest", groups, active, wd)
    own, own_x, own_y = ([rest[3 * g + k] for g in range(groups)] for k in range(3))

    def relay(name, through_x, through_y, low, ahead=(), after=()):
        shares = (own_x[low], own_y[low], own_x[low + 1], own_y[low + 1])
        return block_call(
            relay_kernel,
            [tiles] * (4 + len(ahead)),
            0,
            (through_x, through_y, *shares, *ahead),
            after=after,
            name=name,
        )

    def finish(group, rx, ry, ahead=(), after=()):
        return block_call(
            finish_kernel,
            [tiles] * (1 + len(ahead)),
            0,
            (own[group], rx, ry, *ahead),
            after=after,
            name=f"finish_{group}",
        )

    through_x, through_y = over_x(sent[2]), over_y(sent[3])
    x2, y2, x3, y3, next_x, next_y = relay(
        "relay_far", through_x, through_y, 2, (sent[0], sent[1])
    )
    rx3, ry3 = over_x(x3), over_y(y3)
    through_x, through_y = over_x(next_x), over_y(next_y)
    both3, x2, y2 = finish(3, rx3, ry3, (x2, y2))
    back3 = along(both3, 6)
    rx2, ry2 = over_x(x2), over_y(y2)
    x0, y0, x1, y1 = relay("relay_near", through_x, through_y, 0, after=(both3,))
    rx1, ry1 = over_x(x1), over_y(y1)
    both2, x0, y0 = finish(2, rx2, ry2, (x0, y0))
    back2 = along(both2, 4)
    rx0, ry0 = over_x(x0), over_y(y0)
    back1 = along(finish(1, rx1, ry1, after=(back3,))[0], 2)
    back = [finish(0, rx0, ry0)[0], back1, back2, back3]
    swap = block_call(second_kernel, [jax.ShapeDtypeStruct((2,) + tiles.shape, BF16)], 0, back)[0]
    swap = along(swap, 1)
    return block_call(
        mix_kernel,
        [jax.ShapeDtypeStruct((rows, features), BF16)],
        1,
        (self_id, ids_t, gate_weights.T, swap, *back, stream0, stream1, stream2, stream3),
    )[0]


def entering_2(array, axis, combine, identity):
    devices, mine = (lax.axis_size(axis), lax.axis_index(axis))
    everything = jax.tree.map(
        lambda part, kind: lax.all_gather(part.astype(kind), axis),
        array,
        (jnp.bfloat16, jnp.bfloat16),
    )
    start = jax.tree.map(
        lambda part, zero: jnp.broadcast_to(jnp.asarray(zero, part.dtype), part.shape),
        array,
        identity,
    )

    def hop(k, before):
        reached = k < mine
        new = combine(
            before, jax.tree.map(lambda part, own: part[k].astype(own.dtype), everything, array)
        )
        return jax.tree.map(lambda a, b: jnp.where(reached, a, b), new, before)

    return lax.fori_loop(0, devices, hop, start)


def chain_combine(earlier, later):
    return (earlier[0] + later[0], jnp.exp(later[0])[:, None, None] * earlier[1] + later[1])


def on_device(
    x_in,
    z_gate,
    b_in,
    c_out,
    dt_step,
    rate,
    skip,
    init_state,
    residual,
    norm_gain,
    expert_ids,
    gate_weights,
    w_gate,
    w_up,
    w_down,
):
    token_count, channels = x_in.shape
    heads_here = rate.shape[0]
    head_width = channels // heads_here
    state_width = b_in.shape[1]
    blocks = token_count // GROUP
    inputs = x_in.astype(jnp.float32).reshape(blocks, GROUP, heads_here, head_width)
    keys_in = b_in.astype(jnp.float32).reshape(blocks, GROUP, state_width)
    queries = c_out.astype(jnp.float32).reshape(blocks, GROUP, state_width)
    log_steps = (-rate[None, :] * dt_step).reshape(blocks, GROUP, heads_here)
    cumulative = jnp.cumsum(log_steps, axis=1)
    scores = jnp.einsum("ctn,csn->cts", queries, keys_in, precision=PRECISE)
    causal = jnp.arange(GROUP)[:, None] >= jnp.arange(GROUP)[None, :]
    spread = cumulative[:, :, None, :] - cumulative[:, None, :, :]
    weights = jnp.exp(jnp.where(causal[None, :, :, None], spread, -jnp.inf)) * scores[..., None]
    intra_out = jnp.einsum("ctsh,cshp->cthp", weights, inputs, precision=PRECISE)
    tail_decay = jnp.exp(cumulative[:, -1:, :] - cumulative)
    block_state = jnp.einsum("csh,cshp,csn->chpn", tail_decay, inputs, keys_in, precision=PRECISE)
    block_log = cumulative[:, -1, :]

    def advance(carried, element):
        total_log, total_state = carried
        step_log, step_state = element
        updated = (
            total_log + step_log,
            jnp.exp(step_log)[:, None, None] * total_state + step_state,
        )
        return (updated, (total_log, total_state))

    zero_state = jnp.zeros((heads_here, head_width, state_width), jnp.float32)
    zero_log = jnp.zeros((heads_here,), jnp.float32)
    (device_log, device_state), (enter_log, enter_state) = lax.scan(
        advance, (zero_log, zero_state), (block_log, block_state)
    )
    prior_log, prior_state = entering_2(
        (device_log, device_state), "seq", chain_combine, (zero_log, zero_state)
    )
    incoming = prior_state + jnp.exp(prior_log)[:, None, None] * init_state
    entering = enter_state + jnp.exp(enter_log)[:, :, None, None] * incoming[None]
    inter_out = jnp.exp(cumulative)[..., None] * jnp.einsum(
        "chpn,ctn->cthp", entering, queries, precision=PRECISE
    )
    mixed_out = (intra_out + inter_out + skip[None, None, :, None] * inputs).reshape(
        token_count, channels
    )
    mixer = (mixed_out * jax.nn.silu(z_gate.astype(jnp.float32))).astype(jnp.bfloat16)
    token_mix = lax.all_to_all(mixer, "exp", split_axis=0, concat_axis=1, tiled=True)
    stream = (residual.astype(jnp.float32) + token_mix.astype(jnp.float32)).astype(jnp.bfloat16)
    widened = stream.astype(jnp.float32)
    normed = (
        widened
        * lax.rsqrt(jnp.mean(widened * widened, axis=-1, keepdims=True) + 1e-06)
        * norm_gain[None, :]
    ).astype(jnp.bfloat16)
    rows_here = residual.shape[0]
    owners = lax.axis_size("exp")
    local_experts = w_gate.shape[0]
    experts = owners * local_experts
    capacity = max(2, 2 * rows_here // experts + 1)
    width = residual.shape[1]
    chosen = expert_ids.reshape(-1)
    onehot = (chosen[:, None] == jnp.arange(experts)[None, :]).astype(jnp.int32)
    slot_index = jnp.sum((jnp.cumsum(onehot, axis=0) - onehot) * onehot, axis=1)
    target = chosen * capacity + slot_index
    placing = (target[None, :] == jnp.arange(experts * capacity)[:, None]).astype(jnp.bfloat16)
    pair_rows = jnp.repeat(normed, 2, axis=0)
    outgoing = jnp.dot(placing, pair_rows, preferred_element_type=jnp.float32).astype(jnp.bfloat16)
    outgoing = outgoing.reshape(owners, local_experts, 1, capacity, width)
    arrived = lax.all_to_all(outgoing, "exp", split_axis=0, concat_axis=2, tiled=True)
    segment = lax.all_gather(arrived, "seq", axis=1, tiled=True)
    flattened = segment.reshape(segment.shape[0], -1, segment.shape[-1])
    gate_proj = jnp.einsum("erd,edf->erf", flattened, w_gate, preferred_element_type=jnp.float32)
    up_proj = jnp.einsum("erd,edf->erf", flattened, w_up, preferred_element_type=jnp.float32)
    active = (jax.nn.silu(gate_proj) * up_proj).astype(jnp.bfloat16)
    partial_value = jnp.einsum("erf,efd->erd", active, w_down, preferred_element_type=jnp.float32)
    partials = partial_value.reshape(segment.shape[:-1] + (partial_value.shape[-1],))
    summed = lax.psum_scatter(partials.astype(jnp.bfloat16), "seq", scatter_dimension=1, tiled=True)
    returned = lax.all_to_all(summed, "exp", split_axis=2, concat_axis=0, tiled=True)
    results = returned.reshape(experts * capacity, width)
    picked = results[target].astype(jnp.float32).reshape(rows_here, 2, width)
    mixture = jnp.sum(picked * gate_weights[:, :, None], axis=1)
    return (widened + mixture).astype(jnp.bfloat16)


def solution(mesh):
    square = mesh.shape["seq"] == 4 and mesh.shape["exp"] == 8

    def body(*args):
        rows = args[8].shape[0]
        experts = mesh.shape["exp"] * args[12].shape[0]
        fits = args[12].shape[0] == 1 and 2 * rows // experts + 1 == 9
        return (on_square if square and fits else on_device)(*args)

    return jax.shard_map(
        body,
        mesh=mesh,
        in_specs=(
            P("seq", "exp"),
            P("seq", "exp"),
            P("seq", None),
            P("seq", None),
            P("seq", "exp"),
            P("exp"),
            P("exp"),
            P("exp", None, None),
            P(("seq", "exp"), None),
            P(),
            P(("seq", "exp"), None),
            P(("seq", "exp"), None),
            P("exp", None, "seq"),
            P("exp", None, "seq"),
            P("exp", "seq", None),
        ),
        out_specs=P(("seq", "exp"), None),
        check_vma=False,
    )
```

```python
import functools

import jax
import jax.numpy as jnp
from jax import lax
from jax.experimental import pallas as pl
from jax.experimental.pallas import tpu as pltpu
from jax.sharding import PartitionSpec as P

GROUP = 128
PRECISE = lax.Precision.HIGHEST
F32 = jnp.float32
BF16 = jnp.bfloat16
MIB = 1 << 20
NO_COST = pl.CostEstimate(flops=0, bytes_accessed=0, transcendentals=0)


def block_call(body, outs, scalars, args, held=0, keep=0, after=(), limit=16, out_blocks=False, name=None):
    n_args = len(args)
    kept = [jax.ShapeDtypeStruct(v.shape, v.dtype) for v in args[scalars : scalars + held]]

    def kernel(*refs):
        refs, sems = (refs[:-1], refs[-1]) if held else (refs, None)
        inputs, refs = refs[:n_args], refs[n_args + len(after) :]
        results, refs = refs[: len(outs)], refs[len(outs) :]
        copies = [
            pltpu.make_async_copy(src, dst, sems.at[k])
            for k, (src, dst) in enumerate(zip(inputs[scalars : scalars + held], refs))
        ]
        for copy in copies:
            copy.start()
        for copy in copies:
            copy.wait()
        body(*inputs[:scalars], *refs, *inputs[scalars + held :], *results)

    scratch = [pltpu.VMEM(v.shape, v.dtype) for v in kept[keep:]]
    if held:
        scratch.append(pltpu.SemaphoreType.DMA((held,)))
    return pl.pallas_call(
        kernel,
        name=name or getattr(body, "func", body).__name__,
        out_shape=list(outs) + kept[:keep],
        in_specs=[pl.BlockSpec(memory_space=pltpu.SMEM)] * scalars
        + [pl.BlockSpec(memory_space=pltpu.HBM)] * held
        + [pl.BlockSpec(memory_space=pltpu.VMEM)] * (n_args - scalars - held)
        + [pl.BlockSpec(memory_space=pl.ANY)] * len(after),
        out_specs=[pl.BlockSpec() if out_blocks else pl.BlockSpec(memory_space=pltpu.VMEM)]
        * (len(outs) + keep),
        scratch_shapes=scratch,
        compiler_params=pltpu.CompilerParams(vmem_limit_bytes=limit * MIB),
        cost_estimate=NO_COST,
    )(*args, *after)


def iota(shape, dim):
    return lax.broadcasted_iota(jnp.int32, shape, dim)


def dot(a, b, precision=None):
    return jnp.dot(a, b, precision=precision, preferred_element_type=F32)


def head_spread(heads, channels):
    shape = (heads, channels)
    return (iota(shape, 1) // (channels // heads) == iota(shape, 0)).astype(F32)


def running_logs(dt_t_ref, rate_ref):
    logs = -rate_ref[...] * dt_t_ref[...].T
    tokens = logs.shape[0]
    tri = (iota((tokens, tokens), 0) >= iota((tokens, tokens), 1)).astype(F32)
    return dot(tri, logs, PRECISE)


def pack_kernel(ids_t_ref, residual_ref, out_ref):
    parts, rows, wide = out_ref.shape
    part = wide - 128
    ids = ids_t_ref[...].astype(F32).T
    lane = iota((rows, 128), 1)
    named = jnp.where(lane == 0, ids[:, 0:1], jnp.where(lane == 1, ids[:, 1:2], 0.0)).astype(BF16)
    for k in range(parts):
        out_ref[k, :, 0:part] = residual_ref[:, k * part : (k + 1) * part]
        out_ref[k, :, part:wide] = named


def state_kernel(place, x_ref, b_ref, dt_t_ref, rate_ref, init_ref, payload_ref, init_t_ref):
    tokens, channels = x_ref.shape
    heads = dt_t_ref.shape[0]
    width = b_ref.shape[1]
    cum = running_logs(dt_t_ref, rate_ref)
    total = cum[tokens - 1 : tokens, :]
    spread = head_spread(heads, channels)
    tail = dot(jnp.exp(total - cum), spread, PRECISE)
    scaled = (x_ref[...].astype(F32) * tail).astype(BF16)
    keys = b_ref[...].astype(F32).T.astype(BF16)
    own = dot(keys, scaled)
    decay = dot(jnp.broadcast_to(jnp.exp(total), (8, heads)), spread, PRECISE)
    init_t = init_ref[...].T
    init_t_ref[...] = init_t.astype(BF16)
    first = (place[0] == 0).astype(F32)
    payload_ref[0:width, :] = (own + first * (decay[0:1, :] * init_t)).astype(BF16)
    high = decay.astype(BF16).astype(F32)
    rows = iota((16, channels), 0)
    high16 = jnp.broadcast_to(high[0:1, :], (16, channels))
    low16 = jnp.broadcast_to(decay[0:1, :], (16, channels)) - high16
    payload_ref[width : width + 16, :] = jnp.where(
        rows == 0, high16, jnp.where(rows == 1, low16, 0.0)
    ).astype(BF16)


def intra_kernel(x_ref, z_ref, b_ref, c_ref, dt_t_ref, rate_ref, skip_ref, own_ref, fade_ref, token_ref):
    tokens, channels = x_ref.shape
    heads = dt_t_ref.shape[0]
    width = channels // heads
    token_ref[...] = jnp.zeros_like(token_ref)
    shape = (tokens, tokens)
    causal = iota(shape, 0) >= iota(shape, 1)
    cum = running_logs(dt_t_ref, rate_ref)
    cum_t = cum.T
    scores = lax.dot_general(
        c_ref[...], b_ref[...], (((1,), (1,)), ((), ())), preferred_element_type=F32
    )
    spread = head_spread(heads, channels)
    direct = dot(jnp.broadcast_to(skip_ref[...], (8, heads)), spread, PRECISE)[0:1, :]
    fade = dot(jnp.exp(cum), spread, PRECISE)
    per = 128 // width
    lane_head = iota((tokens, 128), 1) // width
    for group in range(heads // per):
        cols = slice(group * 128, (group + 1) * 128)
        x = x_ref[:, cols]
        total = x.astype(F32) * direct[:, cols]
        for k in range(per):
            h = group * per + k
            gap = jnp.where(causal, cum[:, h : h + 1] - cum_t[h : h + 1, :], -1e30)
            weights = (jnp.exp(gap) * scores).astype(BF16)
            part = dot(weights, x)
            total = total + jnp.where(lane_head == k, part, 0.0)
        z = z_ref[:, cols].astype(F32)
        gate = z / (1.0 + jnp.exp(-z))
        own_ref[:, cols] = total * gate
        fade_ref[:, cols] = fade[:, cols] * gate


def place_kernel(cap, experts, me, packed_ref, *refs):
    count = (len(refs) - 1) // 2
    out_ref = refs[count]
    for source, target in zip(refs[:count], refs[count + 1 :]):
        target[...] = source[...]
    blocks, rows, wide = packed_ref.shape
    tokens = blocks * rows
    slots = out_ref.shape[1] - rows
    ids = packed_ref[:, :, wide - 128 : wide].astype(F32).reshape(tokens, 128).T
    ids = ids[0:8, :].astype(jnp.int32)
    shape = (tokens, tokens)
    before = (iota(shape, 0) < iota(shape, 1)) & (iota(shape, 0) // rows == iota(shape, 1) // rows)
    named = iota((experts, tokens), 0) ^ me[0]
    hit = (ids[0:1, :] == named) | (ids[1:2, :] == named)
    rank = dot(hit.astype(BF16), before.astype(BF16)).astype(jnp.int32)
    block = (iota((experts, tokens), 1) // rows) ^ named
    whole = cap - 1
    row = jnp.where(rank < whole, block * whole + rank, blocks * whole + block)
    row = jnp.where(hit, row, -1)
    shape = (rows + slots, tokens)
    for e in range(experts):
        owned = ((me[0] ^ e) * rows + iota(shape, 0) == iota(shape, 1)) & (iota(shape, 0) < rows)
        placed = (iota(shape, 0) - rows == row[e : e + 1, :]) & (iota(shape, 0) >= rows)
        out_ref[e] = (owned | placed).astype(F32).astype(BF16)


def join_kernel(place, own_ref, other_ref, out_ref):
    width = out_ref.shape[0]
    odd = place[0] % 2 == 1
    own, other = own_ref[0:width, :].astype(F32), other_ref[0:width, :].astype(F32)
    own_decay = own_ref[width : width + 16, :].astype(F32)
    other_decay = other_ref[width : width + 16, :].astype(F32)
    own_decay = own_decay[0:1, :] + own_decay[1:2, :]
    other_decay = other_decay[0:1, :] + other_decay[1:2, :]
    early = jnp.where(odd, other, own)
    late = jnp.where(odd, own, other)
    decay = jnp.where(odd, own_decay, other_decay)
    out_ref[...] = (decay * early + late).astype(BF16)


def stream_kernel(
    place, c_ref, own_ref, fade_ref, init_t_ref, pair_ref, early_ref, res_ref, sel_ref, near_a_ref, near_b_ref, same_ref, other_ref
):
    width = init_t_ref.shape[0]
    at = place[0]
    zero = (at == 0).astype(F32)
    odd = (at % 2 == 1).astype(F32)
    pair = pair_ref[...].astype(F32)
    decay = pair[width : width + 1, :] + pair[width + 1 : width + 2, :]
    factor = jnp.where(at >= 2, jnp.where(at % 2 == 1, decay, 1.0), 0.0)
    entering = zero * init_t_ref[...].astype(F32) + odd * pair[0:width, :] + factor * early_ref[...].astype(F32)
    mixed = own_ref[...] + fade_ref[...] * dot(c_ref[...], entering.astype(BF16))
    mixer = mixed.astype(BF16).astype(F32)
    tokens, channels = mixer.shape
    residual = res_ref[:, :, 0:channels].astype(F32).reshape(tokens, channels)
    stream = (residual + mixer).astype(BF16)
    owned = sel_ref.shape[1] - near_a_ref.shape[0]
    near_a_ref[...] = dot(sel_ref[2, owned:, :], stream).astype(BF16)
    near_b_ref[...] = dot(sel_ref[3, owned:, :], stream).astype(BF16)
    for at, k in enumerate((0, 2, 3, 1)):
        same_ref[at] = dot(sel_ref[2 * k], stream).astype(BF16)
        other_ref[at] = dot(sel_ref[2 * k + 1], stream).astype(BF16)


def up_kernel(first, features, after, me, *refs):
    own, rx, ry, even, odd, gain, wg, wu = refs[:8]
    carry = () if first else refs[8:11]
    rest = refs[(8 if first else 11) + after :]
    sums = rest[2:5] if features else rest
    step = pl.program_id(0)
    steps = pl.num_programs(0)

    if first or features:

        @pl.when(step == 0)
        def _():
            for i, acc in enumerate(sums):
                acc[...] = jnp.zeros_like(acc) if first else carry[i][...]

    gate, up, square = sums
    slots = own.shape[1]
    rows = [r[0].astype(F32) for r in (own, rx, ry)]
    rows.append(jnp.where(step == 0, even[0].astype(F32), odd[0].astype(F32)))
    rows = jnp.concatenate(rows, axis=0)
    square[...] += jnp.broadcast_to(jnp.sum(rows * rows, axis=1, keepdims=True), square.shape)
    scaled = (rows * gain[0]).astype(BF16)
    gate[...] += dot(scaled, wg[0])
    up[...] += dot(scaled, wu[0])

    if features:
        outs, stages = rest[:2], rest[5:]

        @pl.when(step == steps - 1)
        def _():
            inverse = lax.rsqrt(square[:, 0:1] * (1.0 / features) + 1e-06)
            g = gate[...] * inverse
            active = g / (1.0 + jnp.exp(-g)) * (up[...] * inverse)
            main, ninths = slots // 9 * 8, slots // 9
            for d in range(4):
                at = d * slots
                stage, d, shards = (stages[0], 0, 1) if d == 3 else (stages[1], d, 3)
                stage[d * main : (d + 1) * main, :] = active[at : at + main]
                low = shards * main + d * ninths
                stage[low : low + ninths, :] = active[at + main : at + slots]
            for out, stage in zip(outs, stages):
                out[...] = stage[...].astype(BF16)


def up_project(group, last, me, near, far, gain, w_gate, w_up, carry, after=()):
    slots, part = near[0][0].shape[1:]
    hidden = w_gate.shape[2]
    total = 4 * slots
    source = lambda i, me: me[0] ^ (2 * group + i)
    rows = [
        pl.BlockSpec((1, slots, part), lambda i, me, start=start: (start + i, 0, 0))
        for _, start in near
    ] + [
        pl.BlockSpec((1, slots, part), lambda i, me, start=start: (start, 0, 0)) for _, start in far
    ]
    weight = pl.BlockSpec((1, part, hidden), lambda i, me: (source(i, me), 0, 0))
    in_place = pl.BlockSpec(memory_space=pltpu.VMEM)
    specs = rows + [pl.BlockSpec((1, 1, part), lambda i, me: (source(i, me), 0, 0)), weight, weight]
    sums = [
        jax.ShapeDtypeStruct((total, hidden), F32),
        jax.ShapeDtypeStruct((total, hidden), F32),
        jax.ShapeDtypeStruct((total, 128), F32),
    ]
    aliases = {}
    if carry is not None:
        specs += [in_place] * 3
        if not last:
            aliases = {9 + i: i for i in range(3)}
    specs += [pl.BlockSpec(memory_space=pl.ANY)] * len(after)
    sizes = (slots, 3 * slots)
    outs = [jax.ShapeDtypeStruct((n, hidden), BF16) for n in sizes] if last else sums
    scratch = [pltpu.VMEM(s.shape, s.dtype) for s in sums]
    scratch += [pltpu.VMEM((n, hidden), F32) for n in sizes]
    features = gain.shape[0] * part if last else 0
    return pl.pallas_call(
        functools.partial(up_kernel, carry is None, features, len(after)),
        name=f"up_{group}",
        out_shape=outs,
        grid_spec=pltpu.PrefetchScalarGridSpec(
            num_scalar_prefetch=1,
            grid=(2,),
            in_specs=specs,
            out_specs=[in_place] * len(outs),
            scratch_shapes=scratch if last else [],
        ),
        input_output_aliases=aliases,
        compiler_params=pltpu.CompilerParams(vmem_limit_bytes=48 * MIB),
        cost_estimate=NO_COST,
    )(me, *(array for array, _ in near + far), gain, w_gate, w_up, *(carry or ()), *after)


def cut_of(group):
    return 5 if group % 2 else 4


def down_kernel(groups, act_ref, w_ref, *refs):
    outs, (spare, held, sems) = refs[:-3], refs[-3:]
    step = pl.program_id(0)
    steps, _, tile = held.shape

    def load(k):
        columns = pl.ds(pl.multiple_of(k * tile, tile), tile)
        return pltpu.make_async_copy(w_ref.at[:, columns], held.at[k], sems.at[k])

    @pl.when(step == 0)
    def _():
        for k in range(steps):
            load(k).start()

    load(step).wait()
    part = dot(act_ref[...], held[step])
    ninths = part.shape[0] // 9
    main = part.shape[0] - ninths
    shards = ninths // (2 * groups)

    def through(group, tile):
        to_x, to_y = outs[2 * (group // 2) : 2 * (group // 2) + 2]
        cut = cut_of(group)
        return to_x, tile + (0 if group % 2 else 5), to_y, tile - cut + (0 if group % 2 else 4)

    for shard in range(shards):
        for group in range(groups):
            at = (shard * groups + group) * 16
            rows = part[at : at + 16, :].astype(BF16)
            if shards > 1:
                outs[shards * group + shard][step] = rows
                continue
            to_x, place_x, to_y, place_y = through(group, step)

            @pl.when(step < cut_of(group))
            def _():
                to_x[place_x] = rows

            @pl.when(step >= cut_of(group))
            def _():
                to_y[place_y] = rows

    for lanes in range(spare.shape[0]):
        spare[lanes, pl.ds(pl.multiple_of(step * ninths, 8), ninths), :] = part[
            main:, lanes * 128 : (lanes + 1) * 128
        ]

    @pl.when(step == steps - 1)
    def _():
        for shard in range(shards):
            for group in range(groups):
                pair = []
                for side in range(2):
                    row = pl.ds((shard * groups + group) * 2 + side, 8, stride=ninths)
                    ninth = [spare[lanes, row, :] for lanes in range(spare.shape[0])]
                    pair.append(jnp.concatenate(ninth, axis=1))
                pair = jnp.concatenate(pair, axis=0).astype(BF16)
                if shards > 1:
                    outs[shards * group + shard][8] = pair
                else:
                    _, _, to_y, place_y = through(group, 8)
                    to_y[place_y] = pair


def down_project(name, groups, active, w_down):
    total, hidden = active.shape
    features = w_down.shape[1]
    tile = features // 8
    outs = [jax.ShapeDtypeStruct((9, 16, tile), BF16)] * (total // 18)
    return pl.pallas_call(
        functools.partial(down_kernel, groups),
        name=name,
        grid=(8,),
        out_shape=outs,
        in_specs=[
            pl.BlockSpec(memory_space=pltpu.VMEM),
            pl.BlockSpec(memory_space=pltpu.HBM),
        ],
        out_specs=[pl.BlockSpec(memory_space=pltpu.VMEM)] * len(outs),
        scratch_shapes=[
            pltpu.VMEM((tile // 128, 8 * total // 9, 128), F32),
            pltpu.VMEM((8, hidden, tile), BF16),
            pltpu.SemaphoreType.DMA((8,)),
        ],
        compiler_params=pltpu.CompilerParams(vmem_limit_bytes=48 * MIB),
        cost_estimate=NO_COST,
    )(active, w_down)


def pair_kernel(same, other, own_stream, own, far_stream, far, last_stream, last, near_stream):
    owned = same.shape[1] - own.shape[1]
    for side, rows in enumerate((same, other)):
        own_stream[side, 0:owned, :], own[side] = rows[0, 0:owned, :], rows[0, owned:, :]
        far_stream[side, 0:owned, :], far[side] = rows[1, 0:owned, :], rows[1, owned:, :]
        last_stream[side, 0:owned, :], last[side] = rows[2, 0:owned, :], rows[2, owned:, :]
        near_stream[side, 0:owned, :] = rows[3, 0:owned, :]


def near_kernel(same, other, rows):
    rows[0], rows[1] = same[...], other[...]


def second_kernel(*refs):
    parts, out = refs[:-1], refs[-1]
    for h in range(out.shape[0]):
        for k in range(out.shape[1]):
            pair = [ref[k].astype(F32)[8:16] for ref in parts[2 * h : 2 * h + 2]]
            out[h, k] = jnp.concatenate(pair, axis=0).astype(BF16)


def hold_kernel(*refs):
    for source, target in zip(refs[: len(refs) // 2], refs[len(refs) // 2 :]):
        target[...] = source[...]


def half_message_kernel(rx, ry, out_x, out_y):
    out_x[0], out_y[0] = ry[1], rx[0]


def join_message_kernel(own, rx, ry, out_x, out_y):
    out_x[0:2], out_y[0:2] = own[...], own[...]
    out_x[2], out_y[2] = ry[1], rx[0]


def relay_kernel(through_x, through_y, *refs):
    ahead = refs[4 : 4 + (len(refs) - 8) // 2]
    outs, copies = refs[4 + len(ahead) :][:4], refs[8 + len(ahead) :]
    for group in range(2):
        cut = cut_of(group)
        at_x, at_y = (0, -cut) if group else (5, 0)
        for own, out, through, tiles, at in (
            (refs[2 * group], outs[2 * group], through_y, range(cut, 9), at_y),
            (refs[2 * group + 1], outs[2 * group + 1], through_x, range(cut), at_x),
        ):
            for k in range(9):
                if k in tiles:
                    out[k] = (own[k].astype(F32) + through[k + at].astype(F32)).astype(BF16)
                else:
                    out[k] = own[k]
    for source, copy in zip(ahead, copies):
        copy[...] = source[...]


def finish_kernel(own, rx, ry, *refs):
    ahead = refs[: (len(refs) - 1) // 2]
    out, copies = refs[len(ahead)], refs[len(ahead) + 1 :]
    for k in range(9):
        out[k] = (own[k].astype(F32) + rx[k].astype(F32) + ry[k].astype(F32)).astype(BF16)
    for source, copy in zip(ahead, copies):
        copy[...] = source[...]


def mix_kernel(me, ids_t_ref, weight_t_ref, swap_ref, *refs):
    groups = (len(refs) - 1) // 2
    firsts, streams, out_ref = refs[:groups], refs[groups:-1], refs[-1]
    rows = ids_t_ref.shape[1]
    experts = 2 * groups
    pieces = firsts[0].shape[0] - 1
    tile = firsts[0].shape[2]
    ids, weights = ids_t_ref[...].T, weight_t_ref[...].T
    named = iota((rows, experts), 1) ^ me[0]
    first, second = ids[:, 0:1] == named, ids[:, 1:2] == named
    weight = jnp.where(first, weights[:, 0:1], jnp.where(second, weights[:, 1:2], 0.0))
    hit = (first | second).astype(F32)
    before = (iota((rows, rows), 0) > iota((rows, rows), 1)).astype(F32)
    rank = dot(before, hit)
    lanes = 2 * experts * 8
    shape = (experts, lanes)
    spread = ((iota(shape, 1) // 8) % experts == iota(shape, 0)).astype(F32)
    weight = dot(weight, spread, PRECISE)
    rank = dot(rank, spread, PRECISE).astype(jnp.int32)
    lane = iota((rows, lanes), 1)
    main = (lane < experts * 8) & (rank == lane % 8)
    extra = (lane >= experts * 8) & (rank == 8)

    def rows_of(k):
        data = []
        for g in range(groups):
            data.append(firsts[g][k].astype(F32)[0:8])
            data.append(swap_ref[g // 2, k].astype(F32)[g % 2 * 8 : g % 2 * 8 + 8])
        return data

    last = rows_of(pieces)
    for m in range(experts):
        k = me[0] ^ m
        coef = jnp.where(main | (extra & (lane % 8 == k)), weight, 0.0)
        high = coef.astype(BF16)
        low = (coef - high.astype(F32)).astype(BF16)
        data = jnp.concatenate(rows_of(k) + last, axis=0).astype(BF16)
        stream = streams[m // 2][m % 2, 0:rows, :].astype(F32)
        out_ref[:, pl.ds(pl.multiple_of(k * tile, 128), tile)] = (
            stream + (dot(high, data) + dot(low, data))
        ).astype(BF16)


def on_square(
    x_in,
    z_gate,
    b_in,
    c_out,
    dt_step,
    rate,
    skip,
    init_state,
    residual,
    norm_gain,
    expert_ids,
    gate_weights,
    w_gate,
    w_up,
    w_down,
):
    tokens, channels = x_in.shape
    heads = rate.shape[0]
    state = b_in.shape[1]
    owners = lax.axis_size("exp")
    rows, features = residual.shape
    experts = owners
    cap = max(2, 2 * rows // experts + 1)
    slots = owners * cap
    at = lax.axis_index("seq")
    me = lax.axis_index("exp")
    place = jnp.reshape(at, (1,)).astype(jnp.int32)
    self_id = jnp.reshape(me, (1,)).astype(jnp.int32)

    def over_x(v):
        return lax.ppermute(v, "seq", [(i, i ^ 1) for i in range(4)])

    def over_y(v):
        return lax.ppermute(v, "seq", [(i, i ^ 2) for i in range(4)])

    def along(v, mask):
        return lax.ppermute(v, "exp", [(i, i ^ mask) for i in range(owners)])

    rate_row = rate[None, :]
    dt_t = dt_step.T
    ids_t = expert_ids.T
    packed = block_call(
        pack_kernel,
        [jax.ShapeDtypeStruct((owners, rows, channels + 128), BF16)],
        0,
        (ids_t, residual),
        held=2,
        limit=48,
    )[0]
    packed = lax.all_to_all(packed, "exp", split_axis=0, concat_axis=0, tiled=True)
    payload, init_t = block_call(
        state_kernel,
        [
            jax.ShapeDtypeStruct((state + 16, channels), BF16),
            jax.ShapeDtypeStruct((state, channels), BF16),
        ],
        1,
        (place, x_in, b_in, dt_t, rate_row, init_state.reshape(channels, state)),
        held=5,
        limit=62,
    )
    pair = over_x(payload)
    own_part, fade, token = block_call(
        intra_kernel,
        [
            jax.ShapeDtypeStruct((tokens, channels), F32),
            jax.ShapeDtypeStruct((tokens, channels), F32),
            jax.ShapeDtypeStruct((8, 128), F32),
        ],
        0,
        (x_in, z_gate, b_in, c_out, dt_t, rate_row, skip[None, :]),
        held=7,
        limit=61,
    )
    joined = block_call(
        join_kernel,
        [jax.ShapeDtypeStruct((state, channels), BF16)],
        1,
        (place, payload, pair),
        after=(token,),
    )[0]
    early = over_y(joined)
    handed = (own_part, fade, c_out, init_t)
    select, own_part, fade, c, init_t = block_call(
        functools.partial(place_kernel, cap, experts),
        [jax.ShapeDtypeStruct((experts, rows + slots, tokens), BF16)]
        + [jax.ShapeDtypeStruct(v.shape, v.dtype) for v in handed],
        1,
        (self_id, packed, *handed),
        after=(joined,),
    )
    groups = owners // 2
    lanes = jax.ShapeDtypeStruct((groups, rows + slots, channels), BF16)
    one = jax.ShapeDtypeStruct((slots, channels), BF16)
    near_a, near_b, same, other = block_call(
        stream_kernel,
        [one, one, lanes, lanes],
        1,
        (place, c, own_part, fade, init_t, pair, early, packed, select),
    )

    gain = norm_gain.reshape(owners, 1, channels)
    wg = w_gate.reshape(owners, channels, w_gate.shape[2])
    wu = w_up.reshape(owners, channels, w_up.shape[2])
    expert_rows = jax.ShapeDtypeStruct((2, slots, channels), BF16)
    stream_rows = jax.ShapeDtypeStruct((2, 40, channels), BF16)
    near_a, near_b = along(near_a, 2), along(near_b, 3)
    stream0, first, stream2, far, stream3, farthest, stream1 = block_call(
        pair_kernel,
        [stream_rows, expert_rows] * 3 + [stream_rows],
        0,
        (same, along(other, 1)),
    )
    gain = norm_gain.reshape(owners, 1, channels)
    wg = w_gate.reshape(owners, channels, w_gate.shape[2])
    wu = w_up.reshape(owners, channels, w_up.shape[2])
    gain = norm_gain.reshape(owners, 1, channels)
    wg = w_gate.reshape(owners, channels, w_gate.shape[2])
    wu = w_up.reshape(owners, channels, w_up.shape[2])

    def hold(values, after, name):
        outs = [jax.ShapeDtypeStruct(v.shape, BF16) for v in values]
        return block_call(hold_kernel, outs, 0, values, after=after, name=name)

    def project(group, near, far, carry, after=()):
        last = group == groups - 1
        return up_project(group, last, self_id, near, far, gain, wg, wu, carry, after)

    def message(count):
        return [jax.ShapeDtypeStruct((count, slots, channels), BF16)] * 2

    far = along(far, 4)
    rx0, ry0 = over_x(first), over_y(first)
    near = block_call(near_kernel, [expert_rows], 0, (near_a, near_b))[0]
    rx1, ry1 = over_x(near), over_y(near)
    to_x, to_y = block_call(
        half_message_kernel, message(1), 0, (rx0, ry0), after=(near,), name="half_0"
    )
    fx0, fy0 = over_x(to_x), over_y(to_y)
    farthest_held = hold((farthest,), (far,), "hold_farthest")[0]
    farthest = along(farthest_held, 6)
    to_x, to_y = block_call(
        join_message_kernel,
        message(3),
        0,
        (far, rx1, ry1),
        after=(fx0, fy0, farthest_held),
        name="join_2",
    )
    rx2, ry2 = over_x(to_x), over_y(to_y)
    carry = project(0, [(first, 0), (rx0, 0), (ry0, 0)], [(fy0, 0), (fx0, 0)], None)
    to_x, to_y = block_call(
        join_message_kernel, message(3), 0, (farthest, rx2, ry2), after=(carry[2],), name="join_3"
    )
    rx3, ry3 = over_x(to_x), over_y(to_y)
    held = hold((stream1, stream2, stream3), (to_x,), "hold_streams")
    stream1, stream2, stream3 = (along(v, 2 * g + 2) for g, v in enumerate(held))
    carry = project(1, [(near, 0), (rx1, 0), (ry1, 0)], [(ry2, 2), (rx2, 2)], carry, held[:1])
    to_x, to_y = block_call(
        half_message_kernel, message(1), 0, (rx3, ry3), after=(carry[2],), name="half_3"
    )
    fx3, fy3 = over_x(to_x), over_y(to_y)
    carry = project(2, [(far, 0), (rx2, 0), (ry2, 0)], [(ry3, 2), (rx3, 2)], carry, (stream1, stream2, stream3))
    active_far, active = project(
        3, [(farthest, 0), (rx3, 0), (ry3, 0)], [(fy3, 0), (fx3, 0)], carry
    )

    wd = w_down.reshape(w_down.shape[1], features)
    tiles = jax.ShapeDtypeStruct((9, 16, features // 8), BF16)
    sent = down_project("down_through", groups, active_far, wd)
    rest = down_project("down_rest", groups, active, wd)
    own, own_x, own_y = ([rest[3 * g + k] for g in range(groups)] for k in range(3))

    def relay(name, through_x, through_y, low, ahead=(), after=()):
        shares = (own_x[low], own_y[low], own_x[low + 1], own_y[low + 1])
        return block_call(
            relay_kernel,
            [tiles] * (4 + len(ahead)),
            0,
            (through_x, through_y, *shares, *ahead),
            after=after,
            name=name,
        )

    def finish(group, rx, ry, ahead=(), after=()):
        return block_call(
            finish_kernel,
            [tiles] * (1 + len(ahead)),
            0,
            (own[group], rx, ry, *ahead),
            after=after,
            name=f"finish_{group}",
        )

    through_x, through_y = over_x(sent[2]), over_y(sent[3])
    x2, y2, x3, y3, next_x, next_y = relay(
        "relay_far", through_x, through_y, 2, (sent[0], sent[1])
    )
    rx3, ry3 = over_x(x3), over_y(y3)
    through_x, through_y = over_x(next_x), over_y(next_y)
    both3, x2, y2 = finish(3, rx3, ry3, (x2, y2))
    back3 = along(both3, 6)
    rx2, ry2 = over_x(x2), over_y(y2)
    x0, y0, x1, y1 = relay("relay_near", through_x, through_y, 0, after=(both3,))
    rx1, ry1 = over_x(x1), over_y(y1)
    both2, x0, y0 = finish(2, rx2, ry2, (x0, y0))
    back2 = along(both2, 4)
    rx0, ry0 = over_x(x0), over_y(y0)
    back1 = along(finish(1, rx1, ry1, after=(back3,))[0], 2)
    back = [finish(0, rx0, ry0)[0], back1, back2, back3]
    swap = block_call(second_kernel, [jax.ShapeDtypeStruct((2,) + tiles.shape, BF16)], 0, back)[0]
    swap = along(swap, 1)
    return block_call(
        mix_kernel,
        [jax.ShapeDtypeStruct((rows, features), BF16)],
        1,
        (self_id, ids_t, gate_weights.T, swap, *back, stream0, stream1, stream2, stream3),
    )[0]


def entering_2(array, axis, combine, identity):
    devices, mine = (lax.axis_size(axis), lax.axis_index(axis))
    everything = jax.tree.map(
        lambda part, kind: lax.all_gather(part.astype(kind), axis),
        array,
        (jnp.bfloat16, jnp.bfloat16),
    )
    start = jax.tree.map(
        lambda part, zero: jnp.broadcast_to(jnp.asarray(zero, part.dtype), part.shape),
        array,
        identity,
    )

    def hop(k, before):
        reached = k < mine
        new = combine(
            before, jax.tree.map(lambda part, own: part[k].astype(own.dtype), everything, array)
        )
        return jax.tree.map(lambda a, b: jnp.where(reached, a, b), new, before)

    return lax.fori_loop(0, devices, hop, start)


def chain_combine(earlier, later):
    return (earlier[0] + later[0], jnp.exp(later[0])[:, None, None] * earlier[1] + later[1])


def on_device(
    x_in,
    z_gate,
    b_in,
    c_out,
    dt_step,
    rate,
    skip,
    init_state,
    residual,
    norm_gain,
    expert_ids,
    gate_weights,
    w_gate,
    w_up,
    w_down,
):
    token_count, channels = x_in.shape
    heads_here = rate.shape[0]
    head_width = channels // heads_here
    state_width = b_in.shape[1]
    blocks = token_count // GROUP
    inputs = x_in.astype(jnp.float32).reshape(blocks, GROUP, heads_here, head_width)
    keys_in = b_in.astype(jnp.float32).reshape(blocks, GROUP, state_width)
    queries = c_out.astype(jnp.float32).reshape(blocks, GROUP, state_width)
    log_steps = (-rate[None, :] * dt_step).reshape(blocks, GROUP, heads_here)
    cumulative = jnp.cumsum(log_steps, axis=1)
    scores = jnp.einsum("ctn,csn->cts", queries, keys_in, precision=PRECISE)
    causal = jnp.arange(GROUP)[:, None] >= jnp.arange(GROUP)[None, :]
    spread = cumulative[:, :, None, :] - cumulative[:, None, :, :]
    weights = jnp.exp(jnp.where(causal[None, :, :, None], spread, -jnp.inf)) * scores[..., None]
    intra_out = jnp.einsum("ctsh,cshp->cthp", weights, inputs, precision=PRECISE)
    tail_decay = jnp.exp(cumulative[:, -1:, :] - cumulative)
    block_state = jnp.einsum("csh,cshp,csn->chpn", tail_decay, inputs, keys_in, precision=PRECISE)
    block_log = cumulative[:, -1, :]

    def advance(carried, element):
        total_log, total_state = carried
        step_log, step_state = element
        updated = (
            total_log + step_log,
            jnp.exp(step_log)[:, None, None] * total_state + step_state,
        )
        return (updated, (total_log, total_state))

    zero_state = jnp.zeros((heads_here, head_width, state_width), jnp.float32)
    zero_log = jnp.zeros((heads_here,), jnp.float32)
    (device_log, device_state), (enter_log, enter_state) = lax.scan(
        advance, (zero_log, zero_state), (block_log, block_state)
    )
    prior_log, prior_state = entering_2(
        (device_log, device_state), "seq", chain_combine, (zero_log, zero_state)
    )
    incoming = prior_state + jnp.exp(prior_log)[:, None, None] * init_state
    entering = enter_state + jnp.exp(enter_log)[:, :, None, None] * incoming[None]
    inter_out = jnp.exp(cumulative)[..., None] * jnp.einsum(
        "chpn,ctn->cthp", entering, queries, precision=PRECISE
    )
    mixed_out = (intra_out + inter_out + skip[None, None, :, None] * inputs).reshape(
        token_count, channels
    )
    mixer = (mixed_out * jax.nn.silu(z_gate.astype(jnp.float32))).astype(jnp.bfloat16)
    token_mix = lax.all_to_all(mixer, "exp", split_axis=0, concat_axis=1, tiled=True)
    stream = (residual.astype(jnp.float32) + token_mix.astype(jnp.float32)).astype(jnp.bfloat16)
    widened = stream.astype(jnp.float32)
    normed = (
        widened
        * lax.rsqrt(jnp.mean(widened * widened, axis=-1, keepdims=True) + 1e-06)
        * norm_gain[None, :]
    ).astype(jnp.bfloat16)
    rows_here = residual.shape[0]
    owners = lax.axis_size("exp")
    local_experts = w_gate.shape[0]
    experts = owners * local_experts
    capacity = max(2, 2 * rows_here // experts + 1)
    width = residual.shape[1]
    chosen = expert_ids.reshape(-1)
    onehot = (chosen[:, None] == jnp.arange(experts)[None, :]).astype(jnp.int32)
    slot_index = jnp.sum((jnp.cumsum(onehot, axis=0) - onehot) * onehot, axis=1)
    target = chosen * capacity + slot_index
    placing = (target[None, :] == jnp.arange(experts * capacity)[:, None]).astype(jnp.bfloat16)
    pair_rows = jnp.repeat(normed, 2, axis=0)
    outgoing = jnp.dot(placing, pair_rows, preferred_element_type=jnp.float32).astype(jnp.bfloat16)
    outgoing = outgoing.reshape(owners, local_experts, 1, capacity, width)
    arrived = lax.all_to_all(outgoing, "exp", split_axis=0, concat_axis=2, tiled=True)
    segment = lax.all_gather(arrived, "seq", axis=1, tiled=True)
    flattened = segment.reshape(segment.shape[0], -1, segment.shape[-1])
    gate_proj = jnp.einsum("erd,edf->erf", flattened, w_gate, preferred_element_type=jnp.float32)
    up_proj = jnp.einsum("erd,edf->erf", flattened, w_up, preferred_element_type=jnp.float32)
    active = (jax.nn.silu(gate_proj) * up_proj).astype(jnp.bfloat16)
    partial_value = jnp.einsum("erf,efd->erd", active, w_down, preferred_element_type=jnp.float32)
    partials = partial_value.reshape(segment.shape[:-1] + (partial_value.shape[-1],))
    summed = lax.psum_scatter(partials.astype(jnp.bfloat16), "seq", scatter_dimension=1, tiled=True)
    returned = lax.all_to_all(summed, "exp", split_axis=2, concat_axis=0, tiled=True)
    results = returned.reshape(experts * capacity, width)
    picked = results[target].astype(jnp.float32).reshape(rows_here, 2, width)
    mixture = jnp.sum(picked * gate_weights[:, :, None], axis=1)
    return (widened + mixture).astype(jnp.bfloat16)


def solution(mesh):
    square = mesh.shape["seq"] == 4 and mesh.shape["exp"] == 8

    def body(*args):
        rows = args[8].shape[0]
        experts = mesh.shape["exp"] * args[12].shape[0]
        fits = args[12].shape[0] == 1 and 2 * rows // experts + 1 == 9
        return (on_square if square and fits else on_device)(*args)

    return jax.shard_map(
        body,
        mesh=mesh,
        in_specs=(
            P("seq", "exp"),
            P("seq", "exp"),
            P("seq", None),
            P("seq", None),
            P("seq", "exp"),
            P("exp"),
            P("exp"),
            P("exp", None, None),
            P(("seq", "exp"), None),
            P(),
            P(("seq", "exp"), None),
            P(("seq", "exp"), None),
            P("exp", None, "seq"),
            P("exp", None, "seq"),
            P("exp", "seq", None),
        ),
        out_specs=P(("seq", "exp"), None),
        check_vma=False,
    )
```

```python
import functools

import jax
import jax.numpy as jnp
from jax import lax
from jax.experimental import pallas as pl
from jax.experimental.pallas import tpu as pltpu
from jax.sharding import PartitionSpec as P

GROUP = 128
PRECISE = lax.Precision.HIGHEST
F32 = jnp.float32
BF16 = jnp.bfloat16
MIB = 1 << 20
NO_COST = pl.CostEstimate(flops=0, bytes_accessed=0, transcendentals=0)


def block_call(body, outs, scalars, args, held=0, keep=0, after=(), limit=16, out_blocks=False, name=None):
    n_args = len(args)
    kept = [jax.ShapeDtypeStruct(v.shape, v.dtype) for v in args[scalars : scalars + held]]

    def kernel(*refs):
        refs, sems = (refs[:-1], refs[-1]) if held else (refs, None)
        inputs, refs = refs[:n_args], refs[n_args + len(after) :]
        results, refs = refs[: len(outs)], refs[len(outs) :]
        copies = [
            pltpu.make_async_copy(src, dst, sems.at[k])
            for k, (src, dst) in enumerate(zip(inputs[scalars : scalars + held], refs))
        ]
        for copy in copies:
            copy.start()
        for copy in copies:
            copy.wait()
        body(*inputs[:scalars], *refs, *inputs[scalars + held :], *results)

    scratch = [pltpu.VMEM(v.shape, v.dtype) for v in kept[keep:]]
    if held:
        scratch.append(pltpu.SemaphoreType.DMA((held,)))
    return pl.pallas_call(
        kernel,
        name=name or getattr(body, "func", body).__name__,
        out_shape=list(outs) + kept[:keep],
        in_specs=[pl.BlockSpec(memory_space=pltpu.SMEM)] * scalars
        + [pl.BlockSpec(memory_space=pltpu.HBM)] * held
        + [pl.BlockSpec(memory_space=pltpu.VMEM)] * (n_args - scalars - held)
        + [pl.BlockSpec(memory_space=pl.ANY)] * len(after),
        out_specs=[pl.BlockSpec() if out_blocks else pl.BlockSpec(memory_space=pltpu.VMEM)]
        * (len(outs) + keep),
        scratch_shapes=scratch,
        compiler_params=pltpu.CompilerParams(vmem_limit_bytes=limit * MIB),
        cost_estimate=NO_COST,
    )(*args, *after)


def iota(shape, dim):
    return lax.broadcasted_iota(jnp.int32, shape, dim)


def dot(a, b, precision=None):
    return jnp.dot(a, b, precision=precision, preferred_element_type=F32)


def head_spread(heads, channels):
    shape = (heads, channels)
    return (iota(shape, 1) // (channels // heads) == iota(shape, 0)).astype(F32)


def running_logs(dt_t_ref, rate_ref):
    logs = -rate_ref[...] * dt_t_ref[...].T
    tokens = logs.shape[0]
    tri = (iota((tokens, tokens), 0) >= iota((tokens, tokens), 1)).astype(F32)
    return dot(tri, logs, PRECISE)


def pack_kernel(ids_t_ref, residual_ref, out_ref):
    parts, rows, wide = out_ref.shape
    part = wide - 128
    ids = ids_t_ref[...].astype(F32).T
    lane = iota((rows, 128), 1)
    named = jnp.where(lane == 0, ids[:, 0:1], jnp.where(lane == 1, ids[:, 1:2], 0.0)).astype(BF16)
    for k in range(parts):
        out_ref[k, :, 0:part] = residual_ref[:, k * part : (k + 1) * part]
        out_ref[k, :, part:wide] = named


def state_kernel(place, x_ref, b_ref, dt_t_ref, rate_ref, init_ref, payload_ref, init_t_ref):
    tokens, channels = x_ref.shape
    heads = dt_t_ref.shape[0]
    width = b_ref.shape[1]
    cum = running_logs(dt_t_ref, rate_ref)
    total = cum[tokens - 1 : tokens, :]
    spread = head_spread(heads, channels)
    tail = dot(jnp.exp(total - cum), spread, PRECISE)
    scaled = (x_ref[...].astype(F32) * tail).astype(BF16)
    keys = b_ref[...].astype(F32).T.astype(BF16)
    own = dot(keys, scaled)
    decay = dot(jnp.broadcast_to(jnp.exp(total), (8, heads)), spread, PRECISE)
    init_t = init_ref[...].T
    init_t_ref[...] = init_t.astype(BF16)
    first = (place[0] == 0).astype(F32)
    payload_ref[0:width, :] = (own + first * (decay[0:1, :] * init_t)).astype(BF16)
    high = decay.astype(BF16).astype(F32)
    rows = iota((16, channels), 0)
    high16 = jnp.broadcast_to(high[0:1, :], (16, channels))
    low16 = jnp.broadcast_to(decay[0:1, :], (16, channels)) - high16
    payload_ref[width : width + 16, :] = jnp.where(
        rows == 0, high16, jnp.where(rows == 1, low16, 0.0)
    ).astype(BF16)


def intra_kernel(x_ref, z_ref, b_ref, c_ref, dt_t_ref, rate_ref, skip_ref, own_ref, fade_ref, token_ref):
    tokens, channels = x_ref.shape
    heads = dt_t_ref.shape[0]
    width = channels // heads
    token_ref[...] = jnp.zeros_like(token_ref)
    shape = (tokens, tokens)
    causal = iota(shape, 0) >= iota(shape, 1)
    cum = running_logs(dt_t_ref, rate_ref)
    cum_t = cum.T
    scores = lax.dot_general(
        c_ref[...], b_ref[...], (((1,), (1,)), ((), ())), preferred_element_type=F32
    )
    spread = head_spread(heads, channels)
    direct = dot(jnp.broadcast_to(skip_ref[...], (8, heads)), spread, PRECISE)[0:1, :]
    fade = dot(jnp.exp(cum), spread, PRECISE)
    per = 128 // width
    lane_head = iota((tokens, 128), 1) // width
    for group in range(heads // per):
        cols = slice(group * 128, (group + 1) * 128)
        x = x_ref[:, cols]
        total = x.astype(F32) * direct[:, cols]
        for k in range(per):
            h = group * per + k
            gap = jnp.where(causal, cum[:, h : h + 1] - cum_t[h : h + 1, :], -1e30)
            weights = (jnp.exp(gap) * scores).astype(BF16)
            part = dot(weights, x)
            total = total + jnp.where(lane_head == k, part, 0.0)
        z = z_ref[:, cols].astype(F32)
        gate = z / (1.0 + jnp.exp(-z))
        own_ref[:, cols] = total * gate
        fade_ref[:, cols] = fade[:, cols] * gate


def place_kernel(cap, experts, me, packed_ref, *refs):
    count = (len(refs) - 1) // 2
    out_ref = refs[count]
    for source, target in zip(refs[:count], refs[count + 1 :]):
        target[...] = source[...]
    blocks, rows, wide = packed_ref.shape
    tokens = blocks * rows
    slots = out_ref.shape[1] - rows
    ids = packed_ref[:, :, wide - 128 : wide].astype(F32).reshape(tokens, 128).T
    ids = ids[0:8, :].astype(jnp.int32)
    shape = (tokens, tokens)
    before = (iota(shape, 0) < iota(shape, 1)) & (iota(shape, 0) // rows == iota(shape, 1) // rows)
    named = iota((experts, tokens), 0) ^ me[0]
    hit = (ids[0:1, :] == named) | (ids[1:2, :] == named)
    rank = dot(hit.astype(BF16), before.astype(BF16)).astype(jnp.int32)
    block = (iota((experts, tokens), 1) // rows) ^ named
    whole = cap - 1
    row = jnp.where(rank < whole, block * whole + rank, blocks * whole + block)
    row = jnp.where(hit, row, -1)
    shape = (rows + slots, tokens)
    for e in range(experts):
        owned = ((me[0] ^ e) * rows + iota(shape, 0) == iota(shape, 1)) & (iota(shape, 0) < rows)
        placed = (iota(shape, 0) - rows == row[e : e + 1, :]) & (iota(shape, 0) >= rows)
        out_ref[e] = (owned | placed).astype(F32).astype(BF16)


def join_kernel(place, own_ref, other_ref, out_ref):
    width = out_ref.shape[0]
    odd = place[0] % 2 == 1
    own, other = own_ref[0:width, :].astype(F32), other_ref[0:width, :].astype(F32)
    own_decay = own_ref[width : width + 16, :].astype(F32)
    other_decay = other_ref[width : width + 16, :].astype(F32)
    own_decay = own_decay[0:1, :] + own_decay[1:2, :]
    other_decay = other_decay[0:1, :] + other_decay[1:2, :]
    early = jnp.where(odd, other, own)
    late = jnp.where(odd, own, other)
    decay = jnp.where(odd, own_decay, other_decay)
    out_ref[...] = (decay * early + late).astype(BF16)


def stream_kernel(
    place, c_ref, own_ref, fade_ref, init_t_ref, pair_ref, early_ref, res_ref, sel_ref, near_a_ref, near_b_ref, same_ref, other_ref
):
    width = init_t_ref.shape[0]
    at = place[0]
    zero = (at == 0).astype(F32)
    odd = (at % 2 == 1).astype(F32)
    pair = pair_ref[...].astype(F32)
    decay = pair[width : width + 1, :] + pair[width + 1 : width + 2, :]
    factor = jnp.where(at >= 2, jnp.where(at % 2 == 1, decay, 1.0), 0.0)
    entering = zero * init_t_ref[...].astype(F32) + odd * pair[0:width, :] + factor * early_ref[...].astype(F32)
    mixed = own_ref[...] + fade_ref[...] * dot(c_ref[...], entering.astype(BF16))
    mixer = mixed.astype(BF16).astype(F32)
    tokens, channels = mixer.shape
    residual = res_ref[:, :, 0:channels].astype(F32).reshape(tokens, channels)
    stream = (residual + mixer).astype(BF16)
    owned = sel_ref.shape[1] - near_a_ref.shape[0]
    near_a_ref[...] = dot(sel_ref[2, owned:, :], stream).astype(BF16)
    near_b_ref[...] = dot(sel_ref[3, owned:, :], stream).astype(BF16)
    for at, k in enumerate((0, 2, 3, 1)):
        same_ref[at] = dot(sel_ref[2 * k], stream).astype(BF16)
        other_ref[at] = dot(sel_ref[2 * k + 1], stream).astype(BF16)


def up_kernel(first, features, after, me, *refs):
    own, rx, ry, even, odd, gain, wg, wu = refs[:8]
    carry = () if first else refs[8:11]
    rest = refs[(8 if first else 11) + after :]
    sums = rest[2:5] if features else rest
    step = pl.program_id(0)
    steps = pl.num_programs(0)

    if first or features:

        @pl.when(step == 0)
        def _():
            for i, acc in enumerate(sums):
                acc[...] = jnp.zeros_like(acc) if first else carry[i][...]

    gate, up, square = sums
    slots = own.shape[1]
    rows = [r[0].astype(F32) for r in (own, rx, ry)]
    rows.append(jnp.where(step == 0, even[0].astype(F32), odd[0].astype(F32)))
    rows = jnp.concatenate(rows, axis=0)
    square[...] += jnp.broadcast_to(jnp.sum(rows * rows, axis=1, keepdims=True), square.shape)
    scaled = (rows * gain[0]).astype(BF16)
    gate[...] += dot(scaled, wg[0])
    up[...] += dot(scaled, wu[0])

    if features:
        outs, stages = rest[:2], rest[5:]

        @pl.when(step == steps - 1)
        def _():
            inverse = lax.rsqrt(square[:, 0:1] * (1.0 / features) + 1e-06)
            g = gate[...] * inverse
            active = g / (1.0 + jnp.exp(-g)) * (up[...] * inverse)
            main, ninths = slots // 9 * 8, slots // 9
            for d in range(4):
                at = d * slots
                stage, d, shards = (stages[0], 0, 1) if d == 3 else (stages[1], d, 3)
                stage[d * main : (d + 1) * main, :] = active[at : at + main]
                low = shards * main + d * ninths
                stage[low : low + ninths, :] = active[at + main : at + slots]
            for out, stage in zip(outs, stages):
                out[...] = stage[...].astype(BF16)


def up_project(group, last, me, near, far, gain, w_gate, w_up, carry, after=()):
    slots, part = near[0][0].shape[1:]
    hidden = w_gate.shape[2]
    total = 4 * slots
    source = lambda i, me: me[0] ^ (2 * group + i)
    rows = [
        pl.BlockSpec((1, slots, part), lambda i, me, start=start: (start + i, 0, 0))
        for _, start in near
    ] + [
        pl.BlockSpec((1, slots, part), lambda i, me, start=start: (start, 0, 0)) for _, start in far
    ]
    weight = pl.BlockSpec((1, part, hidden), lambda i, me: (source(i, me), 0, 0))
    in_place = pl.BlockSpec(memory_space=pltpu.VMEM)
    specs = rows + [pl.BlockSpec((1, 1, part), lambda i, me: (source(i, me), 0, 0)), weight, weight]
    sums = [
        jax.ShapeDtypeStruct((total, hidden), F32),
        jax.ShapeDtypeStruct((total, hidden), F32),
        jax.ShapeDtypeStruct((total, 128), F32),
    ]
    aliases = {}
    if carry is not None:
        specs += [in_place] * 3
        if not last:
            aliases = {9 + i: i for i in range(3)}
    specs += [pl.BlockSpec(memory_space=pl.ANY)] * len(after)
    sizes = (slots, 3 * slots)
    outs = [jax.ShapeDtypeStruct((n, hidden), BF16) for n in sizes] if last else sums
    scratch = [pltpu.VMEM(s.shape, s.dtype) for s in sums]
    scratch += [pltpu.VMEM((n, hidden), F32) for n in sizes]
    features = gain.shape[0] * part if last else 0
    return pl.pallas_call(
        functools.partial(up_kernel, carry is None, features, len(after)),
        name=f"up_{group}",
        out_shape=outs,
        grid_spec=pltpu.PrefetchScalarGridSpec(
            num_scalar_prefetch=1,
            grid=(2,),
            in_specs=specs,
            out_specs=[in_place] * len(outs),
            scratch_shapes=scratch if last else [],
        ),
        input_output_aliases=aliases,
        compiler_params=pltpu.CompilerParams(vmem_limit_bytes=48 * MIB),
        cost_estimate=NO_COST,
    )(me, *(array for array, _ in near + far), gain, w_gate, w_up, *(carry or ()), *after)


def cut_of(group):
    return 5 if group % 2 else 4


def down_kernel(groups, act_ref, w_ref, *refs):
    outs, (spare, held, sems) = refs[:-3], refs[-3:]
    step = pl.program_id(0)
    steps, _, tile = held.shape

    def load(k):
        columns = pl.ds(pl.multiple_of(k * tile, tile), tile)
        return pltpu.make_async_copy(w_ref.at[:, columns], held.at[k], sems.at[k])

    @pl.when(step == 0)
    def _():
        for k in range(steps):
            load(k).start()

    load(step).wait()
    part = dot(act_ref[...], held[step])
    ninths = part.shape[0] // 9
    main = part.shape[0] - ninths
    shards = ninths // (2 * groups)

    def through(group, tile):
        to_x, to_y = outs[2 * (group // 2) : 2 * (group // 2) + 2]
        cut = cut_of(group)
        return to_x, tile + (0 if group % 2 else 5), to_y, tile - cut + (0 if group % 2 else 4)

    for shard in range(shards):
        for group in range(groups):
            at = (shard * groups + group) * 16
            rows = part[at : at + 16, :].astype(BF16)
            if shards > 1:
                outs[shards * group + shard][step] = rows
                continue
            to_x, place_x, to_y, place_y = through(group, step)

            @pl.when(step < cut_of(group))
            def _():
                to_x[place_x] = rows

            @pl.when(step >= cut_of(group))
            def _():
                to_y[place_y] = rows

    for lanes in range(spare.shape[0]):
        spare[lanes, pl.ds(pl.multiple_of(step * ninths, 8), ninths), :] = part[
            main:, lanes * 128 : (lanes + 1) * 128
        ]

    @pl.when(step == steps - 1)
    def _():
        for shard in range(shards):
            for group in range(groups):
                pair = []
                for side in range(2):
                    row = pl.ds((shard * groups + group) * 2 + side, 8, stride=ninths)
                    ninth = [spare[lanes, row, :] for lanes in range(spare.shape[0])]
                    pair.append(jnp.concatenate(ninth, axis=1))
                pair = jnp.concatenate(pair, axis=0).astype(BF16)
                if shards > 1:
                    outs[shards * group + shard][8] = pair
                else:
                    _, _, to_y, place_y = through(group, 8)
                    to_y[place_y] = pair


def down_project(name, groups, active, w_down):
    total, hidden = active.shape
    features = w_down.shape[1]
    tile = features // 8
    outs = [jax.ShapeDtypeStruct((9, 16, tile), BF16)] * (total // 18)
    return pl.pallas_call(
        functools.partial(down_kernel, groups),
        name=name,
        grid=(8,),
        out_shape=outs,
        in_specs=[
            pl.BlockSpec(memory_space=pltpu.VMEM),
            pl.BlockSpec(memory_space=pltpu.HBM),
        ],
        out_specs=[pl.BlockSpec(memory_space=pltpu.VMEM)] * len(outs),
        scratch_shapes=[
            pltpu.VMEM((tile // 128, 8 * total // 9, 128), F32),
            pltpu.VMEM((8, hidden, tile), BF16),
            pltpu.SemaphoreType.DMA((8,)),
        ],
        compiler_params=pltpu.CompilerParams(vmem_limit_bytes=48 * MIB),
        cost_estimate=NO_COST,
    )(active, w_down)


def pair_kernel(same, other, own_stream, own, far_stream, far, last_stream, last, near_stream):
    owned = same.shape[1] - own.shape[1]
    for side, rows in enumerate((same, other)):
        own_stream[side, 0:owned, :], own[side] = rows[0, 0:owned, :], rows[0, owned:, :]
        far_stream[side, 0:owned, :], far[side] = rows[1, 0:owned, :], rows[1, owned:, :]
        last_stream[side, 0:owned, :], last[side] = rows[2, 0:owned, :], rows[2, owned:, :]
        near_stream[side, 0:owned, :] = rows[3, 0:owned, :]


def near_kernel(same, other, rows):
    rows[0], rows[1] = same[...], other[...]


def second_kernel(*refs):
    parts, out = refs[:-1], refs[-1]
    for h in range(out.shape[0]):
        for k in range(out.shape[1]):
            pair = [ref[k].astype(F32)[8:16] for ref in parts[2 * h : 2 * h + 2]]
            out[h, k] = jnp.concatenate(pair, axis=0).astype(BF16)


def hold_kernel(*refs):
    for source, target in zip(refs[: len(refs) // 2], refs[len(refs) // 2 :]):
        target[...] = source[...]


def half_message_kernel(rx, ry, out_x, out_y):
    out_x[0], out_y[0] = ry[1], rx[0]


def join_message_kernel(own, rx, ry, out_x, out_y):
    out_x[0:2], out_y[0:2] = own[...], own[...]
    out_x[2], out_y[2] = ry[1], rx[0]


def relay_kernel(through_x, through_y, *refs):
    ahead = refs[4 : 4 + (len(refs) - 8) // 2]
    outs, copies = refs[4 + len(ahead) :][:4], refs[8 + len(ahead) :]
    for group in range(2):
        cut = cut_of(group)
        at_x, at_y = (0, -cut) if group else (5, 0)
        for own, out, through, tiles, at in (
            (refs[2 * group], outs[2 * group], through_y, range(cut, 9), at_y),
            (refs[2 * group + 1], outs[2 * group + 1], through_x, range(cut), at_x),
        ):
            for k in range(9):
                if k in tiles:
                    out[k] = (own[k].astype(F32) + through[k + at].astype(F32)).astype(BF16)
                else:
                    out[k] = own[k]
    for source, copy in zip(ahead, copies):
        copy[...] = source[...]


def finish_kernel(own, rx, ry, *refs):
    ahead = refs[: (len(refs) - 1) // 2]
    out, copies = refs[len(ahead)], refs[len(ahead) + 1 :]
    for k in range(9):
        out[k] = (own[k].astype(F32) + rx[k].astype(F32) + ry[k].astype(F32)).astype(BF16)
    for source, copy in zip(ahead, copies):
        copy[...] = source[...]


def mix_kernel(me, ids_t_ref, weight_t_ref, swap_ref, *refs):
    groups = (len(refs) - 1) // 2
    firsts, streams, out_ref = refs[:groups], refs[groups:-1], refs[-1]
    rows = ids_t_ref.shape[1]
    experts = 2 * groups
    pieces = firsts[0].shape[0] - 1
    tile = firsts[0].shape[2]
    ids, weights = ids_t_ref[...].T, weight_t_ref[...].T
    named = iota((rows, experts), 1) ^ me[0]
    first, second = ids[:, 0:1] == named, ids[:, 1:2] == named
    weight = jnp.where(first, weights[:, 0:1], jnp.where(second, weights[:, 1:2], 0.0))
    hit = (first | second).astype(F32)
    before = (iota((rows, rows), 0) > iota((rows, rows), 1)).astype(F32)
    rank = dot(before, hit)
    lanes = 2 * experts * 8
    shape = (experts, lanes)
    spread = ((iota(shape, 1) // 8) % experts == iota(shape, 0)).astype(F32)
    weight = dot(weight, spread, PRECISE)
    rank = dot(rank, spread, PRECISE).astype(jnp.int32)
    lane = iota((rows, lanes), 1)
    main = (lane < experts * 8) & (rank == lane % 8)
    extra = (lane >= experts * 8) & (rank == 8)

    def rows_of(k):
        data = []
        for g in range(groups):
            data.append(firsts[g][k].astype(F32)[0:8])
            data.append(swap_ref[g // 2, k].astype(F32)[g % 2 * 8 : g % 2 * 8 + 8])
        return data

    last = rows_of(pieces)
    for m in range(experts):
        k = me[0] ^ m
        coef = jnp.where(main | (extra & (lane % 8 == k)), weight, 0.0)
        high = coef.astype(BF16)
        low = (coef - high.astype(F32)).astype(BF16)
        data = jnp.concatenate(rows_of(k) + last, axis=0).astype(BF16)
        stream = streams[m // 2][m % 2, 0:rows, :].astype(F32)
        out_ref[:, pl.ds(pl.multiple_of(k * tile, 128), tile)] = (
            stream + (dot(high, data) + dot(low, data))
        ).astype(BF16)


def on_square(
    x_in,
    z_gate,
    b_in,
    c_out,
    dt_step,
    rate,
    skip,
    init_state,
    residual,
    norm_gain,
    expert_ids,
    gate_weights,
    w_gate,
    w_up,
    w_down,
):
    tokens, channels = x_in.shape
    heads = rate.shape[0]
    state = b_in.shape[1]
    owners = lax.axis_size("exp")
    rows, features = residual.shape
    experts = owners
    cap = max(2, 2 * rows // experts + 1)
    slots = owners * cap
    at = lax.axis_index("seq")
    me = lax.axis_index("exp")
    place = jnp.reshape(at, (1,)).astype(jnp.int32)
    self_id = jnp.reshape(me, (1,)).astype(jnp.int32)

    def over_x(v):
        return lax.ppermute(v, "seq", [(i, i ^ 1) for i in range(4)])

    def over_y(v):
        return lax.ppermute(v, "seq", [(i, i ^ 2) for i in range(4)])

    def along(v, mask):
        return lax.ppermute(v, "exp", [(i, i ^ mask) for i in range(owners)])

    rate_row = rate[None, :]
    dt_t = dt_step.T
    ids_t = expert_ids.T
    packed = block_call(
        pack_kernel,
        [jax.ShapeDtypeStruct((owners, rows, channels + 128), BF16)],
        0,
        (ids_t, residual),
        held=2,
        limit=48,
    )[0]
    packed = lax.all_to_all(packed, "exp", split_axis=0, concat_axis=0, tiled=True)
    payload, init_t = block_call(
        state_kernel,
        [
            jax.ShapeDtypeStruct((state + 16, channels), BF16),
            jax.ShapeDtypeStruct((state, channels), BF16),
        ],
        1,
        (place, x_in, b_in, dt_t, rate_row, init_state.reshape(channels, state)),
        held=5,
        limit=62,
    )
    pair = over_x(payload)
    own_part, fade, token = block_call(
        intra_kernel,
        [
            jax.ShapeDtypeStruct((tokens, channels), F32),
            jax.ShapeDtypeStruct((tokens, channels), F32),
            jax.ShapeDtypeStruct((8, 128), F32),
        ],
        0,
        (x_in, z_gate, b_in, c_out, dt_t, rate_row, skip[None, :]),
        held=7,
        limit=61,
    )
    joined = block_call(
        join_kernel,
        [jax.ShapeDtypeStruct((state, channels), BF16)],
        1,
        (place, payload, pair),
        after=(token,),
    )[0]
    early = over_y(joined)
    handed = (own_part, fade, c_out, init_t)
    select, own_part, fade, c, init_t = block_call(
        functools.partial(place_kernel, cap, experts),
        [jax.ShapeDtypeStruct((experts, rows + slots, tokens), BF16)]
        + [jax.ShapeDtypeStruct(v.shape, v.dtype) for v in handed],
        1,
        (self_id, packed, *handed),
        after=(joined,),
    )
    groups = owners // 2
    lanes = jax.ShapeDtypeStruct((groups, rows + slots, channels), BF16)
    one = jax.ShapeDtypeStruct((slots, channels), BF16)
    near_a, near_b, same, other = block_call(
        stream_kernel,
        [one, one, lanes, lanes],
        1,
        (place, c, own_part, fade, init_t, pair, early, packed, select),
    )

    gain = norm_gain.reshape(owners, 1, channels)
    wg = w_gate.reshape(owners, channels, w_gate.shape[2])
    wu = w_up.reshape(owners, channels, w_up.shape[2])
    expert_rows = jax.ShapeDtypeStruct((2, slots, channels), BF16)
    stream_rows = jax.ShapeDtypeStruct((2, 40, channels), BF16)
    near_a, near_b = along(near_a, 2), along(near_b, 3)
    stream0, first, stream2, far, stream3, farthest, stream1 = block_call(
        pair_kernel,
        [stream_rows, expert_rows] * 3 + [stream_rows],
        0,
        (same, along(other, 1)),
    )
    gain = norm_gain.reshape(owners, 1, channels)
    wg = w_gate.reshape(owners, channels, w_gate.shape[2])
    wu = w_up.reshape(owners, channels, w_up.shape[2])
    gain = norm_gain.reshape(owners, 1, channels)
    wg = w_gate.reshape(owners, channels, w_gate.shape[2])
    wu = w_up.reshape(owners, channels, w_up.shape[2])

    def hold(values, after, name):
        outs = [jax.ShapeDtypeStruct(v.shape, BF16) for v in values]
        return block_call(hold_kernel, outs, 0, values, after=after, name=name)

    def project(group, near, far, carry, after=()):
        last = group == groups - 1
        return up_project(group, last, self_id, near, far, gain, wg, wu, carry, after)

    def message(count):
        return [jax.ShapeDtypeStruct((count, slots, channels), BF16)] * 2

    far = along(far, 4)
    rx0, ry0 = over_x(first), over_y(first)
    near = block_call(near_kernel, [expert_rows], 0, (near_a, near_b))[0]
    rx1, ry1 = over_x(near), over_y(near)
    to_x, to_y = block_call(
        half_message_kernel, message(1), 0, (rx0, ry0), after=(near,), name="half_0"
    )
    fx0, fy0 = over_x(to_x), over_y(to_y)
    farthest_held = hold((farthest,), (far,), "hold_farthest")[0]
    farthest = along(farthest_held, 6)
    to_x, to_y = block_call(
        join_message_kernel,
        message(3),
        0,
        (far, rx1, ry1),
        after=(fx0, fy0, farthest_held),
        name="join_2",
    )
    rx2, ry2 = over_x(to_x), over_y(to_y)
    carry = project(0, [(first, 0), (rx0, 0), (ry0, 0)], [(fy0, 0), (fx0, 0)], None)
    to_x, to_y = block_call(
        join_message_kernel, message(3), 0, (farthest, rx2, ry2), after=(carry[2],), name="join_3"
    )
    rx3, ry3 = over_x(to_x), over_y(to_y)
    held = hold((stream1, stream2, stream3), (to_x,), "hold_streams")
    stream1, stream2, stream3 = (along(v, 2 * g + 2) for g, v in enumerate(held))
    carry = project(1, [(near, 0), (rx1, 0), (ry1, 0)], [(ry2, 2), (rx2, 2)], carry, held[:1])
    to_x, to_y = block_call(
        half_message_kernel, message(1), 0, (rx3, ry3), after=(carry[2],), name="half_3"
    )
    fx3, fy3 = over_x(to_x), over_y(to_y)
    carry = project(2, [(far, 0), (rx2, 0), (ry2, 0)], [(ry3, 2), (rx3, 2)], carry)
    active_far, active = project(
        3,
        [(farthest, 0), (rx3, 0), (ry3, 0)],
        [(fy3, 0), (fx3, 0)],
        carry,
        (stream1, stream2, stream3),
    )

    wd = w_down.reshape(w_down.shape[1], features)
    tiles = jax.ShapeDtypeStruct((9, 16, features // 8), BF16)
    sent = down_project("down_through", groups, active_far, wd)
    rest = down_project("down_rest", groups, active, wd)
    own, own_x, own_y = ([rest[3 * g + k] for g in range(groups)] for k in range(3))

    def relay(name, through_x, through_y, low, ahead=(), after=()):
        shares = (own_x[low], own_y[low], own_x[low + 1], own_y[low + 1])
        return block_call(
            relay_kernel,
            [tiles] * (4 + len(ahead)),
            0,
            (through_x, through_y, *shares, *ahead),
            after=after,
            name=name,
        )

    def finish(group, rx, ry, ahead=(), after=()):
        return block_call(
            finish_kernel,
            [tiles] * (1 + len(ahead)),
            0,
            (own[group], rx, ry, *ahead),
            after=after,
            name=f"finish_{group}",
        )

    through_x, through_y = over_x(sent[2]), over_y(sent[3])
    x2, y2, x3, y3, next_x, next_y = relay(
        "relay_far", through_x, through_y, 2, (sent[0], sent[1])
    )
    rx3, ry3 = over_x(x3), over_y(y3)
    through_x, through_y = over_x(next_x), over_y(next_y)
    both3, x2, y2 = finish(3, rx3, ry3, (x2, y2))
    back3 = along(both3, 6)
    rx2, ry2 = over_x(x2), over_y(y2)
    x0, y0, x1, y1 = relay("relay_near", through_x, through_y, 0, after=(both3,))
    rx1, ry1 = over_x(x1), over_y(y1)
    both2, x0, y0 = finish(2, rx2, ry2, (x0, y0))
    back2 = along(both2, 4)
    rx0, ry0 = over_x(x0), over_y(y0)
    back1 = along(finish(1, rx1, ry1, after=(back3,))[0], 2)
    back = [finish(0, rx0, ry0)[0], back1, back2, back3]
    swap = block_call(second_kernel, [jax.ShapeDtypeStruct((2,) + tiles.shape, BF16)], 0, back)[0]
    swap = along(swap, 1)
    return block_call(
        mix_kernel,
        [jax.ShapeDtypeStruct((rows, features), BF16)],
        1,
        (self_id, ids_t, gate_weights.T, swap, *back, stream0, stream1, stream2, stream3),
    )[0]


def entering_2(array, axis, combine, identity):
    devices, mine = (lax.axis_size(axis), lax.axis_index(axis))
    everything = jax.tree.map(
        lambda part, kind: lax.all_gather(part.astype(kind), axis),
        array,
        (jnp.bfloat16, jnp.bfloat16),
    )
    start = jax.tree.map(
        lambda part, zero: jnp.broadcast_to(jnp.asarray(zero, part.dtype), part.shape),
        array,
        identity,
    )

    def hop(k, before):
        reached = k < mine
        new = combine(
            before, jax.tree.map(lambda part, own: part[k].astype(own.dtype), everything, array)
        )
        return jax.tree.map(lambda a, b: jnp.where(reached, a, b), new, before)

    return lax.fori_loop(0, devices, hop, start)


def chain_combine(earlier, later):
    return (earlier[0] + later[0], jnp.exp(later[0])[:, None, None] * earlier[1] + later[1])


def on_device(
    x_in,
    z_gate,
    b_in,
    c_out,
    dt_step,
    rate,
    skip,
    init_state,
    residual,
    norm_gain,
    expert_ids,
    gate_weights,
    w_gate,
    w_up,
    w_down,
):
    token_count, channels = x_in.shape
    heads_here = rate.shape[0]
    head_width = channels // heads_here
    state_width = b_in.shape[1]
    blocks = token_count // GROUP
    inputs = x_in.astype(jnp.float32).reshape(blocks, GROUP, heads_here, head_width)
    keys_in = b_in.astype(jnp.float32).reshape(blocks, GROUP, state_width)
    queries = c_out.astype(jnp.float32).reshape(blocks, GROUP, state_width)
    log_steps = (-rate[None, :] * dt_step).reshape(blocks, GROUP, heads_here)
    cumulative = jnp.cumsum(log_steps, axis=1)
    scores = jnp.einsum("ctn,csn->cts", queries, keys_in, precision=PRECISE)
    causal = jnp.arange(GROUP)[:, None] >= jnp.arange(GROUP)[None, :]
    spread = cumulative[:, :, None, :] - cumulative[:, None, :, :]
    weights = jnp.exp(jnp.where(causal[None, :, :, None], spread, -jnp.inf)) * scores[..., None]
    intra_out = jnp.einsum("ctsh,cshp->cthp", weights, inputs, precision=PRECISE)
    tail_decay = jnp.exp(cumulative[:, -1:, :] - cumulative)
    block_state = jnp.einsum("csh,cshp,csn->chpn", tail_decay, inputs, keys_in, precision=PRECISE)
    block_log = cumulative[:, -1, :]

    def advance(carried, element):
        total_log, total_state = carried
        step_log, step_state = element
        updated = (
            total_log + step_log,
            jnp.exp(step_log)[:, None, None] * total_state + step_state,
        )
        return (updated, (total_log, total_state))

    zero_state = jnp.zeros((heads_here, head_width, state_width), jnp.float32)
    zero_log = jnp.zeros((heads_here,), jnp.float32)
    (device_log, device_state), (enter_log, enter_state) = lax.scan(
        advance, (zero_log, zero_state), (block_log, block_state)
    )
    prior_log, prior_state = entering_2(
        (device_log, device_state), "seq", chain_combine, (zero_log, zero_state)
    )
    incoming = prior_state + jnp.exp(prior_log)[:, None, None] * init_state
    entering = enter_state + jnp.exp(enter_log)[:, :, None, None] * incoming[None]
    inter_out = jnp.exp(cumulative)[..., None] * jnp.einsum(
        "chpn,ctn->cthp", entering, queries, precision=PRECISE
    )
    mixed_out = (intra_out + inter_out + skip[None, None, :, None] * inputs).reshape(
        token_count, channels
    )
    mixer = (mixed_out * jax.nn.silu(z_gate.astype(jnp.float32))).astype(jnp.bfloat16)
    token_mix = lax.all_to_all(mixer, "exp", split_axis=0, concat_axis=1, tiled=True)
    stream = (residual.astype(jnp.float32) + token_mix.astype(jnp.float32)).astype(jnp.bfloat16)
    widened = stream.astype(jnp.float32)
    normed = (
        widened
        * lax.rsqrt(jnp.mean(widened * widened, axis=-1, keepdims=True) + 1e-06)
        * norm_gain[None, :]
    ).astype(jnp.bfloat16)
    rows_here = residual.shape[0]
    owners = lax.axis_size("exp")
    local_experts = w_gate.shape[0]
    experts = owners * local_experts
    capacity = max(2, 2 * rows_here // experts + 1)
    width = residual.shape[1]
    chosen = expert_ids.reshape(-1)
    onehot = (chosen[:, None] == jnp.arange(experts)[None, :]).astype(jnp.int32)
    slot_index = jnp.sum((jnp.cumsum(onehot, axis=0) - onehot) * onehot, axis=1)
    target = chosen * capacity + slot_index
    placing = (target[None, :] == jnp.arange(experts * capacity)[:, None]).astype(jnp.bfloat16)
    pair_rows = jnp.repeat(normed, 2, axis=0)
    outgoing = jnp.dot(placing, pair_rows, preferred_element_type=jnp.float32).astype(jnp.bfloat16)
    outgoing = outgoing.reshape(owners, local_experts, 1, capacity, width)
    arrived = lax.all_to_all(outgoing, "exp", split_axis=0, concat_axis=2, tiled=True)
    segment = lax.all_gather(arrived, "seq", axis=1, tiled=True)
    flattened = segment.reshape(segment.shape[0], -1, segment.shape[-1])
    gate_proj = jnp.einsum("erd,edf->erf", flattened, w_gate, preferred_element_type=jnp.float32)
    up_proj = jnp.einsum("erd,edf->erf", flattened, w_up, preferred_element_type=jnp.float32)
    active = (jax.nn.silu(gate_proj) * up_proj).astype(jnp.bfloat16)
    partial_value = jnp.einsum("erf,efd->erd", active, w_down, preferred_element_type=jnp.float32)
    partials = partial_value.reshape(segment.shape[:-1] + (partial_value.shape[-1],))
    summed = lax.psum_scatter(partials.astype(jnp.bfloat16), "seq", scatter_dimension=1, tiled=True)
    returned = lax.all_to_all(summed, "exp", split_axis=2, concat_axis=0, tiled=True)
    results = returned.reshape(experts * capacity, width)
    picked = results[target].astype(jnp.float32).reshape(rows_here, 2, width)
    mixture = jnp.sum(picked * gate_weights[:, :, None], axis=1)
    return (widened + mixture).astype(jnp.bfloat16)


def solution(mesh):
    square = mesh.shape["seq"] == 4 and mesh.shape["exp"] == 8

    def body(*args):
        rows = args[8].shape[0]
        experts = mesh.shape["exp"] * args[12].shape[0]
        fits = args[12].shape[0] == 1 and 2 * rows // experts + 1 == 9
        return (on_square if square and fits else on_device)(*args)

    return jax.shard_map(
        body,
        mesh=mesh,
        in_specs=(
            P("seq", "exp"),
            P("seq", "exp"),
            P("seq", None),
            P("seq", None),
            P("seq", "exp"),
            P("exp"),
            P("exp"),
            P("exp", None, None),
            P(("seq", "exp"), None),
            P(),
            P(("seq", "exp"), None),
            P(("seq", "exp"), None),
            P("exp", None, "seq"),
            P("exp", None, "seq"),
            P("exp", "seq", None),
        ),
        out_specs=P(("seq", "exp"), None),
        check_vma=False,
    )
```
